32 devices in a mesh: groups: 2 (over x), tensor: 16 (over z, y, core).
Axes of the slice: x: 2, y: 2, z: 4, core: 2. Of those that a mesh axis runs over, the one named last changes fastest.
Arguments:
- tokens: bfloat16 [1536, 16384], P(('groups', 'tensor')), parts along dimension 0, may hold values from -6 to 6
- weight_codes: bfloat16 [16384, 16384], P(None, 'tensor'), may hold values from -127 to 127, as said below
- column_scale: float32 [16384], P('tensor'), may hold values from 4.6875e-05 to 0.0001875
- shrink_store: bfloat16 [32, 16384, 64], P(('groups', 'tensor')), parts along dimension 0, may hold values from -0.046875 to 0.046875
- expand_store: bfloat16 [32, 16384, 64], P('groups', 'tensor'), parts along dimension 0, may hold values from -0.75 to 0.75
- row_adapter: int32 [1536], P('groups'), parts along dimension 0, may hold values from 0 to 15, as said below
- placement: int32 [32], P('groups'), parts along dimension 0, may hold values from 0 to 15, each once
- document_lengths: int32 [16], P('groups'), parts along dimension 0, may hold values from 1 to 384, 768 in all
Outputs:
- queries: bfloat16 [1536, 16384], P('groups', 'tensor'), parts along dimension 0
The draws below stay inside these ranges and needn't reach their ends.
There are 2 independent parts, one for each index of `groups`. The reference program is written for one: setup_inputs(seed, part) draws one part's arguments, and reference() takes and returns one part's arrays. A program takes and returns all parts, laid end to end along the dimension named above; an argument that names none is the same for every part. Nothing has to cross between parts.
Inputs may be any that keep to these rules, and one draw needn't show every extreme that they name: `weight_codes`: every entry is a whole number. `row_adapter`: constant on each aligned block of 128 rows and never falling from row to row.
All inputs are finite; a program needn't handle non-finite values.
Results may differ from the reference program's by a relative error of at most 0.0039.
Values may be sent and summed in bfloat16 or wider, within the bound.
No kernel may reach another device: no remote copies, remote signals or barrier semaphores. Data moves between devices by JAX's collectives and lax.ppermute only.
A program may use at most 192 MiB of HBM per device.

```python
import math
import jax
import jax.numpy as jnp
import numpy as np
from jax import lax

HD = 128
D = 16384
RANK = 64
SEG = 128
SEGS = 6
TOK = 768
ADAPTERS = 16
DOCS = 8
MOST = 384


def draw_weight_codes(key, part):
    key = jax.random.fold_in(key, 11)
    return jax.random.randint(key, (D, D), -127, 128).astype(jnp.bfloat16)


def draw_row_adapter(key, part):
    key = jax.random.fold_in(key, 37)
    first_key, second_key = jax.random.split(key)
    picks = jnp.minimum(jax.random.randint(first_key, (SEGS,), 0, ADAPTERS), jax.random.randint(second_key, (SEGS,), 0, ADAPTERS))
    ordered = jnp.sort(picks)
    return jnp.repeat(ordered, SEG, total_repeat_length=SEGS * SEG).astype(jnp.int32)


def shard_levels(stream_key, dims, pieces, low, high):
    loudness = 1.0
    for dim, shards_of in pieces:
        draws = jax.random.uniform(jax.random.fold_in(jax.random.fold_in(stream_key, 6), dim), (shards_of,), jnp.float32, low / len(pieces), high / len(pieces))
        loudness = loudness * jnp.repeat(jnp.exp(draws), dims[dim] // shards_of).reshape((-1,) + (1,) * (len(dims) - 1 - dim))
    return loudness


def split_up(number_of, total, bound, slope):
    weights = [(1 << 20) // math.isqrt(standing ** slope) + 1 for standing in range(2, number_of + 1)]
    rest, given = total - bound - (number_of - 1), [1] * (number_of - 1)
    while rest > 0:
        candidates = [i for i in range(number_of - 1) if given[i] < bound]
        pool, budget = sum([weights[i] for i in candidates]), rest
        for i in candidates:
            extra = min(bound - given[i], max(1, budget * weights[i] // pool), rest)
            given[i] = given[i] + extra
            rest = rest - extra
    return np.array([bound] + given)


def uneven(key, amount, total, most, lean):
    if amount == 2:
        one = jax.random.randint(key, (), max(1, total - most), min(most, total - 1) + 1)
        return jnp.stack([one, total - one])
    tallies = jnp.asarray(split_up(amount, total, most, lean), jnp.int32)
    couples = (amount - 1) // 2
    giver, sink = tallies[1:1 + 2 * couples:2], tallies[2:2 + 2 * couples:2]
    room = jnp.minimum(giver - 1, most - sink)
    shifted = jax.random.randint(jax.random.fold_in(key, 1), (couples,), 0, 1 << 20) % (room + 1)
    tallies = tallies.at[1:1 + 2 * couples:2].set(giver - shifted).at[2:2 + 2 * couples:2].set(sink + shifted)
    return tallies[jax.random.permutation(jax.random.fold_in(key, 2), amount)]


def centred(own_key, extent, width, reach, cuts=(), kind=jnp.bfloat16):
    level = shard_levels(own_key, extent, cuts, -0.22, 0.18) if cuts else 1.0
    array = jax.random.normal(own_key, extent, jnp.float32) * width * level
    return jnp.minimum(jnp.maximum(array, -reach), reach).astype(kind)


def setup_inputs(seed: int = 0, part: int = 0) -> dict:
    streams_of = jax.random.split(jax.random.key(seed), 9)
    part_splits = jax.random.split(jax.random.fold_in(streams_of[8], part), 9)
    tokens = centred(part_splits[0], (TOK, D), 1.0, 6.0, ((0, 16),))
    weight_codes = draw_weight_codes(jax.random.fold_in(streams_of[8], 71), part)
    column_scale = jnp.clip(jnp.exp(math.log(0.0001875) - 1.3862944 * jax.random.uniform(streams_of[2], (D,), jnp.float32) ** shard_levels(streams_of[2], (D,), ((0, 16),), -0.2, 0.2)), 4.6875000407453626e-05, 0.0001875)
    shrink_store = centred(part_splits[3], (ADAPTERS, D, RANK), D ** -0.5, 0.046875, ((0, 16),))
    expand_store = centred(part_splits[4], (ADAPTERS, D, RANK), RANK ** -0.5, 0.75, ((1, 16),))
    row_adapter = draw_row_adapter(jax.random.fold_in(jax.random.fold_in(streams_of[8], part), 71), part)
    placement = jax.random.permutation(part_splits[6], ADAPTERS).astype(jnp.int32)
    document_lengths = uneven(part_splits[7], DOCS, TOK, MOST, 2).astype(jnp.int32)
    return dict(tokens=tokens, weight_codes=weight_codes, column_scale=column_scale, shrink_store=shrink_store, expand_store=expand_store, row_adapter=row_adapter, placement=placement, document_lengths=document_lengths)


def row_positions(document_lengths, total_rows):
    ends = jnp.cumsum(document_lengths).astype(jnp.int32)
    row_index = jnp.arange(total_rows, dtype=jnp.int32)
    passed = (row_index[:, None] >= ends[None, :]).astype(jnp.int32)
    return row_index - jnp.sum(passed * document_lengths[None, :], axis=1).astype(jnp.int32)


def rotary(values, positions, head_size):
    total_rows = values.shape[0]
    half_size = head_size // 2
    freq_index = jnp.arange(half_size, dtype=jnp.float32)
    inverse = jnp.exp(freq_index * (-2.0 / head_size) * jnp.log(jnp.float32(500000.0)))
    angles = positions.astype(jnp.float32)[:, None] * inverse[None, :]
    cosine = jnp.cos(angles)[:, None, :]
    sine_part = jnp.sin(angles)[:, None, :]
    shaped = values.reshape(total_rows, -1, head_size)
    first = shaped[..., :half_size]
    second = shaped[..., half_size:]
    turned = jnp.concatenate([first * cosine - second * sine_part, second * cosine + first * sine_part], axis=-1)
    return turned.reshape(total_rows, -1)


def reference(tokens, weight_codes, column_scale, shrink_store, expand_store, row_adapter, placement, document_lengths):
    projected = jnp.dot(tokens, weight_codes, preferred_element_type=jnp.float32) * column_scale[None, :]
    segment_slot = placement[row_adapter[::SEG]].astype(jnp.int32)
    shrink_used = shrink_store[segment_slot].astype(jnp.float32)
    expand_used = expand_store[segment_slot].astype(jnp.float32)
    blocks = tokens.reshape(-1, SEG, D).astype(jnp.float32)
    shrunk = jnp.einsum("sqd,sdr->sqr", blocks, shrink_used).astype(jnp.bfloat16)
    shrunk = lax.optimization_barrier(shrunk).astype(jnp.float32)
    update = jnp.einsum("sqr,scr->sqc", shrunk, expand_used).reshape(TOK, D)
    positions = row_positions(document_lengths, TOK)
    return rotary(projected + update, positions, HD).astype(jnp.bfloat16)
```

```python
import functools

import jax
import jax.numpy as jnp
from jax import lax
from jax.experimental import pallas as pl
from jax.experimental.pallas import tpu as pltpu
from jax.sharding import PartitionSpec as P

HD = 128
SEG = 128
VMEM = 48 * 1024 * 1024
F32 = jnp.float32
NT = (((1,), (1,)), ((), ()))


def row_positions(document_lengths, total_rows):
    ends = jnp.cumsum(document_lengths)
    row_index = jnp.arange(total_rows, dtype=jnp.int32)
    passed = (row_index[:, None] >= ends[None, :]).astype(jnp.int32)
    return row_index - jnp.sum(passed * document_lengths[None, :], axis=1)


def rotary_tables(positions):
    half_size = HD // 2
    freq_index = jnp.arange(half_size, dtype=F32)
    inverse = jnp.exp(freq_index * (-2.0 / HD) * jnp.log(F32(500000.0)))
    angles = positions.astype(F32)[:, None] * inverse[None, :]
    cosine, sine = jnp.cos(angles), jnp.sin(angles)
    return jnp.concatenate([cosine, cosine], 1), jnp.concatenate([-sine, sine], 1)


def shrink_kernel(x_ref, s_ref, h_in, h_out):
    @pl.when(pl.program_id(0) == 0)
    def _():
        h_out[...] = h_in[...]

    h_out[...] += lax.dot_general(x_ref[...], s_ref[...], NT, preferred_element_type=F32)


def shrink_chunk(x, shrink, offset, tile, h):
    rows, depth = x.shape
    rank = shrink.shape[0]
    whole = pl.BlockSpec((rows, rank), lambda k: (0, 0))
    return pl.pallas_call(
        shrink_kernel,
        grid=(depth // tile,),
        in_specs=[
            pl.BlockSpec((rows, tile), lambda k: (0, k)),
            pl.BlockSpec((rank, tile), lambda k: (0, k + offset // tile)),
            whole,
        ],
        out_specs=whole,
        out_shape=jax.ShapeDtypeStruct((rows, rank), F32),
        compiler_params=pltpu.CompilerParams(vmem_limit_bytes=VMEM),
        cost_estimate=pl.CostEstimate(
            flops=2 * rows * depth * 256, bytes_accessed=2 * rows * depth, transcendentals=0
        ),
        name="shrink",
    )(x, shrink, h)


def project_kernel(first, x_ref, w_ref, *refs):
    acc_out = refs[-1]

    @pl.when(pl.program_id(0) == 0)
    def _():
        acc_out[...] = jnp.zeros_like(acc_out) if first else refs[0][...]

    acc_out[...] += jnp.dot(x_ref[...], w_ref[...], preferred_element_type=F32)


def project_chunk(x, weights, offset, tile, acc):
    rows, depth = x.shape
    cols = weights.shape[1]
    whole = pl.BlockSpec((rows, cols), lambda k: (0, 0))
    first = acc is None
    return pl.pallas_call(
        functools.partial(project_kernel, first),
        grid=(depth // tile,),
        in_specs=[
            pl.BlockSpec((rows, tile), lambda k: (0, k)),
            pl.BlockSpec((tile, cols), lambda k: (k + offset // tile, 0)),
        ]
        + ([] if first else [whole]),
        out_specs=whole,
        out_shape=jax.ShapeDtypeStruct((rows, cols), F32),
        compiler_params=pltpu.CompilerParams(vmem_limit_bytes=VMEM),
        cost_estimate=pl.CostEstimate(
            flops=2 * rows * depth * cols, bytes_accessed=2 * depth * cols, transcendentals=0
        ),
        name="project",
    )(*((x, weights) if first else (x, weights, acc)))


def finish_kernel(acc_ref, scale_ref, h_ref, expand_ref, cos_ref, sin_ref, out_ref):
    update = jnp.dot(h_ref[...], expand_ref[0], preferred_element_type=F32)
    cosine, sine = cos_ref[...], sin_ref[...]
    for head in range(out_ref.shape[1] // HD):
        cut = slice(head * HD, (head + 1) * HD)
        value = acc_ref[:, cut] * scale_ref[:, cut] + update[:, cut]
        turned = value * cosine + pltpu.roll(value, HD // 2, 1) * sine
        out_ref[:, cut] = turned.astype(out_ref.dtype)


def finish(acc, scale, h, expand, cosine, sine):
    rows, cols = acc.shape
    rank = h.shape[1]
    return pl.pallas_call(
        finish_kernel,
        grid=(rows // SEG,),
        in_specs=[
            pl.BlockSpec((SEG, cols), lambda r: (r, 0)),
            pl.BlockSpec((1, cols), lambda r: (0, 0)),
            pl.BlockSpec((SEG, rank), lambda r: (r, 0)),
            pl.BlockSpec((1, rank, cols), lambda r: (r, 0, 0)),
            pl.BlockSpec((SEG, HD), lambda r: (r, 0)),
            pl.BlockSpec((SEG, HD), lambda r: (r, 0)),
        ],
        out_specs=pl.BlockSpec((SEG, cols), lambda r: (r, 0)),
        out_shape=jax.ShapeDtypeStruct((rows, cols), jnp.bfloat16),
        compiler_params=pltpu.CompilerParams(vmem_limit_bytes=VMEM),
        name="finish",
    )(acc, scale, h, expand, cosine, sine)


def spread(h, parts):
    step = 1
    while step < parts:
        pairs = [(i, i ^ step) for i in range(parts)]
        h = h + lax.ppermute(h, "tensor", pairs)
        step *= 2
    return h


def body(parts, tokens, weight_codes, column_scale, shrink_store, expand_store, row_adapter, placement, document_lengths):
    depth = tokens.shape[1]
    cuts = [0, 5 * depth // 16, 10 * depth // 16, 14 * depth // 16, depth]
    tile = depth // 16
    shard_index = lax.axis_index("tensor")
    total_rows = tokens.shape[0] * parts
    held = shrink_store.shape[0]
    rank = shrink_store.shape[2]
    segment_slot = placement[row_adapter[::SEG]]
    shrinks = jnp.swapaxes(shrink_store, 1, 2)
    expand = jnp.swapaxes(expand_store, 1, 2)[segment_slot]
    cosine, sine = rotary_tables(row_positions(document_lengths, total_rows))

    acc = None
    hs = [jnp.zeros((total_rows, rank), F32) for _ in range(held)]
    for low, high in zip(cuts[:-1], cuts[1:]):
        x = lax.all_gather(tokens[:, low:high], "tensor", axis=0, tiled=True)
        if acc is not None:
            x, acc = lax.optimization_barrier((x, acc))
        hs = [shrink_chunk(x, shrinks[i], low, tile, hs[i]) for i in range(held)]
        acc = project_chunk(x, weight_codes, low, tile, acc)
    row_slot = jnp.repeat(segment_slot, SEG, total_repeat_length=total_rows)
    h = jnp.zeros((total_rows, rank), jnp.bfloat16)
    for i in range(held):
        mine = (row_slot == shard_index * held + i)[:, None]
        h = jnp.where(mine, hs[i].astype(jnp.bfloat16), h)
    h = spread(h, parts)
    return finish(acc, column_scale[None, :], h, expand, cosine, sine)


def solution(mesh):
    placed = (
        P(("groups", "tensor"), None),
        P(None, "tensor"),
        P("tensor"),
        P(("groups", "tensor"), None, None),
        P("groups", "tensor", None),
        P("groups"),
        P("groups"),
        P("groups"),
    )
    return jax.shard_map(
        functools.partial(body, mesh.shape["tensor"]),
        mesh=mesh,
        in_specs=placed,
        out_specs=P("groups", "tensor"),
        check_vma=False,
    )
```

```python
import functools

import jax
import jax.numpy as jnp
import numpy as np
from jax import lax
from jax.experimental import pallas as pl
from jax.experimental.pallas import tpu as pltpu
from jax.sharding import PartitionSpec as P

HD = 128
SEG = 128
VMEM = 40 * 1024 * 1024
F32 = jnp.float32
BF16 = jnp.bfloat16
NT = (((1,), (1,)), ((), ()))
PARAMS = pltpu.CompilerParams(vmem_limit_bytes=VMEM)
SNAKE = (0, 2, 4, 6, 7, 5, 3, 1)
ROUNDS = len(SNAKE) // 2


def row_positions(document_lengths, total_rows):
    ends = jnp.cumsum(document_lengths)
    row_index = jnp.arange(total_rows, dtype=jnp.int32)
    passed = (row_index[:, None] >= ends[None, :]).astype(jnp.int32)
    return row_index - jnp.sum(passed * document_lengths[None, :], axis=1)


def rotary_tables(positions):
    half_size = HD // 2
    freq_index = jnp.arange(half_size, dtype=F32)
    inverse = jnp.exp(freq_index * (-2.0 / HD) * jnp.log(F32(500000.0)))
    angles = positions.astype(F32)[:, None] * inverse[None, :]
    cosine, sine = jnp.cos(angles), jnp.sin(angles)
    return jnp.concatenate([cosine, cosine], 1), jnp.concatenate([-sine, sine], 1)


def rotate(value, cosine, sine):
    return value * cosine + pltpu.roll(value, HD // 2, 1) * sine


def shrink_kernel(x_ref, s_ref, h_out):
    @pl.when(pl.program_id(0) == 0)
    def _():
        h_out[...] = jnp.zeros_like(h_out)

    h_out[...] += lax.dot_general(x_ref[...], s_ref[...], NT, preferred_element_type=F32)


def shrink_all(x, shrink, tile):
    rows, depth = x.shape
    rank = shrink.shape[0]
    return pl.pallas_call(
        shrink_kernel,
        grid=(depth // tile,),
        in_specs=[
            pl.BlockSpec((rows, tile), lambda k: (0, k)),
            pl.BlockSpec((rank, tile), lambda k: (0, k)),
        ],
        out_specs=pl.BlockSpec((rows, rank), lambda k: (0, 0)),
        out_shape=jax.ShapeDtypeStruct((rows, rank), F32),
        compiler_params=PARAMS,
        name="shrink",
    )(x, shrink)


def project_kernel(x_ref, w_ref, acc_out):
    @pl.when(pl.program_id(0) == 0)
    def _():
        acc_out[...] = jnp.zeros_like(acc_out)

    acc_out[...] += jnp.dot(x_ref[...], w_ref[...], preferred_element_type=F32)


def project_all(x, weights, tile):
    rows, depth = x.shape
    cols = weights.shape[1]
    return pl.pallas_call(
        project_kernel,
        grid=(depth // tile,),
        in_specs=[
            pl.BlockSpec((rows, tile), lambda k: (0, k)),
            pl.BlockSpec((tile, cols), lambda k: (k, 0)),
        ],
        out_specs=pl.BlockSpec((rows, cols), lambda k: (0, 0)),
        out_shape=jax.ShapeDtypeStruct((rows, cols), F32),
        compiler_params=PARAMS,
        name="project",
    )(x, weights)


def segment_finish_kernel(acc_ref, scale_ref, h_ref, expand_ref, cos_ref, sin_ref, out_ref):
    update = jnp.dot(h_ref[...], expand_ref[0], preferred_element_type=F32)
    for head in range(out_ref.shape[1] // HD):
        cut = slice(head * HD, (head + 1) * HD)
        value = acc_ref[:, cut] * scale_ref[:, cut] + update[:, cut]
        out_ref[:, cut] = rotate(value, cos_ref[...], sin_ref[...]).astype(out_ref.dtype)


def segment_finish(acc, scale, h, expand, cosine, sine):
    rows, cols = acc.shape
    rank = h.shape[1]
    return pl.pallas_call(
        segment_finish_kernel,
        grid=(rows // SEG,),
        in_specs=[
            pl.BlockSpec((SEG, cols), lambda r: (r, 0)),
            pl.BlockSpec((1, cols), lambda r: (0, 0)),
            pl.BlockSpec((SEG, rank), lambda r: (r, 0)),
            pl.BlockSpec((1, rank, cols), lambda r: (r, 0, 0)),
            pl.BlockSpec((SEG, HD), lambda r: (r, 0)),
            pl.BlockSpec((SEG, HD), lambda r: (r, 0)),
        ],
        out_specs=pl.BlockSpec((SEG, cols), lambda r: (r, 0)),
        out_shape=jax.ShapeDtypeStruct((rows, cols), BF16),
        compiler_params=PARAMS,
        name="finish",
    )(acc, scale, h, expand, cosine, sine)


def spread(h, parts):
    step = 1
    while step < parts:
        h = h + lax.ppermute(h, "tensor", [(i, i ^ step) for i in range(parts)])
        step *= 2
    return h


def gather_plan(parts, tokens, weights, scale, shrinks, expands, segment_slot, cosine, sine):
    held, rank, depth = shrinks.shape
    tile = depth // 16
    x = lax.all_gather(tokens, "tensor", axis=0, tiled=True)
    row_slot = jnp.repeat(segment_slot, SEG, total_repeat_length=x.shape[0])
    h = jnp.zeros((x.shape[0], rank), BF16)
    for i in range(held):
        mine = (row_slot == lax.axis_index("tensor") * held + i)[:, None]
        h = jnp.where(mine, shrink_all(x, shrinks[i], tile).astype(BF16), h)
    h = spread(h, parts)
    acc = project_all(x, weights, tile)
    return segment_finish(acc, scale, h, expands[segment_slot], cosine, sine)


def block_owners():
    chips = len(SNAKE)
    owners = np.zeros((2 * chips, 2 * chips), np.int32)
    for place, chip in enumerate(SNAKE):
        for core in (0, 1):
            row = []
            for r in range(1, ROUNDS):
                before, after = SNAKE[place - r], SNAKE[(place + r) % chips]
                row += [2 * before + core, 2 * after + core, 2 * before + 1 - core, 2 * after + 1 - core]
            across = SNAKE[(place + ROUNDS) % chips]
            row += [2 * chip + core, 2 * chip + 1 - core, 2 * across + core, 2 * across + 1 - core]
            owners[2 * chip + core] = row
    return owners


def ring_pairs(ways):
    chips = len(SNAKE)
    pairs = []
    for place, chip in enumerate(SNAKE):
        for core in (0, 1):
            pairs.append((2 * chip + core, 2 * SNAKE[(place + ways[core]) % chips] + core))
    return pairs


def block_kernel(count, fresh, ranked, *refs):
    xs, refs = refs[:count], refs[count:]
    w_ref, refs = refs[0], refs[1:]
    if ranked:
        s_ref, refs = refs[0], refs[1:]
    acc_in, refs = refs[0], refs[1:]
    if ranked and not fresh:
        h_in, refs = refs[0], refs[1:]
    acc_out = refs[0]
    rows = xs[0].shape[0]

    @pl.when(pl.program_id(0) == 0)
    def _():
        acc_out[...] = jnp.zeros_like(acc_out) if fresh else acc_in[...]
        if ranked:
            refs[1][...] = jnp.zeros_like(refs[1]) if fresh else h_in[...]

    x = jnp.concatenate([ref[...] for ref in xs], 0)
    acc_out[...] += jnp.dot(x, w_ref[...], preferred_element_type=F32).reshape(acc_out.shape)
    if ranked:
        refs[1][...] += lax.dot_general(x, s_ref[...], NT, preferred_element_type=F32)


def block_product(xs, weights, shrink, low, tile, total, place, h, ranked):
    count = len(xs)
    rows, depth = xs[0].shape
    cols = weights.shape[1]
    rank = shrink.shape[0]
    fresh = low == 0
    skip = low // tile
    block = pl.BlockSpec((count, rows, cols), lambda k: (place // count, 0, 0))
    ranks = pl.BlockSpec((count * rows, rank), lambda k: (0, 0))
    operands = list(xs) + [weights]
    specs = [pl.BlockSpec((rows, tile), lambda k: (0, k))] * count
    specs += [pl.BlockSpec((tile, cols), lambda k: (k + skip, 0))]
    if ranked:
        operands.append(shrink)
        specs.append(pl.BlockSpec((rank, tile), lambda k: (0, k + skip)))
    aliases = {len(operands): 0}
    operands.append(total)
    specs.append(pl.BlockSpec(memory_space=pl.ANY) if fresh else block)
    if ranked and not fresh:
        operands.append(h)
        specs.append(ranks)
    outs = [jax.ShapeDtypeStruct(total.shape, F32)]
    out_specs = [block]
    if ranked:
        outs.append(jax.ShapeDtypeStruct((count * rows, rank), F32))
        out_specs.append(ranks)
    result = pl.pallas_call(
        functools.partial(block_kernel, count, fresh, ranked),
        grid=(depth // tile,),
        in_specs=specs,
        out_specs=out_specs,
        out_shape=outs,
        input_output_aliases=aliases,
        compiler_params=PARAMS,
        cost_estimate=pl.CostEstimate(
            flops=2 * count * rows * depth * cols, bytes_accessed=2 * depth * cols, transcendentals=0
        ),
        name="blocks",
    )(*operands)
    return result if ranked else (result[0], h)


def rank_kernel(counts, owners_ref, slot_ref, xa_ref, xb_ref, s_ref, *refs):
    h_refs, out_ref, grown, placed = refs[: len(counts)], refs[-3], refs[-2], refs[-1]
    step = pl.program_id(0)
    rows = xa_ref.shape[0]

    @pl.when(step == 0)
    def _():
        grown[...] = h_refs[-1][...]

    x = jnp.concatenate([xa_ref[...], xb_ref[...]], 0)
    grown[...] += lax.dot_general(x, s_ref[...], NT, preferred_element_type=F32)

    @pl.when(step == pl.num_programs(0) - 1)
    def _():
        block = 0
        for group, count in enumerate(counts):
            source = grown if group == len(counts) - 1 else h_refs[group]
            for i in range(count):
                to = pl.multiple_of(owners_ref[block] * rows, 16)
                placed[pl.ds(to, rows), :] = source[i * rows : (i + 1) * rows, :]
                block += 1
        pieces = []
        for segment in range(placed.shape[0] // SEG):
            piece = placed[segment * SEG : (segment + 1) * SEG, :]
            pieces.append(jnp.where(slot_ref[segment] == slot_ref[slot_ref.shape[0] - 1], piece, 0.0))
        half = len(pieces) // 2
        left, right = jnp.concatenate(pieces[:half], 0), jnp.concatenate(pieces[half:], 0)
        out_ref[...] = jnp.concatenate([left, right], 1).astype(out_ref.dtype)


def rank_terms(owners, slots, xs, shrink, low, tile, hs):
    rows, depth = xs[0].shape
    rank = shrink.shape[0]
    counts = [h.shape[0] // rows for h in hs]
    total_rows = sum(counts) * rows
    skip = low // tile
    whole = [pl.BlockSpec(h.shape, lambda k, *_: (0, 0)) for h in hs]
    return pl.pallas_call(
        functools.partial(rank_kernel, counts),
        grid_spec=pltpu.PrefetchScalarGridSpec(
            num_scalar_prefetch=2,
            grid=(depth // tile,),
            in_specs=[pl.BlockSpec((rows, tile), lambda k, *_: (0, k))] * 2
            + [pl.BlockSpec((rank, tile), lambda k, *_: (0, k + skip))]
            + whole,
            out_specs=pl.BlockSpec((total_rows // 2, 2 * rank), lambda k, *_: (0, 0)),
            scratch_shapes=[pltpu.VMEM(hs[-1].shape, F32), pltpu.VMEM((total_rows, rank), F32)],
        ),
        out_shape=jax.ShapeDtypeStruct((total_rows // 2, 2 * rank), BF16),
        compiler_params=PARAMS,
        name="ranks",
    )(owners, slots, *xs, shrink, *hs)


def block_finish_kernel(blocks, segments, places_ref, slot_ref, *refs):
    accs, refs = refs[:blocks], refs[blocks:]
    expands, refs = refs[:segments], refs[segments:]
    scale_ref, h_ref, cos_ref, sin_ref, out_ref, update = refs
    rank = h_ref.shape[1] // 2
    h = jnp.where(pl.program_id(0) == 0, h_ref[:, :rank], h_ref[:, rank:])
    for segment in range(segments):
        cut = slice(segment * SEG, (segment + 1) * SEG)
        update[cut, :] = jnp.dot(h[cut], expands[segment][0], preferred_element_type=F32)
    rows = accs[0].shape[1]
    for block in range(blocks):
        at = slice(block * rows, (block + 1) * rows)
        cosine, sine = cos_ref[at, :], sin_ref[at, :]
        for head in range(out_ref.shape[1] // HD):
            cut = slice(head * HD, (head + 1) * HD)
            value = accs[block][0, :, cut] * scale_ref[:, cut] + update[at, cut]
            out_ref[at, cut] = rotate(value, cosine, sine).astype(out_ref.dtype)


def block_finish(places, slots, total, expands, scale, h, cosine, sine):
    blocks, rows, cols = total.shape
    half = blocks // 2
    half_rows = half * rows
    segments = half_rows // SEG
    rank = expands.shape[1]

    def acc_at(i):
        return pl.BlockSpec((1, rows, cols), lambda g, places, slots: (places[g * half + i], 0, 0))

    def expand_at(i):
        return pl.BlockSpec((1, rank, cols), lambda g, places, slots: (slots[g * segments + i], 0, 0))

    half_of = lambda width: pl.BlockSpec((half_rows, width), lambda g, *_: (g, 0))
    return pl.pallas_call(
        functools.partial(block_finish_kernel, half, segments),
        grid_spec=pltpu.PrefetchScalarGridSpec(
            num_scalar_prefetch=2,
            grid=(2,),
            in_specs=[acc_at(i) for i in range(half)]
            + [expand_at(i) for i in range(segments)]
            + [
                pl.BlockSpec((1, cols), lambda g, *_: (0, 0)),
                pl.BlockSpec(h.shape, lambda g, *_: (0, 0)),
                half_of(HD),
                half_of(HD),
            ],
            out_specs=half_of(cols),
            scratch_shapes=[pltpu.VMEM((half_rows, cols), F32)],
        ),
        out_shape=jax.ShapeDtypeStruct((blocks * rows, cols), BF16),
        compiler_params=PARAMS,
        name="finish",
    )(places, slots, *([total] * half), *([expands] * segments), scale, h, cosine, sine)


def ring_plan(parts, tokens, weights, scale, shrinks, expands, segment_slot, cosine, sine):
    rows, depth = tokens.shape
    tile = depth // 16
    cuts = [0, depth // 2, depth]
    spans = list(zip(cuts[:-1], cuts[1:]))
    me = lax.axis_index("tensor")
    owners_table = block_owners()
    owners = jnp.asarray(owners_table)[me]
    places = jnp.asarray(np.argsort(owners_table, axis=1).astype(np.int32))[me]
    slots = jnp.concatenate([segment_slot, me[None].astype(jnp.int32)])
    shrink = shrinks[0]
    send = lambda value, pairs: lax.ppermute(value, "tensor", pairs)
    swap = lambda value: send(value, [(i, i ^ 1) for i in range(parts)])
    onward, back = ring_pairs((1, 1)), ring_pairs((-1, -1))
    across = ring_pairs((1, -1))

    own = [tokens[:, low:high] for low, high in spans]
    total = jnp.zeros((parts, rows, weights.shape[1]), F32)
    hs = {}

    def multiply(stage, xs, total):
        j, r = stage
        low = spans[j][0]
        last = r == ROUNDS and j == len(spans) - 1
        place = {0: 12, ROUNDS: 14}.get(r, 4 * (r - 1))
        h = None
        if last:
            order = [hs[i] for i in range(1, ROUNDS)] + [hs[0], hs[ROUNDS]]
            h = rank_terms(owners, slots, xs, shrink, low, tile, order)
        total, hs[r] = block_product(xs, weights, shrink, low, tile, total, place, hs.get(r), not last)
        return total, h

    arriving = {(j, 1): [send(part, onward), send(part, back)] for j, part in enumerate(own)}
    waiting = [((j, 0), [part, swap(part)]) for j, part in enumerate(own)]
    for r in range(1, ROUNDS + 1):
        for j in range(len(spans)):
            arrived = arriving.pop((j, r))
            arrived, total = lax.optimization_barrier((arrived, total))
            if r < ROUNDS - 1:
                arriving[j, r + 1] = [send(arrived[0], onward), send(arrived[1], back)]
            elif r == ROUNDS - 1:
                arriving[j, r + 1] = [send(jnp.where(me % 2 == 0, *arrived), across)]
            waiting.append(((j, r), arrived + [swap(part) for part in arrived]))
            stage, xs = waiting.pop(0)
            if r < ROUNDS:
                xs, _ = lax.optimization_barrier((xs, arrived))
            total, _ = multiply(stage, xs, total)
    for stage, xs in waiting:
        total, h = multiply(stage, xs, total)
    h = spread(h, parts)
    return block_finish(places, segment_slot, total, expands, scale, h, cosine, sine)


def body(parts, tokens, weight_codes, column_scale, shrink_store, expand_store, row_adapter, placement, document_lengths):
    rows = tokens.shape[0]
    total_rows = rows * parts
    segment_slot = placement[row_adapter[::SEG]]
    shrinks = jnp.swapaxes(shrink_store, 1, 2)
    expands = jnp.swapaxes(expand_store, 1, 2)
    cosine, sine = rotary_tables(row_positions(document_lengths, total_rows))
    ring = parts == 2 * len(SNAKE) and rows % 16 == 0 and shrinks.shape[0] == 1 and total_rows % (2 * SEG) == 0
    plan = ring_plan if ring else gather_plan
    return plan(parts, tokens, weight_codes, column_scale[None, :], shrinks, expands, segment_slot, cosine, sine)


def solution(mesh):
    placed = (
        P(("groups", "tensor"), None),
        P(None, "tensor"),
        P("tensor"),
        P(("groups", "tensor"), None, None),
        P("groups", "tensor", None),
        P("groups"),
        P("groups"),
        P("groups"),
    )
    return jax.shard_map(
        functools.partial(body, mesh.shape["tensor"]),
        mesh=mesh,
        in_specs=placed,
        out_specs=P("groups", "tensor"),
        check_vma=False,
    )
```

```python
import functools

import jax
import jax.numpy as jnp
import numpy as np
from jax import lax
from jax.experimental import pallas as pl
from jax.experimental.pallas import tpu as pltpu
from jax.sharding import PartitionSpec as P

HD = 128
SEG = 128
VMEM = 26 * 1024 * 1024
F32 = jnp.float32
BF16 = jnp.bfloat16
NT = (((1,), (1,)), ((), ()))
STREAMS = 4
PARAMS = pltpu.CompilerParams(vmem_limit_bytes=VMEM)
SNAKE = (0, 2, 4, 6, 7, 5, 3, 1)
ROUNDS = len(SNAKE) // 2


def row_positions(document_lengths, total_rows):
    ends = jnp.cumsum(document_lengths)
    row_index = jnp.arange(total_rows, dtype=jnp.int32)
    passed = (row_index[:, None] >= ends[None, :]).astype(jnp.int32)
    return row_index - jnp.sum(passed * document_lengths[None, :], axis=1)


def rotary_tables(positions):
    half_size = HD // 2
    freq_index = jnp.arange(half_size, dtype=F32)
    inverse = jnp.exp(freq_index * (-2.0 / HD) * jnp.log(F32(500000.0)))
    angles = positions.astype(F32)[:, None] * inverse[None, :]
    cosine, sine = jnp.cos(angles), jnp.sin(angles)
    return jnp.concatenate([cosine, cosine], 1), jnp.concatenate([-sine, sine], 1)


def rotate(value, cosine, sine):
    return value * cosine + pltpu.roll(value, HD // 2, 1) * sine


def shrink_kernel(x_ref, s_ref, h_out):
    @pl.when(pl.program_id(0) == 0)
    def _():
        h_out[...] = jnp.zeros_like(h_out)

    h_out[...] += lax.dot_general(x_ref[...], s_ref[...], NT, preferred_element_type=F32)


def shrink_all(x, shrink, tile):
    rows, depth = x.shape
    rank = shrink.shape[0]
    return pl.pallas_call(
        shrink_kernel,
        grid=(depth // tile,),
        in_specs=[
            pl.BlockSpec((rows, tile), lambda k: (0, k)),
            pl.BlockSpec((rank, tile), lambda k: (0, k)),
        ],
        out_specs=pl.BlockSpec((rows, rank), lambda k: (0, 0)),
        out_shape=jax.ShapeDtypeStruct((rows, rank), F32),
        compiler_params=PARAMS,
        name="shrink",
    )(x, shrink)


def project_kernel(x_ref, w_ref, acc_out):
    @pl.when(pl.program_id(0) == 0)
    def _():
        acc_out[...] = jnp.zeros_like(acc_out)

    acc_out[...] += jnp.dot(x_ref[...], w_ref[...], preferred_element_type=F32)


def project_all(x, weights, tile):
    rows, depth = x.shape
    cols = weights.shape[1]
    return pl.pallas_call(
        project_kernel,
        grid=(depth // tile,),
        in_specs=[
            pl.BlockSpec((rows, tile), lambda k: (0, k)),
            pl.BlockSpec((tile, cols), lambda k: (k, 0)),
        ],
        out_specs=pl.BlockSpec((rows, cols), lambda k: (0, 0)),
        out_shape=jax.ShapeDtypeStruct((rows, cols), F32),
        compiler_params=PARAMS,
        name="project",
    )(x, weights)


def segment_finish_kernel(acc_ref, scale_ref, h_ref, expand_ref, cos_ref, sin_ref, out_ref):
    update = jnp.dot(h_ref[...], expand_ref[0], preferred_element_type=F32)
    for head in range(out_ref.shape[1] // HD):
        cut = slice(head * HD, (head + 1) * HD)
        value = acc_ref[:, cut] * scale_ref[:, cut] + update[:, cut]
        out_ref[:, cut] = rotate(value, cos_ref[...], sin_ref[...]).astype(out_ref.dtype)


def segment_finish(acc, scale, h, expand, cosine, sine):
    rows, cols = acc.shape
    rank = h.shape[1]
    return pl.pallas_call(
        segment_finish_kernel,
        grid=(rows // SEG,),
        in_specs=[
            pl.BlockSpec((SEG, cols), lambda r: (r, 0)),
            pl.BlockSpec((1, cols), lambda r: (0, 0)),
            pl.BlockSpec((SEG, rank), lambda r: (r, 0)),
            pl.BlockSpec((1, rank, cols), lambda r: (r, 0, 0)),
            pl.BlockSpec((SEG, HD), lambda r: (r, 0)),
            pl.BlockSpec((SEG, HD), lambda r: (r, 0)),
        ],
        out_specs=pl.BlockSpec((SEG, cols), lambda r: (r, 0)),
        out_shape=jax.ShapeDtypeStruct((rows, cols), BF16),
        compiler_params=PARAMS,
        name="finish",
    )(acc, scale, h, expand, cosine, sine)


def spread(h, parts):
    step = 1
    while step < parts:
        h = h + lax.ppermute(h, "tensor", [(i, i ^ step) for i in range(parts)])
        step *= 2
    return h


def gather_plan(parts, tokens, weights, scale, shrinks, expands, segment_slot, cosine, sine):
    held, rank, depth = shrinks.shape
    tile = depth // 16
    x = lax.all_gather(tokens, "tensor", axis=0, tiled=True)
    row_slot = jnp.repeat(segment_slot, SEG, total_repeat_length=x.shape[0])
    h = jnp.zeros((x.shape[0], rank), BF16)
    for i in range(held):
        mine = (row_slot == lax.axis_index("tensor") * held + i)[:, None]
        h = jnp.where(mine, shrink_all(x, shrinks[i], tile).astype(BF16), h)
    h = spread(h, parts)
    acc = project_all(x, weights, tile)
    return segment_finish(acc, scale, h, expands[segment_slot], cosine, sine)


def block_owners():
    chips = len(SNAKE)
    owners = np.zeros((2 * chips, 2 * chips), np.int32)
    for place, chip in enumerate(SNAKE):
        for core in (0, 1):
            row = [2 * chip + core, 2 * chip + 1 - core]
            for r in range(1, ROUNDS):
                before, after = SNAKE[place - r], SNAKE[(place + r) % chips]
                row += [2 * before + core, 2 * after + core, 2 * before + 1 - core, 2 * after + 1 - core]
            across = SNAKE[(place + ROUNDS) % chips]
            row += [2 * across + core, 2 * across + 1 - core]
            owners[2 * chip + core] = row
    return owners


def ring_pairs(ways):
    chips = len(SNAKE)
    pairs = []
    for place, chip in enumerate(SNAKE):
        for core in (0, 1):
            pairs.append((2 * chip + core, 2 * SNAKE[(place + ways[core]) % chips] + core))
    return pairs


def block_kernel(count, first, base, fresh, ranked, *refs):
    xs, refs = refs[:count], refs[count:]
    ws, refs = refs[:STREAMS], refs[STREAMS:]
    if ranked:
        s_ref, refs = refs[0], refs[1:]
    if not first:
        total_in, refs = refs[0], refs[1:]
    if ranked and not fresh:
        h_in, refs = refs[0], refs[1:]
    total_out, refs = refs[0], refs[1:]
    if ranked:
        h_out, refs = refs[0], refs[1:]
    acc, before, sems = refs
    step, last = pl.program_id(0), pl.num_programs(0) - 1
    rows = xs[0].shape[0]

    def load():
        return pltpu.make_async_copy(total_in.at[pl.ds(base, count)], before, sems.at[0])

    @pl.when(step == 0)
    def _():
        if not fresh:
            load().start()
        acc[...] = jnp.zeros_like(acc)
        if ranked:
            h_out[...] = jnp.zeros_like(h_out) if fresh else h_in[...]

    x = jnp.concatenate([ref[...] for ref in xs], 0)
    w = jnp.concatenate([ref[...] for ref in ws], 0)
    acc[...] += jnp.dot(x, w, preferred_element_type=F32).reshape(acc.shape)
    if ranked:
        h_out[...] += lax.dot_general(x, s_ref[...], NT, preferred_element_type=F32)

    @pl.when(step == last)
    def _():
        if not fresh:
            load().wait()
            acc[...] += before[...]
        store = pltpu.make_async_copy(acc, total_out.at[pl.ds(base, count)], sems.at[1])
        store.start()
        store.wait()


def block_product(xs, weights, shrink, starts, low, high, tile, total, base, h, ranked):
    count = len(xs)
    rows = xs[0].shape[0]
    depth, cols = weights.shape
    rank = shrink.shape[0]
    fresh = low == 0
    skip = low // tile
    starts = starts or [0] * count
    strip = tile // STREAMS
    ranks = pl.BlockSpec((count * rows, rank), lambda k: (0, 0))
    operands = list(xs) + [weights] * STREAMS
    specs = [pl.BlockSpec((rows, tile), lambda k, i=(low - start) // tile: (0, k + i)) for start in starts]
    for i in range(STREAMS):
        specs.append(pl.BlockSpec((strip, cols), lambda k, i=i: (STREAMS * (k + skip) + i, 0)))
    if ranked:
        operands.append(shrink)
        specs.append(pl.BlockSpec((rank, tile), lambda k: (0, k + skip)))
    aliases = {}
    first = total is None
    if not first:
        aliases = {len(operands): 0}
        operands.append(total)
        specs.append(pl.BlockSpec(memory_space=pl.ANY))
    if ranked and not fresh:
        operands.append(h)
        specs.append(ranks)
    outs = [jax.ShapeDtypeStruct(total_shape(rows, cols), F32)]
    out_specs = [pl.BlockSpec(memory_space=pl.ANY)]
    if ranked:
        outs.append(jax.ShapeDtypeStruct((count * rows, rank), F32))
        out_specs.append(ranks)
    result = pl.pallas_call(
        functools.partial(block_kernel, count, first, base, fresh, ranked),
        grid=((high - low) // tile,),
        in_specs=specs,
        out_specs=out_specs,
        out_shape=outs,
        scratch_shapes=[
            pltpu.VMEM((count, rows, cols), F32),
            pltpu.VMEM((1, 8, 128) if fresh else (count, rows, cols), F32),
            pltpu.SemaphoreType.DMA((2,)),
        ],
        input_output_aliases=aliases,
        compiler_params=PARAMS,
        cost_estimate=pl.CostEstimate(
            flops=2 * count * rows * (high - low) * cols,
            bytes_accessed=2 * (high - low) * cols,
            transcendentals=0,
        ),
        name="blocks",
    )(*operands)
    return result if ranked else (result[0], h)


def total_shape(rows, cols):
    return (2 * len(SNAKE), rows, cols)


def rank_kernel(counts, sides, pieces, owners_ref, slot_ref, *refs):
    side, refs = refs[:sides], refs[sides:]
    split, refs = refs[: 2 * pieces], refs[2 * pieces :]
    s_ref, h_refs, out_ref, placed = refs[0], refs[1:-2], refs[-2], refs[-1]
    rows, width = side[0].shape
    x = jnp.concatenate([ref[...] for ref in side], 0)
    grown = lax.dot_general(x, s_ref[...], NT, preferred_element_type=F32)
    last = 0.0
    for piece in range(pieces):
        x = jnp.concatenate([split[2 * piece][...], split[2 * piece + 1][...]], 0)
        cut = slice(piece * width // pieces, (piece + 1) * width // pieces)
        last += lax.dot_general(x, s_ref[:, cut], NT, preferred_element_type=F32)
    late = h_refs[-1][...] + jnp.concatenate([grown, last], 0)
    block = 0
    for count, source in zip(counts, h_refs[:-1] + (late,)):
        for i in range(count):
            to = pl.multiple_of(owners_ref[block] * rows, 16)
            placed[pl.ds(to, rows), :] = source[i * rows : (i + 1) * rows, :]
            block += 1
    parts = []
    for segment in range(placed.shape[0] // SEG):
        part = placed[segment * SEG : (segment + 1) * SEG, :]
        parts.append(jnp.where(slot_ref[segment] == slot_ref[slot_ref.shape[0] - 1], part, 0.0))
    half = len(parts) // 2
    left, right = jnp.concatenate(parts[:half], 0), jnp.concatenate(parts[half:], 0)
    out_ref[...] = jnp.concatenate([left, right], 1).astype(out_ref.dtype)


def rank_terms(owners, slots, side, pieces, shrink, low, hs):
    rows, depth = side[0].shape
    rank = shrink.shape[0]
    counts = [h.shape[0] // rows for h in hs]
    total_rows = sum(counts) * rows
    whole = lambda shape: pl.BlockSpec(shape, lambda _, *rest: (0, 0))
    upper = lambda height: pl.BlockSpec((height, depth - low), lambda _, *rest: (0, low // (depth - low)))
    flat = [part for piece in pieces for part in piece]
    return pl.pallas_call(
        functools.partial(rank_kernel, counts, len(side), len(pieces)),
        grid_spec=pltpu.PrefetchScalarGridSpec(
            num_scalar_prefetch=2,
            grid=(1,),
            in_specs=[upper(rows)] * len(side)
            + [whole(part.shape) for part in flat]
            + [upper(rank)]
            + [whole(h.shape) for h in hs],
            out_specs=whole((total_rows // 2, 2 * rank)),
            scratch_shapes=[pltpu.VMEM((total_rows, rank), F32)],
        ),
        out_shape=jax.ShapeDtypeStruct((total_rows // 2, 2 * rank), BF16),
        compiler_params=PARAMS,
        name="ranks",
    )(owners, slots, *side, *flat, shrink, *hs)


def block_finish_kernel(blocks, segments, places_ref, slot_ref, *refs):
    accs, refs = refs[:blocks], refs[blocks:]
    expands, refs = refs[:segments], refs[segments:]
    scale_ref, h_ref, cos_ref, sin_ref, out_ref, update = refs
    rank = h_ref.shape[1] // 2
    h = jnp.where(pl.program_id(0) == 0, h_ref[:, :rank], h_ref[:, rank:])
    for segment in range(segments):
        cut = slice(segment * SEG, (segment + 1) * SEG)
        update[cut, :] = jnp.dot(h[cut], expands[segment][0], preferred_element_type=F32)
    rows = accs[0].shape[1]
    for block in range(blocks):
        at = slice(block * rows, (block + 1) * rows)
        cosine, sine = cos_ref[at, :], sin_ref[at, :]
        for head in range(out_ref.shape[1] // HD):
            cut = slice(head * HD, (head + 1) * HD)
            value = accs[block][0, :, cut] * scale_ref[:, cut] + update[at, cut]
            out_ref[at, cut] = rotate(value, cosine, sine).astype(out_ref.dtype)


def block_finish(places, slots, total, expands, scale, h, cosine, sine):
    blocks, rows, cols = total.shape
    half = blocks // 2
    half_rows = half * rows
    segments = half_rows // SEG
    rank = expands.shape[1]

    def acc_at(i):
        return pl.BlockSpec((1, rows, cols), lambda g, places, slots: (places[g * half + i], 0, 0))

    def expand_at(i):
        return pl.BlockSpec((1, rank, cols), lambda g, places, slots: (slots[g * segments + i], 0, 0))

    half_of = lambda width: pl.BlockSpec((half_rows, width), lambda g, *_: (g, 0))
    return pl.pallas_call(
        functools.partial(block_finish_kernel, half, segments),
        grid_spec=pltpu.PrefetchScalarGridSpec(
            num_scalar_prefetch=2,
            grid=(2,),
            in_specs=[acc_at(i) for i in range(half)]
            + [expand_at(i) for i in range(segments)]
            + [
                pl.BlockSpec((1, cols), lambda g, *_: (0, 0)),
                pl.BlockSpec(h.shape, lambda g, *_: (0, 0)),
                half_of(HD),
                half_of(HD),
            ],
            out_specs=half_of(cols),
            scratch_shapes=[pltpu.VMEM((half_rows, cols), F32)],
        ),
        out_shape=jax.ShapeDtypeStruct((blocks * rows, cols), BF16),
        compiler_params=PARAMS,
        name="finish",
    )(places, slots, *([total] * half), *([expands] * segments), scale, h, cosine, sine)


def ring_plan(parts, tokens, weights, scale, shrinks, expands, segment_slot, cosine, sine):
    rows, depth = tokens.shape
    tile = depth // 16
    me = lax.axis_index("tensor")
    owners_table = block_owners()
    owners = jnp.asarray(owners_table)[me]
    places = jnp.asarray(np.argsort(owners_table, axis=1).astype(np.int32))[me]
    slots = jnp.concatenate([segment_slot, me[None].astype(jnp.int32)])
    shrink = shrinks[0]
    send = lambda value, pairs: lax.ppermute(value, "tensor", pairs)
    swap = lambda value: send(value, [(i, i ^ 1) for i in range(parts)])
    onward, back = ring_pairs((1, 1)), ring_pairs((-1, -1))
    across = ring_pairs((1, -1))

    total, hs, held = None, [], 0
    blocks = [tokens, swap(tokens)]
    ahead = [tokens, tokens]
    for r in range(1, ROUNDS):
        ahead = [send(ahead[0], onward), send(ahead[1], back)]
        if total is not None:
            ahead, total = lax.optimization_barrier((ahead, total))
        if r == ROUNDS - 1:
            break
        blocks += ahead + [swap(part) for part in ahead]
        total, h = block_product(blocks, weights, shrink, None, 0, depth, tile, total, held, None, True)
        hs.append(h)
        held += len(blocks)
        blocks = []
    side = ahead + [swap(part) for part in ahead]

    picked = jnp.where(me % 2 == 0, *ahead)
    quarter = depth // 4
    cuts = [q * quarter for q in range(4)]
    arriving = [send(picked[:, low : low + quarter], across) for low in cuts]
    pieces = [[part, swap(part)] for part in arriving[:2]]

    def late_product(q, total, h, ranked, tie=None):
        xs = side + pieces[q]
        if tie is not None:
            xs, _ = lax.optimization_barrier((xs, tie))
        starts = [0] * len(side) + [cuts[q]] * 2
        return block_product(
            xs, weights, shrink, starts, cuts[q], cuts[q] + quarter, tile, total, held, h, ranked
        )

    h_late = None
    for q in (0, 1):
        total, h_late = late_product(q, total, h_late, True)
        part, total = lax.optimization_barrier((arriving[q + 2], total))
        pieces.append([part, swap(part)])
    h = rank_terms(owners, slots, side, pieces[2:], shrink, cuts[2], hs + [h_late])
    for q, steps in zip((2, 3, None), ([1], [2, 4, 6], [8])):
        more = [send(h, [(i, i ^ step) for i in range(parts)]) for step in steps]
        if q is not None:
            total, _ = late_product(q, total, None, False, h)
        for part in more:
            h = h + part
        h, total = lax.optimization_barrier((h, total))
    return block_finish(places, segment_slot, total, expands, scale, h, cosine, sine)


def body(parts, tokens, weight_codes, column_scale, shrink_store, expand_store, row_adapter, placement, document_lengths):
    rows = tokens.shape[0]
    total_rows = rows * parts
    segment_slot = placement[row_adapter[::SEG]]
    shrinks = jnp.swapaxes(shrink_store, 1, 2)
    expands = jnp.swapaxes(expand_store, 1, 2)
    cosine, sine = rotary_tables(row_positions(document_lengths, total_rows))
    ring = parts == 2 * len(SNAKE) and rows % 16 == 0 and shrinks.shape[0] == 1 and total_rows % (2 * SEG) == 0
    plan = ring_plan if ring else gather_plan
    return plan(parts, tokens, weight_codes, column_scale[None, :], shrinks, expands, segment_slot, cosine, sine)


def solution(mesh):
    placed = (
        P(("groups", "tensor"), None),
        P(None, "tensor"),
        P("tensor"),
        P(("groups", "tensor"), None, None),
        P("groups", "tensor", None),
        P("groups"),
        P("groups"),
        P("groups"),
    )
    return jax.shard_map(
        functools.partial(body, mesh.shape["tensor"]),
        mesh=mesh,
        in_specs=placed,
        out_specs=P("groups", "tensor"),
        check_vma=False,
    )
```

```python
import functools

import jax
import jax.numpy as jnp
import numpy as np
from jax import lax
from jax.experimental import pallas as pl
from jax.experimental.pallas import tpu as pltpu
from jax.sharding import PartitionSpec as P

HD = 128
SEG = 128
VMEM = 20 * 1024 * 1024
F32 = jnp.float32
BF16 = jnp.bfloat16
NT = (((1,), (1,)), ((), ()))
SLOTS = 4
BIG_VMEM = 24 * 1024 * 1024
PARAMS = pltpu.CompilerParams(vmem_limit_bytes=VMEM)
SNAKE = (0, 2, 4, 6, 7, 5, 3, 1)
ROUNDS = len(SNAKE) // 2


def row_positions(document_lengths, total_rows):
    ends = jnp.cumsum(document_lengths)
    row_index = jnp.arange(total_rows, dtype=jnp.int32)
    passed = (row_index[:, None] >= ends[None, :]).astype(jnp.int32)
    return row_index - jnp.sum(passed * document_lengths[None, :], axis=1)


def rotary_tables(positions):
    half_size = HD // 2
    freq_index = jnp.arange(half_size, dtype=F32)
    inverse = jnp.exp(freq_index * (-2.0 / HD) * jnp.log(F32(500000.0)))
    angles = positions.astype(F32)[:, None] * inverse[None, :]
    cosine, sine = jnp.cos(angles), jnp.sin(angles)
    return jnp.concatenate([cosine, cosine], 1), jnp.concatenate([-sine, sine], 1)


def rotate(value, cosine, sine):
    return value * cosine + pltpu.roll(value, HD // 2, 1) * sine


def shrink_kernel(x_ref, s_ref, h_out):
    @pl.when(pl.program_id(0) == 0)
    def _():
        h_out[...] = jnp.zeros_like(h_out)

    h_out[...] += lax.dot_general(x_ref[...], s_ref[...], NT, preferred_element_type=F32)


def shrink_all(x, shrink, tile):
    rows, depth = x.shape
    rank = shrink.shape[0]
    return pl.pallas_call(
        shrink_kernel,
        grid=(depth // tile,),
        in_specs=[
            pl.BlockSpec((rows, tile), lambda k: (0, k)),
            pl.BlockSpec((rank, tile), lambda k: (0, k)),
        ],
        out_specs=pl.BlockSpec((rows, rank), lambda k: (0, 0)),
        out_shape=jax.ShapeDtypeStruct((rows, rank), F32),
        compiler_params=PARAMS,
        name="shrink",
    )(x, shrink)


def project_kernel(x_ref, w_ref, acc_out):
    @pl.when(pl.program_id(0) == 0)
    def _():
        acc_out[...] = jnp.zeros_like(acc_out)

    acc_out[...] += jnp.dot(x_ref[...], w_ref[...], preferred_element_type=F32)


def project_all(x, weights, tile):
    rows, depth = x.shape
    cols = weights.shape[1]
    return pl.pallas_call(
        project_kernel,
        grid=(depth // tile,),
        in_specs=[
            pl.BlockSpec((rows, tile), lambda k: (0, k)),
            pl.BlockSpec((tile, cols), lambda k: (k, 0)),
        ],
        out_specs=pl.BlockSpec((rows, cols), lambda k: (0, 0)),
        out_shape=jax.ShapeDtypeStruct((rows, cols), F32),
        compiler_params=PARAMS,
        name="project",
    )(x, weights)


def segment_finish_kernel(acc_ref, scale_ref, h_ref, expand_ref, cos_ref, sin_ref, out_ref):
    update = jnp.dot(h_ref[...], expand_ref[0], preferred_element_type=F32)
    for head in range(out_ref.shape[1] // HD):
        cut = slice(head * HD, (head + 1) * HD)
        value = acc_ref[:, cut] * scale_ref[:, cut] + update[:, cut]
        out_ref[:, cut] = rotate(value, cos_ref[...], sin_ref[...]).astype(out_ref.dtype)


def segment_finish(acc, scale, h, expand, cosine, sine):
    rows, cols = acc.shape
    rank = h.shape[1]
    return pl.pallas_call(
        segment_finish_kernel,
        grid=(rows // SEG,),
        in_specs=[
            pl.BlockSpec((SEG, cols), lambda r: (r, 0)),
            pl.BlockSpec((1, cols), lambda r: (0, 0)),
            pl.BlockSpec((SEG, rank), lambda r: (r, 0)),
            pl.BlockSpec((1, rank, cols), lambda r: (r, 0, 0)),
            pl.BlockSpec((SEG, HD), lambda r: (r, 0)),
            pl.BlockSpec((SEG, HD), lambda r: (r, 0)),
        ],
        out_specs=pl.BlockSpec((SEG, cols), lambda r: (r, 0)),
        out_shape=jax.ShapeDtypeStruct((rows, cols), BF16),
        compiler_params=PARAMS,
        name="finish",
    )(acc, scale, h, expand, cosine, sine)


def spread(h, parts):
    step = 1
    while step < parts:
        h = h + lax.ppermute(h, "tensor", [(i, i ^ step) for i in range(parts)])
        step *= 2
    return h


def gather_plan(parts, tokens, weights, scale, shrinks, expands, segment_slot, cosine, sine):
    held, rank, depth = shrinks.shape
    tile = depth // 16
    x = lax.all_gather(tokens, "tensor", axis=0, tiled=True)
    row_slot = jnp.repeat(segment_slot, SEG, total_repeat_length=x.shape[0])
    h = jnp.zeros((x.shape[0], rank), BF16)
    for i in range(held):
        mine = (row_slot == lax.axis_index("tensor") * held + i)[:, None]
        h = jnp.where(mine, shrink_all(x, shrinks[i], tile).astype(BF16), h)
    h = spread(h, parts)
    acc = project_all(x, weights, tile)
    return segment_finish(acc, scale, h, expands[segment_slot], cosine, sine)


def block_owners():
    chips = len(SNAKE)
    owners = np.zeros((2 * chips, 2 * chips), np.int32)
    for place, chip in enumerate(SNAKE):
        for core in (0, 1):
            row = [2 * chip + core, 2 * chip + 1 - core]
            for r in range(1, ROUNDS):
                before, after = SNAKE[place - r], SNAKE[(place + r) % chips]
                row += [2 * before + core, 2 * after + core, 2 * before + 1 - core, 2 * after + 1 - core]
            across = SNAKE[(place + ROUNDS) % chips]
            row += [2 * across + core, 2 * across + 1 - core]
            owners[2 * chip + core] = row
    return owners


def ring_pairs(ways):
    chips = len(SNAKE)
    pairs = []
    for place, chip in enumerate(SNAKE):
        for core in (0, 1):
            pairs.append((2 * chip + core, 2 * SNAKE[(place + ways[core]) % chips] + core))
    return pairs


def block_kernel(starts, low, tile, steps, first, base, fresh, ranked, *refs):
    count = len(starts)
    xs, w_ref, refs = refs[:count], refs[count], refs[count + 1 :]
    if ranked:
        s_ref, refs = refs[0], refs[1:]
    if not first:
        total_in, refs = refs[0], refs[1:]
    if ranked and not fresh:
        h_in, refs = refs[0], refs[1:]
    total_out, refs = refs[0], refs[1:]
    if ranked:
        h_out, refs = refs[0], refs[1:]
    acc, before, x_slots, w_slots, s_slots, sems, total_sems = refs
    rows = xs[0].shape[0]

    def copies(step):
        slot = lax.rem(step, SLOTS)
        at = pl.multiple_of(step * tile, tile)
        sem = lambda i: sems.at[slot, i]
        out = [pltpu.make_async_copy(w_ref.at[pl.ds(low + at, tile)], w_slots.at[slot], sem(count))]
        for i, start in enumerate(starts):
            cut = xs[i].at[:, pl.ds(low - start + at, tile)]
            out.append(pltpu.make_async_copy(cut, x_slots.at[slot, pl.ds(i * rows, rows)], sem(i)))
        if ranked:
            cut = s_ref.at[:, pl.ds(low + at, tile)]
            out.append(pltpu.make_async_copy(cut, s_slots.at[slot], sem(count + 1)))
        return out

    def start(step):
        for copy in copies(step):
            copy.start()

    for step in range(min(SLOTS, steps)):
        start(jnp.int32(step))
    if not fresh:
        load = pltpu.make_async_copy(total_in.at[pl.ds(base, count)], before, total_sems.at[0])
        load.start()
    acc[...] = jnp.zeros_like(acc)
    if ranked:
        h_out[...] = jnp.zeros_like(h_out) if fresh else h_in[...]

    @pl.loop(0, steps)
    def _(step):
        for copy in copies(step):
            copy.wait()
        slot = lax.rem(step, SLOTS)
        x = x_slots[slot]
        acc[...] += jnp.dot(x, w_slots[slot], preferred_element_type=F32).reshape(acc.shape)
        if ranked:
            h_out[...] += lax.dot_general(x, s_slots[slot], NT, preferred_element_type=F32)

        @pl.when(step + SLOTS < steps)
        def _():
            start(step + SLOTS)

    if not fresh:
        load.wait()
        acc[...] += before[...]
    store = pltpu.make_async_copy(acc, total_out.at[pl.ds(base, count)], total_sems.at[1])
    store.start()
    store.wait()


def block_product(xs, weights, shrink, starts, low, high, tile, total, base, h, ranked):
    count = len(xs)
    rows = xs[0].shape[0]
    cols = weights.shape[1]
    rank = shrink.shape[0]
    fresh, first = low == 0, total is None
    anywhere, whole = pl.BlockSpec(memory_space=pl.ANY), pl.BlockSpec(memory_space=pltpu.VMEM)
    operands = list(xs) + [weights]
    specs = [anywhere] * (count + 1)
    if ranked:
        operands.append(shrink)
        specs.append(anywhere)
    aliases = {}
    if not first:
        aliases = {len(operands): 0}
        operands.append(total)
        specs.append(anywhere)
    if ranked and not fresh:
        operands.append(h)
        specs.append(whole)
    outs, out_specs = [jax.ShapeDtypeStruct(total_shape(rows, cols), F32)], [anywhere]
    if ranked:
        outs.append(jax.ShapeDtypeStruct((count * rows, rank), F32))
        out_specs.append(whole)
    steps = (high - low) // tile
    result = pl.pallas_call(
        functools.partial(
            block_kernel, starts or [0] * count, low, tile, steps, first, base, fresh, ranked
        ),
        in_specs=specs,
        out_specs=out_specs,
        out_shape=outs,
        scratch_shapes=[
            pltpu.VMEM((count, rows, cols), F32),
            pltpu.VMEM((1, 8, 128) if fresh else (count, rows, cols), F32),
            pltpu.VMEM((SLOTS, count * rows, tile), BF16),
            pltpu.VMEM((SLOTS, tile, cols), BF16),
            pltpu.VMEM((SLOTS, rank, tile), BF16),
            pltpu.SemaphoreType.DMA((SLOTS, count + 2)),
            pltpu.SemaphoreType.DMA((2,)),
        ],
        input_output_aliases=aliases,
        compiler_params=pltpu.CompilerParams(vmem_limit_bytes=BIG_VMEM),
        cost_estimate=pl.CostEstimate(
            flops=2 * count * rows * (high - low) * cols,
            bytes_accessed=2 * (high - low) * cols,
            transcendentals=0,
        ),
        name="blocks",
    )(*operands)
    return result if ranked else (result[0], h)


def total_shape(rows, cols):
    return (2 * len(SNAKE), rows, cols)


def rank_kernel(counts, sides, pieces, owners_ref, slot_ref, *refs):
    side, refs = refs[:sides], refs[sides:]
    split, refs = refs[: 2 * pieces], refs[2 * pieces :]
    s_ref, h_refs, out_ref, placed = refs[0], refs[1:-2], refs[-2], refs[-1]
    rows, width = side[0].shape
    x = jnp.concatenate([ref[...] for ref in side], 0)
    grown = lax.dot_general(x, s_ref[...], NT, preferred_element_type=F32)
    last = 0.0
    for piece in range(pieces):
        x = jnp.concatenate([split[2 * piece][...], split[2 * piece + 1][...]], 0)
        cut = slice(piece * width // pieces, (piece + 1) * width // pieces)
        last += lax.dot_general(x, s_ref[:, cut], NT, preferred_element_type=F32)
    late = h_refs[-1][...] + jnp.concatenate([grown, last], 0)
    block = 0
    for count, source in zip(counts, h_refs[:-1] + (late,)):
        for i in range(count):
            to = pl.multiple_of(owners_ref[block] * rows, 16)
            placed[pl.ds(to, rows), :] = source[i * rows : (i + 1) * rows, :]
            block += 1
    parts = []
    for segment in range(placed.shape[0] // SEG):
        part = placed[segment * SEG : (segment + 1) * SEG, :]
        parts.append(jnp.where(slot_ref[segment] == slot_ref[slot_ref.shape[0] - 1], part, 0.0))
    half = len(parts) // 2
    left, right = jnp.concatenate(parts[:half], 0), jnp.concatenate(parts[half:], 0)
    out_ref[...] = jnp.concatenate([left, right], 1).astype(out_ref.dtype)


def rank_terms(owners, slots, side, pieces, shrink, low, hs):
    rows, depth = side[0].shape
    rank = shrink.shape[0]
    counts = [h.shape[0] // rows for h in hs]
    total_rows = sum(counts) * rows
    whole = lambda shape: pl.BlockSpec(shape, lambda _, *rest: (0, 0))
    upper = lambda height: pl.BlockSpec((height, depth - low), lambda _, *rest: (0, low // (depth - low)))
    flat = [part for piece in pieces for part in piece]
    return pl.pallas_call(
        functools.partial(rank_kernel, counts, len(side), len(pieces)),
        grid_spec=pltpu.PrefetchScalarGridSpec(
            num_scalar_prefetch=2,
            grid=(1,),
            in_specs=[upper(rows)] * len(side)
            + [whole(part.shape) for part in flat]
            + [upper(rank)]
            + [whole(h.shape) for h in hs],
            out_specs=whole((total_rows // 2, 2 * rank)),
            scratch_shapes=[pltpu.VMEM((total_rows, rank), F32)],
        ),
        out_shape=jax.ShapeDtypeStruct((total_rows // 2, 2 * rank), BF16),
        compiler_params=PARAMS,
        name="ranks",
    )(owners, slots, *side, *flat, shrink, *hs)


def block_finish_kernel(blocks, segments, places_ref, slot_ref, *refs):
    accs, refs = refs[:blocks], refs[blocks:]
    expands, refs = refs[:segments], refs[segments:]
    scale_ref, h_ref, cos_ref, sin_ref, out_ref, update = refs
    rank = h_ref.shape[1] // 2
    h = jnp.where(pl.program_id(0) == 0, h_ref[:, :rank], h_ref[:, rank:])
    for segment in range(segments):
        cut = slice(segment * SEG, (segment + 1) * SEG)
        update[cut, :] = jnp.dot(h[cut], expands[segment][0], preferred_element_type=F32)
    rows = accs[0].shape[1]
    for block in range(blocks):
        at = slice(block * rows, (block + 1) * rows)
        cosine, sine = cos_ref[at, :], sin_ref[at, :]
        for head in range(out_ref.shape[1] // HD):
            cut = slice(head * HD, (head + 1) * HD)
            value = accs[block][0, :, cut] * scale_ref[:, cut] + update[at, cut]
            out_ref[at, cut] = rotate(value, cosine, sine).astype(out_ref.dtype)


def block_finish(places, slots, total, expands, scale, h, cosine, sine):
    blocks, rows, cols = total.shape
    half = blocks // 2
    half_rows = half * rows
    segments = half_rows // SEG
    rank = expands.shape[1]

    def acc_at(i):
        return pl.BlockSpec((1, rows, cols), lambda g, places, slots: (places[g * half + i], 0, 0))

    def expand_at(i):
        return pl.BlockSpec((1, rank, cols), lambda g, places, slots: (slots[g * segments + i], 0, 0))

    half_of = lambda width: pl.BlockSpec((half_rows, width), lambda g, *_: (g, 0))
    return pl.pallas_call(
        functools.partial(block_finish_kernel, half, segments),
        grid_spec=pltpu.PrefetchScalarGridSpec(
            num_scalar_prefetch=2,
            grid=(2,),
            in_specs=[acc_at(i) for i in range(half)]
            + [expand_at(i) for i in range(segments)]
            + [
                pl.BlockSpec((1, cols), lambda g, *_: (0, 0)),
                pl.BlockSpec(h.shape, lambda g, *_: (0, 0)),
                half_of(HD),
                half_of(HD),
            ],
            out_specs=half_of(cols),
            scratch_shapes=[pltpu.VMEM((half_rows, cols), F32)],
        ),
        out_shape=jax.ShapeDtypeStruct((blocks * rows, cols), BF16),
        compiler_params=PARAMS,
        name="finish",
    )(places, slots, *([total] * half), *([expands] * segments), scale, h, cosine, sine)


def ring_plan(parts, tokens, weights, scale, shrinks, expands, segment_slot, cosine, sine):
    rows, depth = tokens.shape
    tile = depth // 16
    me = lax.axis_index("tensor")
    owners_table = block_owners()
    owners = jnp.asarray(owners_table)[me]
    places = jnp.asarray(np.argsort(owners_table, axis=1).astype(np.int32))[me]
    slots = jnp.concatenate([segment_slot, me[None].astype(jnp.int32)])
    shrink = shrinks[0]
    send = lambda value, pairs: lax.ppermute(value, "tensor", pairs)
    swap = lambda value: send(value, [(i, i ^ 1) for i in range(parts)])
    onward, back = ring_pairs((1, 1)), ring_pairs((-1, -1))
    across = ring_pairs((1, -1))

    total, hs, held = None, [], 0
    blocks = [tokens, swap(tokens)]
    ahead = [tokens, tokens]
    for r in range(1, ROUNDS):
        ahead = [send(ahead[0], onward), send(ahead[1], back)]
        if total is not None:
            ahead, total = lax.optimization_barrier((ahead, total))
        if r == ROUNDS - 1:
            break
        blocks += ahead + [swap(part) for part in ahead]
        total, h = block_product(blocks, weights, shrink, None, 0, depth, tile, total, held, None, True)
        hs.append(h)
        held += len(blocks)
        blocks = []
    side = ahead + [swap(part) for part in ahead]

    picked = lambda low: jnp.where(me % 2 == 0, *(part[:, low : low + quarter] for part in ahead))
    quarter = depth // 4
    cuts = [q * quarter for q in range(4)]
    arriving = [send(picked(low), across) for low in cuts]
    pieces = [[part, swap(part)] for part in arriving[:2]]

    def late_product(q, total, h, ranked, tie=None):
        xs = side + pieces[q]
        if tie is not None:
            xs, _ = lax.optimization_barrier((xs, tie))
        starts = [0] * len(side) + [cuts[q]] * 2
        return block_product(
            xs, weights, shrink, starts, cuts[q], cuts[q] + quarter, tile, total, held, h, ranked
        )

    h_late = None
    for q in (0, 1):
        total, h_late = late_product(q, total, h_late, True)
        part, total = lax.optimization_barrier((arriving[q + 2], total))
        pieces.append([part, swap(part)])
    h = rank_terms(owners, slots, side, pieces[2:], shrink, cuts[2], hs + [h_late])
    for q, steps in zip((2, 3, None), ([1], [2, 4, 6], [8])):
        more = [send(h, [(i, i ^ step) for i in range(parts)]) for step in steps]
        if q is not None:
            total, _ = late_product(q, total, None, False, h)
        for part in more:
            h = h + part
        h, total = lax.optimization_barrier((h, total))
    return block_finish(places, segment_slot, total, expands, scale, h, cosine, sine)


def body(parts, tokens, weight_codes, column_scale, shrink_store, expand_store, row_adapter, placement, document_lengths):
    rows = tokens.shape[0]
    total_rows = rows * parts
    segment_slot = placement[row_adapter[::SEG]]
    shrinks = jnp.swapaxes(shrink_store, 1, 2)
    expands = jnp.swapaxes(expand_store, 1, 2)
    cosine, sine = rotary_tables(row_positions(document_lengths, total_rows))
    ring = parts == 2 * len(SNAKE) and rows % 16 == 0 and shrinks.shape[0] == 1 and total_rows % (2 * SEG) == 0
    plan = ring_plan if ring else gather_plan
    return plan(parts, tokens, weight_codes, column_scale[None, :], shrinks, expands, segment_slot, cosine, sine)


def solution(mesh):
    placed = (
        P(("groups", "tensor"), None),
        P(None, "tensor"),
        P("tensor"),
        P(("groups", "tensor"), None, None),
        P("groups", "tensor", None),
        P("groups"),
        P("groups"),
        P("groups"),
    )
    return jax.shard_map(
        functools.partial(body, mesh.shape["tensor"]),
        mesh=mesh,
        in_specs=placed,
        out_specs=P("groups", "tensor"),
        check_vma=False,
    )
```

```python
import functools

import jax
import jax.numpy as jnp
import numpy as np
from jax import lax
from jax.experimental import pallas as pl
from jax.experimental.pallas import tpu as pltpu
from jax.sharding import PartitionSpec as P

HD = 128
SEG = 128
VMEM = 20 * 1024 * 1024
F32 = jnp.float32
BF16 = jnp.bfloat16
NT = (((1,), (1,)), ((), ()))
SLOTS = 4
BIG_VMEM = 24 * 1024 * 1024
PARAMS = pltpu.CompilerParams(vmem_limit_bytes=VMEM)
SNAKE = (0, 2, 4, 6, 7, 5, 3, 1)
ROUNDS = len(SNAKE) // 2


def row_positions(document_lengths, total_rows):
    ends = jnp.cumsum(document_lengths)
    row_index = jnp.arange(total_rows, dtype=jnp.int32)
    passed = (row_index[:, None] >= ends[None, :]).astype(jnp.int32)
    return row_index - jnp.sum(passed * document_lengths[None, :], axis=1)


def rotary_tables(positions):
    half_size = HD // 2
    freq_index = jnp.arange(half_size, dtype=F32)
    inverse = jnp.exp(freq_index * (-2.0 / HD) * jnp.log(F32(500000.0)))
    angles = positions.astype(F32)[:, None] * inverse[None, :]
    cosine, sine = jnp.cos(angles), jnp.sin(angles)
    return jnp.concatenate([cosine, cosine], 1), jnp.concatenate([-sine, sine], 1)


def rotate(value, cosine, sine):
    return value * cosine + pltpu.roll(value, HD // 2, 1) * sine


def shrink_kernel(x_ref, s_ref, h_out):
    @pl.when(pl.program_id(0) == 0)
    def _():
        h_out[...] = jnp.zeros_like(h_out)

    h_out[...] += lax.dot_general(x_ref[...], s_ref[...], NT, preferred_element_type=F32)


def shrink_all(x, shrink, tile):
    rows, depth = x.shape
    rank = shrink.shape[0]
    return pl.pallas_call(
        shrink_kernel,
        grid=(depth // tile,),
        in_specs=[
            pl.BlockSpec((rows, tile), lambda k: (0, k)),
            pl.BlockSpec((rank, tile), lambda k: (0, k)),
        ],
        out_specs=pl.BlockSpec((rows, rank), lambda k: (0, 0)),
        out_shape=jax.ShapeDtypeStruct((rows, rank), F32),
        compiler_params=PARAMS,
        name="shrink",
    )(x, shrink)


def project_kernel(x_ref, w_ref, acc_out):
    @pl.when(pl.program_id(0) == 0)
    def _():
        acc_out[...] = jnp.zeros_like(acc_out)

    acc_out[...] += jnp.dot(x_ref[...], w_ref[...], preferred_element_type=F32)


def project_all(x, weights, tile):
    rows, depth = x.shape
    cols = weights.shape[1]
    return pl.pallas_call(
        project_kernel,
        grid=(depth // tile,),
        in_specs=[
            pl.BlockSpec((rows, tile), lambda k: (0, k)),
            pl.BlockSpec((tile, cols), lambda k: (k, 0)),
        ],
        out_specs=pl.BlockSpec((rows, cols), lambda k: (0, 0)),
        out_shape=jax.ShapeDtypeStruct((rows, cols), F32),
        compiler_params=PARAMS,
        name="project",
    )(x, weights)


def segment_finish_kernel(acc_ref, scale_ref, h_ref, expand_ref, cos_ref, sin_ref, out_ref):
    update = jnp.dot(h_ref[...], expand_ref[0], preferred_element_type=F32)
    for head in range(out_ref.shape[1] // HD):
        cut = slice(head * HD, (head + 1) * HD)
        value = acc_ref[:, cut] * scale_ref[:, cut] + update[:, cut]
        out_ref[:, cut] = rotate(value, cos_ref[...], sin_ref[...]).astype(out_ref.dtype)


def segment_finish(acc, scale, h, expand, cosine, sine):
    rows, cols = acc.shape
    rank = h.shape[1]
    return pl.pallas_call(
        segment_finish_kernel,
        grid=(rows // SEG,),
        in_specs=[
            pl.BlockSpec((SEG, cols), lambda r: (r, 0)),
            pl.BlockSpec((1, cols), lambda r: (0, 0)),
            pl.BlockSpec((SEG, rank), lambda r: (r, 0)),
            pl.BlockSpec((1, rank, cols), lambda r: (r, 0, 0)),
            pl.BlockSpec((SEG, HD), lambda r: (r, 0)),
            pl.BlockSpec((SEG, HD), lambda r: (r, 0)),
        ],
        out_specs=pl.BlockSpec((SEG, cols), lambda r: (r, 0)),
        out_shape=jax.ShapeDtypeStruct((rows, cols), BF16),
        compiler_params=PARAMS,
        name="finish",
    )(acc, scale, h, expand, cosine, sine)


def spread(h, parts):
    step = 1
    while step < parts:
        h = h + lax.ppermute(h, "tensor", [(i, i ^ step) for i in range(parts)])
        step *= 2
    return h


def gather_plan(parts, tokens, weights, scale, shrinks, expands, segment_slot, cosine, sine):
    held, rank, depth = shrinks.shape
    tile = depth // 16
    x = lax.all_gather(tokens, "tensor", axis=0, tiled=True)
    row_slot = jnp.repeat(segment_slot, SEG, total_repeat_length=x.shape[0])
    h = jnp.zeros((x.shape[0], rank), BF16)
    for i in range(held):
        mine = (row_slot == lax.axis_index("tensor") * held + i)[:, None]
        h = jnp.where(mine, shrink_all(x, shrinks[i], tile).astype(BF16), h)
    h = spread(h, parts)
    acc = project_all(x, weights, tile)
    return segment_finish(acc, scale, h, expands[segment_slot], cosine, sine)


def block_owners():
    chips = len(SNAKE)
    owners = np.zeros((2 * chips, 2 * chips), np.int32)
    for place, chip in enumerate(SNAKE):
        for core in (0, 1):
            row = [2 * chip + core, 2 * chip + 1 - core]
            for r in range(1, ROUNDS + 1):
                far, near = place - r * (1 - 2 * core), place + r * (1 - 2 * core)
                far, near = SNAKE[far % chips], SNAKE[near % chips]
                if r < ROUNDS:
                    row += [2 * far + core, 2 * near + core, 2 * near + 1 - core, 2 * far + 1 - core]
                else:
                    row += [2 * far + core, 2 * near + 1 - core]
            owners[2 * chip + core] = row
    return owners


def ring_pairs(ways):
    chips = len(SNAKE)
    pairs = []
    for place, chip in enumerate(SNAKE):
        for core in (0, 1):
            pairs.append((2 * chip + core, 2 * SNAKE[(place + ways[core]) % chips] + core))
    return pairs


def block_kernel(starts, low, tile, steps, first, base, fresh, ranked, *refs):
    count = len(starts)
    xs, w_ref, refs = refs[:count], refs[count], refs[count + 1 :]
    if ranked:
        s_ref, refs = refs[0], refs[1:]
    if not first:
        total_in, refs = refs[0], refs[1:]
    if ranked and not fresh:
        h_in, refs = refs[0], refs[1:]
    total_out, refs = refs[0], refs[1:]
    if ranked:
        h_out, refs = refs[0], refs[1:]
    acc, before, x_slots, w_slots, s_slots, sems, total_sems = refs
    rows = xs[0].shape[0]

    def copies(step):
        slot = lax.rem(step, SLOTS)
        at = pl.multiple_of(step * tile, tile)
        sem = lambda i: sems.at[slot, i]
        out = [pltpu.make_async_copy(w_ref.at[pl.ds(low + at, tile)], w_slots.at[slot], sem(count))]
        for i, start in enumerate(starts):
            cut = xs[i].at[:, pl.ds(low - start + at, tile)]
            out.append(pltpu.make_async_copy(cut, x_slots.at[slot, pl.ds(i * rows, rows)], sem(i)))
        if ranked:
            cut = s_ref.at[:, pl.ds(low + at, tile)]
            out.append(pltpu.make_async_copy(cut, s_slots.at[slot], sem(count + 1)))
        return out

    def start(step):
        for copy in copies(step):
            copy.start()

    for step in range(min(SLOTS, steps)):
        start(jnp.int32(step))
    if not fresh:
        load = pltpu.make_async_copy(total_in.at[pl.ds(base, count)], before, total_sems.at[0])
        load.start()
    acc[...] = jnp.zeros_like(acc)
    if ranked:
        h_out[...] = jnp.zeros_like(h_out) if fresh else h_in[...]

    @pl.loop(0, steps)
    def _(step):
        for copy in copies(step):
            copy.wait()
        slot = lax.rem(step, SLOTS)
        x = x_slots[slot]
        acc[...] += jnp.dot(x, w_slots[slot], preferred_element_type=F32).reshape(acc.shape)
        if ranked:
            h_out[...] += lax.dot_general(x, s_slots[slot], NT, preferred_element_type=F32)

        @pl.when(step + SLOTS < steps)
        def _():
            start(step + SLOTS)

    if not fresh:
        load.wait()
        acc[...] += before[...]
    store = pltpu.make_async_copy(acc, total_out.at[pl.ds(base, count)], total_sems.at[1])
    store.start()
    store.wait()


def block_product(xs, weights, shrink, starts, low, high, tile, total, base, h, ranked):
    count = len(xs)
    rows = xs[0].shape[0]
    cols = weights.shape[1]
    rank = shrink.shape[0]
    fresh, first = low == 0, total is None
    anywhere, whole = pl.BlockSpec(memory_space=pl.ANY), pl.BlockSpec(memory_space=pltpu.VMEM)
    operands = list(xs) + [weights]
    specs = [anywhere] * (count + 1)
    if ranked:
        operands.append(shrink)
        specs.append(anywhere)
    aliases = {}
    if not first:
        aliases = {len(operands): 0}
        operands.append(total)
        specs.append(anywhere)
    if ranked and not fresh:
        operands.append(h)
        specs.append(whole)
    outs, out_specs = [jax.ShapeDtypeStruct(total_shape(rows, cols), F32)], [anywhere]
    if ranked:
        outs.append(jax.ShapeDtypeStruct((count * rows, rank), F32))
        out_specs.append(whole)
    steps = (high - low) // tile
    result = pl.pallas_call(
        functools.partial(
            block_kernel, starts or [0] * count, low, tile, steps, first, base, fresh, ranked
        ),
        in_specs=specs,
        out_specs=out_specs,
        out_shape=outs,
        scratch_shapes=[
            pltpu.VMEM((count, rows, cols), F32),
            pltpu.VMEM((1, 8, 128) if fresh else (count, rows, cols), F32),
            pltpu.VMEM((SLOTS, count * rows, tile), BF16),
            pltpu.VMEM((SLOTS, tile, cols), BF16),
            pltpu.VMEM((SLOTS, rank, tile), BF16),
            pltpu.SemaphoreType.DMA((SLOTS, count + 2)),
            pltpu.SemaphoreType.DMA((2,)),
        ],
        input_output_aliases=aliases,
        compiler_params=pltpu.CompilerParams(vmem_limit_bytes=BIG_VMEM),
        cost_estimate=pl.CostEstimate(
            flops=2 * count * rows * (high - low) * cols,
            bytes_accessed=2 * (high - low) * cols,
            transcendentals=0,
        ),
        name="blocks",
    )(*operands)
    return result if ranked else (result[0], h)


def total_shape(rows, cols):
    return (2 * len(SNAKE), rows, cols)


def rank_kernel(counts, owners_ref, slot_ref, xa_ref, xb_ref, s_ref, *refs):
    h_refs, out_ref, placed = refs[:-2], refs[-2], refs[-1]
    rows = xa_ref.shape[0]
    x = jnp.concatenate([xa_ref[...], xb_ref[...]], 0)
    last = lax.dot_general(x, s_ref[...], NT, preferred_element_type=F32)
    block = 0
    for count, source in zip(counts, h_refs + (last,)):
        for i in range(count):
            to = pl.multiple_of(owners_ref[block] * rows, 16)
            placed[pl.ds(to, rows), :] = source[i * rows : (i + 1) * rows, :]
            block += 1
    parts = []
    for segment in range(placed.shape[0] // SEG):
        part = placed[segment * SEG : (segment + 1) * SEG, :]
        parts.append(jnp.where(slot_ref[segment] == slot_ref[slot_ref.shape[0] - 1], part, 0.0))
    half = len(parts) // 2
    left, right = jnp.concatenate(parts[:half], 0), jnp.concatenate(parts[half:], 0)
    out_ref[...] = jnp.concatenate([left, right], 1).astype(out_ref.dtype)


def rank_terms(owners, slots, xs, shrink, hs):
    rows, depth = xs[0].shape
    rank = shrink.shape[0]
    counts = [h.shape[0] // rows for h in hs] + [len(xs)]
    total_rows = sum(counts) * rows
    whole = lambda shape: pl.BlockSpec(shape, lambda _, *rest: (0, 0))
    return pl.pallas_call(
        functools.partial(rank_kernel, counts),
        grid_spec=pltpu.PrefetchScalarGridSpec(
            num_scalar_prefetch=2,
            grid=(1,),
            in_specs=[whole((rows, depth))] * 2
            + [whole((rank, depth))]
            + [whole(h.shape) for h in hs],
            out_specs=whole((total_rows // 2, 2 * rank)),
            scratch_shapes=[pltpu.VMEM((total_rows, rank), F32)],
        ),
        out_shape=jax.ShapeDtypeStruct((total_rows // 2, 2 * rank), BF16),
        compiler_params=PARAMS,
        name="ranks",
    )(owners, slots, *xs, shrink, *hs)


def block_finish_kernel(blocks, segments, places_ref, slot_ref, *refs):
    accs, refs = refs[:blocks], refs[blocks:]
    expands, refs = refs[:segments], refs[segments:]
    scale_ref, h_ref, cos_ref, sin_ref, out_ref, update = refs
    rank = h_ref.shape[1] // 2
    h = jnp.where(pl.program_id(0) == 0, h_ref[:, :rank], h_ref[:, rank:])
    for segment in range(segments):
        cut = slice(segment * SEG, (segment + 1) * SEG)
        update[cut, :] = jnp.dot(h[cut], expands[segment][0], preferred_element_type=F32)
    rows = accs[0].shape[1]
    for block in range(blocks):
        at = slice(block * rows, (block + 1) * rows)
        cosine, sine = cos_ref[at, :], sin_ref[at, :]
        for head in range(out_ref.shape[1] // HD):
            cut = slice(head * HD, (head + 1) * HD)
            value = accs[block][0, :, cut] * scale_ref[:, cut] + update[at, cut]
            out_ref[at, cut] = rotate(value, cosine, sine).astype(out_ref.dtype)


def block_finish(places, slots, total, expands, scale, h, cosine, sine):
    blocks, rows, cols = total.shape
    half = blocks // 2
    half_rows = half * rows
    segments = half_rows // SEG
    rank = expands.shape[1]

    def acc_at(i):
        return pl.BlockSpec((1, rows, cols), lambda g, places, slots: (places[g * half + i], 0, 0))

    def expand_at(i):
        return pl.BlockSpec((1, rank, cols), lambda g, places, slots: (slots[g * segments + i], 0, 0))

    half_of = lambda width: pl.BlockSpec((half_rows, width), lambda g, *_: (g, 0))
    return pl.pallas_call(
        functools.partial(block_finish_kernel, half, segments),
        grid_spec=pltpu.PrefetchScalarGridSpec(
            num_scalar_prefetch=2,
            grid=(2,),
            in_specs=[acc_at(i) for i in range(half)]
            + [expand_at(i) for i in range(segments)]
            + [
                pl.BlockSpec((1, cols), lambda g, *_: (0, 0)),
                pl.BlockSpec(h.shape, lambda g, *_: (0, 0)),
                half_of(HD),
                half_of(HD),
            ],
            out_specs=half_of(cols),
            scratch_shapes=[pltpu.VMEM((half_rows, cols), F32)],
        ),
        out_shape=jax.ShapeDtypeStruct((blocks * rows, cols), BF16),
        compiler_params=PARAMS,
        name="finish",
    )(places, slots, *([total] * half), *([expands] * segments), scale, h, cosine, sine)


def ring_plan(parts, tokens, weights, scale, shrinks, expands, segment_slot, cosine, sine):
    rows, depth = tokens.shape
    tile = depth // 16
    me = lax.axis_index("tensor")
    owners_table = block_owners()
    owners = jnp.asarray(owners_table)[me]
    places = jnp.asarray(np.argsort(owners_table, axis=1).astype(np.int32))[me]
    slots = jnp.concatenate([segment_slot, me[None].astype(jnp.int32)])
    shrink = shrinks[0]
    send = lambda value, pairs: lax.ppermute(value, "tensor", pairs)
    swap = lambda value: send(value, [(i, i ^ 1) for i in range(parts)])
    out, home = ring_pairs((1, -1)), ring_pairs((-1, 1))

    total, hs, held = None, [], 0
    blocks = [tokens, swap(tokens)]
    tables = (owners, places, slots, segment_slot, cosine, sine)
    blocks, tables = lax.optimization_barrier((blocks, tables))
    owners, places, slots, segment_slot, cosine, sine = tables
    ahead = [tokens, tokens]
    for r in range(1, ROUNDS):
        ahead = [send(ahead[0], out), send(ahead[1], home)]
        if total is not None:
            ahead, total = lax.optimization_barrier((ahead, total))
        blocks += ahead + [swap(part) for part in ahead]
        total, h = block_product(blocks, weights, shrink, None, 0, depth, tile, total, held, None, True)
        hs.append(h)
        held += len(blocks)
        blocks = []

    across, total = lax.optimization_barrier((send(ahead[0], out), total))
    across = [across, swap(across)]
    h = rank_terms(owners, slots, across, shrink, hs)
    half = depth // 2
    for low, steps in ((0, [1]), (half, [2, 4, 6]), (None, [8])):
        more = [send(h, [(i, i ^ step) for i in range(parts)]) for step in steps]
        if low is not None:
            xs, _ = lax.optimization_barrier((across, h))
            total = block_product(xs, weights, shrink, None, low, low + half, tile, total, held, None, False)[0]
        for part in more:
            h = h + part
        h, total = lax.optimization_barrier((h, total))
    return block_finish(places, segment_slot, total, expands, scale, h, cosine, sine)


def body(parts, tokens, weight_codes, column_scale, shrink_store, expand_store, row_adapter, placement, document_lengths):
    rows = tokens.shape[0]
    total_rows = rows * parts
    segment_slot = placement[row_adapter[::SEG]]
    shrinks = jnp.swapaxes(shrink_store, 1, 2)
    expands = jnp.swapaxes(expand_store, 1, 2)
    cosine, sine = rotary_tables(row_positions(document_lengths, total_rows))
    ring = parts == 2 * len(SNAKE) and rows % 16 == 0 and shrinks.shape[0] == 1 and total_rows % (2 * SEG) == 0
    plan = ring_plan if ring else gather_plan
    return plan(parts, tokens, weight_codes, column_scale[None, :], shrinks, expands, segment_slot, cosine, sine)


def solution(mesh):
    placed = (
        P(("groups", "tensor"), None),
        P(None, "tensor"),
        P("tensor"),
        P(("groups", "tensor"), None, None),
        P("groups", "tensor", None),
        P("groups"),
        P("groups"),
        P("groups"),
    )
    return jax.shard_map(
        functools.partial(body, mesh.shape["tensor"]),
        mesh=mesh,
        in_specs=placed,
        out_specs=P("groups", "tensor"),
        check_vma=False,
    )
```

```python
import functools

import jax
import jax.numpy as jnp
import numpy as np
from jax import lax
from jax.experimental import pallas as pl
from jax.experimental.pallas import tpu as pltpu
from jax.sharding import PartitionSpec as P

HD = 128
SEG = 128
VMEM = 20 * 1024 * 1024
F32 = jnp.float32
BF16 = jnp.bfloat16
NT = (((1,), (1,)), ((), ()))
SLOTS = 4
BIG_VMEM = 24 * 1024 * 1024
PARAMS = pltpu.CompilerParams(vmem_limit_bytes=VMEM)
SNAKE = (0, 2, 4, 6, 7, 5, 3, 1)
ROUNDS = len(SNAKE) // 2


def row_positions(document_lengths, total_rows):
    ends = jnp.cumsum(document_lengths)
    row_index = jnp.arange(total_rows, dtype=jnp.int32)
    passed = (row_index[:, None] >= ends[None, :]).astype(jnp.int32)
    return row_index - jnp.sum(passed * document_lengths[None, :], axis=1)


def rotary_tables(positions):
    half_size = HD // 2
    freq_index = jnp.arange(half_size, dtype=F32)
    inverse = jnp.exp(freq_index * (-2.0 / HD) * jnp.log(F32(500000.0)))
    angles = positions.astype(F32)[:, None] * inverse[None, :]
    cosine, sine = jnp.cos(angles), jnp.sin(angles)
    return jnp.concatenate([cosine, cosine], 1), jnp.concatenate([-sine, sine], 1)


def rotate(value, cosine, sine):
    return value * cosine + pltpu.roll(value, HD // 2, 1) * sine


def shrink_kernel(x_ref, s_ref, h_out):
    @pl.when(pl.program_id(0) == 0)
    def _():
        h_out[...] = jnp.zeros_like(h_out)

    h_out[...] += lax.dot_general(x_ref[...], s_ref[...], NT, preferred_element_type=F32)


def shrink_all(x, shrink, tile):
    rows, depth = x.shape
    rank = shrink.shape[0]
    return pl.pallas_call(
        shrink_kernel,
        grid=(depth // tile,),
        in_specs=[
            pl.BlockSpec((rows, tile), lambda k: (0, k)),
            pl.BlockSpec((rank, tile), lambda k: (0, k)),
        ],
        out_specs=pl.BlockSpec((rows, rank), lambda k: (0, 0)),
        out_shape=jax.ShapeDtypeStruct((rows, rank), F32),
        compiler_params=PARAMS,
        name="shrink",
    )(x, shrink)


def project_kernel(x_ref, w_ref, acc_out):
    @pl.when(pl.program_id(0) == 0)
    def _():
        acc_out[...] = jnp.zeros_like(acc_out)

    acc_out[...] += jnp.dot(x_ref[...], w_ref[...], preferred_element_type=F32)


def project_all(x, weights, tile):
    rows, depth = x.shape
    cols = weights.shape[1]
    return pl.pallas_call(
        project_kernel,
        grid=(depth // tile,),
        in_specs=[
            pl.BlockSpec((rows, tile), lambda k: (0, k)),
            pl.BlockSpec((tile, cols), lambda k: (k, 0)),
        ],
        out_specs=pl.BlockSpec((rows, cols), lambda k: (0, 0)),
        out_shape=jax.ShapeDtypeStruct((rows, cols), F32),
        compiler_params=PARAMS,
        name="project",
    )(x, weights)


def segment_finish_kernel(acc_ref, scale_ref, h_ref, expand_ref, cos_ref, sin_ref, out_ref):
    update = jnp.dot(h_ref[...], expand_ref[0], preferred_element_type=F32)
    for head in range(out_ref.shape[1] // HD):
        cut = slice(head * HD, (head + 1) * HD)
        value = acc_ref[:, cut] * scale_ref[:, cut] + update[:, cut]
        out_ref[:, cut] = rotate(value, cos_ref[...], sin_ref[...]).astype(out_ref.dtype)


def segment_finish(acc, scale, h, expand, cosine, sine):
    rows, cols = acc.shape
    rank = h.shape[1]
    return pl.pallas_call(
        segment_finish_kernel,
        grid=(rows // SEG,),
        in_specs=[
            pl.BlockSpec((SEG, cols), lambda r: (r, 0)),
            pl.BlockSpec((1, cols), lambda r: (0, 0)),
            pl.BlockSpec((SEG, rank), lambda r: (r, 0)),
            pl.BlockSpec((1, rank, cols), lambda r: (r, 0, 0)),
            pl.BlockSpec((SEG, HD), lambda r: (r, 0)),
            pl.BlockSpec((SEG, HD), lambda r: (r, 0)),
        ],
        out_specs=pl.BlockSpec((SEG, cols), lambda r: (r, 0)),
        out_shape=jax.ShapeDtypeStruct((rows, cols), BF16),
        compiler_params=PARAMS,
        name="finish",
    )(acc, scale, h, expand, cosine, sine)


def spread(h, parts):
    step = 1
    while step < parts:
        h = h + lax.ppermute(h, "tensor", [(i, i ^ step) for i in range(parts)])
        step *= 2
    return h


def gather_plan(parts, tokens, weights, scale, shrinks, expands, segment_slot, cosine, sine):
    held, rank, depth = shrinks.shape
    tile = depth // 16
    x = lax.all_gather(tokens, "tensor", axis=0, tiled=True)
    row_slot = jnp.repeat(segment_slot, SEG, total_repeat_length=x.shape[0])
    h = jnp.zeros((x.shape[0], rank), BF16)
    for i in range(held):
        mine = (row_slot == lax.axis_index("tensor") * held + i)[:, None]
        h = jnp.where(mine, shrink_all(x, shrinks[i], tile).astype(BF16), h)
    h = spread(h, parts)
    acc = project_all(x, weights, tile)
    return segment_finish(acc, scale, h, expands[segment_slot], cosine, sine)


def block_owners():
    chips = len(SNAKE)
    owners = np.zeros((2 * chips, 2 * chips), np.int32)
    for place, chip in enumerate(SNAKE):
        for core in (0, 1):
            row = [2 * chip + core, 2 * chip + 1 - core]
            for r in range(1, ROUNDS + 1):
                far, near = place - r * (1 - 2 * core), place + r * (1 - 2 * core)
                far, near = 2 * SNAKE[far % chips], 2 * SNAKE[near % chips]
                row += [far + core, near + 1 - core]
                if r < ROUNDS:
                    row += [near + core, far + 1 - core]
            owners[2 * chip + core] = row
    return owners


def ring_pairs(ways):
    chips = len(SNAKE)
    pairs = []
    for place, chip in enumerate(SNAKE):
        for core in (0, 1):
            pairs.append((2 * chip + core, 2 * SNAKE[(place + ways[core]) % chips] + core))
    return pairs


def block_kernel(starts, low, tile, steps, first, base, fresh, ranked, *refs):
    count = len(starts)
    xs, w_ref, refs = refs[:count], refs[count], refs[count + 1 :]
    if ranked:
        s_ref, refs = refs[0], refs[1:]
    if not first:
        total_in, refs = refs[0], refs[1:]
    if ranked and not fresh:
        h_in, refs = refs[0], refs[1:]
    total_out, refs = refs[0], refs[1:]
    if ranked:
        h_out, refs = refs[0], refs[1:]
    acc, before, x_slots, w_slots, s_slots, sems, total_sems = refs
    rows = xs[0].shape[0]

    def copies(step):
        slot = lax.rem(step, SLOTS)
        at = pl.multiple_of(step * tile, tile)
        sem = lambda i: sems.at[slot, i]
        out = [pltpu.make_async_copy(w_ref.at[pl.ds(low + at, tile)], w_slots.at[slot], sem(count))]
        for i, start in enumerate(starts):
            cut = xs[i].at[:, pl.ds(low - start + at, tile)]
            out.append(pltpu.make_async_copy(cut, x_slots.at[slot, pl.ds(i * rows, rows)], sem(i)))
        if ranked:
            cut = s_ref.at[:, pl.ds(low + at, tile)]
            out.append(pltpu.make_async_copy(cut, s_slots.at[slot], sem(count + 1)))
        return out

    def start(step):
        for copy in copies(step):
            copy.start()

    for step in range(min(SLOTS, steps)):
        start(jnp.int32(step))
    if not fresh:
        load = pltpu.make_async_copy(total_in.at[pl.ds(base, count)], before, total_sems.at[0])
        load.start()
    acc[...] = jnp.zeros_like(acc)
    if ranked:
        h_out[...] = jnp.zeros_like(h_out) if fresh else h_in[...]

    @pl.loop(0, steps)
    def _(step):
        for copy in copies(step):
            copy.wait()
        slot = lax.rem(step, SLOTS)
        x = x_slots[slot]
        acc[...] += jnp.dot(x, w_slots[slot], preferred_element_type=F32).reshape(acc.shape)
        if ranked:
            h_out[...] += lax.dot_general(x, s_slots[slot], NT, preferred_element_type=F32)

        @pl.when(step + SLOTS < steps)
        def _():
            start(step + SLOTS)

    if not fresh:
        load.wait()
        acc[...] += before[...]
    store = pltpu.make_async_copy(acc, total_out.at[pl.ds(base, count)], total_sems.at[1])
    store.start()
    store.wait()


def block_product(xs, weights, shrink, starts, low, high, tile, total, base, h, ranked):
    count = len(xs)
    rows = xs[0].shape[0]
    cols = weights.shape[1]
    rank = shrink.shape[0]
    fresh, first = low == 0, total is None
    anywhere, whole = pl.BlockSpec(memory_space=pl.ANY), pl.BlockSpec(memory_space=pltpu.VMEM)
    operands = list(xs) + [weights]
    specs = [anywhere] * (count + 1)
    if ranked:
        operands.append(shrink)
        specs.append(anywhere)
    aliases = {}
    if not first:
        aliases = {len(operands): 0}
        operands.append(total)
        specs.append(anywhere)
    if ranked and not fresh:
        operands.append(h)
        specs.append(whole)
    outs, out_specs = [jax.ShapeDtypeStruct(total_shape(rows, cols), F32)], [anywhere]
    if ranked:
        outs.append(jax.ShapeDtypeStruct((count * rows, rank), F32))
        out_specs.append(whole)
    steps = (high - low) // tile
    result = pl.pallas_call(
        functools.partial(
            block_kernel, starts or [0] * count, low, tile, steps, first, base, fresh, ranked
        ),
        in_specs=specs,
        out_specs=out_specs,
        out_shape=outs,
        scratch_shapes=[
            pltpu.VMEM((count, rows, cols), F32),
            pltpu.VMEM((1, 8, 128) if fresh else (count, rows, cols), F32),
            pltpu.VMEM((SLOTS, count * rows, tile), BF16),
            pltpu.VMEM((SLOTS, tile, cols), BF16),
            pltpu.VMEM((SLOTS, rank, tile), BF16),
            pltpu.SemaphoreType.DMA((SLOTS, count + 2)),
            pltpu.SemaphoreType.DMA((2,)),
        ],
        input_output_aliases=aliases,
        compiler_params=pltpu.CompilerParams(vmem_limit_bytes=BIG_VMEM),
        cost_estimate=pl.CostEstimate(
            flops=2 * count * rows * (high - low) * cols,
            bytes_accessed=2 * (high - low) * cols,
            transcendentals=0,
        ),
        name="blocks",
    )(*operands)
    return result if ranked else (result[0], h)


def total_shape(rows, cols):
    return (2 * len(SNAKE), rows, cols)


def some_ranks_kernel(*refs):
    xs, s_ref, out_ref = refs[:-2], refs[-2], refs[-1]
    x = jnp.concatenate([ref[...] for ref in xs], 0)
    out_ref[...] = lax.dot_general(x, s_ref[...], NT, preferred_element_type=F32)


def some_ranks(xs, shrink):
    rows, depth = xs[0].shape
    rank = shrink.shape[0]
    whole = lambda shape: pl.BlockSpec(shape, lambda _: (0, 0))
    return pl.pallas_call(
        some_ranks_kernel,
        grid=(1,),
        in_specs=[whole((rows, depth))] * len(xs) + [whole((rank, depth))],
        out_specs=whole((len(xs) * rows, rank)),
        out_shape=jax.ShapeDtypeStruct((len(xs) * rows, rank), F32),
        compiler_params=PARAMS,
        name="some_ranks",
    )(*xs, shrink)


def rank_kernel(counts, owners_ref, slot_ref, xa_ref, xb_ref, s_ref, *refs):
    h_refs, out_ref, placed = refs[:-2], refs[-2], refs[-1]
    rows = xa_ref.shape[0]
    x = jnp.concatenate([xa_ref[...], xb_ref[...]], 0)
    last = lax.dot_general(x, s_ref[...], NT, preferred_element_type=F32)
    block = 0
    for count, source in zip(counts, h_refs + (last,)):
        for i in range(count):
            to = pl.multiple_of(owners_ref[block] * rows, 16)
            placed[pl.ds(to, rows), :] = source[i * rows : (i + 1) * rows, :]
            block += 1
    parts = []
    for segment in range(placed.shape[0] // SEG):
        part = placed[segment * SEG : (segment + 1) * SEG, :]
        parts.append(jnp.where(slot_ref[segment] == slot_ref[slot_ref.shape[0] - 1], part, 0.0))
    half = len(parts) // 2
    left, right = jnp.concatenate(parts[:half], 0), jnp.concatenate(parts[half:], 0)
    out_ref[...] = jnp.concatenate([left, right], 1).astype(out_ref.dtype)


def rank_terms(owners, slots, xs, shrink, hs):
    rows, depth = xs[0].shape
    rank = shrink.shape[0]
    counts = [h.shape[0] // rows for h in hs] + [len(xs)]
    total_rows = sum(counts) * rows
    whole = lambda shape: pl.BlockSpec(shape, lambda _, *rest: (0, 0))
    return pl.pallas_call(
        functools.partial(rank_kernel, counts),
        grid_spec=pltpu.PrefetchScalarGridSpec(
            num_scalar_prefetch=2,
            grid=(1,),
            in_specs=[whole((rows, depth))] * 2
            + [whole((rank, depth))]
            + [whole(h.shape) for h in hs],
            out_specs=whole((total_rows // 2, 2 * rank)),
            scratch_shapes=[pltpu.VMEM((total_rows, rank), F32)],
        ),
        out_shape=jax.ShapeDtypeStruct((total_rows // 2, 2 * rank), BF16),
        compiler_params=PARAMS,
        name="ranks",
    )(owners, slots, *xs, shrink, *hs)


def block_finish_kernel(blocks, segments, places_ref, slot_ref, *refs):
    accs, refs = refs[:blocks], refs[blocks:]
    expands, refs = refs[:segments], refs[segments:]
    scale_ref, h_ref, cos_ref, sin_ref, out_ref, update = refs
    rank = h_ref.shape[1] // 2
    h = jnp.where(pl.program_id(0) == 0, h_ref[:, :rank], h_ref[:, rank:])
    for segment in range(segments):
        cut = slice(segment * SEG, (segment + 1) * SEG)
        update[cut, :] = jnp.dot(h[cut], expands[segment][0], preferred_element_type=F32)
    rows = accs[0].shape[1]
    for block in range(blocks):
        at = slice(block * rows, (block + 1) * rows)
        cosine, sine = cos_ref[at, :], sin_ref[at, :]
        for head in range(out_ref.shape[1] // HD):
            cut = slice(head * HD, (head + 1) * HD)
            value = accs[block][0, :, cut] * scale_ref[:, cut] + update[at, cut]
            out_ref[at, cut] = rotate(value, cosine, sine).astype(out_ref.dtype)


def block_finish(places, slots, total, expands, scale, h, cosine, sine):
    blocks, rows, cols = total.shape
    half = blocks // 2
    half_rows = half * rows
    segments = half_rows // SEG
    rank = expands.shape[1]

    def acc_at(i):
        return pl.BlockSpec((1, rows, cols), lambda g, places, slots: (places[g * half + i], 0, 0))

    def expand_at(i):
        return pl.BlockSpec((1, rank, cols), lambda g, places, slots: (slots[g * segments + i], 0, 0))

    half_of = lambda width: pl.BlockSpec((half_rows, width), lambda g, *_: (g, 0))
    return pl.pallas_call(
        functools.partial(block_finish_kernel, half, segments),
        grid_spec=pltpu.PrefetchScalarGridSpec(
            num_scalar_prefetch=2,
            grid=(2,),
            in_specs=[acc_at(i) for i in range(half)]
            + [expand_at(i) for i in range(segments)]
            + [
                pl.BlockSpec((1, cols), lambda g, *_: (0, 0)),
                pl.BlockSpec(h.shape, lambda g, *_: (0, 0)),
                half_of(HD),
                half_of(HD),
            ],
            out_specs=half_of(cols),
            scratch_shapes=[pltpu.VMEM((half_rows, cols), F32)],
        ),
        out_shape=jax.ShapeDtypeStruct((blocks * rows, cols), BF16),
        compiler_params=PARAMS,
        name="finish",
    )(places, slots, *([total] * half), *([expands] * segments), scale, h, cosine, sine)


def ring_plan(parts, tokens, weights, scale, shrinks, expands, segment_slot, cosine, sine):
    rows, depth = tokens.shape
    tile = depth // 16
    me = lax.axis_index("tensor")
    owners_table = block_owners()
    owners = jnp.asarray(owners_table)[me]
    places = jnp.asarray(np.argsort(owners_table, axis=1).astype(np.int32))[me]
    slots = jnp.concatenate([segment_slot, me[None].astype(jnp.int32)])
    shrink = shrinks[0]
    send = lambda value, pairs: lax.ppermute(value, "tensor", pairs)
    swap = lambda value: send(value, [(i, i ^ 1) for i in range(parts)])
    out, home = ring_pairs((1, -1)), ring_pairs((-1, 1))

    half = depth // 2
    hs, counts = [], []

    def multiply(xs, total, low=0, high=depth):
        if low == 0:
            hs.append(None)
            counts.append(len(xs))
        held = sum(counts[:-1])
        total, hs[-1] = block_product(xs, weights, shrink, None, low, high, tile, total, held, hs[-1], True)
        return total

    streams = [send(tokens, out), None]
    own = [tokens, swap(tokens)]
    total = multiply(own, None, 0, half)
    second, total = lax.optimization_barrier((tokens, total))
    streams[1] = send(second, home)
    tables = (owners, places, slots, segment_slot, cosine, sine)
    total, tables = lax.optimization_barrier((total, tables))
    owners, places, slots, segment_slot, cosine, sine = tables
    total = multiply(own, total, half, depth)

    blocks, hops = [], 2 * ROUNDS - 1
    totals = [total] * 2
    for hop in range(hops):
        arrived, _ = lax.optimization_barrier((streams[hop % 2], totals[min(hop, hops - 2)]))
        if hop + 2 < hops:
            streams[hop % 2] = send(arrived, home if hop % 2 else out)
        blocks += [arrived, swap(arrived)]
        if hop < hops - 3:
            total = multiply(blocks, total)
            totals.append(total)
            blocks = []
    early = some_ranks(blocks[:-2], shrink)
    hs.append(early)
    held = sum(counts)

    h = rank_terms(owners, slots, blocks[-2:], shrink, hs)
    low = 0
    for high, steps in ((4, [1]), (10, [2, 4, 6]), (16, [8])):
        more = [send(h, [(i, i ^ step) for i in range(parts)]) for step in steps]
        xs, _ = lax.optimization_barrier((blocks, h))
        total = block_product(xs, weights, shrink, None, low * tile, high * tile, tile, total, held, None, False)[0]
        for part in more:
            h = h + part
        h, total = lax.optimization_barrier((h, total))
        low = high
    return block_finish(places, segment_slot, total, expands, scale, h, cosine, sine)


def body(parts, tokens, weight_codes, column_scale, shrink_store, expand_store, row_adapter, placement, document_lengths):
    rows = tokens.shape[0]
    total_rows = rows * parts
    segment_slot = placement[row_adapter[::SEG]]
    shrinks = jnp.swapaxes(shrink_store, 1, 2)
    expands = jnp.swapaxes(expand_store, 1, 2)
    cosine, sine = rotary_tables(row_positions(document_lengths, total_rows))
    ring = parts == 2 * len(SNAKE) and rows % 16 == 0 and shrinks.shape[0] == 1 and total_rows % (2 * SEG) == 0
    plan = ring_plan if ring else gather_plan
    return plan(parts, tokens, weight_codes, column_scale[None, :], shrinks, expands, segment_slot, cosine, sine)


def solution(mesh):
    placed = (
        P(("groups", "tensor"), None),
        P(None, "tensor"),
        P("tensor"),
        P(("groups", "tensor"), None, None),
        P("groups", "tensor", None),
        P("groups"),
        P("groups"),
        P("groups"),
    )
    return jax.shard_map(
        functools.partial(body, mesh.shape["tensor"]),
        mesh=mesh,
        in_specs=placed,
        out_specs=P("groups", "tensor"),
        check_vma=False,
    )
```

```python
import functools

import jax
import jax.numpy as jnp
import numpy as np
from jax import lax
from jax.experimental import pallas as pl
from jax.experimental.pallas import tpu as pltpu
from jax.sharding import PartitionSpec as P

HD = 128
SEG = 128
VMEM = 20 * 1024 * 1024
F32 = jnp.float32
BF16 = jnp.bfloat16
NT = (((1,), (1,)), ((), ()))
SLOTS = 4
CHUNK = 256
BIG_VMEM = 24 * 1024 * 1024
PARAMS = pltpu.CompilerParams(vmem_limit_bytes=VMEM)
SNAKE = (0, 2, 4, 6, 7, 5, 3, 1)
ROUNDS = len(SNAKE) // 2


def row_positions(document_lengths, total_rows):
    ends = jnp.cumsum(document_lengths)
    row_index = jnp.arange(total_rows, dtype=jnp.int32)
    passed = (row_index[:, None] >= ends[None, :]).astype(jnp.int32)
    return row_index - jnp.sum(passed * document_lengths[None, :], axis=1)


def rotary_tables(positions):
    half_size = HD // 2
    freq_index = jnp.arange(half_size, dtype=F32)
    inverse = jnp.exp(freq_index * (-2.0 / HD) * jnp.log(F32(500000.0)))
    angles = positions.astype(F32)[:, None] * inverse[None, :]
    cosine, sine = jnp.cos(angles), jnp.sin(angles)
    return jnp.concatenate([cosine, cosine], 1), jnp.concatenate([-sine, sine], 1)


def rotate(value, cosine, sine):
    return value * cosine + pltpu.roll(value, HD // 2, 1) * sine


def shrink_kernel(x_ref, s_ref, h_out):
    @pl.when(pl.program_id(0) == 0)
    def _():
        h_out[...] = jnp.zeros_like(h_out)

    h_out[...] += lax.dot_general(x_ref[...], s_ref[...], NT, preferred_element_type=F32)


def shrink_all(x, shrink, tile):
    rows, depth = x.shape
    rank = shrink.shape[0]
    return pl.pallas_call(
        shrink_kernel,
        grid=(depth // tile,),
        in_specs=[
            pl.BlockSpec((rows, tile), lambda k: (0, k)),
            pl.BlockSpec((rank, tile), lambda k: (0, k)),
        ],
        out_specs=pl.BlockSpec((rows, rank), lambda k: (0, 0)),
        out_shape=jax.ShapeDtypeStruct((rows, rank), F32),
        compiler_params=PARAMS,
        name="shrink",
    )(x, shrink)


def project_kernel(x_ref, w_ref, acc_out):
    @pl.when(pl.program_id(0) == 0)
    def _():
        acc_out[...] = jnp.zeros_like(acc_out)

    acc_out[...] += jnp.dot(x_ref[...], w_ref[...], preferred_element_type=F32)


def project_all(x, weights, tile):
    rows, depth = x.shape
    cols = weights.shape[1]
    return pl.pallas_call(
        project_kernel,
        grid=(depth // tile,),
        in_specs=[
            pl.BlockSpec((rows, tile), lambda k: (0, k)),
            pl.BlockSpec((tile, cols), lambda k: (k, 0)),
        ],
        out_specs=pl.BlockSpec((rows, cols), lambda k: (0, 0)),
        out_shape=jax.ShapeDtypeStruct((rows, cols), F32),
        compiler_params=PARAMS,
        name="project",
    )(x, weights)


def segment_finish_kernel(acc_ref, scale_ref, h_ref, expand_ref, cos_ref, sin_ref, out_ref):
    update = jnp.dot(h_ref[...], expand_ref[0], preferred_element_type=F32)
    for head in range(out_ref.shape[1] // HD):
        cut = slice(head * HD, (head + 1) * HD)
        value = acc_ref[:, cut] * scale_ref[:, cut] + update[:, cut]
        out_ref[:, cut] = rotate(value, cos_ref[...], sin_ref[...]).astype(out_ref.dtype)


def segment_finish(acc, scale, h, expand, cosine, sine):
    rows, cols = acc.shape
    rank = h.shape[1]
    return pl.pallas_call(
        segment_finish_kernel,
        grid=(rows // SEG,),
        in_specs=[
            pl.BlockSpec((SEG, cols), lambda r: (r, 0)),
            pl.BlockSpec((1, cols), lambda r: (0, 0)),
            pl.BlockSpec((SEG, rank), lambda r: (r, 0)),
            pl.BlockSpec((1, rank, cols), lambda r: (r, 0, 0)),
            pl.BlockSpec((SEG, HD), lambda r: (r, 0)),
            pl.BlockSpec((SEG, HD), lambda r: (r, 0)),
        ],
        out_specs=pl.BlockSpec((SEG, cols), lambda r: (r, 0)),
        out_shape=jax.ShapeDtypeStruct((rows, cols), BF16),
        compiler_params=PARAMS,
        name="finish",
    )(acc, scale, h, expand, cosine, sine)


def spread(h, parts):
    step = 1
    while step < parts:
        h = h + lax.ppermute(h, "tensor", [(i, i ^ step) for i in range(parts)])
        step *= 2
    return h


def gather_plan(parts, tokens, weights, scale, shrinks, expands, segment_slot, cosine, sine):
    held, rank, depth = shrinks.shape
    tile = depth // 16
    x = lax.all_gather(tokens, "tensor", axis=0, tiled=True)
    row_slot = jnp.repeat(segment_slot, SEG, total_repeat_length=x.shape[0])
    h = jnp.zeros((x.shape[0], rank), BF16)
    for i in range(held):
        mine = (row_slot == lax.axis_index("tensor") * held + i)[:, None]
        h = jnp.where(mine, shrink_all(x, shrinks[i], tile).astype(BF16), h)
    h = spread(h, parts)
    acc = project_all(x, weights, tile)
    return segment_finish(acc, scale, h, expands[segment_slot], cosine, sine)


def block_owners():
    chips = len(SNAKE)
    owners = np.zeros((2 * chips, 2 * chips), np.int32)
    for place, chip in enumerate(SNAKE):
        for core in (0, 1):
            row = [2 * chip + core, 2 * chip + 1 - core]
            for r in range(1, ROUNDS + 1):
                far, near = place - r * (1 - 2 * core), place + r * (1 - 2 * core)
                far, near = 2 * SNAKE[far % chips], 2 * SNAKE[near % chips]
                row += [far + core, near + 1 - core]
                if r < ROUNDS:
                    row += [near + core, far + 1 - core]
            owners[2 * chip + core] = row
    return owners


def ring_pairs(ways):
    chips = len(SNAKE)
    pairs = []
    for place, chip in enumerate(SNAKE):
        for core in (0, 1):
            pairs.append((2 * chip + core, 2 * SNAKE[(place + ways[core]) % chips] + core))
    return pairs


def block_kernel(count, low, tile, steps, first, base, fresh, ranked, *refs):
    xs, w_ref, refs = refs[:count], refs[count], refs[count + 1 :]
    if ranked:
        s_refs, refs = refs[:2], refs[2:]
    if not first:
        total_in, refs = refs[0], refs[1:]
    if ranked and not fresh:
        h_in, refs = refs[0], refs[1:]
    total_out, refs = refs[0], refs[1:]
    if ranked:
        h_out, refs = refs[0], refs[1:]
    acc, before, x_slots, w_slots, s_slots, sems, total_sems = refs
    rows = xs[0].shape[0]

    def copies(step):
        slot = lax.rem(step, SLOTS)
        at = pl.multiple_of(step * tile, tile)
        sem = lambda i: sems.at[slot, i]
        out = [pltpu.make_async_copy(w_ref.at[pl.ds(low + at, tile)], w_slots.at[slot], sem(count))]
        for i in range(count):
            cut = xs[i].at[:, pl.ds(low + at, tile)]
            out.append(pltpu.make_async_copy(cut, x_slots.at[slot, pl.ds(i * rows, rows)], sem(i)))
        if ranked:
            for i, s_ref in enumerate(s_refs):
                cut, rank = s_ref.at[:, pl.ds(low + at, tile)], s_ref.shape[0]
                to = s_slots.at[slot, pl.ds(i * rank, rank)]
                out.append(pltpu.make_async_copy(cut, to, sem(count + 1 + i)))
        return out

    def start(step):
        for copy in copies(step):
            copy.start()

    for step in range(min(SLOTS, steps)):
        start(jnp.int32(step))
    if not fresh:
        load = pltpu.make_async_copy(total_in.at[pl.ds(base, count)], before, total_sems.at[0])
        load.start()
    acc[...] = jnp.zeros_like(acc)
    if ranked:
        h_out[...] = jnp.zeros_like(h_out) if fresh else h_in[...]

    @pl.loop(0, steps)
    def _(step):
        for copy in copies(step):
            copy.wait()
        slot = lax.rem(step, SLOTS)
        x = x_slots[slot]
        for left in range(0, acc.shape[2], CHUNK):
            cut = slice(left, left + CHUNK)
            product = jnp.dot(x, w_slots[slot, :, cut], preferred_element_type=F32)
            acc[:, :, cut] += product.reshape(count, rows, CHUNK)
        if ranked:
            h_out[...] += lax.dot_general(x[:rows], s_slots[slot], NT, preferred_element_type=F32)

        @pl.when(step + SLOTS < steps)
        def _():
            start(step + SLOTS)

    if not fresh:
        load.wait()
        acc[...] += before[...]
    store = pltpu.make_async_copy(acc, total_out.at[pl.ds(base, count)], total_sems.at[1])
    store.start()
    store.wait()


def block_product(xs, weights, factors, low, high, tile, total, base, h, ranked):
    count = len(xs)
    rows = xs[0].shape[0]
    cols = weights.shape[1]
    rank = 2 * factors[0].shape[0]
    fresh, first = low == 0, total is None
    anywhere, whole = pl.BlockSpec(memory_space=pl.ANY), pl.BlockSpec(memory_space=pltpu.VMEM)
    operands = list(xs) + [weights]
    specs = [anywhere] * (count + 1)
    if ranked:
        operands += factors
        specs += [anywhere] * 2
    aliases = {}
    if not first:
        aliases = {len(operands): 0}
        operands.append(total)
        specs.append(anywhere)
    if ranked and not fresh:
        operands.append(h)
        specs.append(whole)
    outs, out_specs = [jax.ShapeDtypeStruct(total_shape(rows, cols), F32)], [anywhere]
    if ranked:
        outs.append(jax.ShapeDtypeStruct((rows, rank), F32))
        out_specs.append(whole)
    steps = (high - low) // tile
    result = pl.pallas_call(
        functools.partial(block_kernel, count, low, tile, steps, first, base, fresh, ranked),
        in_specs=specs,
        out_specs=out_specs,
        out_shape=outs,
        scratch_shapes=[
            pltpu.VMEM((count, rows, cols), F32),
            pltpu.VMEM((1, 8, 128) if fresh else (count, rows, cols), F32),
            pltpu.VMEM((SLOTS, count * rows, tile), BF16),
            pltpu.VMEM((SLOTS, tile, cols), BF16),
            pltpu.VMEM((SLOTS, rank, tile), BF16),
            pltpu.SemaphoreType.DMA((SLOTS, count + 3)),
            pltpu.SemaphoreType.DMA((2,)),
        ],
        input_output_aliases=aliases,
        compiler_params=pltpu.CompilerParams(vmem_limit_bytes=BIG_VMEM),
        cost_estimate=pl.CostEstimate(
            flops=2 * count * rows * (high - low) * cols,
            bytes_accessed=2 * (high - low) * cols,
            transcendentals=0,
        ),
        name="blocks",
    )(*operands)
    return result if ranked else (result[0], h)


def total_shape(rows, cols):
    return (2 * len(SNAKE), rows, cols)


def both_ranks(x, factors):
    return jnp.concatenate([lax.dot_general(x, s, NT, preferred_element_type=F32) for s in factors], 1)


def some_ranks_kernel(x_ref, sa_ref, sb_ref, out_ref):
    out_ref[...] = both_ranks(x_ref[...], (sa_ref[...], sb_ref[...]))


def some_ranks(x, factors):
    whole = lambda shape: pl.BlockSpec(shape, lambda _: (0, 0))
    shape = (x.shape[0], 2 * factors[0].shape[0])
    return pl.pallas_call(
        some_ranks_kernel,
        grid=(1,),
        in_specs=[whole(value.shape) for value in (x, *factors)],
        out_specs=whole(shape),
        out_shape=jax.ShapeDtypeStruct(shape, F32),
        compiler_params=PARAMS,
        name="some_ranks",
    )(x, *factors)


def rank_kernel(owners_ref, slot_ref, x_ref, sa_ref, sb_ref, *refs):
    h_refs, out_ref, placed = refs[:-2], refs[-2], refs[-1]
    rows, rank = x_ref.shape[0], sa_ref.shape[0]
    last = both_ranks(x_ref[...], (sa_ref[...], sb_ref[...]))
    placed[...] = jnp.zeros_like(placed)
    for i, source in enumerate(h_refs + (last,)):
        to = pl.multiple_of(owners_ref[2 * i] * rows, 16)
        placed[pl.ds(to, rows), :] = source[...]
    parts = []
    segments = placed.shape[0] // SEG
    for segment in range(segments):
        part = placed[segment * SEG : (segment + 1) * SEG, :]
        mine, other = (slot_ref[segment] == slot_ref[segments + i] for i in (0, 1))
        parts.append(jnp.where(mine, part[:, :rank], jnp.where(other, part[:, rank:], 0.0)))
    half = len(parts) // 2
    left, right = jnp.concatenate(parts[:half], 0), jnp.concatenate(parts[half:], 0)
    out_ref[...] = jnp.concatenate([left, right], 1).astype(out_ref.dtype)


def rank_terms(owners, slots, x, factors, hs):
    rank = factors[0].shape[0]
    total_rows = owners.shape[0] * x.shape[0]
    whole = lambda shape: pl.BlockSpec(shape, lambda _, *rest: (0, 0))
    return pl.pallas_call(
        rank_kernel,
        grid_spec=pltpu.PrefetchScalarGridSpec(
            num_scalar_prefetch=2,
            grid=(1,),
            in_specs=[whole(value.shape) for value in (x, *factors, *hs)],
            out_specs=whole((total_rows // 2, 2 * rank)),
            scratch_shapes=[pltpu.VMEM((total_rows, 2 * rank), F32)],
        ),
        out_shape=jax.ShapeDtypeStruct((total_rows // 2, 2 * rank), BF16),
        compiler_params=PARAMS,
        name="ranks",
    )(owners, slots, x, *factors, *hs)


def block_finish_kernel(blocks, segments, places_ref, slot_ref, *refs):
    accs, refs = refs[:blocks], refs[blocks:]
    expands, refs = refs[:segments], refs[segments:]
    scale_ref, h_ref, cos_ref, sin_ref, out_ref, update = refs
    rank = h_ref.shape[1] // 2
    h = jnp.where(pl.program_id(0) == 0, h_ref[:, :rank], h_ref[:, rank:])
    for segment in range(segments):
        cut = slice(segment * SEG, (segment + 1) * SEG)
        update[cut, :] = jnp.dot(h[cut], expands[segment][0], preferred_element_type=F32)
    rows = accs[0].shape[1]
    for block in range(blocks):
        at = slice(block * rows, (block + 1) * rows)
        cosine, sine = cos_ref[at, :], sin_ref[at, :]
        for head in range(out_ref.shape[1] // HD):
            cut = slice(head * HD, (head + 1) * HD)
            value = accs[block][0, :, cut] * scale_ref[:, cut] + update[at, cut]
            out_ref[at, cut] = rotate(value, cosine, sine).astype(out_ref.dtype)


def block_finish(places, slots, total, expands, scale, h, cosine, sine):
    blocks, rows, cols = total.shape
    half = blocks // 2
    half_rows = half * rows
    segments = half_rows // SEG
    rank = expands.shape[1]

    def acc_at(i):
        return pl.BlockSpec((1, rows, cols), lambda g, places, slots: (places[g * half + i], 0, 0))

    def expand_at(i):
        return pl.BlockSpec((1, rank, cols), lambda g, places, slots: (slots[g * segments + i], 0, 0))

    half_of = lambda width: pl.BlockSpec((half_rows, width), lambda g, *_: (g, 0))
    return pl.pallas_call(
        functools.partial(block_finish_kernel, half, segments),
        grid_spec=pltpu.PrefetchScalarGridSpec(
            num_scalar_prefetch=2,
            grid=(2,),
            in_specs=[acc_at(i) for i in range(half)]
            + [expand_at(i) for i in range(segments)]
            + [
                pl.BlockSpec((1, cols), lambda g, *_: (0, 0)),
                pl.BlockSpec(h.shape, lambda g, *_: (0, 0)),
                half_of(HD),
                half_of(HD),
            ],
            out_specs=half_of(cols),
            scratch_shapes=[pltpu.VMEM((half_rows, cols), F32)],
        ),
        out_shape=jax.ShapeDtypeStruct((blocks * rows, cols), BF16),
        compiler_params=PARAMS,
        name="finish",
    )(places, slots, *([total] * half), *([expands] * segments), scale, h, cosine, sine)


def ring_plan(parts, tokens, weights, scale, shrinks, expands, segment_slot, cosine, sine):
    rows, depth = tokens.shape
    tile = depth // 16
    me = lax.axis_index("tensor")
    owners_table = block_owners()
    owners = jnp.asarray(owners_table)[me]
    places = jnp.asarray(np.argsort(owners_table, axis=1).astype(np.int32))[me]
    slots = jnp.concatenate([segment_slot, jnp.stack([me, me ^ 1]).astype(jnp.int32)])
    send = lambda value, pairs: lax.ppermute(value, "tensor", pairs)
    swap = lambda value: send(value, [(i, i ^ 1) for i in range(parts)])
    out, home = ring_pairs((1, -1)), ring_pairs((-1, 1))

    half, cut = depth // 2, 10 * tile
    hs, counts = [], []

    def multiply(xs, total, low=0, high=depth):
        if low == 0:
            hs.append(None)
            counts.append(len(xs))
        held = sum(counts[:-1])
        total, hs[-1] = block_product(xs, weights, factors, low, high, tile, total, held, hs[-1], True)
        return total

    streams = [send(tokens, out), None]
    own = [tokens, swap(tokens)]
    factors = [shrinks[0], swap(shrinks[0])]
    total = multiply(own, None, 0, half)
    second, total = lax.optimization_barrier((tokens, total))
    streams[1] = send(second, home)
    tables = (owners, places, slots, segment_slot, cosine, sine)
    total, tables = lax.optimization_barrier((total, tables))
    owners, places, slots, segment_slot, cosine, sine = tables
    total = multiply(own, total, half, depth)

    blocks, hops = [], 2 * ROUNDS - 1
    totals, waits = [total] * 2, [0, 1, 2, 3, 4, 6, 7]
    for hop in range(hops):
        arrived, _ = lax.optimization_barrier((streams[hop % 2], totals[waits[hop]]))
        if hop + 2 < hops:
            streams[hop % 2] = send(arrived, home if hop % 2 else out)
        blocks += [arrived, swap(arrived)]
        if hop < hops - 3:
            total = multiply(blocks, total)
            totals.append(total)
            blocks = []
        elif hop == hops - 2:
            hs += [some_ranks(part, factors) for part in blocks[::2]]
            held = sum(counts)
            total = block_product(blocks[:2], weights, factors, 0, cut, tile, total, held, None, False)[0]
            totals.append((total, hs))
        else:
            totals.append(total)
    h = rank_terms(owners, slots, blocks[4], factors, hs)
    for steps, start, low, high in (([1], None, None, None), ([2, 4, 6], 2, 0, cut), ([8], 0, cut, depth)):
        more = [send(h, [(i, i ^ step) for i in range(parts)]) for step in steps]
        if start is not None:
            xs, _ = lax.optimization_barrier((blocks[start:], h))
            total = block_product(xs, weights, factors, low, high, tile, total, held + start, None, False)[0]
        for part in more:
            h = h + part
        h, total = lax.optimization_barrier((h, total))
    return block_finish(places, segment_slot, total, expands, scale, h, cosine, sine)


def body(parts, tokens, weight_codes, column_scale, shrink_store, expand_store, row_adapter, placement, document_lengths):
    rows = tokens.shape[0]
    total_rows = rows * parts
    segment_slot = placement[row_adapter[::SEG]]
    shrinks = jnp.swapaxes(shrink_store, 1, 2)
    expands = jnp.swapaxes(expand_store, 1, 2)
    cosine, sine = rotary_tables(row_positions(document_lengths, total_rows))
    ring = parts == 2 * len(SNAKE) and rows % 16 == 0 and shrinks.shape[0] == 1 and total_rows % (2 * SEG) == 0
    plan = ring_plan if ring else gather_plan
    return plan(parts, tokens, weight_codes, column_scale[None, :], shrinks, expands, segment_slot, cosine, sine)


def solution(mesh):
    placed = (
        P(("groups", "tensor"), None),
        P(None, "tensor"),
        P("tensor"),
        P(("groups", "tensor"), None, None),
        P("groups", "tensor", None),
        P("groups"),
        P("groups"),
        P("groups"),
    )
    return jax.shard_map(
        functools.partial(body, mesh.shape["tensor"]),
        mesh=mesh,
        in_specs=placed,
        out_specs=P("groups", "tensor"),
        check_vma=False,
    )
```

```python
import functools

import jax
import jax.numpy as jnp
import numpy as np
from jax import lax
from jax.experimental import pallas as pl
from jax.experimental.pallas import tpu as pltpu
from jax.sharding import PartitionSpec as P

HD = 128
SEG = 128
VMEM = 20 * 1024 * 1024
F32 = jnp.float32
BF16 = jnp.bfloat16
NT = (((1,), (1,)), ((), ()))
SLOTS = 4
CHUNK = 256
BIG_VMEM = 24 * 1024 * 1024
PARAMS = pltpu.CompilerParams(vmem_limit_bytes=VMEM)
SNAKE = (0, 2, 4, 6, 7, 5, 3, 1)
ROUNDS = len(SNAKE) // 2


def row_positions(document_lengths, total_rows):
    ends = jnp.cumsum(document_lengths)
    row_index = jnp.arange(total_rows, dtype=jnp.int32)
    passed = (row_index[:, None] >= ends[None, :]).astype(jnp.int32)
    return row_index - jnp.sum(passed * document_lengths[None, :], axis=1)


def rotary_tables(positions):
    half_size = HD // 2
    freq_index = jnp.arange(half_size, dtype=F32)
    inverse = jnp.exp(freq_index * (-2.0 / HD) * jnp.log(F32(500000.0)))
    angles = positions.astype(F32)[:, None] * inverse[None, :]
    cosine, sine = jnp.cos(angles), jnp.sin(angles)
    return jnp.concatenate([cosine, cosine], 1), jnp.concatenate([-sine, sine], 1)


def rotate(value, cosine, sine):
    return value * cosine + pltpu.roll(value, HD // 2, 1) * sine


def shrink_kernel(x_ref, s_ref, h_out):
    @pl.when(pl.program_id(0) == 0)
    def _():
        h_out[...] = jnp.zeros_like(h_out)

    h_out[...] += lax.dot_general(x_ref[...], s_ref[...], NT, preferred_element_type=F32)


def shrink_all(x, shrink, tile):
    rows, depth = x.shape
    rank = shrink.shape[0]
    return pl.pallas_call(
        shrink_kernel,
        grid=(depth // tile,),
        in_specs=[
            pl.BlockSpec((rows, tile), lambda k: (0, k)),
            pl.BlockSpec((rank, tile), lambda k: (0, k)),
        ],
        out_specs=pl.BlockSpec((rows, rank), lambda k: (0, 0)),
        out_shape=jax.ShapeDtypeStruct((rows, rank), F32),
        compiler_params=PARAMS,
        name="shrink",
    )(x, shrink)


def project_kernel(x_ref, w_ref, acc_out):
    @pl.when(pl.program_id(0) == 0)
    def _():
        acc_out[...] = jnp.zeros_like(acc_out)

    acc_out[...] += jnp.dot(x_ref[...], w_ref[...], preferred_element_type=F32)


def project_all(x, weights, tile):
    rows, depth = x.shape
    cols = weights.shape[1]
    return pl.pallas_call(
        project_kernel,
        grid=(depth // tile,),
        in_specs=[
            pl.BlockSpec((rows, tile), lambda k: (0, k)),
            pl.BlockSpec((tile, cols), lambda k: (k, 0)),
        ],
        out_specs=pl.BlockSpec((rows, cols), lambda k: (0, 0)),
        out_shape=jax.ShapeDtypeStruct((rows, cols), F32),
        compiler_params=PARAMS,
        name="project",
    )(x, weights)


def segment_finish_kernel(acc_ref, scale_ref, h_ref, expand_ref, cos_ref, sin_ref, out_ref):
    update = jnp.dot(h_ref[...], expand_ref[0], preferred_element_type=F32)
    for head in range(out_ref.shape[1] // HD):
        cut = slice(head * HD, (head + 1) * HD)
        value = acc_ref[:, cut] * scale_ref[:, cut] + update[:, cut]
        out_ref[:, cut] = rotate(value, cos_ref[...], sin_ref[...]).astype(out_ref.dtype)


def segment_finish(acc, scale, h, expand, cosine, sine):
    rows, cols = acc.shape
    rank = h.shape[1]
    return pl.pallas_call(
        segment_finish_kernel,
        grid=(rows // SEG,),
        in_specs=[
            pl.BlockSpec((SEG, cols), lambda r: (r, 0)),
            pl.BlockSpec((1, cols), lambda r: (0, 0)),
            pl.BlockSpec((SEG, rank), lambda r: (r, 0)),
            pl.BlockSpec((1, rank, cols), lambda r: (r, 0, 0)),
            pl.BlockSpec((SEG, HD), lambda r: (r, 0)),
            pl.BlockSpec((SEG, HD), lambda r: (r, 0)),
        ],
        out_specs=pl.BlockSpec((SEG, cols), lambda r: (r, 0)),
        out_shape=jax.ShapeDtypeStruct((rows, cols), BF16),
        compiler_params=PARAMS,
        name="finish",
    )(acc, scale, h, expand, cosine, sine)


def spread(h, parts):
    step = 1
    while step < parts:
        h = h + lax.ppermute(h, "tensor", [(i, i ^ step) for i in range(parts)])
        step *= 2
    return h


def gather_plan(parts, tokens, weights, scale, shrinks, expands, segment_slot, cosine, sine):
    held, rank, depth = shrinks.shape
    tile = depth // 16
    x = lax.all_gather(tokens, "tensor", axis=0, tiled=True)
    row_slot = jnp.repeat(segment_slot, SEG, total_repeat_length=x.shape[0])
    h = jnp.zeros((x.shape[0], rank), BF16)
    for i in range(held):
        mine = (row_slot == lax.axis_index("tensor") * held + i)[:, None]
        h = jnp.where(mine, shrink_all(x, shrinks[i], tile).astype(BF16), h)
    h = spread(h, parts)
    acc = project_all(x, weights, tile)
    return segment_finish(acc, scale, h, expands[segment_slot], cosine, sine)


def block_owners():
    chips = len(SNAKE)
    owners = np.zeros((2 * chips, 2 * chips), np.int32)
    for place, chip in enumerate(SNAKE):
        for core in (0, 1):
            row = [2 * chip + core, 2 * chip + 1 - core]
            for r in range(1, ROUNDS + 1):
                far, near = place - r * (1 - 2 * core), place + r * (1 - 2 * core)
                far, near = 2 * SNAKE[far % chips], 2 * SNAKE[near % chips]
                row += [far + core, near + 1 - core]
                if r < ROUNDS:
                    row += [near + core, far + 1 - core]
            owners[2 * chip + core] = row
    return owners


def ring_pairs(ways):
    chips = len(SNAKE)
    pairs = []
    for place, chip in enumerate(SNAKE):
        for core in (0, 1):
            pairs.append((2 * chip + core, 2 * SNAKE[(place + ways[core]) % chips] + core))
    return pairs


def block_kernel(count, low, tile, steps, first, base, fresh, ranked, *refs):
    xs, w_ref, refs = refs[:count], refs[count], refs[count + 1 :]
    if ranked:
        s_refs, refs = refs[:2], refs[2:]
    if not first:
        total_in, refs = refs[0], refs[1:]
    if ranked and not fresh:
        h_in, refs = refs[0], refs[1:]
    total_out, refs = refs[0], refs[1:]
    if ranked:
        h_out, refs = refs[0], refs[1:]
    acc, before, x_slots, w_slots, s_slots, sems, total_sems = refs
    rows = xs[0].shape[0]

    def copies(step):
        slot = lax.rem(step, SLOTS)
        at = pl.multiple_of(step * tile, tile)
        sem = lambda i: sems.at[slot, i]
        out = [pltpu.make_async_copy(w_ref.at[pl.ds(low + at, tile)], w_slots.at[slot], sem(count))]
        for i in range(count):
            cut = xs[i].at[:, pl.ds(low + at, tile)]
            out.append(pltpu.make_async_copy(cut, x_slots.at[slot, pl.ds(i * rows, rows)], sem(i)))
        if ranked:
            for i, s_ref in enumerate(s_refs):
                cut, rank = s_ref.at[:, pl.ds(low + at, tile)], s_ref.shape[0]
                to = s_slots.at[slot, pl.ds(i * rank, rank)]
                out.append(pltpu.make_async_copy(cut, to, sem(count + 1 + i)))
        return out

    def start(step):
        for copy in copies(step):
            copy.start()

    for step in range(min(SLOTS, steps)):
        start(jnp.int32(step))
    if not fresh:
        load = pltpu.make_async_copy(total_in.at[pl.ds(base, count)], before, total_sems.at[0])
        load.start()
    acc[...] = jnp.zeros_like(acc)
    if ranked:
        h_out[...] = jnp.zeros_like(h_out) if fresh else h_in[...]

    @pl.loop(0, steps)
    def _(step):
        for copy in copies(step):
            copy.wait()
        slot = lax.rem(step, SLOTS)
        x = x_slots[slot]
        for left in range(0, acc.shape[2], CHUNK):
            cut = slice(left, left + CHUNK)
            product = jnp.dot(x, w_slots[slot, :, cut], preferred_element_type=F32)
            acc[:, :, cut] += product.reshape(count, rows, CHUNK)
        if ranked:
            h_out[...] += lax.dot_general(x[:rows], s_slots[slot], NT, preferred_element_type=F32)

        @pl.when(step + SLOTS < steps)
        def _():
            start(step + SLOTS)

    if not fresh:
        load.wait()
        acc[...] += before[...]
    store = pltpu.make_async_copy(acc, total_out.at[pl.ds(base, count)], total_sems.at[1])
    store.start()
    store.wait()


def block_product(xs, weights, factors, low, high, tile, total, base, h, ranked):
    count = len(xs)
    rows = xs[0].shape[0]
    cols = weights.shape[1]
    rank = 2 * factors[0].shape[0]
    fresh, first = low == 0, total is None
    anywhere, whole = pl.BlockSpec(memory_space=pl.ANY), pl.BlockSpec(memory_space=pltpu.VMEM)
    operands = list(xs) + [weights]
    specs = [anywhere] * (count + 1)
    if ranked:
        operands += factors
        specs += [anywhere] * 2
    aliases = {}
    if not first:
        aliases = {len(operands): 0}
        operands.append(total)
        specs.append(anywhere)
    if ranked and not fresh:
        operands.append(h)
        specs.append(whole)
    outs, out_specs = [jax.ShapeDtypeStruct(total_shape(rows, cols), F32)], [anywhere]
    if ranked:
        outs.append(jax.ShapeDtypeStruct((rows, rank), F32))
        out_specs.append(whole)
    steps = (high - low) // tile
    result = pl.pallas_call(
        functools.partial(block_kernel, count, low, tile, steps, first, base, fresh, ranked),
        in_specs=specs,
        out_specs=out_specs,
        out_shape=outs,
        scratch_shapes=[
            pltpu.VMEM((count, rows, cols), F32),
            pltpu.VMEM((1, 8, 128) if fresh else (count, rows, cols), F32),
            pltpu.VMEM((SLOTS, count * rows, tile), BF16),
            pltpu.VMEM((SLOTS, tile, cols), BF16),
            pltpu.VMEM((SLOTS, rank, tile), BF16),
            pltpu.SemaphoreType.DMA((SLOTS, count + 3)),
            pltpu.SemaphoreType.DMA((2,)),
        ],
        input_output_aliases=aliases,
        compiler_params=pltpu.CompilerParams(vmem_limit_bytes=BIG_VMEM),
        cost_estimate=pl.CostEstimate(
            flops=2 * count * rows * (high - low) * cols,
            bytes_accessed=2 * (high - low) * cols,
            transcendentals=0,
        ),
        name="blocks",
    )(*operands)
    return result if ranked else (result[0], h)


def total_shape(rows, cols):
    return (2 * len(SNAKE), rows, cols)


def both_ranks(x, factors):
    return jnp.concatenate([lax.dot_general(x, s, NT, preferred_element_type=F32) for s in factors], 1)


def some_ranks_kernel(x_ref, sa_ref, sb_ref, out_ref):
    out_ref[...] = both_ranks(x_ref[...], (sa_ref[...], sb_ref[...]))


def some_ranks(x, factors):
    whole = lambda shape: pl.BlockSpec(shape, lambda _: (0, 0))
    shape = (x.shape[0], 2 * factors[0].shape[0])
    return pl.pallas_call(
        some_ranks_kernel,
        grid=(1,),
        in_specs=[whole(value.shape) for value in (x, *factors)],
        out_specs=whole(shape),
        out_shape=jax.ShapeDtypeStruct(shape, F32),
        compiler_params=PARAMS,
        name="some_ranks",
    )(x, *factors)


def rank_kernel(owners_ref, slot_ref, x_ref, sa_ref, sb_ref, *refs):
    h_refs, out_ref, placed = refs[:-2], refs[-2], refs[-1]
    rows, rank = x_ref.shape[0], sa_ref.shape[0]
    last = both_ranks(x_ref[...], (sa_ref[...], sb_ref[...]))
    segments = slot_ref.shape[0] - 2
    for i, source in enumerate(h_refs + (last,)):
        owner = owners_ref[2 * i]
        segment = owner * rows // SEG
        after = jnp.minimum(segment + 1, segments - 1)
        row = owner * rows + lax.broadcasted_iota(jnp.int32, (rows, rank), 0)
        slot = jnp.where(row < (segment + 1) * SEG, slot_ref[segment], slot_ref[after])
        terms = jnp.where(slot == slot_ref[segments + 1], source[:, rank:], 0.0)
        terms = jnp.where(slot == slot_ref[segments], source[:, :rank], terms)
        placed[pl.ds(pl.multiple_of(owner // 2 * rows, 16), rows), :] = terms
    half = placed.shape[0] // 2
    out_ref[...] = jnp.concatenate([placed[:half, :], placed[half:, :]], 1).astype(out_ref.dtype)


def rank_terms(owners, slots, x, factors, hs):
    rank = factors[0].shape[0]
    core_rows = owners.shape[0] // 2 * x.shape[0]
    whole = lambda shape: pl.BlockSpec(shape, lambda _, *rest: (0, 0))
    return pl.pallas_call(
        rank_kernel,
        grid_spec=pltpu.PrefetchScalarGridSpec(
            num_scalar_prefetch=2,
            grid=(1,),
            in_specs=[whole(value.shape) for value in (x, *factors, *hs)],
            out_specs=whole((core_rows // 2, 2 * rank)),
            scratch_shapes=[pltpu.VMEM((core_rows, rank), F32)],
        ),
        out_shape=jax.ShapeDtypeStruct((core_rows // 2, 2 * rank), BF16),
        compiler_params=PARAMS,
        name="ranks",
    )(owners, slots, x, *factors, *hs)


def block_finish_kernel(blocks, segments, places_ref, slot_ref, core_ref, *refs):
    accs, refs = refs[:blocks], refs[blocks:]
    expands, refs = refs[:segments], refs[segments:]
    scale_ref, mine_ref, other_ref, cos_ref, sin_ref, out_ref, h, update = refs
    rank = mine_ref.shape[1] // 2
    rows = accs[0].shape[1]
    first = pl.program_id(0) == 0
    even = core_ref[0] == 0
    mine, other = (jnp.where(first, ref[:, :rank], ref[:, rank:]) for ref in (mine_ref, other_ref))
    for core, terms in enumerate((jnp.where(even, mine, other), jnp.where(even, other, mine))):
        for i in range(blocks // 2):
            at = (2 * i + core) * rows
            h[at : at + rows, :] = terms[i * rows : (i + 1) * rows]
    for segment in range(segments):
        cut = slice(segment * SEG, (segment + 1) * SEG)
        update[cut, :] = jnp.dot(h[cut, :], expands[segment][0], preferred_element_type=F32)
    for block in range(blocks):
        at = slice(block * rows, (block + 1) * rows)
        cosine, sine = cos_ref[at, :], sin_ref[at, :]
        for head in range(out_ref.shape[1] // HD):
            cut = slice(head * HD, (head + 1) * HD)
            value = accs[block][0, :, cut] * scale_ref[:, cut] + update[at, cut]
            out_ref[at, cut] = rotate(value, cosine, sine).astype(out_ref.dtype)


def block_finish(places, slots, core, total, expands, scale, mine, other, cosine, sine):
    blocks, rows, cols = total.shape
    half = blocks // 2
    half_rows = half * rows
    segments = half_rows // SEG
    rank = expands.shape[1]

    def acc_at(i):
        return pl.BlockSpec((1, rows, cols), lambda g, places, *_: (places[g * half + i], 0, 0))

    def expand_at(i):
        return pl.BlockSpec((1, rank, cols), lambda g, places, slots, _: (slots[g * segments + i], 0, 0))

    half_of = lambda width: pl.BlockSpec((half_rows, width), lambda g, *_: (g, 0))
    return pl.pallas_call(
        functools.partial(block_finish_kernel, half, segments),
        grid_spec=pltpu.PrefetchScalarGridSpec(
            num_scalar_prefetch=3,
            grid=(2,),
            in_specs=[acc_at(i) for i in range(half)]
            + [expand_at(i) for i in range(segments)]
            + [
                pl.BlockSpec((1, cols), lambda g, *_: (0, 0)),
                pl.BlockSpec(mine.shape, lambda g, *_: (0, 0)),
                pl.BlockSpec(other.shape, lambda g, *_: (0, 0)),
                half_of(HD),
                half_of(HD),
            ],
            out_specs=half_of(cols),
            scratch_shapes=[pltpu.VMEM((half_rows, rank), BF16), pltpu.VMEM((half_rows, cols), F32)],
        ),
        out_shape=jax.ShapeDtypeStruct((blocks * rows, cols), BF16),
        compiler_params=PARAMS,
        name="finish",
    )(places, slots, core, *([total] * half), *([expands] * segments), scale, mine, other, cosine, sine)


def ring_plan(parts, tokens, weights, scale, shrinks, expands, segment_slot, cosine, sine):
    rows, depth = tokens.shape
    tile = depth // 16
    me = lax.axis_index("tensor")
    owners_table = block_owners()
    owners = jnp.asarray(owners_table)[me]
    places = jnp.asarray(np.argsort(owners_table, axis=1).astype(np.int32))[me]
    slots = jnp.concatenate([segment_slot, jnp.stack([me, me ^ 1]).astype(jnp.int32)])
    send = lambda value, pairs: lax.ppermute(value, "tensor", pairs)
    swap = lambda value: send(value, [(i, i ^ 1) for i in range(parts)])
    out, home = ring_pairs((1, -1)), ring_pairs((-1, 1))

    half, cut = depth // 2, 10 * tile
    hs, counts = [], []

    def multiply(xs, total, low=0, high=depth):
        if low == 0:
            hs.append(None)
            counts.append(len(xs))
        held = sum(counts[:-1])
        total, hs[-1] = block_product(xs, weights, factors, low, high, tile, total, held, hs[-1], True)
        return total

    streams = [send(tokens, out), None]
    own = [tokens, swap(tokens)]
    factors = [shrinks[0], swap(shrinks[0])]
    total = multiply(own, None, 0, half)
    second, total = lax.optimization_barrier((tokens, total))
    streams[1] = send(second, home)
    core = (me % 2)[None].astype(jnp.int32)
    tables = (owners, places, slots, core, segment_slot, cosine, sine)
    total, tables = lax.optimization_barrier((total, tables))
    owners, places, slots, core, segment_slot, cosine, sine = tables
    total = multiply(own, total, half, depth)

    blocks, hops = [], 2 * ROUNDS - 1
    totals, waits = [total] * 2, [0, 1, 2, 3, 4, 6, 7]
    for hop in range(hops):
        arrived, _ = lax.optimization_barrier((streams[hop % 2], totals[waits[hop]]))
        if hop + 2 < hops:
            streams[hop % 2] = send(arrived, home if hop % 2 else out)
        blocks += [arrived, swap(arrived)]
        if hop < hops - 3:
            total = multiply(blocks, total)
            totals.append(total)
            blocks = []
        elif hop == hops - 2:
            hs += [some_ranks(part, factors) for part in blocks[::2]]
            held = sum(counts)
            total = block_product(blocks[:2], weights, factors, 0, cut, tile, total, held, None, False)[0]
            totals.append((total, hs))
        else:
            totals.append(total)
    h = rank_terms(owners, slots, blocks[4], factors, hs)
    beside = lambda step: send(h, [(i, i ^ step) for i in range(parts)])

    def last_product(start, low, high, total):
        xs, _ = lax.optimization_barrier((blocks[start:], h))
        return block_product(xs, weights, factors, low, high, tile, total, held + start, None, False)[0]

    near = [beside(step) for step in (2, 4, 6)]
    near, total = lax.optimization_barrier((near, last_product(2, 0, cut, total)))
    h = h + near[0] + near[1] + near[2]
    far = [beside(step) for step in (8, 1, 9)]
    far, total = lax.optimization_barrier((far, last_product(0, cut, depth, total)))
    mine, other = h + far[0], far[1] + far[2]
    return block_finish(places, segment_slot, core, total, expands, scale, mine, other, cosine, sine)


def body(parts, tokens, weight_codes, column_scale, shrink_store, expand_store, row_adapter, placement, document_lengths):
    rows = tokens.shape[0]
    total_rows = rows * parts
    segment_slot = placement[row_adapter[::SEG]]
    shrinks = jnp.swapaxes(shrink_store, 1, 2)
    expands = jnp.swapaxes(expand_store, 1, 2)
    cosine, sine = rotary_tables(row_positions(document_lengths, total_rows))
    ring = parts == 2 * len(SNAKE) and rows % 16 == 0 and shrinks.shape[0] == 1 and total_rows % (2 * SEG) == 0
    plan = ring_plan if ring else gather_plan
    return plan(parts, tokens, weight_codes, column_scale[None, :], shrinks, expands, segment_slot, cosine, sine)


def solution(mesh):
    placed = (
        P(("groups", "tensor"), None),
        P(None, "tensor"),
        P("tensor"),
        P(("groups", "tensor"), None, None),
        P("groups", "tensor", None),
        P("groups"),
        P("groups"),
        P("groups"),
    )
    return jax.shard_map(
        functools.partial(body, mesh.shape["tensor"]),
        mesh=mesh,
        in_specs=placed,
        out_specs=P("groups", "tensor"),
        check_vma=False,
    )
```

```python
import functools

import jax
import jax.numpy as jnp
import numpy as np
from jax import lax
from jax.experimental import pallas as pl
from jax.experimental.pallas import tpu as pltpu
from jax.sharding import PartitionSpec as P

HD = 128
SEG = 128
VMEM = 20 * 1024 * 1024
F32 = jnp.float32
BF16 = jnp.bfloat16
NT = (((1,), (1,)), ((), ()))
SLOTS = 4
CHUNK = 256
BIG_VMEM = 24 * 1024 * 1024
PARAMS = pltpu.CompilerParams(vmem_limit_bytes=VMEM)
SNAKE = (0, 2, 4, 6, 7, 5, 3, 1)
ROUNDS = len(SNAKE) // 2


def row_positions(document_lengths, total_rows):
    ends = jnp.cumsum(document_lengths)
    row_index = jnp.arange(total_rows, dtype=jnp.int32)
    passed = (row_index[:, None] >= ends[None, :]).astype(jnp.int32)
    return row_index - jnp.sum(passed * document_lengths[None, :], axis=1)


def rotary_tables(positions):
    half_size = HD // 2
    freq_index = jnp.arange(half_size, dtype=F32)
    inverse = jnp.exp(freq_index * (-2.0 / HD) * jnp.log(F32(500000.0)))
    angles = positions.astype(F32)[:, None] * inverse[None, :]
    cosine, sine = jnp.cos(angles), jnp.sin(angles)
    return jnp.concatenate([cosine, cosine], 1), jnp.concatenate([-sine, sine], 1)


def small_tables(row_adapter, placement, document_lengths, total_rows):
    segment_slot = placement[row_adapter[::SEG]]
    return segment_slot, *rotary_tables(row_positions(document_lengths, total_rows))


def rotate(value, cosine, sine):
    return value * cosine + pltpu.roll(value, HD // 2, 1) * sine


def shrink_kernel(x_ref, s_ref, h_out):
    @pl.when(pl.program_id(0) == 0)
    def _():
        h_out[...] = jnp.zeros_like(h_out)

    h_out[...] += lax.dot_general(x_ref[...], s_ref[...], NT, preferred_element_type=F32)


def shrink_all(x, shrink, tile):
    rows, depth = x.shape
    rank = shrink.shape[0]
    return pl.pallas_call(
        shrink_kernel,
        grid=(depth // tile,),
        in_specs=[
            pl.BlockSpec((rows, tile), lambda k: (0, k)),
            pl.BlockSpec((rank, tile), lambda k: (0, k)),
        ],
        out_specs=pl.BlockSpec((rows, rank), lambda k: (0, 0)),
        out_shape=jax.ShapeDtypeStruct((rows, rank), F32),
        compiler_params=PARAMS,
        name="shrink",
    )(x, shrink)


def project_kernel(x_ref, w_ref, acc_out):
    @pl.when(pl.program_id(0) == 0)
    def _():
        acc_out[...] = jnp.zeros_like(acc_out)

    acc_out[...] += jnp.dot(x_ref[...], w_ref[...], preferred_element_type=F32)


def project_all(x, weights, tile):
    rows, depth = x.shape
    cols = weights.shape[1]
    return pl.pallas_call(
        project_kernel,
        grid=(depth // tile,),
        in_specs=[
            pl.BlockSpec((rows, tile), lambda k: (0, k)),
            pl.BlockSpec((tile, cols), lambda k: (k, 0)),
        ],
        out_specs=pl.BlockSpec((rows, cols), lambda k: (0, 0)),
        out_shape=jax.ShapeDtypeStruct((rows, cols), F32),
        compiler_params=PARAMS,
        name="project",
    )(x, weights)


def segment_finish_kernel(acc_ref, scale_ref, h_ref, expand_ref, cos_ref, sin_ref, out_ref):
    update = jnp.dot(h_ref[...], expand_ref[0], preferred_element_type=F32)
    for head in range(out_ref.shape[1] // HD):
        cut = slice(head * HD, (head + 1) * HD)
        value = acc_ref[:, cut] * scale_ref[:, cut] + update[:, cut]
        out_ref[:, cut] = rotate(value, cos_ref[...], sin_ref[...]).astype(out_ref.dtype)


def segment_finish(acc, scale, h, expand, cosine, sine):
    rows, cols = acc.shape
    rank = h.shape[1]
    return pl.pallas_call(
        segment_finish_kernel,
        grid=(rows // SEG,),
        in_specs=[
            pl.BlockSpec((SEG, cols), lambda r: (r, 0)),
            pl.BlockSpec((1, cols), lambda r: (0, 0)),
            pl.BlockSpec((SEG, rank), lambda r: (r, 0)),
            pl.BlockSpec((1, rank, cols), lambda r: (r, 0, 0)),
            pl.BlockSpec((SEG, HD), lambda r: (r, 0)),
            pl.BlockSpec((SEG, HD), lambda r: (r, 0)),
        ],
        out_specs=pl.BlockSpec((SEG, cols), lambda r: (r, 0)),
        out_shape=jax.ShapeDtypeStruct((rows, cols), BF16),
        compiler_params=PARAMS,
        name="finish",
    )(acc, scale, h, expand, cosine, sine)


def spread(h, parts):
    step = 1
    while step < parts:
        h = h + lax.ppermute(h, "tensor", [(i, i ^ step) for i in range(parts)])
        step *= 2
    return h


def gather_plan(parts, tokens, weights, scale, shrinks, expands, indices):
    segment_slot, cosine, sine = small_tables(*indices, tokens.shape[0] * parts)
    held, rank, depth = shrinks.shape
    tile = depth // 16
    x = lax.all_gather(tokens, "tensor", axis=0, tiled=True)
    row_slot = jnp.repeat(segment_slot, SEG, total_repeat_length=x.shape[0])
    h = jnp.zeros((x.shape[0], rank), BF16)
    for i in range(held):
        mine = (row_slot == lax.axis_index("tensor") * held + i)[:, None]
        h = jnp.where(mine, shrink_all(x, shrinks[i], tile).astype(BF16), h)
    h = spread(h, parts)
    acc = project_all(x, weights, tile)
    return segment_finish(acc, scale, h, expands[segment_slot], cosine, sine)


def block_owners():
    chips = len(SNAKE)
    owners = np.zeros((2 * chips, 2 * chips), np.int32)
    for place, chip in enumerate(SNAKE):
        for core in (0, 1):
            row = [2 * chip + core, 2 * chip + 1 - core]
            for r in range(1, ROUNDS + 1):
                far, near = place - r * (1 - 2 * core), place + r * (1 - 2 * core)
                far, near = 2 * SNAKE[far % chips], 2 * SNAKE[near % chips]
                row += [far + core, near + 1 - core]
                if r < ROUNDS:
                    row += [near + core, far + 1 - core]
            owners[2 * chip + core] = row
    return owners


def ring_pairs(ways):
    chips = len(SNAKE)
    pairs = []
    for place, chip in enumerate(SNAKE):
        for core in (0, 1):
            pairs.append((2 * chip + core, 2 * SNAKE[(place + ways[core]) % chips] + core))
    return pairs


def block_kernel(count, low, tile, steps, first, base, fresh, ranked, *refs):
    xs, w_ref, refs = refs[:count], refs[count], refs[count + 1 :]
    if ranked:
        s_refs, refs = refs[:2], refs[2:]
    if not first:
        total_in, refs = refs[0], refs[1:]
    total_out, refs = refs[0], refs[1:]
    if ranked:
        h_out, refs = refs[0], refs[1:]
    acc, before, x_slots, w_slots, s_slots, sems, total_sems = refs
    rows = xs[0].shape[0]

    def copies(step):
        slot = lax.rem(step, SLOTS)
        at = pl.multiple_of(step * tile, tile)
        sem = lambda i: sems.at[slot, i]
        out = [pltpu.make_async_copy(w_ref.at[pl.ds(low + at, tile)], w_slots.at[slot], sem(count))]
        for i in range(count):
            cut = xs[i].at[:, pl.ds(low + at, tile)]
            out.append(pltpu.make_async_copy(cut, x_slots.at[slot, pl.ds(i * rows, rows)], sem(i)))
        if ranked:
            for i, s_ref in enumerate(s_refs):
                cut, rank = s_ref.at[:, pl.ds(low + at, tile)], s_ref.shape[0]
                to = s_slots.at[slot, pl.ds(i * rank, rank)]
                out.append(pltpu.make_async_copy(cut, to, sem(count + 1 + i)))
        return out

    def start(step):
        for copy in copies(step):
            copy.start()

    for step in range(min(SLOTS, steps)):
        start(jnp.int32(step))
    if not fresh:
        load = pltpu.make_async_copy(total_in.at[pl.ds(base, count)], before, total_sems.at[0])
        load.start()
    acc[...] = jnp.zeros_like(acc)
    if ranked:
        h_out[...] = jnp.zeros_like(h_out)

    @pl.loop(0, steps)
    def _(step):
        for copy in copies(step):
            copy.wait()
        slot = lax.rem(step, SLOTS)
        x = x_slots[slot]
        for left in range(0, acc.shape[2], CHUNK):
            cut = slice(left, left + CHUNK)
            product = jnp.dot(x, w_slots[slot, :, cut], preferred_element_type=F32)
            acc[:, :, cut] += product.reshape(count, rows, CHUNK)
        if ranked:
            mine = jnp.concatenate([x[i * rows : (i + 1) * rows] for i in range(0, count, 2)], 0)
            h_out[...] += lax.dot_general(mine, s_slots[slot], NT, preferred_element_type=F32)

        @pl.when(step + SLOTS < steps)
        def _():
            start(step + SLOTS)

    if not fresh:
        load.wait()
        acc[...] += before[...]
    store = pltpu.make_async_copy(acc, total_out.at[pl.ds(base, count)], total_sems.at[1])
    store.start()
    store.wait()


def block_product(xs, weights, factors, low, high, tile, total, base, ranked):
    count = len(xs)
    rows = xs[0].shape[0]
    cols = weights.shape[1]
    rank = 2 * factors[0].shape[0]
    fresh, first = low == 0, total is None
    anywhere, whole = pl.BlockSpec(memory_space=pl.ANY), pl.BlockSpec(memory_space=pltpu.VMEM)
    operands = list(xs) + [weights]
    specs = [anywhere] * (count + 1)
    if ranked:
        operands += factors
        specs += [anywhere] * 2
    aliases = {}
    if not first:
        aliases = {len(operands): 0}
        operands.append(total)
        specs.append(anywhere)
    outs, out_specs = [jax.ShapeDtypeStruct(total_shape(rows, cols), F32)], [anywhere]
    if ranked:
        outs.append(jax.ShapeDtypeStruct((count // 2 * rows, rank), F32))
        out_specs.append(whole)
    steps = (high - low) // tile
    result = pl.pallas_call(
        functools.partial(block_kernel, count, low, tile, steps, first, base, fresh, ranked),
        in_specs=specs,
        out_specs=out_specs,
        out_shape=outs,
        scratch_shapes=[
            pltpu.VMEM((count, rows, cols), F32),
            pltpu.VMEM((1, 8, 128) if fresh else (count, rows, cols), F32),
            pltpu.VMEM((SLOTS, count * rows, tile), BF16),
            pltpu.VMEM((SLOTS, tile, cols), BF16),
            pltpu.VMEM((SLOTS, rank, tile), BF16),
            pltpu.SemaphoreType.DMA((SLOTS, count + 3)),
            pltpu.SemaphoreType.DMA((2,)),
        ],
        input_output_aliases=aliases,
        compiler_params=pltpu.CompilerParams(vmem_limit_bytes=BIG_VMEM),
        cost_estimate=pl.CostEstimate(
            flops=2 * count * rows * (high - low) * cols,
            bytes_accessed=2 * (high - low) * cols,
            transcendentals=0,
        ),
        name="blocks",
    )(*operands)
    return result[0], result[1:]


def total_shape(rows, cols):
    return (2 * len(SNAKE), rows, cols)


def both_ranks(x, factors):
    return jnp.concatenate([lax.dot_general(x, s, NT, preferred_element_type=F32) for s in factors], 1)


def some_ranks_kernel(x_ref, sa_ref, sb_ref, out_ref):
    out_ref[...] = both_ranks(x_ref[...], (sa_ref[...], sb_ref[...]))


def some_ranks(x, factors):
    whole = lambda shape: pl.BlockSpec(shape, lambda _: (0, 0))
    shape = (x.shape[0], 2 * factors[0].shape[0])
    return pl.pallas_call(
        some_ranks_kernel,
        grid=(1,),
        in_specs=[whole(value.shape) for value in (x, *factors)],
        out_specs=whole(shape),
        out_shape=jax.ShapeDtypeStruct(shape, F32),
        compiler_params=PARAMS,
        name="some_ranks",
    )(x, *factors)


def rank_kernel(owners_ref, slot_ref, x_ref, sa_ref, sb_ref, *refs):
    h_refs, out_ref, placed = refs[:-2], refs[-2], refs[-1]
    rows, rank = x_ref.shape[0], sa_ref.shape[0]
    last = both_ranks(x_ref[...], (sa_ref[...], sb_ref[...]))
    segments = slot_ref.shape[0] - 2
    block = 0
    for source in h_refs + (last,):
        for low in range(0, source.shape[0], rows):
            owner = owners_ref[2 * block]
            segment = owner * rows // SEG
            after = jnp.minimum(segment + 1, segments - 1)
            row = owner * rows + lax.broadcasted_iota(jnp.int32, (rows, rank), 0)
            slot = jnp.where(row < (segment + 1) * SEG, slot_ref[segment], slot_ref[after])
            terms = jnp.where(slot == slot_ref[segments + 1], source[low : low + rows, rank:], 0.0)
            terms = jnp.where(slot == slot_ref[segments], source[low : low + rows, :rank], terms)
            placed[pl.ds(pl.multiple_of(owner // 2 * rows, 16), rows), :] = terms
            block += 1
    half = placed.shape[0] // 2
    out_ref[...] = jnp.concatenate([placed[:half, :], placed[half:, :]], 1).astype(out_ref.dtype)


def rank_terms(owners, slots, x, factors, hs):
    rank = factors[0].shape[0]
    core_rows = owners.shape[0] // 2 * x.shape[0]
    whole = lambda shape: pl.BlockSpec(shape, lambda _, *rest: (0, 0))
    return pl.pallas_call(
        rank_kernel,
        grid_spec=pltpu.PrefetchScalarGridSpec(
            num_scalar_prefetch=2,
            grid=(1,),
            in_specs=[whole(value.shape) for value in (x, *factors, *hs)],
            out_specs=whole((core_rows // 2, 2 * rank)),
            scratch_shapes=[pltpu.VMEM((core_rows, rank), F32)],
        ),
        out_shape=jax.ShapeDtypeStruct((core_rows // 2, 2 * rank), BF16),
        compiler_params=PARAMS,
        name="ranks",
    )(owners, slots, x, *factors, *hs)


def block_finish_kernel(blocks, segments, places_ref, slot_ref, core_ref, *refs):
    accs, refs = refs[:blocks], refs[blocks:]
    expands, refs = refs[:segments], refs[segments:]
    scale_ref, mine_ref, other_ref, cos_ref, sin_ref, out_ref, h, update = refs
    rank = mine_ref.shape[1] // 2
    rows = accs[0].shape[1]
    first = pl.program_id(0) == 0
    even = core_ref[0] == 0
    mine, other = (jnp.where(first, ref[:, :rank], ref[:, rank:]) for ref in (mine_ref, other_ref))
    for core, terms in enumerate((jnp.where(even, mine, other), jnp.where(even, other, mine))):
        for i in range(blocks // 2):
            at = (2 * i + core) * rows
            h[at : at + rows, :] = terms[i * rows : (i + 1) * rows]
    for segment in range(segments):
        cut = slice(segment * SEG, (segment + 1) * SEG)
        update[cut, :] = jnp.dot(h[cut, :], expands[segment][0], preferred_element_type=F32)
    for block in range(blocks):
        at = slice(block * rows, (block + 1) * rows)
        cosine, sine = cos_ref[at, :], sin_ref[at, :]
        for head in range(out_ref.shape[1] // HD):
            cut = slice(head * HD, (head + 1) * HD)
            value = accs[block][0, :, cut] * scale_ref[:, cut] + update[at, cut]
            out_ref[at, cut] = rotate(value, cosine, sine).astype(out_ref.dtype)


def block_finish(places, slots, core, total, expands, scale, mine, other, cosine, sine):
    blocks, rows, cols = total.shape
    half = blocks // 2
    half_rows = half * rows
    segments = half_rows // SEG
    rank = expands.shape[1]

    def acc_at(i):
        return pl.BlockSpec((1, rows, cols), lambda g, places, *_: (places[g * half + i], 0, 0))

    def expand_at(i):
        return pl.BlockSpec((1, rank, cols), lambda g, places, slots, _: (slots[g * segments + i], 0, 0))

    half_of = lambda width: pl.BlockSpec((half_rows, width), lambda g, *_: (g, 0))
    return pl.pallas_call(
        functools.partial(block_finish_kernel, half, segments),
        grid_spec=pltpu.PrefetchScalarGridSpec(
            num_scalar_prefetch=3,
            grid=(2,),
            in_specs=[acc_at(i) for i in range(half)]
            + [expand_at(i) for i in range(segments)]
            + [
                pl.BlockSpec((1, cols), lambda g, *_: (0, 0)),
                pl.BlockSpec(mine.shape, lambda g, *_: (0, 0)),
                pl.BlockSpec(other.shape, lambda g, *_: (0, 0)),
                half_of(HD),
                half_of(HD),
            ],
            out_specs=half_of(cols),
            scratch_shapes=[pltpu.VMEM((half_rows, rank), BF16), pltpu.VMEM((half_rows, cols), F32)],
        ),
        out_shape=jax.ShapeDtypeStruct((blocks * rows, cols), BF16),
        compiler_params=PARAMS,
        name="finish",
    )(places, slots, core, *([total] * half), *([expands] * segments), scale, mine, other, cosine, sine)


def ring_plan(parts, tokens, weights, scale, shrinks, expands, indices):
    rows, depth = tokens.shape
    tile = depth // 16
    me = lax.axis_index("tensor")
    owners_table = block_owners()
    send = lambda value, pairs: lax.ppermute(value, "tensor", pairs)
    swap = lambda value: send(value, [(i, i ^ 1) for i in range(parts)])
    out, home = ring_pairs((1, -1)), ring_pairs((-1, 1))

    half = depth // 2
    hs, counts = [], []

    def multiply(xs, total):
        total, h = block_product(xs, weights, factors, 0, depth, tile, total, sum(counts), True)
        hs.extend(h)
        counts.append(len(xs))
        return total

    streams = [send(tokens, out), None]
    own, part = [tokens, swap(tokens)], 2 * tile
    factors = [shrinks[0], swap(shrinks[0])]
    total, _ = block_product(own, weights, factors, 0, part, tile, None, 0, False)
    second, total = lax.optimization_barrier((tokens, total))
    streams[1] = send(second, home)
    total, _ = block_product(own, weights, factors, part, depth, tile, total, 0, False)
    hs, total = lax.optimization_barrier(([some_ranks(tokens, factors)], total))
    counts.append(len(own))

    def make_tables(me, indices):
        segment_slot, cosine, sine = small_tables(*indices, parts * rows)
        owners = jnp.asarray(owners_table)[me]
        places = jnp.asarray(np.argsort(owners_table, axis=1).astype(np.int32))[me]
        slots = jnp.concatenate([segment_slot, jnp.stack([me, me ^ 1]).astype(jnp.int32)])
        core = (me % 2)[None].astype(jnp.int32)
        return owners, places, slots, core, segment_slot, cosine, sine

    blocks, hops = [], 2 * ROUNDS - 1
    totals = [total] * 2
    for hop in range(hops):
        arrived, _ = lax.optimization_barrier((streams[hop % 2], totals[hop if hop % 2 else hop + 1]))
        if hop + 2 < hops:
            streams[hop % 2] = send(arrived, home if hop % 2 else out)
        if hop % 2:
            late = [arrived, swap(arrived)]
            if hop == hops - 2:
                early = some_ranks(arrived, factors)
            total = multiply(blocks, total)
            blocks = late
        else:
            blocks += [arrived, swap(arrived)]
        if hop == 1:
            known, total = lax.optimization_barrier(((me, indices), total))
            tables, total = lax.optimization_barrier((make_tables(*known), total))
        totals.append((total, early) if hop == hops - 2 else total)
    held = sum(counts)
    hs.append(early)
    owners, places, slots, core, segment_slot, cosine, sine = tables
    h = rank_terms(owners, slots, blocks[2], factors, hs)
    beside = lambda step: send(h, [(i, i ^ step) for i in range(parts)])

    def last_product(low, high, total):
        xs, _ = lax.optimization_barrier((blocks, h))
        return block_product(xs, weights, factors, low, high, tile, total, held, False)[0]

    near = [beside(step) for step in (2, 4, 6)]
    near, total = lax.optimization_barrier((near, last_product(0, half, total)))
    h = h + near[0] + near[1] + near[2]
    far = [beside(step) for step in (8, 1, 9)]
    far, total = lax.optimization_barrier((far, last_product(half, depth, total)))
    mine, other = h + far[0], far[1] + far[2]
    return block_finish(places, segment_slot, core, total, expands, scale, mine, other, cosine, sine)


def body(parts, tokens, weight_codes, column_scale, shrink_store, expand_store, row_adapter, placement, document_lengths):
    rows = tokens.shape[0]
    total_rows = rows * parts
    shrinks = jnp.swapaxes(shrink_store, 1, 2)
    expands = jnp.swapaxes(expand_store, 1, 2)
    ring = parts == 2 * len(SNAKE) and rows % 16 == 0 and shrinks.shape[0] == 1 and total_rows % (2 * SEG) == 0
    plan = ring_plan if ring else gather_plan
    indices = (row_adapter, placement, document_lengths)
    return plan(parts, tokens, weight_codes, column_scale[None, :], shrinks, expands, indices)


def solution(mesh):
    placed = (
        P(("groups", "tensor"), None),
        P(None, "tensor"),
        P("tensor"),
        P(("groups", "tensor"), None, None),
        P("groups", "tensor", None),
        P("groups"),
        P("groups"),
        P("groups"),
    )
    return jax.shard_map(
        functools.partial(body, mesh.shape["tensor"]),
        mesh=mesh,
        in_specs=placed,
        out_specs=P("groups", "tensor"),
        check_vma=False,
    )
```

```python
import functools

import jax
import jax.numpy as jnp
import numpy as np
from jax import lax
from jax.experimental import pallas as pl
from jax.experimental.pallas import tpu as pltpu
from jax.sharding import PartitionSpec as P

HD = 128
SEG = 128
VMEM = 20 * 1024 * 1024
F32 = jnp.float32
BF16 = jnp.bfloat16
NT = (((1,), (1,)), ((), ()))
SLOTS = 4
CHUNK = 256
BIG_VMEM = 24 * 1024 * 1024
PARAMS = pltpu.CompilerParams(vmem_limit_bytes=VMEM)
SNAKE = (0, 2, 4, 6, 7, 5, 3, 1)
ROUNDS = len(SNAKE) // 2


def row_positions(document_lengths, total_rows):
    ends = jnp.cumsum(document_lengths)
    row_index = jnp.arange(total_rows, dtype=jnp.int32)
    passed = (row_index[:, None] >= ends[None, :]).astype(jnp.int32)
    return row_index - jnp.sum(passed * document_lengths[None, :], axis=1)


def rotary_tables(positions):
    half_size = HD // 2
    freq_index = jnp.arange(half_size, dtype=F32)
    inverse = jnp.exp(freq_index * (-2.0 / HD) * jnp.log(F32(500000.0)))
    angles = positions.astype(F32)[:, None] * inverse[None, :]
    cosine, sine = jnp.cos(angles), jnp.sin(angles)
    return jnp.concatenate([cosine, cosine], 1), jnp.concatenate([-sine, sine], 1)


def small_tables(row_adapter, placement, document_lengths, total_rows):
    segment_slot = placement[row_adapter[::SEG]]
    return segment_slot, *rotary_tables(row_positions(document_lengths, total_rows))


def rotate(value, cosine, sine):
    return value * cosine + pltpu.roll(value, HD // 2, 1) * sine


def shrink_kernel(x_ref, s_ref, h_out):
    @pl.when(pl.program_id(0) == 0)
    def _():
        h_out[...] = jnp.zeros_like(h_out)

    h_out[...] += lax.dot_general(x_ref[...], s_ref[...], NT, preferred_element_type=F32)


def shrink_all(x, shrink, tile):
    rows, depth = x.shape
    rank = shrink.shape[0]
    return pl.pallas_call(
        shrink_kernel,
        grid=(depth // tile,),
        in_specs=[
            pl.BlockSpec((rows, tile), lambda k: (0, k)),
            pl.BlockSpec((rank, tile), lambda k: (0, k)),
        ],
        out_specs=pl.BlockSpec((rows, rank), lambda k: (0, 0)),
        out_shape=jax.ShapeDtypeStruct((rows, rank), F32),
        compiler_params=PARAMS,
        name="shrink",
    )(x, shrink)


def project_kernel(x_ref, w_ref, acc_out):
    @pl.when(pl.program_id(0) == 0)
    def _():
        acc_out[...] = jnp.zeros_like(acc_out)

    acc_out[...] += jnp.dot(x_ref[...], w_ref[...], preferred_element_type=F32)


def project_all(x, weights, tile):
    rows, depth = x.shape
    cols = weights.shape[1]
    return pl.pallas_call(
        project_kernel,
        grid=(depth // tile,),
        in_specs=[
            pl.BlockSpec((rows, tile), lambda k: (0, k)),
            pl.BlockSpec((tile, cols), lambda k: (k, 0)),
        ],
        out_specs=pl.BlockSpec((rows, cols), lambda k: (0, 0)),
        out_shape=jax.ShapeDtypeStruct((rows, cols), F32),
        compiler_params=PARAMS,
        name="project",
    )(x, weights)


def segment_finish_kernel(acc_ref, scale_ref, h_ref, expand_ref, cos_ref, sin_ref, out_ref):
    update = jnp.dot(h_ref[...], expand_ref[0], preferred_element_type=F32)
    for head in range(out_ref.shape[1] // HD):
        cut = slice(head * HD, (head + 1) * HD)
        value = acc_ref[:, cut] * scale_ref[:, cut] + update[:, cut]
        out_ref[:, cut] = rotate(value, cos_ref[...], sin_ref[...]).astype(out_ref.dtype)


def segment_finish(acc, scale, h, expand, cosine, sine):
    rows, cols = acc.shape
    rank = h.shape[1]
    return pl.pallas_call(
        segment_finish_kernel,
        grid=(rows // SEG,),
        in_specs=[
            pl.BlockSpec((SEG, cols), lambda r: (r, 0)),
            pl.BlockSpec((1, cols), lambda r: (0, 0)),
            pl.BlockSpec((SEG, rank), lambda r: (r, 0)),
            pl.BlockSpec((1, rank, cols), lambda r: (r, 0, 0)),
            pl.BlockSpec((SEG, HD), lambda r: (r, 0)),
            pl.BlockSpec((SEG, HD), lambda r: (r, 0)),
        ],
        out_specs=pl.BlockSpec((SEG, cols), lambda r: (r, 0)),
        out_shape=jax.ShapeDtypeStruct((rows, cols), BF16),
        compiler_params=PARAMS,
        name="finish",
    )(acc, scale, h, expand, cosine, sine)


def spread(h, parts):
    step = 1
    while step < parts:
        h = h + lax.ppermute(h, "tensor", [(i, i ^ step) for i in range(parts)])
        step *= 2
    return h


def gather_plan(parts, tokens, weights, scale, shrinks, expands, indices):
    segment_slot, cosine, sine = small_tables(*indices, tokens.shape[0] * parts)
    held, rank, depth = shrinks.shape
    tile = depth // 16
    x = lax.all_gather(tokens, "tensor", axis=0, tiled=True)
    row_slot = jnp.repeat(segment_slot, SEG, total_repeat_length=x.shape[0])
    h = jnp.zeros((x.shape[0], rank), BF16)
    for i in range(held):
        mine = (row_slot == lax.axis_index("tensor") * held + i)[:, None]
        h = jnp.where(mine, shrink_all(x, shrinks[i], tile).astype(BF16), h)
    h = spread(h, parts)
    acc = project_all(x, weights, tile)
    return segment_finish(acc, scale, h, expands[segment_slot], cosine, sine)


def block_owners():
    chips = len(SNAKE)
    owners = np.zeros((2 * chips, 2 * chips), np.int32)
    for place, chip in enumerate(SNAKE):
        for core in (0, 1):
            row = [2 * chip + core, 2 * chip + 1 - core]
            for r in range(1, ROUNDS + 1):
                far, near = place - r * (1 - 2 * core), place + r * (1 - 2 * core)
                far, near = 2 * SNAKE[far % chips], 2 * SNAKE[near % chips]
                row += [far + core, near + 1 - core]
                if r < ROUNDS:
                    row += [near + core, far + 1 - core]
            owners[2 * chip + core] = row
    return owners


def ring_pairs(ways):
    chips = len(SNAKE)
    pairs = []
    for place, chip in enumerate(SNAKE):
        for core in (0, 1):
            pairs.append((2 * chip + core, 2 * SNAKE[(place + ways[core]) % chips] + core))
    return pairs


def block_kernel(count, low, tile, steps, first, base, fresh, ranked, *refs):
    xs, w_ref, refs = refs[:count], refs[count], refs[count + 1 :]
    if ranked:
        s_refs, refs = refs[:2], refs[2:]
    if not first:
        total_in, refs = refs[0], refs[1:]
    total_out, refs = refs[0], refs[1:]
    if ranked:
        h_out, refs = refs[0], refs[1:]
    acc, before, x_slots, w_slots, s_slots, sems, total_sems = refs
    rows = xs[0].shape[0]

    def copies(step):
        slot = lax.rem(step, SLOTS)
        at = pl.multiple_of(step * tile, tile)
        sem = lambda i: sems.at[slot, i]
        out = [pltpu.make_async_copy(w_ref.at[pl.ds(low + at, tile)], w_slots.at[slot], sem(count))]
        for i in range(count):
            cut = xs[i].at[:, pl.ds(low + at, tile)]
            out.append(pltpu.make_async_copy(cut, x_slots.at[slot, pl.ds(i * rows, rows)], sem(i)))
        if ranked:
            for i, s_ref in enumerate(s_refs):
                cut, rank = s_ref.at[:, pl.ds(low + at, tile)], s_ref.shape[0]
                to = s_slots.at[slot, pl.ds(i * rank, rank)]
                out.append(pltpu.make_async_copy(cut, to, sem(count + 1 + i)))
        return out

    def start(step):
        for copy in copies(step):
            copy.start()

    for step in range(min(SLOTS, steps)):
        start(jnp.int32(step))
    if not fresh:
        load = pltpu.make_async_copy(total_in.at[pl.ds(base, count)], before, total_sems.at[0])
        load.start()
    acc[...] = jnp.zeros_like(acc)
    if ranked:
        h_out[...] = jnp.zeros_like(h_out)

    @pl.loop(0, steps)
    def _(step):
        for copy in copies(step):
            copy.wait()
        slot = lax.rem(step, SLOTS)
        x = x_slots[slot]
        for left in range(0, acc.shape[2], CHUNK):
            cut = slice(left, left + CHUNK)
            product = jnp.dot(x, w_slots[slot, :, cut], preferred_element_type=F32)
            acc[:, :, cut] += product.reshape(count, rows, CHUNK)
        if ranked:
            mine = jnp.concatenate([x[i * rows : (i + 1) * rows] for i in range(0, count, 2)], 0)
            h_out[...] += lax.dot_general(mine, s_slots[slot], NT, preferred_element_type=F32)

        @pl.when(step + SLOTS < steps)
        def _():
            start(step + SLOTS)

    if not fresh:
        load.wait()
        acc[...] += before[...]
    store = pltpu.make_async_copy(acc, total_out.at[pl.ds(base, count)], total_sems.at[1])
    store.start()
    store.wait()


def block_product(xs, weights, factors, low, high, tile, total, base, ranked):
    count = len(xs)
    rows = xs[0].shape[0]
    cols = weights.shape[1]
    rank = 2 * factors[0].shape[0]
    fresh, first = low == 0, total is None
    anywhere, whole = pl.BlockSpec(memory_space=pl.ANY), pl.BlockSpec(memory_space=pltpu.VMEM)
    operands = list(xs) + [weights]
    specs = [anywhere] * (count + 1)
    if ranked:
        operands += factors
        specs += [anywhere] * 2
    aliases = {}
    if not first:
        aliases = {len(operands): 0}
        operands.append(total)
        specs.append(anywhere)
    outs, out_specs = [jax.ShapeDtypeStruct(total_shape(rows, cols), F32)], [anywhere]
    if ranked:
        outs.append(jax.ShapeDtypeStruct((count // 2 * rows, rank), F32))
        out_specs.append(whole)
    steps = (high - low) // tile
    result = pl.pallas_call(
        functools.partial(block_kernel, count, low, tile, steps, first, base, fresh, ranked),
        in_specs=specs,
        out_specs=out_specs,
        out_shape=outs,
        scratch_shapes=[
            pltpu.VMEM((count, rows, cols), F32),
            pltpu.VMEM((1, 8, 128) if fresh else (count, rows, cols), F32),
            pltpu.VMEM((SLOTS, count * rows, tile), BF16),
            pltpu.VMEM((SLOTS, tile, cols), BF16),
            pltpu.VMEM((SLOTS, rank, tile), BF16),
            pltpu.SemaphoreType.DMA((SLOTS, count + 3)),
            pltpu.SemaphoreType.DMA((2,)),
        ],
        input_output_aliases=aliases,
        compiler_params=pltpu.CompilerParams(vmem_limit_bytes=BIG_VMEM),
        cost_estimate=pl.CostEstimate(
            flops=2 * count * rows * (high - low) * cols,
            bytes_accessed=2 * (high - low) * cols,
            transcendentals=0,
        ),
        name="blocks",
    )(*operands)
    return result[0], result[1:]


def total_shape(rows, cols):
    return (2 * len(SNAKE), rows, cols)


def some_ranks_kernel(x_ref, s_ref, out_ref):
    out_ref[...] = lax.dot_general(x_ref[...], s_ref[...], NT, preferred_element_type=F32)


def some_ranks(x, factor):
    whole = lambda shape: pl.BlockSpec(shape, lambda _: (0, 0))
    shape = (x.shape[0], factor.shape[0])
    return pl.pallas_call(
        some_ranks_kernel,
        grid=(1,),
        in_specs=[whole(x.shape), whole(factor.shape)],
        out_specs=whole(shape),
        out_shape=jax.ShapeDtypeStruct(shape, F32),
        compiler_params=PARAMS,
        name="some_ranks",
    )(x, factor)


def rank_kernel(count, owners_ref, slot_ref, *refs):
    xs, refs = refs[:count], refs[count:]
    sa_ref, sb_ref, h_refs, out_ref, placed = refs[0], refs[1], refs[2:-2], refs[-2], refs[-1]
    rows, rank = xs[0].shape[0], sa_ref.shape[0]
    x = jnp.concatenate([ref[...] for ref in xs], 0)
    last = [lax.dot_general(x, ref[...], NT, preferred_element_type=F32) for ref in (sa_ref, sb_ref)]
    last = jnp.concatenate(last, 1)
    segments = slot_ref.shape[0] - 2
    block = 0
    for source in h_refs + (last,):
        for low in range(0, source.shape[0], rows):
            owner = owners_ref[2 * block]
            segment = owner * rows // SEG
            after = jnp.minimum(segment + 1, segments - 1)
            row = owner * rows + lax.broadcasted_iota(jnp.int32, (rows, rank), 0)
            slot = jnp.where(row < (segment + 1) * SEG, slot_ref[segment], slot_ref[after])
            terms = jnp.where(slot == slot_ref[segments + 1], source[low : low + rows, rank:], 0.0)
            terms = jnp.where(slot == slot_ref[segments], source[low : low + rows, :rank], terms)
            placed[pl.ds(pl.multiple_of(owner // 2 * rows, 16), rows), :] = terms
            block += 1
    half = placed.shape[0] // 2
    out_ref[...] = jnp.concatenate([placed[:half, :], placed[half:, :]], 1).astype(out_ref.dtype)


def rank_terms(owners, slots, xs, factors, hs):
    rank = factors[0].shape[0]
    core_rows = owners.shape[0] // 2 * xs[0].shape[0]
    whole = lambda shape: pl.BlockSpec(shape, lambda _, *rest: (0, 0))
    return pl.pallas_call(
        functools.partial(rank_kernel, len(xs)),
        grid_spec=pltpu.PrefetchScalarGridSpec(
            num_scalar_prefetch=2,
            grid=(1,),
            in_specs=[whole(value.shape) for value in (*xs, *factors, *hs)],
            out_specs=whole((core_rows // 2, 2 * rank)),
            scratch_shapes=[pltpu.VMEM((core_rows, rank), F32)],
        ),
        out_shape=jax.ShapeDtypeStruct((core_rows // 2, 2 * rank), BF16),
        compiler_params=PARAMS,
        name="ranks",
    )(owners, slots, *xs, *factors, *hs)


def block_finish_kernel(blocks, segments, places_ref, slot_ref, core_ref, *refs):
    accs, refs = refs[:blocks], refs[blocks:]
    expands, refs = refs[:segments], refs[segments:]
    scale_ref, mine_ref, other_ref, cos_ref, sin_ref, out_ref, h, update = refs
    rank = mine_ref.shape[1] // 2
    rows = accs[0].shape[1]
    first = pl.program_id(0) == 0
    even = core_ref[0] == 0
    mine, other = (jnp.where(first, ref[:, :rank], ref[:, rank:]) for ref in (mine_ref, other_ref))
    for core, terms in enumerate((jnp.where(even, mine, other), jnp.where(even, other, mine))):
        for i in range(blocks // 2):
            at = (2 * i + core) * rows
            h[at : at + rows, :] = terms[i * rows : (i + 1) * rows]
    for segment in range(segments):
        cut = slice(segment * SEG, (segment + 1) * SEG)
        update[cut, :] = jnp.dot(h[cut, :], expands[segment][0], preferred_element_type=F32)
    for block in range(blocks):
        at = slice(block * rows, (block + 1) * rows)
        cosine, sine = cos_ref[at, :], sin_ref[at, :]
        for head in range(out_ref.shape[1] // HD):
            cut = slice(head * HD, (head + 1) * HD)
            value = accs[block][0, :, cut] * scale_ref[:, cut] + update[at, cut]
            out_ref[at, cut] = rotate(value, cosine, sine).astype(out_ref.dtype)


def block_finish(places, slots, core, total, expands, scale, mine, other, cosine, sine):
    blocks, rows, cols = total.shape
    half = blocks // 2
    half_rows = half * rows
    segments = half_rows // SEG
    rank = expands.shape[1]

    def acc_at(i):
        return pl.BlockSpec((1, rows, cols), lambda g, places, *_: (places[g * half + i], 0, 0))

    def expand_at(i):
        return pl.BlockSpec((1, rank, cols), lambda g, places, slots, _: (slots[g * segments + i], 0, 0))

    half_of = lambda width: pl.BlockSpec((half_rows, width), lambda g, *_: (g, 0))
    return pl.pallas_call(
        functools.partial(block_finish_kernel, half, segments),
        grid_spec=pltpu.PrefetchScalarGridSpec(
            num_scalar_prefetch=3,
            grid=(2,),
            in_specs=[acc_at(i) for i in range(half)]
            + [expand_at(i) for i in range(segments)]
            + [
                pl.BlockSpec((1, cols), lambda g, *_: (0, 0)),
                pl.BlockSpec(mine.shape, lambda g, *_: (0, 0)),
                pl.BlockSpec(other.shape, lambda g, *_: (0, 0)),
                half_of(HD),
                half_of(HD),
            ],
            out_specs=half_of(cols),
            scratch_shapes=[pltpu.VMEM((half_rows, rank), BF16), pltpu.VMEM((half_rows, cols), F32)],
        ),
        out_shape=jax.ShapeDtypeStruct((blocks * rows, cols), BF16),
        compiler_params=PARAMS,
        name="finish",
    )(places, slots, core, *([total] * half), *([expands] * segments), scale, mine, other, cosine, sine)


def ring_plan(parts, tokens, weights, scale, shrinks, expands, indices):
    rows, depth = tokens.shape
    tile = depth // 16
    me = lax.axis_index("tensor")
    owners_table = block_owners()
    send = lambda value, pairs: lax.ppermute(value, "tensor", pairs)
    swap = lambda value: send(value, [(i, i ^ 1) for i in range(parts)])
    out, home = ring_pairs((1, -1)), ring_pairs((-1, 1))

    half = depth // 2
    hs, counts = [], []

    def multiply(xs, total):
        total, h = block_product(xs, weights, factors, 0, depth, tile, total, sum(counts), True)
        hs.extend(h)
        counts.append(len(xs))
        return total

    streams = [send(tokens, out), None]
    own, factors = [tokens, swap(tokens)], [shrinks[0], swap(shrinks[0])]
    mine = some_ranks(tokens, factors[0])
    second, mine = lax.optimization_barrier((tokens, mine))
    streams[1] = send(second, home)
    total, _ = block_product(own, weights, factors, 0, depth, tile, None, 0, False)
    mine = jnp.concatenate([mine, some_ranks(tokens, factors[1])], 1)
    hs, total = lax.optimization_barrier(([mine], total))
    counts.append(len(own))

    def make_tables(me, indices):
        segment_slot, cosine, sine = small_tables(*indices, parts * rows)
        owners = jnp.asarray(owners_table)[me]
        places = jnp.asarray(np.argsort(owners_table, axis=1).astype(np.int32))[me]
        slots = jnp.concatenate([segment_slot, jnp.stack([me, me ^ 1]).astype(jnp.int32)])
        core = (me % 2)[None].astype(jnp.int32)
        return owners, places, slots, core, segment_slot, cosine, sine

    blocks, hops = [], 2 * ROUNDS - 1
    totals = [total] * 2
    for hop in range(hops):
        arrived, _ = lax.optimization_barrier((streams[hop % 2], totals[hop if hop % 2 else hop + 1]))
        if hop + 2 < hops:
            streams[hop % 2] = send(arrived, home if hop % 2 else out)
        if hop % 2:
            late = [arrived, swap(arrived)]
            total = multiply(blocks, total)
            blocks = late
        else:
            blocks += [arrived, swap(arrived)]
        if hop == 1:
            known, total = lax.optimization_barrier(((me, indices), total))
            tables, total = lax.optimization_barrier((make_tables(*known), total))
        totals.append(total)
    held = sum(counts)
    owners, places, slots, core, segment_slot, cosine, sine = tables
    h = rank_terms(owners, slots, blocks[::2], factors, hs)
    beside = lambda step: send(h, [(i, i ^ step) for i in range(parts)])

    def last_product(low, high, total):
        xs, _ = lax.optimization_barrier((blocks, h))
        return block_product(xs, weights, factors, low, high, tile, total, held, False)[0]

    near = [beside(step) for step in (2, 4, 6)]
    near, total = lax.optimization_barrier((near, last_product(0, half, total)))
    h = h + near[0] + near[1] + near[2]
    far = [beside(step) for step in (8, 1, 9)]
    far, total = lax.optimization_barrier((far, last_product(half, depth, total)))
    mine, other = h + far[0], far[1] + far[2]
    return block_finish(places, segment_slot, core, total, expands, scale, mine, other, cosine, sine)


def body(parts, tokens, weight_codes, column_scale, shrink_store, expand_store, row_adapter, placement, document_lengths):
    rows = tokens.shape[0]
    total_rows = rows * parts
    shrinks = jnp.swapaxes(shrink_store, 1, 2)
    expands = jnp.swapaxes(expand_store, 1, 2)
    ring = parts == 2 * len(SNAKE) and rows % 16 == 0 and shrinks.shape[0] == 1 and total_rows % (2 * SEG) == 0
    plan = ring_plan if ring else gather_plan
    indices = (row_adapter, placement, document_lengths)
    return plan(parts, tokens, weight_codes, column_scale[None, :], shrinks, expands, indices)


def solution(mesh):
    placed = (
        P(("groups", "tensor"), None),
        P(None, "tensor"),
        P("tensor"),
        P(("groups", "tensor"), None, None),
        P("groups", "tensor", None),
        P("groups"),
        P("groups"),
        P("groups"),
    )
    return jax.shard_map(
        functools.partial(body, mesh.shape["tensor"]),
        mesh=mesh,
        in_specs=placed,
        out_specs=P("groups", "tensor"),
        check_vma=False,
    )
```

```python
import functools

import jax
import jax.numpy as jnp
import numpy as np
from jax import lax
from jax.experimental import pallas as pl
from jax.experimental.pallas import tpu as pltpu
from jax.sharding import PartitionSpec as P

HD = 128
SEG = 128
VMEM = 16 * 1024 * 1024
F32 = jnp.float32
BF16 = jnp.bfloat16
NT = (((1,), (1,)), ((), ()))
SLOTS = 4
CHUNK = 256
KEEP = 6
BIG_VMEM = 16 * 1024 * 1024
PARAMS = pltpu.CompilerParams(vmem_limit_bytes=VMEM)
SNAKE = (0, 2, 4, 6, 7, 5, 3, 1)
ROUNDS = len(SNAKE) // 2


def row_positions(document_lengths, total_rows):
    ends = jnp.cumsum(document_lengths)
    row_index = jnp.arange(total_rows, dtype=jnp.int32)
    passed = (row_index[:, None] >= ends[None, :]).astype(jnp.int32)
    return row_index - jnp.sum(passed * document_lengths[None, :], axis=1)


def rotary_tables(positions):
    half_size = HD // 2
    freq_index = jnp.arange(half_size, dtype=F32)
    inverse = jnp.exp(freq_index * (-2.0 / HD) * jnp.log(F32(500000.0)))
    angles = positions.astype(F32)[:, None] * inverse[None, :]
    cosine, sine = jnp.cos(angles), jnp.sin(angles)
    return jnp.concatenate([cosine, cosine], 1), jnp.concatenate([-sine, sine], 1)


def small_tables(row_adapter, placement, document_lengths, total_rows):
    segment_slot = placement[row_adapter[::SEG]]
    return segment_slot, *rotary_tables(row_positions(document_lengths, total_rows))


def rotate(value, cosine, sine):
    return value * cosine + pltpu.roll(value, HD // 2, 1) * sine


def shrink_kernel(x_ref, s_ref, h_out):
    @pl.when(pl.program_id(0) == 0)
    def _():
        h_out[...] = jnp.zeros_like(h_out)

    h_out[...] += lax.dot_general(x_ref[...], s_ref[...], NT, preferred_element_type=F32)


def shrink_all(x, shrink, tile):
    rows, depth = x.shape
    rank = shrink.shape[0]
    return pl.pallas_call(
        shrink_kernel,
        grid=(depth // tile,),
        in_specs=[
            pl.BlockSpec((rows, tile), lambda k: (0, k)),
            pl.BlockSpec((rank, tile), lambda k: (0, k)),
        ],
        out_specs=pl.BlockSpec((rows, rank), lambda k: (0, 0)),
        out_shape=jax.ShapeDtypeStruct((rows, rank), F32),
        compiler_params=PARAMS,
        name="shrink",
    )(x, shrink)


def project_kernel(x_ref, w_ref, acc_out):
    @pl.when(pl.program_id(0) == 0)
    def _():
        acc_out[...] = jnp.zeros_like(acc_out)

    acc_out[...] += jnp.dot(x_ref[...], w_ref[...], preferred_element_type=F32)


def project_all(x, weights, tile):
    rows, depth = x.shape
    cols = weights.shape[1]
    return pl.pallas_call(
        project_kernel,
        grid=(depth // tile,),
        in_specs=[
            pl.BlockSpec((rows, tile), lambda k: (0, k)),
            pl.BlockSpec((tile, cols), lambda k: (k, 0)),
        ],
        out_specs=pl.BlockSpec((rows, cols), lambda k: (0, 0)),
        out_shape=jax.ShapeDtypeStruct((rows, cols), F32),
        compiler_params=PARAMS,
        name="project",
    )(x, weights)


def segment_finish_kernel(acc_ref, scale_ref, h_ref, expand_ref, cos_ref, sin_ref, out_ref):
    update = jnp.dot(h_ref[...], expand_ref[0], preferred_element_type=F32)
    for head in range(out_ref.shape[1] // HD):
        cut = slice(head * HD, (head + 1) * HD)
        value = acc_ref[:, cut] * scale_ref[:, cut] + update[:, cut]
        out_ref[:, cut] = rotate(value, cos_ref[...], sin_ref[...]).astype(out_ref.dtype)


def segment_finish(acc, scale, h, expand, cosine, sine):
    rows, cols = acc.shape
    rank = h.shape[1]
    return pl.pallas_call(
        segment_finish_kernel,
        grid=(rows // SEG,),
        in_specs=[
            pl.BlockSpec((SEG, cols), lambda r: (r, 0)),
            pl.BlockSpec((1, cols), lambda r: (0, 0)),
            pl.BlockSpec((SEG, rank), lambda r: (r, 0)),
            pl.BlockSpec((1, rank, cols), lambda r: (r, 0, 0)),
            pl.BlockSpec((SEG, HD), lambda r: (r, 0)),
            pl.BlockSpec((SEG, HD), lambda r: (r, 0)),
        ],
        out_specs=pl.BlockSpec((SEG, cols), lambda r: (r, 0)),
        out_shape=jax.ShapeDtypeStruct((rows, cols), BF16),
        compiler_params=PARAMS,
        name="finish",
    )(acc, scale, h, expand, cosine, sine)


def spread(h, parts):
    step = 1
    while step < parts:
        h = h + lax.ppermute(h, "tensor", [(i, i ^ step) for i in range(parts)])
        step *= 2
    return h


def gather_plan(parts, tokens, weights, scale, shrinks, expands, indices):
    segment_slot, cosine, sine = small_tables(*indices, tokens.shape[0] * parts)
    held, rank, depth = shrinks.shape
    tile = depth // 16
    x = lax.all_gather(tokens, "tensor", axis=0, tiled=True)
    row_slot = jnp.repeat(segment_slot, SEG, total_repeat_length=x.shape[0])
    h = jnp.zeros((x.shape[0], rank), BF16)
    for i in range(held):
        mine = (row_slot == lax.axis_index("tensor") * held + i)[:, None]
        h = jnp.where(mine, shrink_all(x, shrinks[i], tile).astype(BF16), h)
    h = spread(h, parts)
    acc = project_all(x, weights, tile)
    return segment_finish(acc, scale, h, expands[segment_slot], cosine, sine)


def block_owners():
    chips = len(SNAKE)
    owners = np.zeros((2 * chips, 2 * chips), np.int32)
    for place, chip in enumerate(SNAKE):
        for core in (0, 1):
            row = [2 * chip + core, 2 * chip + 1 - core]
            for r in range(1, ROUNDS + 1):
                far, near = place - r * (1 - 2 * core), place + r * (1 - 2 * core)
                far, near = 2 * SNAKE[far % chips], 2 * SNAKE[near % chips]
                row += [far + core, near + 1 - core]
                if r < ROUNDS:
                    row += [near + core, far + 1 - core]
            owners[2 * chip + core] = row
    return owners


def ring_pairs(ways):
    chips = len(SNAKE)
    pairs = []
    for place, chip in enumerate(SNAKE):
        for core in (0, 1):
            pairs.append((2 * chip + core, 2 * SNAKE[(place + ways[core]) % chips] + core))
    return pairs


def block_kernel(count, low, tile, steps, keep, kept, first, base, fresh, ranked, *refs):
    xs, w_ref, refs = refs[:count], refs[count], refs[count + 1 :]
    if ranked:
        s_refs, refs = refs[:2], refs[2:]
    if kept:
        w_kept, refs = refs[0], refs[1:]
    if not first:
        total_in, refs = refs[0], refs[1:]
    total_out, refs = refs[0], refs[1:]
    if ranked:
        h_out, refs = refs[0], refs[1:]
    if keep:
        w_keep, refs = refs[0], refs[1:]
    acc, before, x_slots, w_slots, s_slots, sems, w_sems, total_sems = refs
    rows = xs[0].shape[0]
    streamed = steps - kept
    to_slots = streamed - keep

    def other_copies(step):
        slot = lax.rem(step, SLOTS)
        at = low + (step - kept) * tile
        if kept:
            at = jnp.where(step < kept, w_ref.shape[0] + (step - kept) * tile, at)
        at = pl.multiple_of(at, tile)
        out = []
        for i in range(count):
            cut = xs[i].at[:, pl.ds(at, tile)]
            out.append(pltpu.make_async_copy(cut, x_slots.at[slot, pl.ds(i * rows, rows)], sems.at[slot, i]))
        if ranked:
            for i, s_ref in enumerate(s_refs):
                cut, rank = s_ref.at[:, pl.ds(at, tile)], s_ref.shape[0]
                to = s_slots.at[slot, pl.ds(i * rank, rank)]
                out.append(pltpu.make_async_copy(cut, to, sems.at[slot, count + i]))
        return out

    def weight_copy(index, to):
        source = w_ref.at[pl.ds(pl.multiple_of(low + index * tile, tile), tile)]
        return pltpu.make_async_copy(source, to, w_sems.at[lax.rem(index, SLOTS)])

    def slot_copy(index):
        return weight_copy(index, w_slots.at[lax.rem(index, SLOTS)])

    def kept_rows(index):
        return pl.ds(pl.multiple_of((index - to_slots) * tile, tile), tile)

    def start_other(step):
        for copy in other_copies(step):
            copy.start()

    def start_weights(index):
        @pl.when(index < to_slots)
        def _():
            slot_copy(index).start()

        if keep:
            @pl.when(index >= to_slots)
            def _():
                weight_copy(index, w_keep.at[kept_rows(index)]).start()

    def take(step, weight):
        slot = lax.rem(step, SLOTS)
        x = x_slots[slot]
        for left in range(0, acc.shape[2], CHUNK):
            cut = slice(left, left + CHUNK)
            product = jnp.dot(x, weight(cut), preferred_element_type=F32)
            acc[:, :, cut] += product.reshape(count, rows, CHUNK)
        if ranked:
            mine = jnp.concatenate([x[i * rows : (i + 1) * rows] for i in range(0, count, 2)], 0)
            h_out[...] += lax.dot_general(mine, s_slots[slot], NT, preferred_element_type=F32)

        @pl.when(step + SLOTS < steps)
        def _():
            start_other(step + SLOTS)

    for index in range(min(SLOTS, streamed)):
        start_weights(jnp.int32(index))
    for step in range(min(SLOTS, steps)):
        start_other(jnp.int32(step))
    if not fresh:
        load = pltpu.make_async_copy(total_in.at[pl.ds(base, count)], before, total_sems.at[0])
        load.start()
    acc[...] = jnp.zeros_like(acc)
    if ranked:
        h_out[...] = jnp.zeros_like(h_out)

    if kept:
        @pl.loop(0, kept)
        def _(step):
            for copy in other_copies(step):
                copy.wait()
            take(step, lambda cut: w_kept[pl.ds(pl.multiple_of(step * tile, tile), tile), cut])

    @pl.loop(0, to_slots)
    def _(index):
        for copy in other_copies(index + kept) + [slot_copy(index)]:
            copy.wait()
        take(index + kept, lambda cut: w_slots[lax.rem(index, SLOTS), :, cut])

        @pl.when(index + SLOTS < streamed)
        def _():
            start_weights(index + SLOTS)

    if keep:
        @pl.loop(to_slots, streamed)
        def _(index):
            for copy in other_copies(index + kept) + [weight_copy(index, w_keep.at[kept_rows(index)])]:
                copy.wait()
            take(index + kept, lambda cut: w_keep[kept_rows(index), cut])

            @pl.when(index + SLOTS < streamed)
            def _():
                start_weights(index + SLOTS)

    if not fresh:
        load.wait()
        acc[...] += before[...]
    store = pltpu.make_async_copy(acc, total_out.at[pl.ds(base, count)], total_sems.at[1])
    store.start()
    store.wait()


def block_product(xs, weights, factors, low, high, tile, total, base, ranked=False, fresh=None, keep=0, kept=None):
    count = len(xs)
    rows = xs[0].shape[0]
    cols = weights.shape[1]
    rank = 2 * factors[0].shape[0]
    fresh, first = low == 0 if fresh is None else fresh, total is None
    anywhere, whole = pl.BlockSpec(memory_space=pl.ANY), pl.BlockSpec(memory_space=pltpu.VMEM)
    operands = list(xs) + [weights]
    specs = [anywhere] * (count + 1)
    if ranked:
        operands += factors
        specs += [anywhere] * 2
    kept_steps = 0
    if kept is not None:
        operands.append(kept)
        specs.append(whole)
        kept_steps = kept.shape[0] // tile
    aliases = {}
    if not first:
        aliases = {len(operands): 0}
        operands.append(total)
        specs.append(anywhere)
    outs, out_specs = [jax.ShapeDtypeStruct(total_shape(rows, cols), F32)], [anywhere]
    if ranked:
        outs.append(jax.ShapeDtypeStruct((count // 2 * rows, rank), F32))
        out_specs.append(whole)
    if keep:
        outs.append(jax.ShapeDtypeStruct((keep * tile, cols), weights.dtype))
        out_specs.append(whole)
    steps = (high - low) // tile + kept_steps
    result = pl.pallas_call(
        functools.partial(block_kernel, count, low, tile, steps, keep, kept_steps, first, base, fresh, ranked),
        in_specs=specs,
        out_specs=out_specs,
        out_shape=outs,
        scratch_shapes=[
            pltpu.VMEM((count, rows, cols), F32),
            pltpu.VMEM((1, 8, 128) if fresh else (count, rows, cols), F32),
            pltpu.VMEM((SLOTS, count * rows, tile), BF16),
            pltpu.VMEM((SLOTS, tile, cols), BF16),
            pltpu.VMEM((SLOTS, rank, tile), BF16),
            pltpu.SemaphoreType.DMA((SLOTS, count + 2)),
            pltpu.SemaphoreType.DMA((SLOTS,)),
            pltpu.SemaphoreType.DMA((2,)),
        ],
        input_output_aliases=aliases,
        compiler_params=pltpu.CompilerParams(vmem_limit_bytes=BIG_VMEM),
        cost_estimate=pl.CostEstimate(
            flops=2 * count * rows * (high - low) * cols,
            bytes_accessed=2 * (high - low) * cols,
            transcendentals=0,
        ),
        name="blocks",
    )(*operands)
    return result[0], result[1:]


def total_shape(rows, cols):
    return (2 * len(SNAKE), rows, cols)


def some_ranks_kernel(x_ref, *refs):
    factors, out_ref = refs[:-1], refs[-1]
    terms = [lax.dot_general(x_ref[...], ref[...], NT, preferred_element_type=F32) for ref in factors]
    out_ref[...] = jnp.concatenate(terms, 1)


def some_ranks(x, factors):
    whole = lambda shape: pl.BlockSpec(shape, lambda _: (0, 0))
    shape = (x.shape[0], 2 * factors[0].shape[0])
    return pl.pallas_call(
        some_ranks_kernel,
        grid=(1,),
        in_specs=[whole(value.shape) for value in (x, *factors)],
        out_specs=whole(shape),
        out_shape=jax.ShapeDtypeStruct(shape, F32),
        compiler_params=PARAMS,
        name="some_ranks",
    )(x, *factors)


def rank_kernel(count, owners_ref, slot_ref, *refs):
    xs, refs = refs[:count], refs[count:]
    sa_ref, sb_ref, h_refs, out_ref, placed = refs[0], refs[1], refs[2:-2], refs[-2], refs[-1]
    rows, rank = xs[0].shape[0], sa_ref.shape[0]
    x = jnp.concatenate([ref[...] for ref in xs], 0)
    last = [lax.dot_general(x, ref[...], NT, preferred_element_type=F32) for ref in (sa_ref, sb_ref)]
    last = jnp.concatenate(last, 1)
    segments = slot_ref.shape[0] - 2
    block = 0
    for source in h_refs + (last,):
        for low in range(0, source.shape[0], rows):
            owner = owners_ref[2 * block]
            segment = owner * rows // SEG
            after = jnp.minimum(segment + 1, segments - 1)
            row = owner * rows + lax.broadcasted_iota(jnp.int32, (rows, rank), 0)
            slot = jnp.where(row < (segment + 1) * SEG, slot_ref[segment], slot_ref[after])
            terms = jnp.where(slot == slot_ref[segments + 1], source[low : low + rows, rank:], 0.0)
            terms = jnp.where(slot == slot_ref[segments], source[low : low + rows, :rank], terms)
            placed[pl.ds(pl.multiple_of(owner // 2 * rows, 16), rows), :] = terms
            block += 1
    half = placed.shape[0] // 2
    out_ref[...] = jnp.concatenate([placed[:half, :], placed[half:, :]], 1).astype(out_ref.dtype)


def rank_terms(owners, slots, xs, factors, hs):
    rank = factors[0].shape[0]
    core_rows = owners.shape[0] // 2 * xs[0].shape[0]
    whole = lambda shape: pl.BlockSpec(shape, lambda _, *rest: (0, 0))
    return pl.pallas_call(
        functools.partial(rank_kernel, len(xs)),
        grid_spec=pltpu.PrefetchScalarGridSpec(
            num_scalar_prefetch=2,
            grid=(1,),
            in_specs=[whole(value.shape) for value in (*xs, *factors, *hs)],
            out_specs=whole((core_rows // 2, 2 * rank)),
            scratch_shapes=[pltpu.VMEM((core_rows, rank), F32)],
        ),
        out_shape=jax.ShapeDtypeStruct((core_rows // 2, 2 * rank), BF16),
        compiler_params=PARAMS,
        name="ranks",
    )(owners, slots, *xs, *factors, *hs)


def block_finish_kernel(blocks, segments, places_ref, slot_ref, core_ref, *refs):
    accs, refs = refs[:blocks], refs[blocks:]
    expands, refs = refs[:segments], refs[segments:]
    scale_ref, mine_ref, other_ref, cos_ref, sin_ref, out_ref, h, update = refs
    rank = mine_ref.shape[1] // 2
    rows = accs[0].shape[1]
    first = pl.program_id(0) == 0
    even = core_ref[0] == 0
    mine, other = (jnp.where(first, ref[:, :rank], ref[:, rank:]) for ref in (mine_ref, other_ref))
    for core, terms in enumerate((jnp.where(even, mine, other), jnp.where(even, other, mine))):
        for i in range(blocks // 2):
            at = (2 * i + core) * rows
            h[at : at + rows, :] = terms[i * rows : (i + 1) * rows]
    for segment in range(segments):
        cut = slice(segment * SEG, (segment + 1) * SEG)
        update[cut, :] = jnp.dot(h[cut, :], expands[segment][0], preferred_element_type=F32)
    for block in range(blocks):
        at = slice(block * rows, (block + 1) * rows)
        cosine, sine = cos_ref[at, :], sin_ref[at, :]
        for head in range(out_ref.shape[1] // HD):
            cut = slice(head * HD, (head + 1) * HD)
            value = accs[block][0, :, cut] * scale_ref[:, cut] + update[at, cut]
            out_ref[at, cut] = rotate(value, cosine, sine).astype(out_ref.dtype)


def block_finish(places, slots, core, total, expands, scale, mine, other, cosine, sine):
    blocks, rows, cols = total.shape
    half = blocks // 2
    half_rows = half * rows
    segments = half_rows // SEG
    rank = expands.shape[1]

    def acc_at(i):
        return pl.BlockSpec((1, rows, cols), lambda g, places, *_: (places[g * half + i], 0, 0))

    def expand_at(i):
        return pl.BlockSpec((1, rank, cols), lambda g, places, slots, _: (slots[g * segments + i], 0, 0))

    half_of = lambda width: pl.BlockSpec((half_rows, width), lambda g, *_: (g, 0))
    return pl.pallas_call(
        functools.partial(block_finish_kernel, half, segments),
        grid_spec=pltpu.PrefetchScalarGridSpec(
            num_scalar_prefetch=3,
            grid=(2,),
            in_specs=[acc_at(i) for i in range(half)]
            + [expand_at(i) for i in range(segments)]
            + [
                pl.BlockSpec((1, cols), lambda g, *_: (0, 0)),
                pl.BlockSpec(mine.shape, lambda g, *_: (0, 0)),
                pl.BlockSpec(other.shape, lambda g, *_: (0, 0)),
                half_of(HD),
                half_of(HD),
            ],
            out_specs=half_of(cols),
            scratch_shapes=[pltpu.VMEM((half_rows, rank), BF16), pltpu.VMEM((half_rows, cols), F32)],
        ),
        out_shape=jax.ShapeDtypeStruct((blocks * rows, cols), BF16),
        compiler_params=PARAMS,
        name="finish",
    )(places, slots, core, *([total] * half), *([expands] * segments), scale, mine, other, cosine, sine)


def ring_plan(parts, tokens, weights, scale, shrinks, expands, indices):
    rows, depth = tokens.shape
    tile = depth // 16
    me = lax.axis_index("tensor")
    owners_table = block_owners()
    send = lambda value, pairs: lax.ppermute(value, "tensor", pairs)
    swap = lambda value: send(value, [(i, i ^ 1) for i in range(parts)])
    out, home = ring_pairs((1, -1)), ring_pairs((-1, 1))

    hs, counts = [], []

    def multiply(xs, total, keep=0):
        total, more = block_product(xs, weights, factors, 0, depth, tile, total, sum(counts), True, keep=keep)
        hs.append(more[0])
        counts.append(len(xs))
        return total, more[1:]

    streams = [send(tokens, out), None]
    own, factors = [tokens, swap(tokens)], [shrinks[0], swap(shrinks[0])]
    part = 2 * tile
    total, _ = block_product(own, weights, factors, 0, part, tile, None, 0)
    second, total = lax.optimization_barrier((tokens, total))
    streams[1] = send(second, home)
    total, _ = block_product(own, weights, factors, part, depth, tile, total, 0)
    hs, total = lax.optimization_barrier(([some_ranks(tokens, factors)], total))
    counts.append(len(own))

    def make_tables(me, indices):
        segment_slot, cosine, sine = small_tables(*indices, parts * rows)
        owners = jnp.asarray(owners_table)[me]
        places = jnp.asarray(np.argsort(owners_table, axis=1).astype(np.int32))[me]
        slots = jnp.concatenate([segment_slot, jnp.stack([me, me ^ 1]).astype(jnp.int32)])
        core = (me % 2)[None].astype(jnp.int32)
        return owners, places, slots, core, segment_slot, cosine, sine

    blocks, hops = [], 2 * ROUNDS - 1
    totals = [total] * 2
    for hop in range(hops):
        arrived, _ = lax.optimization_barrier((streams[hop % 2], totals[hop if hop % 2 else hop + 1]))
        if hop + 2 < hops:
            streams[hop % 2] = send(arrived, home if hop % 2 else out)
        if hop % 2:
            late = [arrived, swap(arrived)]
            total, kept = multiply(blocks, total, KEEP if hop == hops - 2 else 0)
            blocks = late
        else:
            blocks += [arrived, swap(arrived)]
        if hop == 1:
            known, total = lax.optimization_barrier(((me, indices), total))
            tables, total = lax.optimization_barrier((make_tables(*known), total))
        totals.append(total)
    held = sum(counts)
    owners, places, slots, core, segment_slot, cosine, sine = tables
    h = rank_terms(owners, slots, blocks[::2], factors, hs)
    beside = lambda step: send(h, [(i, i ^ step) for i in range(parts)])

    def last_product(low, high, total, **more):
        xs, _ = lax.optimization_barrier((blocks, h))
        return block_product(xs, weights, factors, low, high, tile, total, held, **more)[0]

    streamed = depth - KEEP * tile
    middle = (16 - KEEP) // 2 * tile
    near = [beside(step) for step in (2, 4, 6)]
    near, total = lax.optimization_barrier((near, last_product(0, middle, total, kept=kept[0])))
    h = h + near[0] + near[1] + near[2]
    far = [beside(step) for step in (8, 1, 9)]
    far, total = lax.optimization_barrier((far, last_product(middle, streamed, total)))
    mine, other = h + far[0], far[1] + far[2]
    return block_finish(places, segment_slot, core, total, expands, scale, mine, other, cosine, sine)


def body(parts, tokens, weight_codes, column_scale, shrink_store, expand_store, row_adapter, placement, document_lengths):
    rows = tokens.shape[0]
    total_rows = rows * parts
    shrinks = jnp.swapaxes(shrink_store, 1, 2)
    expands = jnp.swapaxes(expand_store, 1, 2)
    ring = parts == 2 * len(SNAKE) and rows % 16 == 0 and shrinks.shape[0] == 1 and total_rows % (2 * SEG) == 0
    plan = ring_plan if ring else gather_plan
    indices = (row_adapter, placement, document_lengths)
    return plan(parts, tokens, weight_codes, column_scale[None, :], shrinks, expands, indices)


def solution(mesh):
    placed = (
        P(("groups", "tensor"), None),
        P(None, "tensor"),
        P("tensor"),
        P(("groups", "tensor"), None, None),
        P("groups", "tensor", None),
        P("groups"),
        P("groups"),
        P("groups"),
    )
    return jax.shard_map(
        functools.partial(body, mesh.shape["tensor"]),
        mesh=mesh,
        in_specs=placed,
        out_specs=P("groups", "tensor"),
        check_vma=False,
    )
```

```python
import functools

import jax
import jax.numpy as jnp
import numpy as np
from jax import lax
from jax.experimental import pallas as pl
from jax.experimental.pallas import tpu as pltpu
from jax.sharding import PartitionSpec as P

HD = 128
SEG = 128
VMEM = 20 * 1024 * 1024
F32 = jnp.float32
BF16 = jnp.bfloat16
NT = (((1,), (1,)), ((), ()))
SLOTS = 4
CHUNK = 256
BIG_VMEM = 24 * 1024 * 1024
PARAMS = pltpu.CompilerParams(vmem_limit_bytes=VMEM)
SNAKE = (0, 2, 4, 6, 7, 5, 3, 1)
ROUNDS = len(SNAKE) // 2


def row_positions(document_lengths, total_rows):
    ends = jnp.cumsum(document_lengths)
    row_index = jnp.arange(total_rows, dtype=jnp.int32)
    passed = (row_index[:, None] >= ends[None, :]).astype(jnp.int32)
    return row_index - jnp.sum(passed * document_lengths[None, :], axis=1)


def rotary_tables(positions):
    half_size = HD // 2
    freq_index = jnp.arange(half_size, dtype=F32)
    inverse = jnp.exp(freq_index * (-2.0 / HD) * jnp.log(F32(500000.0)))
    angles = positions.astype(F32)[:, None] * inverse[None, :]
    cosine, sine = jnp.cos(angles), jnp.sin(angles)
    return jnp.concatenate([cosine, cosine], 1), jnp.concatenate([-sine, sine], 1)


def small_tables(row_adapter, placement, document_lengths, total_rows):
    segment_slot = placement[row_adapter[::SEG]]
    return segment_slot, *rotary_tables(row_positions(document_lengths, total_rows))


def rotate(value, cosine, sine):
    return value * cosine + pltpu.roll(value, HD // 2, 1) * sine


def shrink_kernel(x_ref, s_ref, h_out):
    @pl.when(pl.program_id(0) == 0)
    def _():
        h_out[...] = jnp.zeros_like(h_out)

    h_out[...] += lax.dot_general(x_ref[...], s_ref[...], NT, preferred_element_type=F32)


def shrink_all(x, shrink, tile):
    rows, depth = x.shape
    rank = shrink.shape[0]
    return pl.pallas_call(
        shrink_kernel,
        grid=(depth // tile,),
        in_specs=[
            pl.BlockSpec((rows, tile), lambda k: (0, k)),
            pl.BlockSpec((rank, tile), lambda k: (0, k)),
        ],
        out_specs=pl.BlockSpec((rows, rank), lambda k: (0, 0)),
        out_shape=jax.ShapeDtypeStruct((rows, rank), F32),
        compiler_params=PARAMS,
        name="shrink",
    )(x, shrink)


def project_kernel(x_ref, w_ref, acc_out):
    @pl.when(pl.program_id(0) == 0)
    def _():
        acc_out[...] = jnp.zeros_like(acc_out)

    acc_out[...] += jnp.dot(x_ref[...], w_ref[...], preferred_element_type=F32)


def project_all(x, weights, tile):
    rows, depth = x.shape
    cols = weights.shape[1]
    return pl.pallas_call(
        project_kernel,
        grid=(depth // tile,),
        in_specs=[
            pl.BlockSpec((rows, tile), lambda k: (0, k)),
            pl.BlockSpec((tile, cols), lambda k: (k, 0)),
        ],
        out_specs=pl.BlockSpec((rows, cols), lambda k: (0, 0)),
        out_shape=jax.ShapeDtypeStruct((rows, cols), F32),
        compiler_params=PARAMS,
        name="project",
    )(x, weights)


def segment_finish_kernel(acc_ref, scale_ref, h_ref, expand_ref, cos_ref, sin_ref, out_ref):
    update = jnp.dot(h_ref[...], expand_ref[0], preferred_element_type=F32)
    for head in range(out_ref.shape[1] // HD):
        cut = slice(head * HD, (head + 1) * HD)
        value = acc_ref[:, cut] * scale_ref[:, cut] + update[:, cut]
        out_ref[:, cut] = rotate(value, cos_ref[...], sin_ref[...]).astype(out_ref.dtype)


def segment_finish(acc, scale, h, expand, cosine, sine):
    rows, cols = acc.shape
    rank = h.shape[1]
    return pl.pallas_call(
        segment_finish_kernel,
        grid=(rows // SEG,),
        in_specs=[
            pl.BlockSpec((SEG, cols), lambda r: (r, 0)),
            pl.BlockSpec((1, cols), lambda r: (0, 0)),
            pl.BlockSpec((SEG, rank), lambda r: (r, 0)),
            pl.BlockSpec((1, rank, cols), lambda r: (r, 0, 0)),
            pl.BlockSpec((SEG, HD), lambda r: (r, 0)),
            pl.BlockSpec((SEG, HD), lambda r: (r, 0)),
        ],
        out_specs=pl.BlockSpec((SEG, cols), lambda r: (r, 0)),
        out_shape=jax.ShapeDtypeStruct((rows, cols), BF16),
        compiler_params=PARAMS,
        name="finish",
    )(acc, scale, h, expand, cosine, sine)


def spread(h, parts):
    step = 1
    while step < parts:
        h = h + lax.ppermute(h, "tensor", [(i, i ^ step) for i in range(parts)])
        step *= 2
    return h


def gather_plan(parts, tokens, weights, scale, shrinks, expands, indices):
    segment_slot, cosine, sine = small_tables(*indices, tokens.shape[0] * parts)
    held, rank, depth = shrinks.shape
    tile = depth // 16
    x = lax.all_gather(tokens, "tensor", axis=0, tiled=True)
    row_slot = jnp.repeat(segment_slot, SEG, total_repeat_length=x.shape[0])
    h = jnp.zeros((x.shape[0], rank), BF16)
    for i in range(held):
        mine = (row_slot == lax.axis_index("tensor") * held + i)[:, None]
        h = jnp.where(mine, shrink_all(x, shrinks[i], tile).astype(BF16), h)
    h = spread(h, parts)
    acc = project_all(x, weights, tile)
    return segment_finish(acc, scale, h, expands[segment_slot], cosine, sine)


def block_owners():
    chips = len(SNAKE)
    owners = np.zeros((2 * chips, 2 * chips), np.int32)
    for place, chip in enumerate(SNAKE):
        for core in (0, 1):
            row = [2 * chip + core, 2 * chip + 1 - core]
            for r in range(1, ROUNDS + 1):
                far, near = place - r * (1 - 2 * core), place + r * (1 - 2 * core)
                far, near = 2 * SNAKE[far % chips], 2 * SNAKE[near % chips]
                row += [far + core, near + 1 - core]
                if r < ROUNDS:
                    row += [near + core, far + 1 - core]
            owners[2 * chip + core] = row
    return owners


def ring_pairs(ways):
    chips = len(SNAKE)
    pairs = []
    for place, chip in enumerate(SNAKE):
        for core in (0, 1):
            pairs.append((2 * chip + core, 2 * SNAKE[(place + ways[core]) % chips] + core))
    return pairs


def block_kernel(count, low, tile, steps, first, base, fresh, ranked, *refs):
    xs, w_ref, refs = refs[:count], refs[count], refs[count + 1 :]
    if ranked:
        s_refs, refs = refs[:2], refs[2:]
    if not first:
        total_in, refs = refs[0], refs[1:]
    total_out, refs = refs[0], refs[1:]
    if ranked:
        h_out, refs = refs[0], refs[1:]
    acc, before, x_slots, w_slots, s_slots, sems, total_sems = refs
    rows = xs[0].shape[0]

    def copies(step):
        slot = lax.rem(step, SLOTS)
        at = pl.multiple_of(step * tile, tile)
        sem = lambda i: sems.at[slot, i]
        out = [pltpu.make_async_copy(w_ref.at[pl.ds(low + at, tile)], w_slots.at[slot], sem(count))]
        for i in range(count):
            cut = xs[i].at[:, pl.ds(low + at, tile)]
            out.append(pltpu.make_async_copy(cut, x_slots.at[slot, pl.ds(i * rows, rows)], sem(i)))
        if ranked:
            for i, s_ref in enumerate(s_refs):
                cut, rank = s_ref.at[:, pl.ds(low + at, tile)], s_ref.shape[0]
                to = s_slots.at[slot, pl.ds(i * rank, rank)]
                out.append(pltpu.make_async_copy(cut, to, sem(count + 1 + i)))
        return out

    def start(step):
        for copy in copies(step):
            copy.start()

    for step in range(min(SLOTS, steps)):
        start(jnp.int32(step))
    if not fresh:
        load = pltpu.make_async_copy(total_in.at[pl.ds(base, count)], before, total_sems.at[0])
        load.start()
    acc[...] = jnp.zeros_like(acc)
    if ranked:
        h_out[...] = jnp.zeros_like(h_out)

    @pl.loop(0, steps)
    def _(step):
        for copy in copies(step):
            copy.wait()
        slot = lax.rem(step, SLOTS)
        x = x_slots[slot]
        for left in range(0, acc.shape[2], CHUNK):
            cut = slice(left, left + CHUNK)
            product = jnp.dot(x, w_slots[slot, :, cut], preferred_element_type=F32)
            acc[:, :, cut] += product.reshape(count, rows, CHUNK)
        if ranked:
            mine = jnp.concatenate([x[i * rows : (i + 1) * rows] for i in range(0, count, 2)], 0)
            h_out[...] += lax.dot_general(mine, s_slots[slot], NT, preferred_element_type=F32)

        @pl.when(step + SLOTS < steps)
        def _():
            start(step + SLOTS)

    if not fresh:
        load.wait()
        acc[...] += before[...]
    store = pltpu.make_async_copy(acc, total_out.at[pl.ds(base, count)], total_sems.at[1])
    store.start()
    store.wait()


def block_product(xs, weights, factors, low, high, tile, total, base, ranked):
    count = len(xs)
    rows = xs[0].shape[0]
    cols = weights.shape[1]
    rank = 2 * factors[0].shape[0]
    fresh, first = low == 0, total is None
    anywhere, whole = pl.BlockSpec(memory_space=pl.ANY), pl.BlockSpec(memory_space=pltpu.VMEM)
    operands = list(xs) + [weights]
    specs = [anywhere] * (count + 1)
    if ranked:
        operands += factors
        specs += [anywhere] * 2
    aliases = {}
    if not first:
        aliases = {len(operands): 0}
        operands.append(total)
        specs.append(anywhere)
    outs, out_specs = [jax.ShapeDtypeStruct(total_shape(rows, cols), F32)], [anywhere]
    if ranked:
        outs.append(jax.ShapeDtypeStruct((count // 2 * rows, rank), F32))
        out_specs.append(whole)
    steps = (high - low) // tile
    result = pl.pallas_call(
        functools.partial(block_kernel, count, low, tile, steps, first, base, fresh, ranked),
        in_specs=specs,
        out_specs=out_specs,
        out_shape=outs,
        scratch_shapes=[
            pltpu.VMEM((count, rows, cols), F32),
            pltpu.VMEM((1, 8, 128) if fresh else (count, rows, cols), F32),
            pltpu.VMEM((SLOTS, count * rows, tile), BF16),
            pltpu.VMEM((SLOTS, tile, cols), BF16),
            pltpu.VMEM((SLOTS, rank, tile), BF16),
            pltpu.SemaphoreType.DMA((SLOTS, count + 3)),
            pltpu.SemaphoreType.DMA((2,)),
        ],
        input_output_aliases=aliases,
        compiler_params=pltpu.CompilerParams(vmem_limit_bytes=BIG_VMEM),
        cost_estimate=pl.CostEstimate(
            flops=2 * count * rows * (high - low) * cols,
            bytes_accessed=2 * (high - low) * cols,
            transcendentals=0,
        ),
        name="blocks",
    )(*operands)
    return result[0], result[1:]


def total_shape(rows, cols):
    return (2 * len(SNAKE), rows, cols)


def some_ranks_kernel(x_ref, *refs):
    factors, out_ref = refs[:-1], refs[-1]
    terms = [lax.dot_general(x_ref[...], ref[...], NT, preferred_element_type=F32) for ref in factors]
    out_ref[...] = jnp.concatenate(terms, 1)


def some_ranks(x, factors):
    whole = lambda shape: pl.BlockSpec(shape, lambda _: (0, 0))
    shape = (x.shape[0], 2 * factors[0].shape[0])
    return pl.pallas_call(
        some_ranks_kernel,
        grid=(1,),
        in_specs=[whole(value.shape) for value in (x, *factors)],
        out_specs=whole(shape),
        out_shape=jax.ShapeDtypeStruct(shape, F32),
        compiler_params=PARAMS,
        name="some_ranks",
    )(x, *factors)


def rank_kernel(count, owners_ref, slot_ref, *refs):
    xs, refs = refs[:count], refs[count:]
    sa_ref, sb_ref, h_refs, out_ref, placed = refs[0], refs[1], refs[2:-2], refs[-2], refs[-1]
    rows, rank = xs[0].shape[0], sa_ref.shape[0]
    x = jnp.concatenate([ref[...] for ref in xs], 0)
    last = [lax.dot_general(x, ref[...], NT, preferred_element_type=F32) for ref in (sa_ref, sb_ref)]
    last = jnp.concatenate(last, 1)
    segments = slot_ref.shape[0] - 2
    block = 0
    for source in h_refs + (last,):
        for low in range(0, source.shape[0], rows):
            owner = owners_ref[2 * block]
            segment = owner * rows // SEG
            after = jnp.minimum(segment + 1, segments - 1)
            row = owner * rows + lax.broadcasted_iota(jnp.int32, (rows, rank), 0)
            slot = jnp.where(row < (segment + 1) * SEG, slot_ref[segment], slot_ref[after])
            terms = jnp.where(slot == slot_ref[segments + 1], source[low : low + rows, rank:], 0.0)
            terms = jnp.where(slot == slot_ref[segments], source[low : low + rows, :rank], terms)
            placed[pl.ds(pl.multiple_of(owner // 2 * rows, 16), rows), :] = terms
            block += 1
    half = placed.shape[0] // 2
    out_ref[...] = jnp.concatenate([placed[:half, :], placed[half:, :]], 1).astype(out_ref.dtype)


def rank_terms(owners, slots, xs, factors, hs):
    rank = factors[0].shape[0]
    core_rows = owners.shape[0] // 2 * xs[0].shape[0]
    scalars, whole = pl.BlockSpec(memory_space=pltpu.SMEM), pl.BlockSpec(memory_space=pltpu.VMEM)
    return pl.pallas_call(
        functools.partial(rank_kernel, len(xs)),
        in_specs=[scalars] * 2 + [whole] * (len(xs) + len(factors) + len(hs)),
        out_specs=whole,
        scratch_shapes=[pltpu.VMEM((core_rows, rank), F32)],
        out_shape=jax.ShapeDtypeStruct((core_rows // 2, 2 * rank), BF16),
        compiler_params=PARAMS,
        name="ranks",
    )(owners, slots, *xs, *factors, *hs)


def block_finish_kernel(places_ref, slot_ref, core_ref, total_ref, expand_ref, scale_ref, mine_ref, other_ref, *refs):
    cos_ref, sin_ref, out_ref, h, update, done, sems = refs
    blocks, rows, cols = total_ref.shape
    rank = mine_ref.shape[1] // 2
    even = core_ref[0] == 0
    mine, other = mine_ref[...], other_ref[...]
    for core, terms in enumerate((jnp.where(even, mine, other), jnp.where(even, other, mine))):
        for chip in range(blocks // 2):
            side, at = divmod(chip * rows, terms.shape[0])
            to = (2 * chip + core) * rows
            h[to : to + rows, :] = terms[at : at + rows, side * rank : (side + 1) * rank]
    for segment in range(h.shape[0] // SEG):
        cut = slice(segment * SEG, (segment + 1) * SEG)
        expand = expand_ref[slot_ref[segment]]
        update[cut, :] = jnp.dot(h[cut, :], expand, preferred_element_type=F32)
    copies = []
    for block in range(blocks):
        at = slice(block * rows, (block + 1) * rows)
        cosine, sine = cos_ref[at, :], sin_ref[at, :]
        place = places_ref[block]
        for left in range(0, cols, HD):
            cut = slice(left, left + HD)
            value = total_ref[place, :, cut] * scale_ref[:, cut] + update[at, cut]
            done[at, cut] = rotate(value, cosine, sine).astype(done.dtype)
        if block % 2:
            strip = pl.ds((block - 1) * rows, 2 * rows)
            copies.append(pltpu.make_async_copy(done.at[strip], out_ref.at[strip], sems.at[block // 2]))
            copies[-1].start()
    for copy in copies:
        copy.wait()


def block_finish(places, slots, core, total, expands, scale, mine, other, cosine, sine):
    blocks, rows, cols = total.shape
    rank = expands.shape[1]
    scalars, whole = pl.BlockSpec(memory_space=pltpu.SMEM), pl.BlockSpec(memory_space=pltpu.VMEM)
    return pl.pallas_call(
        block_finish_kernel,
        in_specs=[scalars] * 3 + [whole] * 7,
        out_specs=pl.BlockSpec(memory_space=pl.ANY),
        scratch_shapes=[
            pltpu.VMEM((blocks * rows, rank), BF16),
            pltpu.VMEM((blocks * rows, cols), F32),
            pltpu.VMEM((blocks * rows, cols), BF16),
            pltpu.SemaphoreType.DMA((blocks // 2,)),
        ],
        out_shape=jax.ShapeDtypeStruct((blocks * rows, cols), BF16),
        compiler_params=PARAMS,
        name="finish",
    )(places, slots, core, total, expands, scale, mine, other, cosine, sine)


def ring_plan(parts, tokens, weights, scale, shrinks, expands, indices):
    rows, depth = tokens.shape
    tile = depth // 16
    me = lax.axis_index("tensor")
    owners_table = block_owners()
    send = lambda value, pairs: lax.ppermute(value, "tensor", pairs)
    swap = lambda value: send(value, [(i, i ^ 1) for i in range(parts)])
    out, home = ring_pairs((1, -1)), ring_pairs((-1, 1))

    half = depth // 2
    hs, counts = [], []

    def multiply(xs, total):
        total, h = block_product(xs, weights, factors, 0, depth, tile, total, sum(counts), True)
        hs.extend(h)
        counts.append(len(xs))
        return total

    streams = [send(tokens, out), None]
    own, factors = [tokens, swap(tokens)], [shrinks[0], swap(shrinks[0])]
    part = 2 * tile
    total, _ = block_product(own, weights, factors, 0, part, tile, None, 0, False)
    second, total = lax.optimization_barrier((tokens, total))
    streams[1] = send(second, home)
    total, _ = block_product(own, weights, factors, part, depth, tile, total, 0, False)
    hs, total = lax.optimization_barrier(([some_ranks(tokens, factors)], total))
    counts.append(len(own))

    def make_tables(me, indices):
        segment_slot, cosine, sine = small_tables(*indices, parts * rows)
        owners = jnp.asarray(owners_table)[me]
        places = jnp.asarray(np.argsort(owners_table, axis=1).astype(np.int32))[me]
        slots = jnp.concatenate([segment_slot, jnp.stack([me, me ^ 1]).astype(jnp.int32)])
        core = (me % 2)[None].astype(jnp.int32)
        return owners, places, slots, core, segment_slot, cosine, sine

    blocks, hops = [], 2 * ROUNDS - 1
    totals = [total] * 2
    for hop in range(hops):
        arrived, _ = lax.optimization_barrier((streams[hop % 2], totals[hop if hop % 2 else hop + 1]))
        if hop + 2 < hops:
            streams[hop % 2] = send(arrived, home if hop % 2 else out)
        if hop % 2:
            late = [arrived, swap(arrived)]
            total = multiply(blocks, total)
            blocks = late
        else:
            blocks += [arrived, swap(arrived)]
        if hop == 1:
            known, total = lax.optimization_barrier(((me, indices), total))
            tables, total = lax.optimization_barrier((make_tables(*known), total))
        totals.append(total)
    held = sum(counts)
    owners, places, slots, core, segment_slot, cosine, sine = tables
    h = rank_terms(owners, slots, blocks[::2], factors, hs)
    beside = lambda step: send(h, [(i, i ^ step) for i in range(parts)])

    def last_product(low, high, total):
        xs, _ = lax.optimization_barrier((blocks, h))
        return block_product(xs, weights, factors, low, high, tile, total, held, False)[0]

    near = [beside(step) for step in (2, 4, 6)]
    near, total = lax.optimization_barrier((near, last_product(0, half, total)))
    h = h + near[0] + near[1] + near[2]
    far = [beside(step) for step in (8, 1, 9)]
    far, total = lax.optimization_barrier((far, last_product(half, depth, total)))
    mine, other = h + far[0], far[1] + far[2]
    return block_finish(places, segment_slot, core, total, expands, scale, mine, other, cosine, sine)


def body(parts, tokens, weight_codes, column_scale, shrink_store, expand_store, row_adapter, placement, document_lengths):
    rows = tokens.shape[0]
    total_rows = rows * parts
    shrinks = jnp.swapaxes(shrink_store, 1, 2)
    expands = jnp.swapaxes(expand_store, 1, 2)
    ring = parts == 2 * len(SNAKE) and rows % 16 == 0 and shrinks.shape[0] == 1 and total_rows % (2 * SEG) == 0
    plan = ring_plan if ring else gather_plan
    indices = (row_adapter, placement, document_lengths)
    return plan(parts, tokens, weight_codes, column_scale[None, :], shrinks, expands, indices)


def solution(mesh):
    placed = (
        P(("groups", "tensor"), None),
        P(None, "tensor"),
        P("tensor"),
        P(("groups", "tensor"), None, None),
        P("groups", "tensor", None),
        P("groups"),
        P("groups"),
        P("groups"),
    )
    return jax.shard_map(
        functools.partial(body, mesh.shape["tensor"]),
        mesh=mesh,
        in_specs=placed,
        out_specs=P("groups", "tensor"),
        check_vma=False,
    )
```

```python
import functools

import jax
import jax.numpy as jnp
import numpy as np
from jax import lax
from jax.experimental import pallas as pl
from jax.experimental.pallas import tpu as pltpu
from jax.sharding import PartitionSpec as P

HD = 128
SEG = 128
VMEM = 20 * 1024 * 1024
F32 = jnp.float32
BF16 = jnp.bfloat16
NT = (((1,), (1,)), ((), ()))
SLOTS = 4
CHUNK = 256
BIG_VMEM = 24 * 1024 * 1024
PARAMS = pltpu.CompilerParams(vmem_limit_bytes=VMEM)
SNAKE = (0, 2, 4, 6, 7, 5, 3, 1)
ROUNDS = len(SNAKE) // 2


def row_positions(document_lengths, total_rows):
    ends = jnp.cumsum(document_lengths)
    row_index = jnp.arange(total_rows, dtype=jnp.int32)
    passed = (row_index[:, None] >= ends[None, :]).astype(jnp.int32)
    return row_index - jnp.sum(passed * document_lengths[None, :], axis=1)


def rotary_tables(positions):
    half_size = HD // 2
    freq_index = jnp.arange(half_size, dtype=F32)
    inverse = jnp.exp(freq_index * (-2.0 / HD) * jnp.log(F32(500000.0)))
    angles = positions.astype(F32)[:, None] * inverse[None, :]
    cosine, sine = jnp.cos(angles), jnp.sin(angles)
    return jnp.concatenate([cosine, cosine], 1), jnp.concatenate([-sine, sine], 1)


def small_tables(row_adapter, placement, document_lengths, total_rows):
    segment_slot = placement[row_adapter[::SEG]]
    return segment_slot, *rotary_tables(row_positions(document_lengths, total_rows))


def rotate(value, cosine, sine):
    return value * cosine + pltpu.roll(value, HD // 2, 1) * sine


def shrink_kernel(x_ref, s_ref, h_out):
    @pl.when(pl.program_id(0) == 0)
    def _():
        h_out[...] = jnp.zeros_like(h_out)

    h_out[...] += lax.dot_general(x_ref[...], s_ref[...], NT, preferred_element_type=F32)


def shrink_all(x, shrink, tile):
    rows, depth = x.shape
    rank = shrink.shape[0]
    return pl.pallas_call(
        shrink_kernel,
        grid=(depth // tile,),
        in_specs=[
            pl.BlockSpec((rows, tile), lambda k: (0, k)),
            pl.BlockSpec((rank, tile), lambda k: (0, k)),
        ],
        out_specs=pl.BlockSpec((rows, rank), lambda k: (0, 0)),
        out_shape=jax.ShapeDtypeStruct((rows, rank), F32),
        compiler_params=PARAMS,
        name="shrink",
    )(x, shrink)


def project_kernel(x_ref, w_ref, acc_out):
    @pl.when(pl.program_id(0) == 0)
    def _():
        acc_out[...] = jnp.zeros_like(acc_out)

    acc_out[...] += jnp.dot(x_ref[...], w_ref[...], preferred_element_type=F32)


def project_all(x, weights, tile):
    rows, depth = x.shape
    cols = weights.shape[1]
    return pl.pallas_call(
        project_kernel,
        grid=(depth // tile,),
        in_specs=[
            pl.BlockSpec((rows, tile), lambda k: (0, k)),
            pl.BlockSpec((tile, cols), lambda k: (k, 0)),
        ],
        out_specs=pl.BlockSpec((rows, cols), lambda k: (0, 0)),
        out_shape=jax.ShapeDtypeStruct((rows, cols), F32),
        compiler_params=PARAMS,
        name="project",
    )(x, weights)


def segment_finish_kernel(acc_ref, scale_ref, h_ref, expand_ref, cos_ref, sin_ref, out_ref):
    update = jnp.dot(h_ref[...], expand_ref[0], preferred_element_type=F32)
    for head in range(out_ref.shape[1] // HD):
        cut = slice(head * HD, (head + 1) * HD)
        value = acc_ref[:, cut] * scale_ref[:, cut] + update[:, cut]
        out_ref[:, cut] = rotate(value, cos_ref[...], sin_ref[...]).astype(out_ref.dtype)


def segment_finish(acc, scale, h, expand, cosine, sine):
    rows, cols = acc.shape
    rank = h.shape[1]
    return pl.pallas_call(
        segment_finish_kernel,
        grid=(rows // SEG,),
        in_specs=[
            pl.BlockSpec((SEG, cols), lambda r: (r, 0)),
            pl.BlockSpec((1, cols), lambda r: (0, 0)),
            pl.BlockSpec((SEG, rank), lambda r: (r, 0)),
            pl.BlockSpec((1, rank, cols), lambda r: (r, 0, 0)),
            pl.BlockSpec((SEG, HD), lambda r: (r, 0)),
            pl.BlockSpec((SEG, HD), lambda r: (r, 0)),
        ],
        out_specs=pl.BlockSpec((SEG, cols), lambda r: (r, 0)),
        out_shape=jax.ShapeDtypeStruct((rows, cols), BF16),
        compiler_params=PARAMS,
        name="finish",
    )(acc, scale, h, expand, cosine, sine)


def spread(h, parts):
    step = 1
    while step < parts:
        h = h + lax.ppermute(h, "tensor", [(i, i ^ step) for i in range(parts)])
        step *= 2
    return h


def gather_plan(parts, tokens, weights, scale, shrinks, expands, indices):
    segment_slot, cosine, sine = small_tables(*indices, tokens.shape[0] * parts)
    held, rank, depth = shrinks.shape
    tile = depth // 16
    x = lax.all_gather(tokens, "tensor", axis=0, tiled=True)
    row_slot = jnp.repeat(segment_slot, SEG, total_repeat_length=x.shape[0])
    h = jnp.zeros((x.shape[0], rank), BF16)
    for i in range(held):
        mine = (row_slot == lax.axis_index("tensor") * held + i)[:, None]
        h = jnp.where(mine, shrink_all(x, shrinks[i], tile).astype(BF16), h)
    h = spread(h, parts)
    acc = project_all(x, weights, tile)
    return segment_finish(acc, scale, h, expands[segment_slot], cosine, sine)


def block_owners():
    chips = len(SNAKE)
    owners = np.zeros((2 * chips, 2 * chips), np.int32)
    for place, chip in enumerate(SNAKE):
        for core in (0, 1):
            row = [2 * chip + core, 2 * chip + 1 - core]
            for r in range(1, ROUNDS + 1):
                far, near = place - r * (1 - 2 * core), place + r * (1 - 2 * core)
                far, near = 2 * SNAKE[far % chips], 2 * SNAKE[near % chips]
                row += [far + core, near + 1 - core]
                if r < ROUNDS:
                    row += [near + core, far + 1 - core]
            owners[2 * chip + core] = row
    return owners


def ring_pairs(ways):
    chips = len(SNAKE)
    pairs = []
    for place, chip in enumerate(SNAKE):
        for core in (0, 1):
            pairs.append((2 * chip + core, 2 * SNAKE[(place + ways[core]) % chips] + core))
    return pairs


def block_kernel(count, low, tile, steps, first, base, fresh, ranked, *refs):
    xs, w_ref, refs = refs[:count], refs[count], refs[count + 1 :]
    if ranked:
        s_ref, refs = refs[0], refs[1:]
    if not first:
        total_in, refs = refs[0], refs[1:]
    total_out, refs = refs[0], refs[1:]
    if ranked:
        h_out, refs = refs[0], refs[1:]
    acc, before, x_slots, w_slots, s_slots, sems, total_sems = refs
    rows = xs[0].shape[0]

    def copies(step):
        slot = lax.rem(step, SLOTS)
        at = pl.multiple_of(step * tile, tile)
        sem = lambda i: sems.at[slot, i]
        out = [pltpu.make_async_copy(w_ref.at[pl.ds(low + at, tile)], w_slots.at[slot], sem(count))]
        for i in range(count):
            cut = xs[i].at[:, pl.ds(low + at, tile)]
            out.append(pltpu.make_async_copy(cut, x_slots.at[slot, pl.ds(i * rows, rows)], sem(i)))
        if ranked:
            cut = s_ref.at[:, pl.ds(low + at, tile)]
            out.append(pltpu.make_async_copy(cut, s_slots.at[slot], sem(count + 1)))
        return out

    def start(step):
        for copy in copies(step):
            copy.start()

    for step in range(min(SLOTS, steps)):
        start(jnp.int32(step))
    if not fresh:
        load = pltpu.make_async_copy(total_in.at[pl.ds(base, count)], before, total_sems.at[0])
        load.start()
    acc[...] = jnp.zeros_like(acc)
    if ranked:
        h_out[...] = jnp.zeros_like(h_out)

    @pl.loop(0, steps)
    def _(step):
        for copy in copies(step):
            copy.wait()
        slot = lax.rem(step, SLOTS)
        x = x_slots[slot]
        for left in range(0, acc.shape[2], CHUNK):
            cut = slice(left, left + CHUNK)
            product = jnp.dot(x, w_slots[slot, :, cut], preferred_element_type=F32)
            acc[:, :, cut] += product.reshape(count, rows, CHUNK)
        if ranked:
            mine = jnp.concatenate([x[i * rows : (i + 1) * rows] for i in range(0, count, 2)], 0)
            h_out[...] += lax.dot_general(mine, s_slots[slot], NT, preferred_element_type=F32)

        @pl.when(step + SLOTS < steps)
        def _():
            start(step + SLOTS)

    if not fresh:
        load.wait()
        acc[...] += before[...]
    store = pltpu.make_async_copy(acc, total_out.at[pl.ds(base, count)], total_sems.at[1])
    store.start()
    store.wait()


def block_product(xs, weights, factors, low, high, tile, total, base, ranked):
    count = len(xs)
    rows = xs[0].shape[0]
    cols = weights.shape[1]
    rank = factors.shape[0]
    fresh, first = low == 0, total is None
    anywhere, whole = pl.BlockSpec(memory_space=pl.ANY), pl.BlockSpec(memory_space=pltpu.VMEM)
    operands = list(xs) + [weights]
    specs = [anywhere] * (count + 1)
    if ranked:
        operands.append(factors)
        specs.append(anywhere)
    aliases = {}
    if not first:
        aliases = {len(operands): 0}
        operands.append(total)
        specs.append(anywhere)
    outs, out_specs = [jax.ShapeDtypeStruct(total_shape(rows, cols), F32)], [anywhere]
    if ranked:
        outs.append(jax.ShapeDtypeStruct((count // 2 * rows, rank), F32))
        out_specs.append(whole)
    steps = (high - low) // tile
    result = pl.pallas_call(
        functools.partial(block_kernel, count, low, tile, steps, first, base, fresh, ranked),
        in_specs=specs,
        out_specs=out_specs,
        out_shape=outs,
        scratch_shapes=[
            pltpu.VMEM((count, rows, cols), F32),
            pltpu.VMEM((1, 8, 128) if fresh else (count, rows, cols), F32),
            pltpu.VMEM((SLOTS, count * rows, tile), BF16),
            pltpu.VMEM((SLOTS, tile, cols), BF16),
            pltpu.VMEM((SLOTS, rank, tile), BF16),
            pltpu.SemaphoreType.DMA((SLOTS, count + 2)),
            pltpu.SemaphoreType.DMA((2,)),
        ],
        input_output_aliases=aliases,
        compiler_params=pltpu.CompilerParams(vmem_limit_bytes=BIG_VMEM),
        cost_estimate=pl.CostEstimate(
            flops=2 * count * rows * (high - low) * cols,
            bytes_accessed=2 * (high - low) * cols,
            transcendentals=0,
        ),
        name="blocks",
    )(*operands)
    return result[0], result[1:]


def total_shape(rows, cols):
    return (2 * len(SNAKE), rows, cols)


def some_ranks_kernel(x_ref, s_ref, out_ref):
    out_ref[...] = lax.dot_general(x_ref[...], s_ref[...], NT, preferred_element_type=F32)


def some_ranks(x, factors):
    whole = pl.BlockSpec(memory_space=pltpu.VMEM)
    return pl.pallas_call(
        some_ranks_kernel,
        in_specs=[whole] * 2,
        out_specs=whole,
        out_shape=jax.ShapeDtypeStruct((x.shape[0], factors.shape[0]), F32),
        compiler_params=PARAMS,
        name="some_ranks",
    )(x, factors)


def rank_kernel(count, owners_ref, slot_ref, *refs):
    xs, refs = refs[:count], refs[count:]
    s_ref, h_refs, out_ref, placed = refs[0], refs[1:-2], refs[-2], refs[-1]
    rows, rank = xs[0].shape[0], s_ref.shape[0] // 2
    x = jnp.concatenate([ref[...] for ref in xs], 0)
    last = lax.dot_general(x, s_ref[...], NT, preferred_element_type=F32)
    segments = slot_ref.shape[0] - 2
    block = 0
    for source in h_refs + (last,):
        for low in range(0, source.shape[0], rows):
            owner = owners_ref[2 * block]
            segment = owner * rows // SEG
            after = jnp.minimum(segment + 1, segments - 1)
            row = owner * rows + lax.broadcasted_iota(jnp.int32, (rows, rank), 0)
            slot = jnp.where(row < (segment + 1) * SEG, slot_ref[segment], slot_ref[after])
            terms = jnp.where(slot == slot_ref[segments + 1], source[low : low + rows, rank:], 0.0)
            terms = jnp.where(slot == slot_ref[segments], source[low : low + rows, :rank], terms)
            placed[pl.ds(pl.multiple_of(owner // 2 * rows, 16), rows), :] = terms
            block += 1
    half = placed.shape[0] // 2
    out_ref[...] = jnp.concatenate([placed[:half, :], placed[half:, :]], 1).astype(out_ref.dtype)


def rank_terms(owners, slots, xs, factors, hs):
    rank = factors.shape[0] // 2
    core_rows = owners.shape[0] // 2 * xs[0].shape[0]
    scalars, whole = pl.BlockSpec(memory_space=pltpu.SMEM), pl.BlockSpec(memory_space=pltpu.VMEM)
    return pl.pallas_call(
        functools.partial(rank_kernel, len(xs)),
        in_specs=[scalars] * 2 + [whole] * (len(xs) + 1 + len(hs)),
        out_specs=whole,
        scratch_shapes=[pltpu.VMEM((core_rows, rank), F32)],
        out_shape=jax.ShapeDtypeStruct((core_rows // 2, 2 * rank), BF16),
        compiler_params=PARAMS,
        name="ranks",
    )(owners, slots, *xs, factors, *hs)


def block_finish_kernel(places_ref, slot_ref, core_ref, total_ref, expand_ref, scale_ref, mine_ref, other_ref, *refs):
    cos_ref, sin_ref, out_ref, h, update, done, sems = refs
    blocks, rows, cols = total_ref.shape
    rank = mine_ref.shape[1] // 2
    even = core_ref[0] == 0
    mine, other = mine_ref[...], other_ref[...]
    for core, terms in enumerate((jnp.where(even, mine, other), jnp.where(even, other, mine))):
        for chip in range(blocks // 2):
            side, at = divmod(chip * rows, terms.shape[0])
            to = (2 * chip + core) * rows
            h[to : to + rows, :] = terms[at : at + rows, side * rank : (side + 1) * rank]
    for segment in range(h.shape[0] // SEG):
        cut = slice(segment * SEG, (segment + 1) * SEG)
        expand = expand_ref[slot_ref[segment]]
        update[cut, :] = jnp.dot(h[cut, :], expand, preferred_element_type=F32)
    copies = []
    for block in range(blocks):
        at = slice(block * rows, (block + 1) * rows)
        cosine, sine = cos_ref[at, :], sin_ref[at, :]
        place = places_ref[block]
        for left in range(0, cols, HD):
            cut = slice(left, left + HD)
            value = total_ref[place, :, cut] * scale_ref[:, cut] + update[at, cut]
            done[at, cut] = rotate(value, cosine, sine).astype(done.dtype)
        if block % 2:
            strip = pl.ds((block - 1) * rows, 2 * rows)
            copies.append(pltpu.make_async_copy(done.at[strip], out_ref.at[strip], sems.at[block // 2]))
            copies[-1].start()
    for copy in copies:
        copy.wait()


def block_finish(places, slots, core, total, expands, scale, mine, other, cosine, sine):
    blocks, rows, cols = total.shape
    rank = expands.shape[1]
    scalars, whole = pl.BlockSpec(memory_space=pltpu.SMEM), pl.BlockSpec(memory_space=pltpu.VMEM)
    return pl.pallas_call(
        block_finish_kernel,
        in_specs=[scalars] * 3 + [whole] * 7,
        out_specs=pl.BlockSpec(memory_space=pl.ANY),
        scratch_shapes=[
            pltpu.VMEM((blocks * rows, rank), BF16),
            pltpu.VMEM((blocks * rows, cols), F32),
            pltpu.VMEM((blocks * rows, cols), BF16),
            pltpu.SemaphoreType.DMA((blocks // 2,)),
        ],
        out_shape=jax.ShapeDtypeStruct((blocks * rows, cols), BF16),
        compiler_params=PARAMS,
        name="finish",
    )(places, slots, core, total, expands, scale, mine, other, cosine, sine)


def ring_plan(parts, tokens, weights, scale, shrinks, expands, indices):
    rows, depth = tokens.shape
    tile = depth // 16
    me = lax.axis_index("tensor")
    owners_table = block_owners()
    send = lambda value, pairs: lax.ppermute(value, "tensor", pairs)
    swap = lambda value: send(value, [(i, i ^ 1) for i in range(parts)])
    out, home = ring_pairs((1, -1)), ring_pairs((-1, 1))

    half = depth // 2
    hs, counts = [], []

    def multiply(xs, total, ranked):
        total, h = block_product(xs, weights, factors, 0, depth, tile, total, sum(counts), ranked)
        hs.extend(h)
        counts.append(len(xs))
        return total

    streams = [send(tokens, out), None]
    own, factors = [tokens, swap(tokens)], jnp.concatenate([shrinks[0], swap(shrinks[0])], 0)
    part = 2 * tile
    total, _ = block_product(own, weights, factors, 0, part, tile, None, 0, False)
    second, total = lax.optimization_barrier((tokens, total))
    streams[1] = send(second, home)
    total, _ = block_product(own, weights, factors, part, depth, tile, total, 0, False)
    hs, total = lax.optimization_barrier(([some_ranks(tokens, factors)], total))
    counts.append(len(own))

    def make_tables(me, indices):
        segment_slot, cosine, sine = small_tables(*indices, parts * rows)
        owners = jnp.asarray(owners_table)[me]
        places = jnp.asarray(np.argsort(owners_table, axis=1).astype(np.int32))[me]
        slots = jnp.concatenate([segment_slot, jnp.stack([me, me ^ 1]).astype(jnp.int32)])
        core = (me % 2)[None].astype(jnp.int32)
        return owners, places, slots, core, segment_slot, cosine, sine

    blocks, hops = [], 2 * ROUNDS - 1
    totals = [total] * 2
    for hop in range(hops):
        arrived, _ = lax.optimization_barrier((streams[hop % 2], totals[hop if hop % 2 else hop + 1]))
        if hop + 2 < hops:
            streams[hop % 2] = send(arrived, home if hop % 2 else out)
        if hop % 2:
            late = [arrived, swap(arrived)]
            total = multiply(blocks, total, hop < hops - 2)
            unranked = blocks if hop == hops - 2 else []
            blocks = late
        else:
            blocks += [arrived, swap(arrived)]
        if hop == 1:
            known, total = lax.optimization_barrier(((me, indices), total))
            tables, total = lax.optimization_barrier((make_tables(*known), total))
        totals.append(total)
    held = sum(counts)
    owners, places, slots, core, segment_slot, cosine, sine = tables
    h = rank_terms(owners, slots, (unranked + blocks)[::2], factors, hs)
    beside = lambda step: send(h, [(i, i ^ step) for i in range(parts)])

    def last_product(low, high, total):
        xs, _ = lax.optimization_barrier((blocks, h))
        return block_product(xs, weights, factors, low, high, tile, total, held, False)[0]

    near = [beside(step) for step in (2, 4, 6)]
    near, total = lax.optimization_barrier((near, last_product(0, half, total)))
    h = h + near[0] + near[1] + near[2]
    far = [beside(step) for step in (8, 1, 9)]
    far, total = lax.optimization_barrier((far, last_product(half, depth, total)))
    mine, other = h + far[0], far[1] + far[2]
    return block_finish(places, segment_slot, core, total, expands, scale, mine, other, cosine, sine)


def body(parts, tokens, weight_codes, column_scale, shrink_store, expand_store, row_adapter, placement, document_lengths):
    rows = tokens.shape[0]
    total_rows = rows * parts
    shrinks = jnp.swapaxes(shrink_store, 1, 2)
    expands = jnp.swapaxes(expand_store, 1, 2)
    ring = parts == 2 * len(SNAKE) and rows % 16 == 0 and shrinks.shape[0] == 1 and total_rows % (2 * SEG) == 0
    plan = ring_plan if ring else gather_plan
    indices = (row_adapter, placement, document_lengths)
    return plan(parts, tokens, weight_codes, column_scale[None, :], shrinks, expands, indices)


def solution(mesh):
    placed = (
        P(("groups", "tensor"), None),
        P(None, "tensor"),
        P("tensor"),
        P(("groups", "tensor"), None, None),
        P("groups", "tensor", None),
        P("groups"),
        P("groups"),
        P("groups"),
    )
    return jax.shard_map(
        functools.partial(body, mesh.shape["tensor"]),
        mesh=mesh,
        in_specs=placed,
        out_specs=P("groups", "tensor"),
        check_vma=False,
    )
```

```python
import functools

import jax
import jax.numpy as jnp
import numpy as np
from jax import lax
from jax.experimental import pallas as pl
from jax.experimental.pallas import tpu as pltpu
from jax.sharding import PartitionSpec as P

HD = 128
SEG = 128
VMEM = 20 * 1024 * 1024
F32 = jnp.float32
BF16 = jnp.bfloat16
NT = (((1,), (1,)), ((), ()))
SLOTS = 4
CHUNK = 256
BIG_VMEM = 24 * 1024 * 1024
PARAMS = pltpu.CompilerParams(vmem_limit_bytes=VMEM)
SNAKE = (0, 2, 4, 6, 7, 5, 3, 1)
ROUNDS = len(SNAKE) // 2


def row_positions(document_lengths, total_rows):
    ends = jnp.cumsum(document_lengths)
    row_index = jnp.arange(total_rows, dtype=jnp.int32)
    passed = (row_index[:, None] >= ends[None, :]).astype(jnp.int32)
    return row_index - jnp.sum(passed * document_lengths[None, :], axis=1)


def rotary_tables(positions):
    half_size = HD // 2
    freq_index = jnp.arange(half_size, dtype=F32)
    inverse = jnp.exp(freq_index * (-2.0 / HD) * jnp.log(F32(500000.0)))
    angles = positions.astype(F32)[:, None] * inverse[None, :]
    cosine, sine = jnp.cos(angles), jnp.sin(angles)
    return jnp.concatenate([cosine, cosine], 1), jnp.concatenate([-sine, sine], 1)


def small_tables(row_adapter, placement, document_lengths, total_rows):
    segment_slot = placement[row_adapter[::SEG]]
    return segment_slot, *rotary_tables(row_positions(document_lengths, total_rows))


def rotate(value, cosine, sine):
    return value * cosine + pltpu.roll(value, HD // 2, 1) * sine


def shrink_kernel(x_ref, s_ref, h_out):
    @pl.when(pl.program_id(0) == 0)
    def _():
        h_out[...] = jnp.zeros_like(h_out)

    h_out[...] += lax.dot_general(x_ref[...], s_ref[...], NT, preferred_element_type=F32)


def shrink_all(x, shrink, tile):
    rows, depth = x.shape
    rank = shrink.shape[0]
    return pl.pallas_call(
        shrink_kernel,
        grid=(depth // tile,),
        in_specs=[
            pl.BlockSpec((rows, tile), lambda k: (0, k)),
            pl.BlockSpec((rank, tile), lambda k: (0, k)),
        ],
        out_specs=pl.BlockSpec((rows, rank), lambda k: (0, 0)),
        out_shape=jax.ShapeDtypeStruct((rows, rank), F32),
        compiler_params=PARAMS,
        name="shrink",
    )(x, shrink)


def project_kernel(x_ref, w_ref, acc_out):
    @pl.when(pl.program_id(0) == 0)
    def _():
        acc_out[...] = jnp.zeros_like(acc_out)

    acc_out[...] += jnp.dot(x_ref[...], w_ref[...], preferred_element_type=F32)


def project_all(x, weights, tile):
    rows, depth = x.shape
    cols = weights.shape[1]
    return pl.pallas_call(
        project_kernel,
        grid=(depth // tile,),
        in_specs=[
            pl.BlockSpec((rows, tile), lambda k: (0, k)),
            pl.BlockSpec((tile, cols), lambda k: (k, 0)),
        ],
        out_specs=pl.BlockSpec((rows, cols), lambda k: (0, 0)),
        out_shape=jax.ShapeDtypeStruct((rows, cols), F32),
        compiler_params=PARAMS,
        name="project",
    )(x, weights)


def segment_finish_kernel(acc_ref, scale_ref, h_ref, expand_ref, cos_ref, sin_ref, out_ref):
    update = jnp.dot(h_ref[...], expand_ref[0], preferred_element_type=F32)
    for head in range(out_ref.shape[1] // HD):
        cut = slice(head * HD, (head + 1) * HD)
        value = acc_ref[:, cut] * scale_ref[:, cut] + update[:, cut]
        out_ref[:, cut] = rotate(value, cos_ref[...], sin_ref[...]).astype(out_ref.dtype)


def segment_finish(acc, scale, h, expand, cosine, sine):
    rows, cols = acc.shape
    rank = h.shape[1]
    return pl.pallas_call(
        segment_finish_kernel,
        grid=(rows // SEG,),
        in_specs=[
            pl.BlockSpec((SEG, cols), lambda r: (r, 0)),
            pl.BlockSpec((1, cols), lambda r: (0, 0)),
            pl.BlockSpec((SEG, rank), lambda r: (r, 0)),
            pl.BlockSpec((1, rank, cols), lambda r: (r, 0, 0)),
            pl.BlockSpec((SEG, HD), lambda r: (r, 0)),
            pl.BlockSpec((SEG, HD), lambda r: (r, 0)),
        ],
        out_specs=pl.BlockSpec((SEG, cols), lambda r: (r, 0)),
        out_shape=jax.ShapeDtypeStruct((rows, cols), BF16),
        compiler_params=PARAMS,
        name="finish",
    )(acc, scale, h, expand, cosine, sine)


def spread(h, parts):
    step = 1
    while step < parts:
        h = h + lax.ppermute(h, "tensor", [(i, i ^ step) for i in range(parts)])
        step *= 2
    return h


def gather_plan(parts, tokens, weights, scale, shrinks, expands, indices):
    segment_slot, cosine, sine = small_tables(*indices, tokens.shape[0] * parts)
    held, rank, depth = shrinks.shape
    tile = depth // 16
    x = lax.all_gather(tokens, "tensor", axis=0, tiled=True)
    row_slot = jnp.repeat(segment_slot, SEG, total_repeat_length=x.shape[0])
    h = jnp.zeros((x.shape[0], rank), BF16)
    for i in range(held):
        mine = (row_slot == lax.axis_index("tensor") * held + i)[:, None]
        h = jnp.where(mine, shrink_all(x, shrinks[i], tile).astype(BF16), h)
    h = spread(h, parts)
    acc = project_all(x, weights, tile)
    return segment_finish(acc, scale, h, expands[segment_slot], cosine, sine)


def block_owners():
    chips = len(SNAKE)
    owners = np.zeros((2 * chips, 2 * chips), np.int32)
    for place, chip in enumerate(SNAKE):
        for core in (0, 1):
            row = [2 * chip + core, 2 * chip + 1 - core]
            for r in range(1, ROUNDS + 1):
                far, near = place - r * (1 - 2 * core), place + r * (1 - 2 * core)
                far, near = 2 * SNAKE[far % chips], 2 * SNAKE[near % chips]
                row += [far + core, near + 1 - core]
                if r < ROUNDS:
                    row += [near + core, far + 1 - core]
            owners[2 * chip + core] = row
    return owners


def ring_pairs(ways):
    chips = len(SNAKE)
    pairs = []
    for place, chip in enumerate(SNAKE):
        for core in (0, 1):
            pairs.append((2 * chip + core, 2 * SNAKE[(place + ways[core]) % chips] + core))
    return pairs


def block_kernel(count, low, tile, steps, first, base, fresh, ranked, *refs):
    xs, w_ref, refs = refs[:count], refs[count], refs[count + 1 :]
    if ranked:
        s_ref, refs = refs[0], refs[1:]
    if not first:
        total_in, refs = refs[0], refs[1:]
    total_out, refs = refs[0], refs[1:]
    if ranked:
        h_out, refs = refs[0], refs[1:]
    acc, before, x_slots, w_slots, s_slots, sems, total_sems = refs
    rows = xs[0].shape[0]

    def copies(step):
        slot = lax.rem(step, SLOTS)
        at = pl.multiple_of(step * tile, tile)
        sem = lambda i: sems.at[slot, i]
        out = [pltpu.make_async_copy(w_ref.at[pl.ds(low + at, tile)], w_slots.at[slot], sem(count))]
        for i in range(count):
            cut = xs[i].at[:, pl.ds(low + at, tile)]
            out.append(pltpu.make_async_copy(cut, x_slots.at[slot, pl.ds(i * rows, rows)], sem(i)))
        if ranked:
            cut = s_ref.at[:, pl.ds(low + at, tile)]
            out.append(pltpu.make_async_copy(cut, s_slots.at[slot], sem(count + 1)))
        return out

    def start(step):
        for copy in copies(step):
            copy.start()

    for step in range(min(SLOTS, steps)):
        start(jnp.int32(step))
    if not fresh:
        load = pltpu.make_async_copy(total_in.at[pl.ds(base, count)], before, total_sems.at[0])
        load.start()
    acc[...] = jnp.zeros_like(acc)
    if ranked:
        h_out[...] = jnp.zeros_like(h_out)

    @pl.loop(0, steps)
    def _(step):
        for copy in copies(step):
            copy.wait()
        slot = lax.rem(step, SLOTS)
        x = x_slots[slot]
        for left in range(0, acc.shape[2], CHUNK):
            cut = slice(left, left + CHUNK)
            product = jnp.dot(x, w_slots[slot, :, cut], preferred_element_type=F32)
            acc[:, :, cut] += product.reshape(count, rows, CHUNK)
        if ranked:
            mine = jnp.concatenate([x[i * rows : (i + 1) * rows] for i in range(0, count, 2)], 0)
            h_out[...] += lax.dot_general(mine, s_slots[slot], NT, preferred_element_type=F32)

        @pl.when(step + SLOTS < steps)
        def _():
            start(step + SLOTS)

    if not fresh:
        load.wait()
        acc[...] += before[...]
    store = pltpu.make_async_copy(acc, total_out.at[pl.ds(base, count)], total_sems.at[1])
    store.start()
    store.wait()


def block_product(xs, weights, factors, low, high, tile, total, base, ranked):
    count = len(xs)
    rows = xs[0].shape[0]
    cols = weights.shape[1]
    rank = factors.shape[0]
    fresh, first = low == 0, total is None
    anywhere, whole = pl.BlockSpec(memory_space=pl.ANY), pl.BlockSpec(memory_space=pltpu.VMEM)
    operands = list(xs) + [weights]
    specs = [anywhere] * (count + 1)
    if ranked:
        operands.append(factors)
        specs.append(anywhere)
    aliases = {}
    if not first:
        aliases = {len(operands): 0}
        operands.append(total)
        specs.append(anywhere)
    outs, out_specs = [jax.ShapeDtypeStruct(total_shape(rows, cols), F32)], [anywhere]
    if ranked:
        outs.append(jax.ShapeDtypeStruct((count // 2 * rows, rank), F32))
        out_specs.append(whole)
    steps = (high - low) // tile
    result = pl.pallas_call(
        functools.partial(block_kernel, count, low, tile, steps, first, base, fresh, ranked),
        in_specs=specs,
        out_specs=out_specs,
        out_shape=outs,
        scratch_shapes=[
            pltpu.VMEM((count, rows, cols), F32),
            pltpu.VMEM((1, 8, 128) if fresh else (count, rows, cols), F32),
            pltpu.VMEM((SLOTS, count * rows, tile), BF16),
            pltpu.VMEM((SLOTS, tile, cols), BF16),
            pltpu.VMEM((SLOTS, rank, tile), BF16),
            pltpu.SemaphoreType.DMA((SLOTS, count + 2)),
            pltpu.SemaphoreType.DMA((2,)),
        ],
        input_output_aliases=aliases,
        compiler_params=pltpu.CompilerParams(vmem_limit_bytes=BIG_VMEM),
        cost_estimate=pl.CostEstimate(
            flops=2 * count * rows * (high - low) * cols,
            bytes_accessed=2 * (high - low) * cols,
            transcendentals=0,
        ),
        name="blocks",
    )(*operands)
    return result[0], result[1:]


def total_shape(rows, cols):
    return (2 * len(SNAKE), rows, cols)


def some_ranks_kernel(x_ref, s_ref, out_ref):
    out_ref[...] = lax.dot_general(x_ref[...], s_ref[...], NT, preferred_element_type=F32)


def some_ranks(x, factors):
    whole = pl.BlockSpec(memory_space=pltpu.VMEM)
    return pl.pallas_call(
        some_ranks_kernel,
        in_specs=[whole] * 2,
        out_specs=whole,
        out_shape=jax.ShapeDtypeStruct((x.shape[0], factors.shape[0]), F32),
        compiler_params=PARAMS,
        name="some_ranks",
    )(x, factors)


def rank_kernel(count, owners_ref, slot_ref, *refs):
    xs, refs = refs[:count], refs[count:]
    s_ref, h_refs, out_ref, placed = refs[0], refs[1:-2], refs[-2], refs[-1]
    rows, rank = xs[0].shape[0], s_ref.shape[0] // 2
    x = jnp.concatenate([ref[...] for ref in xs], 0)
    last = lax.dot_general(x, s_ref[...], NT, preferred_element_type=F32)
    segments = slot_ref.shape[0] - 2
    block = 0
    for source in h_refs + (last,):
        for low in range(0, source.shape[0], rows):
            owner = owners_ref[2 * block]
            segment = owner * rows // SEG
            after = jnp.minimum(segment + 1, segments - 1)
            row = owner * rows + lax.broadcasted_iota(jnp.int32, (rows, rank), 0)
            slot = jnp.where(row < (segment + 1) * SEG, slot_ref[segment], slot_ref[after])
            terms = jnp.where(slot == slot_ref[segments + 1], source[low : low + rows, rank:], 0.0)
            terms = jnp.where(slot == slot_ref[segments], source[low : low + rows, :rank], terms)
            placed[pl.ds(pl.multiple_of(owner // 2 * rows, 16), rows), :] = terms
            block += 1
    half = placed.shape[0] // 2
    out_ref[...] = jnp.concatenate([placed[:half, :], placed[half:, :]], 1).astype(out_ref.dtype)


def rank_terms(owners, slots, xs, factors, hs):
    rank = factors.shape[0] // 2
    core_rows = owners.shape[0] // 2 * xs[0].shape[0]
    scalars, whole = pl.BlockSpec(memory_space=pltpu.SMEM), pl.BlockSpec(memory_space=pltpu.VMEM)
    return pl.pallas_call(
        functools.partial(rank_kernel, len(xs)),
        in_specs=[scalars] * 2 + [whole] * (len(xs) + 1 + len(hs)),
        out_specs=whole,
        scratch_shapes=[pltpu.VMEM((core_rows, rank), F32)],
        out_shape=jax.ShapeDtypeStruct((core_rows // 2, 2 * rank), BF16),
        compiler_params=PARAMS,
        name="ranks",
    )(owners, slots, *xs, factors, *hs)


def block_finish_kernel(places_ref, slot_ref, core_ref, total_ref, expand_ref, scale_ref, mine_ref, other_ref, *refs):
    cos_ref, sin_ref, out_ref, h, update, done, sems = refs
    blocks, rows, cols = total_ref.shape
    rank = mine_ref.shape[1] // 2
    even = core_ref[0] == 0
    mine, other = mine_ref[...], other_ref[...]
    for core, terms in enumerate((jnp.where(even, mine, other), jnp.where(even, other, mine))):
        for chip in range(blocks // 2):
            side, at = divmod(chip * rows, terms.shape[0])
            to = (2 * chip + core) * rows
            h[to : to + rows, :] = terms[at : at + rows, side * rank : (side + 1) * rank]
    for segment in range(h.shape[0] // SEG):
        cut = slice(segment * SEG, (segment + 1) * SEG)
        expand = expand_ref[slot_ref[segment]]
        update[cut, :] = jnp.dot(h[cut, :], expand, preferred_element_type=F32)
    copies = []
    for block in range(blocks):
        at = slice(block * rows, (block + 1) * rows)
        cosine, sine = cos_ref[at, :], sin_ref[at, :]
        place = places_ref[block]
        for left in range(0, cols, HD):
            cut = slice(left, left + HD)
            value = total_ref[place, :, cut] * scale_ref[:, cut] + update[at, cut]
            done[at, cut] = rotate(value, cosine, sine).astype(done.dtype)
        if block % 2:
            strip = pl.ds((block - 1) * rows, 2 * rows)
            copies.append(pltpu.make_async_copy(done.at[strip], out_ref.at[strip], sems.at[block // 2]))
            copies[-1].start()
    for copy in copies:
        copy.wait()


def block_finish(places, slots, core, total, expands, scale, mine, other, cosine, sine):
    blocks, rows, cols = total.shape
    rank = expands.shape[1]
    scalars, whole = pl.BlockSpec(memory_space=pltpu.SMEM), pl.BlockSpec(memory_space=pltpu.VMEM)
    return pl.pallas_call(
        block_finish_kernel,
        in_specs=[scalars] * 3 + [whole] * 7,
        out_specs=pl.BlockSpec(memory_space=pl.ANY),
        scratch_shapes=[
            pltpu.VMEM((blocks * rows, rank), BF16),
            pltpu.VMEM((blocks * rows, cols), F32),
            pltpu.VMEM((blocks * rows, cols), BF16),
            pltpu.SemaphoreType.DMA((blocks // 2,)),
        ],
        out_shape=jax.ShapeDtypeStruct((blocks * rows, cols), BF16),
        compiler_params=PARAMS,
        name="finish",
    )(places, slots, core, total, expands, scale, mine, other, cosine, sine)


def ring_plan(parts, tokens, weights, scale, shrinks, expands, indices):
    rows, depth = tokens.shape
    tile = depth // 16
    me = lax.axis_index("tensor")
    owners_table = block_owners()
    send = lambda value, pairs: lax.ppermute(value, "tensor", pairs)
    swap = lambda value: send(value, [(i, i ^ 1) for i in range(parts)])
    out, home = ring_pairs((1, -1)), ring_pairs((-1, 1))

    half = depth // 2
    hs, counts = [], []

    def multiply(xs, total, ranked):
        total, h = block_product(xs, weights, factors, 0, depth, tile, total, sum(counts), ranked)
        hs.extend(h)
        counts.append(len(xs))
        return total

    streams = [send(tokens, out), None]
    own, factors = [tokens, swap(tokens)], jnp.concatenate([shrinks[0], swap(shrinks[0])], 0)
    part = 2 * tile
    total, _ = block_product(own, weights, factors, 0, part, tile, None, 0, False)
    second, total = lax.optimization_barrier((tokens, total))
    streams[1] = send(second, home)
    total, _ = block_product(own, weights, factors, part, depth, tile, total, 0, False)
    hs, total = lax.optimization_barrier(([some_ranks(tokens, factors)], total))
    counts.append(len(own))

    def make_tables(me, indices):
        segment_slot, cosine, sine = small_tables(*indices, parts * rows)
        owners = jnp.asarray(owners_table)[me]
        places = jnp.asarray(np.argsort(owners_table, axis=1).astype(np.int32))[me]
        slots = jnp.concatenate([segment_slot, jnp.stack([me, me ^ 1]).astype(jnp.int32)])
        core = (me % 2)[None].astype(jnp.int32)
        return owners, places, slots, core, segment_slot, cosine, sine

    blocks, hops = [], 2 * ROUNDS - 1
    totals = [total] * 2
    for hop in range(hops):
        arrived, _ = lax.optimization_barrier((streams[hop % 2], totals[hop if hop % 2 else hop + 1]))
        if hop + 2 < hops:
            streams[hop % 2] = send(arrived, home if hop % 2 else out)
        if hop % 2:
            late = [arrived, swap(arrived)]
            total = multiply(blocks, total, hop < hops - 2)
            blocks = late
        else:
            blocks += [arrived, swap(arrived)]
        if hop == hops - 3:
            early = [some_ranks(part, factors) for part in blocks[::2]]
            early, total = lax.optimization_barrier((early, total))
        if hop == hops - 2:
            hs += early
            last, _ = lax.optimization_barrier((arrived, total))
            hs.append(some_ranks(last, factors))
            hs, total = lax.optimization_barrier((hs, total))
        if hop == 1:
            known, total = lax.optimization_barrier(((me, indices), total))
            tables, total = lax.optimization_barrier((make_tables(*known), total))
        totals.append(total)
    held = sum(counts)
    owners, places, slots, core, segment_slot, cosine, sine = tables
    h = rank_terms(owners, slots, blocks[2:3], factors, hs)
    beside = lambda step: send(h, [(i, i ^ step) for i in range(parts)])

    def last_product(low, high, total):
        xs, _ = lax.optimization_barrier((blocks, h))
        return block_product(xs, weights, factors, low, high, tile, total, held, False)[0]

    near = [beside(step) for step in (2, 4, 6)]
    near, total = lax.optimization_barrier((near, last_product(0, half, total)))
    h = h + near[0] + near[1] + near[2]
    far = [beside(step) for step in (8, 1, 9)]
    far, total = lax.optimization_barrier((far, last_product(half, depth, total)))
    mine, other = h + far[0], far[1] + far[2]
    return block_finish(places, segment_slot, core, total, expands, scale, mine, other, cosine, sine)


def body(parts, tokens, weight_codes, column_scale, shrink_store, expand_store, row_adapter, placement, document_lengths):
    rows = tokens.shape[0]
    total_rows = rows * parts
    shrinks = jnp.swapaxes(shrink_store, 1, 2)
    expands = jnp.swapaxes(expand_store, 1, 2)
    ring = parts == 2 * len(SNAKE) and rows % 16 == 0 and shrinks.shape[0] == 1 and total_rows % (2 * SEG) == 0
    plan = ring_plan if ring else gather_plan
    indices = (row_adapter, placement, document_lengths)
    return plan(parts, tokens, weight_codes, column_scale[None, :], shrinks, expands, indices)


def solution(mesh):
    placed = (
        P(("groups", "tensor"), None),
        P(None, "tensor"),
        P("tensor"),
        P(("groups", "tensor"), None, None),
        P("groups", "tensor", None),
        P("groups"),
        P("groups"),
        P("groups"),
    )
    return jax.shard_map(
        functools.partial(body, mesh.shape["tensor"]),
        mesh=mesh,
        in_specs=placed,
        out_specs=P("groups", "tensor"),
        check_vma=False,
    )
```

```python
import functools

import jax
import jax.numpy as jnp
import numpy as np
from jax import lax
from jax.experimental import pallas as pl
from jax.experimental.pallas import tpu as pltpu
from jax.sharding import PartitionSpec as P

HD = 128
SEG = 128
VMEM = 20 * 1024 * 1024
F32 = jnp.float32
BF16 = jnp.bfloat16
NT = (((1,), (1,)), ((), ()))
SLOTS = 4
CHUNK = 256
BIG_VMEM = 24 * 1024 * 1024
PARAMS = pltpu.CompilerParams(vmem_limit_bytes=VMEM)
SNAKE = (0, 2, 4, 6, 7, 5, 3, 1)
ROUNDS = len(SNAKE) // 2


def row_positions(document_lengths, total_rows):
    ends = jnp.cumsum(document_lengths)
    row_index = jnp.arange(total_rows, dtype=jnp.int32)
    passed = (row_index[:, None] >= ends[None, :]).astype(jnp.int32)
    return row_index - jnp.sum(passed * document_lengths[None, :], axis=1)


def rotary_tables(positions):
    half_size = HD // 2
    freq_index = jnp.arange(half_size, dtype=F32)
    inverse = jnp.exp(freq_index * (-2.0 / HD) * jnp.log(F32(500000.0)))
    angles = positions.astype(F32)[:, None] * inverse[None, :]
    cosine, sine = jnp.cos(angles), jnp.sin(angles)
    return jnp.concatenate([cosine, cosine], 1), jnp.concatenate([-sine, sine], 1)


def small_tables(row_adapter, placement, document_lengths, total_rows):
    segment_slot = placement[row_adapter[::SEG]]
    return segment_slot, *rotary_tables(row_positions(document_lengths, total_rows))


def rotate(value, cosine, sine):
    return value * cosine + pltpu.roll(value, HD // 2, 1) * sine


def shrink_kernel(x_ref, s_ref, h_out):
    @pl.when(pl.program_id(0) == 0)
    def _():
        h_out[...] = jnp.zeros_like(h_out)

    h_out[...] += lax.dot_general(x_ref[...], s_ref[...], NT, preferred_element_type=F32)


def shrink_all(x, shrink, tile):
    rows, depth = x.shape
    rank = shrink.shape[0]
    return pl.pallas_call(
        shrink_kernel,
        grid=(depth // tile,),
        in_specs=[
            pl.BlockSpec((rows, tile), lambda k: (0, k)),
            pl.BlockSpec((rank, tile), lambda k: (0, k)),
        ],
        out_specs=pl.BlockSpec((rows, rank), lambda k: (0, 0)),
        out_shape=jax.ShapeDtypeStruct((rows, rank), F32),
        compiler_params=PARAMS,
        name="shrink",
    )(x, shrink)


def project_kernel(x_ref, w_ref, acc_out):
    @pl.when(pl.program_id(0) == 0)
    def _():
        acc_out[...] = jnp.zeros_like(acc_out)

    acc_out[...] += jnp.dot(x_ref[...], w_ref[...], preferred_element_type=F32)


def project_all(x, weights, tile):
    rows, depth = x.shape
    cols = weights.shape[1]
    return pl.pallas_call(
        project_kernel,
        grid=(depth // tile,),
        in_specs=[
            pl.BlockSpec((rows, tile), lambda k: (0, k)),
            pl.BlockSpec((tile, cols), lambda k: (k, 0)),
        ],
        out_specs=pl.BlockSpec((rows, cols), lambda k: (0, 0)),
        out_shape=jax.ShapeDtypeStruct((rows, cols), F32),
        compiler_params=PARAMS,
        name="project",
    )(x, weights)


def segment_finish_kernel(acc_ref, scale_ref, h_ref, expand_ref, cos_ref, sin_ref, out_ref):
    update = jnp.dot(h_ref[...], expand_ref[0], preferred_element_type=F32)
    for head in range(out_ref.shape[1] // HD):
        cut = slice(head * HD, (head + 1) * HD)
        value = acc_ref[:, cut] * scale_ref[:, cut] + update[:, cut]
        out_ref[:, cut] = rotate(value, cos_ref[...], sin_ref[...]).astype(out_ref.dtype)


def segment_finish(acc, scale, h, expand, cosine, sine):
    rows, cols = acc.shape
    rank = h.shape[1]
    return pl.pallas_call(
        segment_finish_kernel,
        grid=(rows // SEG,),
        in_specs=[
            pl.BlockSpec((SEG, cols), lambda r: (r, 0)),
            pl.BlockSpec((1, cols), lambda r: (0, 0)),
            pl.BlockSpec((SEG, rank), lambda r: (r, 0)),
            pl.BlockSpec((1, rank, cols), lambda r: (r, 0, 0)),
            pl.BlockSpec((SEG, HD), lambda r: (r, 0)),
            pl.BlockSpec((SEG, HD), lambda r: (r, 0)),
        ],
        out_specs=pl.BlockSpec((SEG, cols), lambda r: (r, 0)),
        out_shape=jax.ShapeDtypeStruct((rows, cols), BF16),
        compiler_params=PARAMS,
        name="finish",
    )(acc, scale, h, expand, cosine, sine)


def spread(h, parts):
    step = 1
    while step < parts:
        h = h + lax.ppermute(h, "tensor", [(i, i ^ step) for i in range(parts)])
        step *= 2
    return h


def gather_plan(parts, tokens, weights, scale, shrinks, expands, indices):
    segment_slot, cosine, sine = small_tables(*indices, tokens.shape[0] * parts)
    held, rank, depth = shrinks.shape
    tile = depth // 16
    x = lax.all_gather(tokens, "tensor", axis=0, tiled=True)
    row_slot = jnp.repeat(segment_slot, SEG, total_repeat_length=x.shape[0])
    h = jnp.zeros((x.shape[0], rank), BF16)
    for i in range(held):
        mine = (row_slot == lax.axis_index("tensor") * held + i)[:, None]
        h = jnp.where(mine, shrink_all(x, shrinks[i], tile).astype(BF16), h)
    h = spread(h, parts)
    acc = project_all(x, weights, tile)
    return segment_finish(acc, scale, h, expands[segment_slot], cosine, sine)


def block_owners():
    chips = len(SNAKE)
    owners = np.zeros((2 * chips, 2 * chips), np.int32)
    for place, chip in enumerate(SNAKE):
        for core in (0, 1):
            row = [2 * chip + core, 2 * chip + 1 - core]
            for r in range(1, ROUNDS + 1):
                far, near = place - r * (1 - 2 * core), place + r * (1 - 2 * core)
                far, near = 2 * SNAKE[far % chips], 2 * SNAKE[near % chips]
                row += [far + core, near + 1 - core]
                if r < ROUNDS:
                    row += [near + core, far + 1 - core]
            owners[2 * chip + core] = row
    return owners


def ring_pairs(ways):
    chips = len(SNAKE)
    pairs = []
    for place, chip in enumerate(SNAKE):
        for core in (0, 1):
            pairs.append((2 * chip + core, 2 * SNAKE[(place + ways[core]) % chips] + core))
    return pairs


def block_kernel(count, low, tile, steps, first, base, fresh, ranked, *refs):
    xs, w_ref, refs = refs[:count], refs[count], refs[count + 1 :]
    if ranked:
        s_ref, refs = refs[0], refs[1:]
    if not first:
        total_in, refs = refs[0], refs[1:]
    total_out, refs = refs[0], refs[1:]
    if ranked:
        h_out, refs = refs[0], refs[1:]
    acc, before, x_slots, w_slots, s_slots, sems, total_sems = refs
    rows = xs[0].shape[0]

    def copies(step):
        slot = lax.rem(step, SLOTS)
        at = pl.multiple_of(step * tile, tile)
        sem = lambda i: sems.at[slot, i]
        out = [pltpu.make_async_copy(w_ref.at[pl.ds(low + at, tile)], w_slots.at[slot], sem(count))]
        for i in range(count):
            cut = xs[i].at[:, pl.ds(low + at, tile)]
            out.append(pltpu.make_async_copy(cut, x_slots.at[slot, pl.ds(i * rows, rows)], sem(i)))
        if ranked:
            cut = s_ref.at[pl.ds(low + at, tile)]
            out.append(pltpu.make_async_copy(cut, s_slots.at[slot], sem(count + 1)))
        return out

    def start(step):
        for copy in copies(step):
            copy.start()

    for step in range(min(SLOTS, steps)):
        start(jnp.int32(step))
    if not fresh:
        load = pltpu.make_async_copy(total_in.at[pl.ds(base, count)], before, total_sems.at[0])
        load.start()
    acc[...] = jnp.zeros_like(acc)
    if ranked:
        h_out[...] = jnp.zeros_like(h_out)

    @pl.loop(0, steps)
    def _(step):
        for copy in copies(step):
            copy.wait()
        slot = lax.rem(step, SLOTS)
        x = x_slots[slot]
        for left in range(0, acc.shape[2], CHUNK):
            cut = slice(left, left + CHUNK)
            product = jnp.dot(x, w_slots[slot, :, cut], preferred_element_type=F32)
            acc[:, :, cut] += product.reshape(count, rows, CHUNK)
        if ranked:
            mine = jnp.concatenate([x[i * rows : (i + 1) * rows] for i in range(0, count, 2)], 0)
            h_out[...] += jnp.dot(mine, s_slots[slot], preferred_element_type=F32)

        @pl.when(step + SLOTS < steps)
        def _():
            start(step + SLOTS)

    if not fresh:
        load.wait()
        acc[...] += before[...]
    store = pltpu.make_async_copy(acc, total_out.at[pl.ds(base, count)], total_sems.at[1])
    store.start()
    store.wait()


def block_product(xs, weights, factors, low, high, tile, total, base, ranked):
    count = len(xs)
    rows = xs[0].shape[0]
    cols = weights.shape[1]
    rank = factors.shape[1]
    fresh, first = low == 0, total is None
    anywhere, whole = pl.BlockSpec(memory_space=pl.ANY), pl.BlockSpec(memory_space=pltpu.VMEM)
    operands = list(xs) + [weights]
    specs = [anywhere] * (count + 1)
    if ranked:
        operands.append(factors)
        specs.append(anywhere)
    aliases = {}
    if not first:
        aliases = {len(operands): 0}
        operands.append(total)
        specs.append(anywhere)
    outs, out_specs = [jax.ShapeDtypeStruct(total_shape(rows, cols), F32)], [anywhere]
    if ranked:
        outs.append(jax.ShapeDtypeStruct((count // 2 * rows, rank), F32))
        out_specs.append(whole)
    steps = (high - low) // tile
    result = pl.pallas_call(
        functools.partial(block_kernel, count, low, tile, steps, first, base, fresh, ranked),
        in_specs=specs,
        out_specs=out_specs,
        out_shape=outs,
        scratch_shapes=[
            pltpu.VMEM((count, rows, cols), F32),
            pltpu.VMEM((1, 8, 128) if fresh else (count, rows, cols), F32),
            pltpu.VMEM((SLOTS, count * rows, tile), BF16),
            pltpu.VMEM((SLOTS, tile, cols), BF16),
            pltpu.VMEM((SLOTS, tile, rank), BF16),
            pltpu.SemaphoreType.DMA((SLOTS, count + 2)),
            pltpu.SemaphoreType.DMA((2,)),
        ],
        input_output_aliases=aliases,
        compiler_params=pltpu.CompilerParams(vmem_limit_bytes=BIG_VMEM),
        cost_estimate=pl.CostEstimate(
            flops=2 * count * rows * (high - low) * cols,
            bytes_accessed=2 * (high - low) * cols,
            transcendentals=0,
        ),
        name="blocks",
    )(*operands)
    return result[0], result[1:]


def total_shape(rows, cols):
    return (2 * len(SNAKE), rows, cols)


def some_ranks_kernel(x_ref, s_ref, out_ref):
    out_ref[...] = jnp.dot(x_ref[...], s_ref[...], preferred_element_type=F32)


def some_ranks(x, factors):
    whole = pl.BlockSpec(memory_space=pltpu.VMEM)
    return pl.pallas_call(
        some_ranks_kernel,
        in_specs=[whole] * 2,
        out_specs=whole,
        out_shape=jax.ShapeDtypeStruct((x.shape[0], factors.shape[1]), F32),
        compiler_params=PARAMS,
        name="some_ranks",
    )(x, factors)


def rank_kernel(count, owners_ref, slot_ref, *refs):
    xs, refs = refs[:count], refs[count:]
    s_ref, h_refs, out_ref, placed = refs[0], refs[1:-2], refs[-2], refs[-1]
    rows, rank = xs[0].shape[0], s_ref.shape[1] // 2
    x = jnp.concatenate([ref[...] for ref in xs], 0)
    last = jnp.dot(x, s_ref[...], preferred_element_type=F32)
    segments = slot_ref.shape[0] - 2
    block = 0
    for source in h_refs + (last,):
        for low in range(0, source.shape[0], rows):
            owner = owners_ref[2 * block]
            segment = owner * rows // SEG
            after = jnp.minimum(segment + 1, segments - 1)
            row = owner * rows + lax.broadcasted_iota(jnp.int32, (rows, rank), 0)
            slot = jnp.where(row < (segment + 1) * SEG, slot_ref[segment], slot_ref[after])
            terms = jnp.where(slot == slot_ref[segments + 1], source[low : low + rows, rank:], 0.0)
            terms = jnp.where(slot == slot_ref[segments], source[low : low + rows, :rank], terms)
            placed[pl.ds(pl.multiple_of(owner // 2 * rows, 16), rows), :] = terms
            block += 1
    half = placed.shape[0] // 2
    out_ref[...] = jnp.concatenate([placed[:half, :], placed[half:, :]], 1).astype(out_ref.dtype)


def rank_terms(owners, slots, xs, factors, hs):
    rank = factors.shape[1] // 2
    core_rows = owners.shape[0] // 2 * xs[0].shape[0]
    scalars, whole = pl.BlockSpec(memory_space=pltpu.SMEM), pl.BlockSpec(memory_space=pltpu.VMEM)
    return pl.pallas_call(
        functools.partial(rank_kernel, len(xs)),
        in_specs=[scalars] * 2 + [whole] * (len(xs) + 1 + len(hs)),
        out_specs=whole,
        scratch_shapes=[pltpu.VMEM((core_rows, rank), F32)],
        out_shape=jax.ShapeDtypeStruct((core_rows // 2, 2 * rank), BF16),
        compiler_params=PARAMS,
        name="ranks",
    )(owners, slots, *xs, factors, *hs)


def block_finish_kernel(places_ref, slot_ref, core_ref, total_ref, expand_ref, scale_ref, mine_ref, other_ref, *refs):
    cos_ref, sin_ref, out_ref, h, update, done, sems = refs
    blocks, rows, cols = total_ref.shape
    rank = mine_ref.shape[1] // 2
    even = core_ref[0] == 0
    mine, other = mine_ref[...], other_ref[...]
    for core, terms in enumerate((jnp.where(even, mine, other), jnp.where(even, other, mine))):
        for chip in range(blocks // 2):
            side, at = divmod(chip * rows, terms.shape[0])
            to = (2 * chip + core) * rows
            h[to : to + rows, :] = terms[at : at + rows, side * rank : (side + 1) * rank]
    for segment in range(h.shape[0] // SEG):
        cut = slice(segment * SEG, (segment + 1) * SEG)
        expand = expand_ref[slot_ref[segment]]
        update[cut, :] = jnp.dot(h[cut, :], expand, preferred_element_type=F32)
    copies = []
    for block in range(blocks):
        at = slice(block * rows, (block + 1) * rows)
        cosine, sine = cos_ref[at, :], sin_ref[at, :]
        place = places_ref[block]
        for left in range(0, cols, HD):
            cut = slice(left, left + HD)
            value = total_ref[place, :, cut] * scale_ref[:, cut] + update[at, cut]
            done[at, cut] = rotate(value, cosine, sine).astype(done.dtype)
        if block % 2:
            strip = pl.ds((block - 1) * rows, 2 * rows)
            copies.append(pltpu.make_async_copy(done.at[strip], out_ref.at[strip], sems.at[block // 2]))
            copies[-1].start()
    for copy in copies:
        copy.wait()


def block_finish(places, slots, core, total, expands, scale, mine, other, cosine, sine):
    blocks, rows, cols = total.shape
    rank = expands.shape[1]
    scalars, whole = pl.BlockSpec(memory_space=pltpu.SMEM), pl.BlockSpec(memory_space=pltpu.VMEM)
    return pl.pallas_call(
        block_finish_kernel,
        in_specs=[scalars] * 3 + [whole] * 7,
        out_specs=pl.BlockSpec(memory_space=pl.ANY),
        scratch_shapes=[
            pltpu.VMEM((blocks * rows, rank), BF16),
            pltpu.VMEM((blocks * rows, cols), F32),
            pltpu.VMEM((blocks * rows, cols), BF16),
            pltpu.SemaphoreType.DMA((blocks // 2,)),
        ],
        out_shape=jax.ShapeDtypeStruct((blocks * rows, cols), BF16),
        compiler_params=PARAMS,
        name="finish",
    )(places, slots, core, total, expands, scale, mine, other, cosine, sine)


def ring_plan(parts, tokens, weights, scale, shrinks, expands, indices):
    rows, depth = tokens.shape
    tile = depth // 16
    me = lax.axis_index("tensor")
    owners_table = block_owners()
    send = lambda value, pairs: lax.ppermute(value, "tensor", pairs)
    swap = lambda value: send(value, [(i, i ^ 1) for i in range(parts)])
    out, home = ring_pairs((1, -1)), ring_pairs((-1, 1))

    half = depth // 2
    hs, counts = [], []

    def multiply(xs, total, ranked):
        total, h = block_product(xs, weights, factors, 0, depth, tile, total, sum(counts), ranked)
        hs.extend(h)
        counts.append(len(xs))
        return total

    streams = [send(tokens, out), None]
    own, factors = [tokens, swap(tokens)], jnp.concatenate([shrinks[0], swap(shrinks[0])], 0).T
    part = 2 * tile
    total, _ = block_product(own, weights, factors, 0, part, tile, None, 0, False)
    second, total = lax.optimization_barrier((tokens, total))
    streams[1] = send(second, home)
    total, _ = block_product(own, weights, factors, part, depth, tile, total, 0, False)
    hs, total = lax.optimization_barrier(([some_ranks(tokens, factors)], total))
    counts.append(len(own))

    def make_tables(me, indices):
        segment_slot, cosine, sine = small_tables(*indices, parts * rows)
        owners = jnp.asarray(owners_table)[me]
        places = jnp.asarray(np.argsort(owners_table, axis=1).astype(np.int32))[me]
        slots = jnp.concatenate([segment_slot, jnp.stack([me, me ^ 1]).astype(jnp.int32)])
        core = (me % 2)[None].astype(jnp.int32)
        return owners, places, slots, core, segment_slot, cosine, sine

    blocks, hops = [], 2 * ROUNDS - 1
    totals = [total] * 2
    for hop in range(hops):
        arrived, _ = lax.optimization_barrier((streams[hop % 2], totals[hop if hop % 2 else hop + 1]))
        if hop + 2 < hops:
            streams[hop % 2] = send(arrived, home if hop % 2 else out)
        if hop % 2:
            late = [arrived, swap(arrived)]
            total = multiply(blocks, total, hop < hops - 2)
            blocks = late
        else:
            blocks += [arrived, swap(arrived)]
        if hop == hops - 3:
            early = [some_ranks(part, factors) for part in blocks[::2]]
            early, total = lax.optimization_barrier((early, total))
        if hop == hops - 2:
            hs += early
            last, _ = lax.optimization_barrier((arrived, total))
            hs.append(some_ranks(last, factors))
            hs, total = lax.optimization_barrier((hs, total))
        if hop == 1:
            known, total = lax.optimization_barrier(((me, indices), total))
            tables, total = lax.optimization_barrier((make_tables(*known), total))
        totals.append(total)
    held = sum(counts)
    owners, places, slots, core, segment_slot, cosine, sine = tables
    h = rank_terms(owners, slots, blocks[2:3], factors, hs)
    beside = lambda step: send(h, [(i, i ^ step) for i in range(parts)])

    def last_product(low, high, total):
        xs, _ = lax.optimization_barrier((blocks, h))
        return block_product(xs, weights, factors, low, high, tile, total, held, False)[0]

    near = [beside(step) for step in (2, 4, 6)]
    near, total = lax.optimization_barrier((near, last_product(0, half, total)))
    h = h + near[0] + near[1] + near[2]
    far = [beside(step) for step in (8, 1, 9)]
    far, total = lax.optimization_barrier((far, last_product(half, depth, total)))
    mine, other = h + far[0], far[1] + far[2]
    return block_finish(places, segment_slot, core, total, expands, scale, mine, other, cosine, sine)


def body(parts, tokens, weight_codes, column_scale, shrink_store, expand_store, row_adapter, placement, document_lengths):
    rows = tokens.shape[0]
    total_rows = rows * parts
    shrinks = jnp.swapaxes(shrink_store, 1, 2)
    expands = jnp.swapaxes(expand_store, 1, 2)
    ring = parts == 2 * len(SNAKE) and rows % 16 == 0 and shrinks.shape[0] == 1 and total_rows % (2 * SEG) == 0
    plan = ring_plan if ring else gather_plan
    indices = (row_adapter, placement, document_lengths)
    return plan(parts, tokens, weight_codes, column_scale[None, :], shrinks, expands, indices)


def solution(mesh):
    placed = (
        P(("groups", "tensor"), None),
        P(None, "tensor"),
        P("tensor"),
        P(("groups", "tensor"), None, None),
        P("groups", "tensor", None),
        P("groups"),
        P("groups"),
        P("groups"),
    )
    return jax.shard_map(
        functools.partial(body, mesh.shape["tensor"]),
        mesh=mesh,
        in_specs=placed,
        out_specs=P("groups", "tensor"),
        check_vma=False,
    )
```

```python
import functools

import jax
import jax.numpy as jnp
import numpy as np
from jax import lax
from jax.experimental import pallas as pl
from jax.experimental.pallas import tpu as pltpu
from jax.sharding import PartitionSpec as P

HD = 128
SEG = 128
VMEM = 20 * 1024 * 1024
F32 = jnp.float32
BF16 = jnp.bfloat16
NT = (((1,), (1,)), ((), ()))
SLOTS = 4
CHUNK = 256
BIG_VMEM = 24 * 1024 * 1024
PARAMS = pltpu.CompilerParams(vmem_limit_bytes=VMEM)
SNAKE = (0, 2, 4, 6, 7, 5, 3, 1)
ROUNDS = len(SNAKE) // 2


def row_positions(document_lengths, total_rows):
    ends = jnp.cumsum(document_lengths)
    row_index = jnp.arange(total_rows, dtype=jnp.int32)
    passed = (row_index[:, None] >= ends[None, :]).astype(jnp.int32)
    return row_index - jnp.sum(passed * document_lengths[None, :], axis=1)


def rotary_tables(positions):
    half_size = HD // 2
    freq_index = jnp.arange(half_size, dtype=F32)
    inverse = jnp.exp(freq_index * (-2.0 / HD) * jnp.log(F32(500000.0)))
    angles = positions.astype(F32)[:, None] * inverse[None, :]
    cosine, sine = jnp.cos(angles), jnp.sin(angles)
    return jnp.concatenate([cosine, cosine], 1), jnp.concatenate([-sine, sine], 1)


def small_tables(row_adapter, placement, document_lengths, total_rows):
    segment_slot = placement[row_adapter[::SEG]]
    return segment_slot, *rotary_tables(row_positions(document_lengths, total_rows))


def rotate(value, cosine, sine):
    return value * cosine + pltpu.roll(value, HD // 2, 1) * sine


def shrink_kernel(x_ref, s_ref, h_out):
    @pl.when(pl.program_id(0) == 0)
    def _():
        h_out[...] = jnp.zeros_like(h_out)

    h_out[...] += lax.dot_general(x_ref[...], s_ref[...], NT, preferred_element_type=F32)


def shrink_all(x, shrink, tile):
    rows, depth = x.shape
    rank = shrink.shape[0]
    return pl.pallas_call(
        shrink_kernel,
        grid=(depth // tile,),
        in_specs=[
            pl.BlockSpec((rows, tile), lambda k: (0, k)),
            pl.BlockSpec((rank, tile), lambda k: (0, k)),
        ],
        out_specs=pl.BlockSpec((rows, rank), lambda k: (0, 0)),
        out_shape=jax.ShapeDtypeStruct((rows, rank), F32),
        compiler_params=PARAMS,
        name="shrink",
    )(x, shrink)


def project_kernel(x_ref, w_ref, acc_out):
    @pl.when(pl.program_id(0) == 0)
    def _():
        acc_out[...] = jnp.zeros_like(acc_out)

    acc_out[...] += jnp.dot(x_ref[...], w_ref[...], preferred_element_type=F32)


def project_all(x, weights, tile):
    rows, depth = x.shape
    cols = weights.shape[1]
    return pl.pallas_call(
        project_kernel,
        grid=(depth // tile,),
        in_specs=[
            pl.BlockSpec((rows, tile), lambda k: (0, k)),
            pl.BlockSpec((tile, cols), lambda k: (k, 0)),
        ],
        out_specs=pl.BlockSpec((rows, cols), lambda k: (0, 0)),
        out_shape=jax.ShapeDtypeStruct((rows, cols), F32),
        compiler_params=PARAMS,
        name="project",
    )(x, weights)


def segment_finish_kernel(acc_ref, scale_ref, h_ref, expand_ref, cos_ref, sin_ref, out_ref):
    update = jnp.dot(h_ref[...], expand_ref[0], preferred_element_type=F32)
    for head in range(out_ref.shape[1] // HD):
        cut = slice(head * HD, (head + 1) * HD)
        value = acc_ref[:, cut] * scale_ref[:, cut] + update[:, cut]
        out_ref[:, cut] = rotate(value, cos_ref[...], sin_ref[...]).astype(out_ref.dtype)


def segment_finish(acc, scale, h, expand, cosine, sine):
    rows, cols = acc.shape
    rank = h.shape[1]
    return pl.pallas_call(
        segment_finish_kernel,
        grid=(rows // SEG,),
        in_specs=[
            pl.BlockSpec((SEG, cols), lambda r: (r, 0)),
            pl.BlockSpec((1, cols), lambda r: (0, 0)),
            pl.BlockSpec((SEG, rank), lambda r: (r, 0)),
            pl.BlockSpec((1, rank, cols), lambda r: (r, 0, 0)),
            pl.BlockSpec((SEG, HD), lambda r: (r, 0)),
            pl.BlockSpec((SEG, HD), lambda r: (r, 0)),
        ],
        out_specs=pl.BlockSpec((SEG, cols), lambda r: (r, 0)),
        out_shape=jax.ShapeDtypeStruct((rows, cols), BF16),
        compiler_params=PARAMS,
        name="finish",
    )(acc, scale, h, expand, cosine, sine)


def spread(h, parts):
    step = 1
    while step < parts:
        h = h + lax.ppermute(h, "tensor", [(i, i ^ step) for i in range(parts)])
        step *= 2
    return h


def gather_plan(parts, tokens, weights, scale, shrinks, expands, indices):
    segment_slot, cosine, sine = small_tables(*indices, tokens.shape[0] * parts)
    held, rank, depth = shrinks.shape
    tile = depth // 16
    x = lax.all_gather(tokens, "tensor", axis=0, tiled=True)
    row_slot = jnp.repeat(segment_slot, SEG, total_repeat_length=x.shape[0])
    h = jnp.zeros((x.shape[0], rank), BF16)
    for i in range(held):
        mine = (row_slot == lax.axis_index("tensor") * held + i)[:, None]
        h = jnp.where(mine, shrink_all(x, shrinks[i], tile).astype(BF16), h)
    h = spread(h, parts)
    acc = project_all(x, weights, tile)
    return segment_finish(acc, scale, h, expands[segment_slot], cosine, sine)


def block_owners():
    chips = len(SNAKE)
    owners = np.zeros((2 * chips, 2 * chips), np.int32)
    for place, chip in enumerate(SNAKE):
        for core in (0, 1):
            row = [2 * chip + core, 2 * chip + 1 - core]
            for r in range(1, ROUNDS + 1):
                far, near = place - r * (1 - 2 * core), place + r * (1 - 2 * core)
                far, near = 2 * SNAKE[far % chips], 2 * SNAKE[near % chips]
                row += [far + core, near + 1 - core]
                if r < ROUNDS:
                    row += [near + core, far + 1 - core]
            owners[2 * chip + core] = row
    return owners


def ring_pairs(ways):
    chips = len(SNAKE)
    pairs = []
    for place, chip in enumerate(SNAKE):
        for core in (0, 1):
            pairs.append((2 * chip + core, 2 * SNAKE[(place + ways[core]) % chips] + core))
    return pairs


def block_kernel(count, low, tile, steps, first, base, fresh, ranked, *refs):
    xs, w_ref, refs = refs[:count], refs[count], refs[count + 1 :]
    if ranked:
        s_ref, refs = refs[0], refs[1:]
    if not first:
        total_in, refs = refs[0], refs[1:]
    total_out, refs = refs[0], refs[1:]
    if ranked:
        h_out, refs = refs[0], refs[1:]
    acc, before, x_slots, w_slots, s_slots, sems, total_sems = refs
    rows = xs[0].shape[0]

    def copies(step):
        slot = lax.rem(step, SLOTS)
        at = pl.multiple_of(step * tile, tile)
        sem = lambda i: sems.at[slot, i]
        out = [pltpu.make_async_copy(w_ref.at[pl.ds(low + at, tile)], w_slots.at[slot], sem(count))]
        for i in range(count):
            cut = xs[i].at[:, pl.ds(low + at, tile)]
            out.append(pltpu.make_async_copy(cut, x_slots.at[slot, pl.ds(i * rows, rows)], sem(i)))
        if ranked:
            cut = s_ref.at[pl.ds(low + at, tile)]
            out.append(pltpu.make_async_copy(cut, s_slots.at[slot], sem(count + 1)))
        return out

    def start(step):
        for copy in copies(step):
            copy.start()

    for step in range(min(SLOTS, steps)):
        start(jnp.int32(step))
    if not fresh:
        load = pltpu.make_async_copy(total_in.at[pl.ds(base, count)], before, total_sems.at[0])
        load.start()
    acc[...] = jnp.zeros_like(acc)
    if ranked:
        h_out[...] = jnp.zeros_like(h_out)

    @pl.loop(0, steps)
    def _(step):
        for copy in copies(step):
            copy.wait()
        slot = lax.rem(step, SLOTS)
        x = x_slots[slot]
        for left in range(0, acc.shape[2], CHUNK):
            cut = slice(left, left + CHUNK)
            product = jnp.dot(x, w_slots[slot, :, cut], preferred_element_type=F32)
            acc[:, :, cut] += product.reshape(count, rows, CHUNK)
        if ranked:
            mine = jnp.concatenate([x[i * rows : (i + 1) * rows] for i in range(0, count, 2)], 0)
            h_out[...] += jnp.dot(mine, s_slots[slot], preferred_element_type=F32)

        @pl.when(step + SLOTS < steps)
        def _():
            start(step + SLOTS)

    if not fresh:
        load.wait()
        acc[...] += before[...]
    store = pltpu.make_async_copy(acc, total_out.at[pl.ds(base, count)], total_sems.at[1])
    store.start()
    store.wait()


def block_product(xs, weights, factors, low, high, tile, total, base, ranked):
    count = len(xs)
    rows = xs[0].shape[0]
    cols = weights.shape[1]
    rank = factors.shape[1] if ranked else 128
    fresh, first = low == 0, total is None
    anywhere, whole = pl.BlockSpec(memory_space=pl.ANY), pl.BlockSpec(memory_space=pltpu.VMEM)
    operands = list(xs) + [weights]
    specs = [anywhere] * (count + 1)
    if ranked:
        operands.append(factors)
        specs.append(anywhere)
    aliases = {}
    if not first:
        aliases = {len(operands): 0}
        operands.append(total)
        specs.append(anywhere)
    outs, out_specs = [jax.ShapeDtypeStruct(total_shape(rows, cols), F32)], [anywhere]
    if ranked:
        outs.append(jax.ShapeDtypeStruct((count // 2 * rows, rank), F32))
        out_specs.append(whole)
    steps = (high - low) // tile
    result = pl.pallas_call(
        functools.partial(block_kernel, count, low, tile, steps, first, base, fresh, ranked),
        in_specs=specs,
        out_specs=out_specs,
        out_shape=outs,
        scratch_shapes=[
            pltpu.VMEM((count, rows, cols), F32),
            pltpu.VMEM((1, 8, 128) if fresh else (count, rows, cols), F32),
            pltpu.VMEM((SLOTS, count * rows, tile), BF16),
            pltpu.VMEM((SLOTS, tile, cols), BF16),
            pltpu.VMEM((SLOTS, tile, rank), BF16),
            pltpu.SemaphoreType.DMA((SLOTS, count + 2)),
            pltpu.SemaphoreType.DMA((2,)),
        ],
        input_output_aliases=aliases,
        compiler_params=pltpu.CompilerParams(vmem_limit_bytes=BIG_VMEM),
        cost_estimate=pl.CostEstimate(
            flops=2 * count * rows * (high - low) * cols,
            bytes_accessed=2 * (high - low) * cols,
            transcendentals=0,
        ),
        name="blocks",
    )(*operands)
    return result[0], result[1:]


def total_shape(rows, cols):
    return (2 * len(SNAKE), rows, cols)


def turn_kernel(a_ref, b_ref, out_ref):
    width = 2 * a_ref.shape[0]

    @pl.loop(0, a_ref.shape[1] // width)
    def _(step):
        cut = pl.ds(pl.multiple_of(step * width, width), width)
        both = jnp.concatenate([a_ref[:, cut], b_ref[:, cut]], 0)
        out_ref[cut, :] = both.astype(F32).T.astype(out_ref.dtype)


def turn(factors):
    rank, depth = factors[0].shape
    whole = pl.BlockSpec(memory_space=pltpu.VMEM)
    return pl.pallas_call(
        turn_kernel,
        in_specs=[whole] * 2,
        out_specs=whole,
        out_shape=jax.ShapeDtypeStruct((depth, 2 * rank), BF16),
        compiler_params=PARAMS,
        name="turn",
    )(*factors)


def some_ranks_kernel(x_ref, s_ref, out_ref):
    out_ref[...] = jnp.dot(x_ref[...], s_ref[...], preferred_element_type=F32)


def some_ranks(x, factors):
    whole = pl.BlockSpec(memory_space=pltpu.VMEM)
    return pl.pallas_call(
        some_ranks_kernel,
        in_specs=[whole] * 2,
        out_specs=whole,
        out_shape=jax.ShapeDtypeStruct((x.shape[0], factors.shape[1]), F32),
        compiler_params=PARAMS,
        name="some_ranks",
    )(x, factors)


def rank_kernel(count, owners_ref, slot_ref, *refs):
    xs, refs = refs[:count], refs[count:]
    s_ref, h_refs, out_ref, placed = refs[0], refs[1:-2], refs[-2], refs[-1]
    rows, rank = xs[0].shape[0], s_ref.shape[1] // 2
    x = jnp.concatenate([ref[...] for ref in xs], 0)
    last = jnp.dot(x, s_ref[...], preferred_element_type=F32)
    segments = slot_ref.shape[0] - 2
    block = 0
    for source in h_refs + (last,):
        for low in range(0, source.shape[0], rows):
            owner = owners_ref[2 * block]
            segment = owner * rows // SEG
            after = jnp.minimum(segment + 1, segments - 1)
            row = owner * rows + lax.broadcasted_iota(jnp.int32, (rows, rank), 0)
            slot = jnp.where(row < (segment + 1) * SEG, slot_ref[segment], slot_ref[after])
            terms = jnp.where(slot == slot_ref[segments + 1], source[low : low + rows, rank:], 0.0)
            terms = jnp.where(slot == slot_ref[segments], source[low : low + rows, :rank], terms)
            placed[pl.ds(pl.multiple_of(owner // 2 * rows, 16), rows), :] = terms
            block += 1
    half = placed.shape[0] // 2
    out_ref[...] = jnp.concatenate([placed[:half, :], placed[half:, :]], 1).astype(out_ref.dtype)


def rank_terms(owners, slots, xs, factors, hs):
    rank = factors.shape[1] // 2
    core_rows = owners.shape[0] // 2 * xs[0].shape[0]
    scalars, whole = pl.BlockSpec(memory_space=pltpu.SMEM), pl.BlockSpec(memory_space=pltpu.VMEM)
    return pl.pallas_call(
        functools.partial(rank_kernel, len(xs)),
        in_specs=[scalars] * 2 + [whole] * (len(xs) + 1 + len(hs)),
        out_specs=whole,
        scratch_shapes=[pltpu.VMEM((core_rows, rank), F32)],
        out_shape=jax.ShapeDtypeStruct((core_rows // 2, 2 * rank), BF16),
        compiler_params=PARAMS,
        name="ranks",
    )(owners, slots, *xs, factors, *hs)


def block_finish_kernel(places_ref, slot_ref, core_ref, total_ref, expand_ref, scale_ref, mine_ref, other_ref, *refs):
    cos_ref, sin_ref, out_ref, h, update, done, sems = refs
    blocks, rows, cols = total_ref.shape
    rank = mine_ref.shape[1] // 2
    even = core_ref[0] == 0
    mine, other = mine_ref[...], other_ref[...]
    for core, terms in enumerate((jnp.where(even, mine, other), jnp.where(even, other, mine))):
        for chip in range(blocks // 2):
            side, at = divmod(chip * rows, terms.shape[0])
            to = (2 * chip + core) * rows
            h[to : to + rows, :] = terms[at : at + rows, side * rank : (side + 1) * rank]
    for segment in range(h.shape[0] // SEG):
        cut = slice(segment * SEG, (segment + 1) * SEG)
        expand = expand_ref[slot_ref[segment]]
        update[cut, :] = jnp.dot(h[cut, :], expand, preferred_element_type=F32)
    copies = []
    for block in range(blocks):
        at = slice(block * rows, (block + 1) * rows)
        cosine, sine = cos_ref[at, :], sin_ref[at, :]
        place = places_ref[block]
        for left in range(0, cols, HD):
            cut = slice(left, left + HD)
            value = total_ref[place, :, cut] * scale_ref[:, cut] + update[at, cut]
            done[at, cut] = rotate(value, cosine, sine).astype(done.dtype)
        if block % 2:
            strip = pl.ds((block - 1) * rows, 2 * rows)
            copies.append(pltpu.make_async_copy(done.at[strip], out_ref.at[strip], sems.at[block // 2]))
            copies[-1].start()
    for copy in copies:
        copy.wait()


def block_finish(places, slots, core, total, expands, scale, mine, other, cosine, sine):
    blocks, rows, cols = total.shape
    rank = expands.shape[1]
    scalars, whole = pl.BlockSpec(memory_space=pltpu.SMEM), pl.BlockSpec(memory_space=pltpu.VMEM)
    return pl.pallas_call(
        block_finish_kernel,
        in_specs=[scalars] * 3 + [whole] * 7,
        out_specs=pl.BlockSpec(memory_space=pl.ANY),
        scratch_shapes=[
            pltpu.VMEM((blocks * rows, rank), BF16),
            pltpu.VMEM((blocks * rows, cols), F32),
            pltpu.VMEM((blocks * rows, cols), BF16),
            pltpu.SemaphoreType.DMA((blocks // 2,)),
        ],
        out_shape=jax.ShapeDtypeStruct((blocks * rows, cols), BF16),
        compiler_params=PARAMS,
        name="finish",
    )(places, slots, core, total, expands, scale, mine, other, cosine, sine)


def ring_plan(parts, tokens, weights, scale, shrinks, expands, indices):
    rows, depth = tokens.shape
    tile = depth // 16
    me = lax.axis_index("tensor")
    owners_table = block_owners()
    send = lambda value, pairs: lax.ppermute(value, "tensor", pairs)
    swap = lambda value: send(value, [(i, i ^ 1) for i in range(parts)])
    out, home = ring_pairs((1, -1)), ring_pairs((-1, 1))

    half = depth // 2
    hs, counts = [], []

    def multiply(xs, total, ranked):
        total, h = block_product(xs, weights, factors, 0, depth, tile, total, sum(counts), ranked)
        hs.extend(h)
        counts.append(len(xs))
        return total

    streams = [send(tokens, out), None]
    own, raw = [tokens, swap(tokens)], [shrinks[0], swap(shrinks[0])]
    part = 2 * tile
    total, _ = block_product(own, weights, None, 0, part, tile, None, 0, False)
    second, total = lax.optimization_barrier((tokens, total))
    streams[1] = send(second, home)
    total, _ = block_product(own, weights, None, part, depth, tile, total, 0, False)
    factors = turn(raw)
    hs, total = lax.optimization_barrier(([some_ranks(tokens, factors)], total))
    counts.append(len(own))

    def make_tables(me, indices):
        segment_slot, cosine, sine = small_tables(*indices, parts * rows)
        owners = jnp.asarray(owners_table)[me]
        places = jnp.asarray(np.argsort(owners_table, axis=1).astype(np.int32))[me]
        slots = jnp.concatenate([segment_slot, jnp.stack([me, me ^ 1]).astype(jnp.int32)])
        core = (me % 2)[None].astype(jnp.int32)
        return owners, places, slots, core, segment_slot, cosine, sine

    blocks, hops = [], 2 * ROUNDS - 1
    totals = [total] * 2
    for hop in range(hops):
        arrived, _ = lax.optimization_barrier((streams[hop % 2], totals[hop if hop % 2 else hop + 1]))
        if hop + 2 < hops:
            streams[hop % 2] = send(arrived, home if hop % 2 else out)
        if hop % 2:
            late = [arrived, swap(arrived)]
            total = multiply(blocks, total, hop < hops - 2)
            blocks = late
        else:
            blocks += [arrived, swap(arrived)]
        if hop == hops - 3:
            early = [some_ranks(part, factors) for part in blocks[::2]]
            early, total = lax.optimization_barrier((early, total))
        if hop == hops - 2:
            hs += early
            last, _ = lax.optimization_barrier((arrived, total))
            hs.append(some_ranks(last, factors))
            hs, total = lax.optimization_barrier((hs, total))
        if hop == 1:
            known, total = lax.optimization_barrier(((me, indices), total))
            tables, total = lax.optimization_barrier((make_tables(*known), total))
        totals.append(total)
    held = sum(counts)
    owners, places, slots, core, segment_slot, cosine, sine = tables
    h = rank_terms(owners, slots, blocks[2:3], factors, hs)
    beside = lambda step: send(h, [(i, i ^ step) for i in range(parts)])

    def last_product(low, high, total):
        xs, _ = lax.optimization_barrier((blocks, h))
        return block_product(xs, weights, factors, low, high, tile, total, held, False)[0]

    near = [beside(step) for step in (2, 4, 6)]
    near, total = lax.optimization_barrier((near, last_product(0, half, total)))
    h = h + near[0] + near[1] + near[2]
    far = [beside(step) for step in (8, 1, 9)]
    far, total = lax.optimization_barrier((far, last_product(half, depth, total)))
    mine, other = h + far[0], far[1] + far[2]
    return block_finish(places, segment_slot, core, total, expands, scale, mine, other, cosine, sine)


def body(parts, tokens, weight_codes, column_scale, shrink_store, expand_store, row_adapter, placement, document_lengths):
    rows = tokens.shape[0]
    total_rows = rows * parts
    shrinks = jnp.swapaxes(shrink_store, 1, 2)
    expands = jnp.swapaxes(expand_store, 1, 2)
    ring = parts == 2 * len(SNAKE) and rows % 16 == 0 and shrinks.shape[0] == 1 and total_rows % (2 * SEG) == 0
    plan = ring_plan if ring else gather_plan
    indices = (row_adapter, placement, document_lengths)
    return plan(parts, tokens, weight_codes, column_scale[None, :], shrinks, expands, indices)


def solution(mesh):
    placed = (
        P(("groups", "tensor"), None),
        P(None, "tensor"),
        P("tensor"),
        P(("groups", "tensor"), None, None),
        P("groups", "tensor", None),
        P("groups"),
        P("groups"),
        P("groups"),
    )
    return jax.shard_map(
        functools.partial(body, mesh.shape["tensor"]),
        mesh=mesh,
        in_specs=placed,
        out_specs=P("groups", "tensor"),
        check_vma=False,
    )
```

```python
import functools

import jax
import jax.numpy as jnp
import numpy as np
from jax import lax
from jax.experimental import pallas as pl
from jax.experimental.pallas import tpu as pltpu
from jax.sharding import PartitionSpec as P

HD = 128
SEG = 128
VMEM = 20 * 1024 * 1024
F32 = jnp.float32
BF16 = jnp.bfloat16
NT = (((1,), (1,)), ((), ()))
SLOTS = 4
CHUNK = 256
BIG_VMEM = 24 * 1024 * 1024
PARAMS = pltpu.CompilerParams(vmem_limit_bytes=VMEM)
SNAKE = (0, 2, 4, 6, 7, 5, 3, 1)
ROUNDS = len(SNAKE) // 2


def row_positions(document_lengths, total_rows):
    ends = jnp.cumsum(document_lengths)
    row_index = jnp.arange(total_rows, dtype=jnp.int32)
    passed = (row_index[:, None] >= ends[None, :]).astype(jnp.int32)
    return row_index - jnp.sum(passed * document_lengths[None, :], axis=1)


def rotary_tables(positions):
    half_size = HD // 2
    freq_index = jnp.arange(half_size, dtype=F32)
    inverse = jnp.exp(freq_index * (-2.0 / HD) * jnp.log(F32(500000.0)))
    angles = positions.astype(F32)[:, None] * inverse[None, :]
    cosine, sine = jnp.cos(angles), jnp.sin(angles)
    return jnp.concatenate([cosine, cosine], 1), jnp.concatenate([-sine, sine], 1)


def small_tables(row_adapter, placement, document_lengths, total_rows):
    segment_slot = placement[row_adapter[::SEG]]
    return segment_slot, *rotary_tables(row_positions(document_lengths, total_rows))


def rotate(value, cosine, sine):
    return value * cosine + pltpu.roll(value, HD // 2, 1) * sine


def shrink_kernel(x_ref, s_ref, h_out):
    @pl.when(pl.program_id(0) == 0)
    def _():
        h_out[...] = jnp.zeros_like(h_out)

    h_out[...] += lax.dot_general(x_ref[...], s_ref[...], NT, preferred_element_type=F32)


def shrink_all(x, shrink, tile):
    rows, depth = x.shape
    rank = shrink.shape[0]
    return pl.pallas_call(
        shrink_kernel,
        grid=(depth // tile,),
        in_specs=[
            pl.BlockSpec((rows, tile), lambda k: (0, k)),
            pl.BlockSpec((rank, tile), lambda k: (0, k)),
        ],
        out_specs=pl.BlockSpec((rows, rank), lambda k: (0, 0)),
        out_shape=jax.ShapeDtypeStruct((rows, rank), F32),
        compiler_params=PARAMS,
        name="shrink",
    )(x, shrink)


def project_kernel(x_ref, w_ref, acc_out):
    @pl.when(pl.program_id(0) == 0)
    def _():
        acc_out[...] = jnp.zeros_like(acc_out)

    acc_out[...] += jnp.dot(x_ref[...], w_ref[...], preferred_element_type=F32)


def project_all(x, weights, tile):
    rows, depth = x.shape
    cols = weights.shape[1]
    return pl.pallas_call(
        project_kernel,
        grid=(depth // tile,),
        in_specs=[
            pl.BlockSpec((rows, tile), lambda k: (0, k)),
            pl.BlockSpec((tile, cols), lambda k: (k, 0)),
        ],
        out_specs=pl.BlockSpec((rows, cols), lambda k: (0, 0)),
        out_shape=jax.ShapeDtypeStruct((rows, cols), F32),
        compiler_params=PARAMS,
        name="project",
    )(x, weights)


def segment_finish_kernel(acc_ref, scale_ref, h_ref, expand_ref, cos_ref, sin_ref, out_ref):
    update = jnp.dot(h_ref[...], expand_ref[0], preferred_element_type=F32)
    for head in range(out_ref.shape[1] // HD):
        cut = slice(head * HD, (head + 1) * HD)
        value = acc_ref[:, cut] * scale_ref[:, cut] + update[:, cut]
        out_ref[:, cut] = rotate(value, cos_ref[...], sin_ref[...]).astype(out_ref.dtype)


def segment_finish(acc, scale, h, expand, cosine, sine):
    rows, cols = acc.shape
    rank = h.shape[1]
    return pl.pallas_call(
        segment_finish_kernel,
        grid=(rows // SEG,),
        in_specs=[
            pl.BlockSpec((SEG, cols), lambda r: (r, 0)),
            pl.BlockSpec((1, cols), lambda r: (0, 0)),
            pl.BlockSpec((SEG, rank), lambda r: (r, 0)),
            pl.BlockSpec((1, rank, cols), lambda r: (r, 0, 0)),
            pl.BlockSpec((SEG, HD), lambda r: (r, 0)),
            pl.BlockSpec((SEG, HD), lambda r: (r, 0)),
        ],
        out_specs=pl.BlockSpec((SEG, cols), lambda r: (r, 0)),
        out_shape=jax.ShapeDtypeStruct((rows, cols), BF16),
        compiler_params=PARAMS,
        name="finish",
    )(acc, scale, h, expand, cosine, sine)


def spread(h, parts):
    step = 1
    while step < parts:
        h = h + lax.ppermute(h, "tensor", [(i, i ^ step) for i in range(parts)])
        step *= 2
    return h


def gather_plan(parts, tokens, weights, scale, shrinks, expands, indices):
    segment_slot, cosine, sine = small_tables(*indices, tokens.shape[0] * parts)
    held, rank, depth = shrinks.shape
    tile = depth // 16
    x = lax.all_gather(tokens, "tensor", axis=0, tiled=True)
    row_slot = jnp.repeat(segment_slot, SEG, total_repeat_length=x.shape[0])
    h = jnp.zeros((x.shape[0], rank), BF16)
    for i in range(held):
        mine = (row_slot == lax.axis_index("tensor") * held + i)[:, None]
        h = jnp.where(mine, shrink_all(x, shrinks[i], tile).astype(BF16), h)
    h = spread(h, parts)
    acc = project_all(x, weights, tile)
    return segment_finish(acc, scale, h, expands[segment_slot], cosine, sine)


def block_owners():
    chips = len(SNAKE)
    owners = np.zeros((2 * chips, 2 * chips), np.int32)
    for place, chip in enumerate(SNAKE):
        for core in (0, 1):
            row = [2 * chip + core, 2 * chip + 1 - core]
            for r in range(1, ROUNDS + 1):
                far, near = place - r * (1 - 2 * core), place + r * (1 - 2 * core)
                far, near = 2 * SNAKE[far % chips], 2 * SNAKE[near % chips]
                row += [far + core, near + 1 - core]
                if r < ROUNDS:
                    row += [near + core, far + 1 - core]
            owners[2 * chip + core] = row
    return owners


def ring_pairs(ways):
    chips = len(SNAKE)
    pairs = []
    for place, chip in enumerate(SNAKE):
        for core in (0, 1):
            pairs.append((2 * chip + core, 2 * SNAKE[(place + ways[core]) % chips] + core))
    return pairs


def block_kernel(count, low, tile, steps, first, base, fresh, ranked, *refs):
    xs, w_ref, refs = refs[:count], refs[count], refs[count + 1 :]
    if ranked:
        s_ref, refs = refs[0], refs[1:]
    if not first:
        total_in, refs = refs[0], refs[1:]
    total_out, refs = refs[0], refs[1:]
    if ranked:
        h_out, refs = refs[0], refs[1:]
    acc, before, x_slots, w_slots, s_slots, sems, total_sems = refs
    rows = xs[0].shape[0]

    def copies(step):
        slot = lax.rem(step, SLOTS)
        at = pl.multiple_of(step * tile, tile)
        sem = lambda i: sems.at[slot, i]
        out = [pltpu.make_async_copy(w_ref.at[pl.ds(low + at, tile)], w_slots.at[slot], sem(count))]
        for i in range(count):
            cut = xs[i].at[:, pl.ds(low + at, tile)]
            out.append(pltpu.make_async_copy(cut, x_slots.at[slot, pl.ds(i * rows, rows)], sem(i)))
        if ranked:
            cut = s_ref.at[pl.ds(low + at, tile)]
            out.append(pltpu.make_async_copy(cut, s_slots.at[slot], sem(count + 1)))
        return out

    def start(step):
        for copy in copies(step):
            copy.start()

    for step in range(min(SLOTS, steps)):
        start(jnp.int32(step))
    if not fresh:
        load = pltpu.make_async_copy(total_in.at[pl.ds(base, count)], before, total_sems.at[0])
        load.start()
    acc[...] = jnp.zeros_like(acc)
    if ranked:
        h_out[...] = jnp.zeros_like(h_out)

    @pl.loop(0, steps)
    def _(step):
        for copy in copies(step):
            copy.wait()
        slot = lax.rem(step, SLOTS)
        x = x_slots[slot]
        for left in range(0, acc.shape[2], CHUNK):
            cut = slice(left, left + CHUNK)
            product = jnp.dot(x, w_slots[slot, :, cut], preferred_element_type=F32)
            acc[:, :, cut] += product.reshape(count, rows, CHUNK)
        if ranked:
            mine = jnp.concatenate([x[i * rows : (i + 1) * rows] for i in range(0, count, 2)], 0)
            h_out[...] += jnp.dot(mine, s_slots[slot], preferred_element_type=F32)

        @pl.when(step + SLOTS < steps)
        def _():
            start(step + SLOTS)

    if not fresh:
        load.wait()
        acc[...] += before[...]
    store = pltpu.make_async_copy(acc, total_out.at[pl.ds(base, count)], total_sems.at[1])
    store.start()
    store.wait()


def block_product(xs, weights, factors, low, high, tile, total, base, ranked):
    count = len(xs)
    rows = xs[0].shape[0]
    cols = weights.shape[1]
    rank = factors.shape[1] if ranked else 128
    fresh, first = low == 0, total is None
    anywhere, whole = pl.BlockSpec(memory_space=pl.ANY), pl.BlockSpec(memory_space=pltpu.VMEM)
    operands = list(xs) + [weights]
    specs = [anywhere] * (count + 1)
    if ranked:
        operands.append(factors)
        specs.append(anywhere)
    aliases = {}
    if not first:
        aliases = {len(operands): 0}
        operands.append(total)
        specs.append(anywhere)
    outs, out_specs = [jax.ShapeDtypeStruct(total_shape(rows, cols), F32)], [anywhere]
    if ranked:
        outs.append(jax.ShapeDtypeStruct((count // 2 * rows, rank), F32))
        out_specs.append(whole)
    steps = (high - low) // tile
    result = pl.pallas_call(
        functools.partial(block_kernel, count, low, tile, steps, first, base, fresh, ranked),
        in_specs=specs,
        out_specs=out_specs,
        out_shape=outs,
        scratch_shapes=[
            pltpu.VMEM((count, rows, cols), F32),
            pltpu.VMEM((1, 8, 128) if fresh else (count, rows, cols), F32),
            pltpu.VMEM((SLOTS, count * rows, tile), BF16),
            pltpu.VMEM((SLOTS, tile, cols), BF16),
            pltpu.VMEM((SLOTS, tile, rank), BF16),
            pltpu.SemaphoreType.DMA((SLOTS, count + 2)),
            pltpu.SemaphoreType.DMA((2,)),
        ],
        input_output_aliases=aliases,
        compiler_params=pltpu.CompilerParams(vmem_limit_bytes=BIG_VMEM),
        cost_estimate=pl.CostEstimate(
            flops=2 * count * rows * (high - low) * cols,
            bytes_accessed=2 * (high - low) * cols,
            transcendentals=0,
        ),
        name="blocks",
    )(*operands)
    return result[0], result[1:]


def total_shape(rows, cols):
    return (2 * len(SNAKE), rows, cols)


def turn_kernel(a_ref, b_ref, out_ref):
    width = 2 * a_ref.shape[0]
    together = 16

    @pl.loop(0, a_ref.shape[1] // (width * together))
    def _(step):
        for i in range(together):
            cut = pl.ds(pl.multiple_of((step * together + i) * width, width), width)
            both = jnp.concatenate([a_ref[:, cut], b_ref[:, cut]], 0)
            out_ref[cut, :] = both.T


def turn(factors):
    rank, depth = factors[0].shape
    whole = pl.BlockSpec(memory_space=pltpu.VMEM)
    return pl.pallas_call(
        turn_kernel,
        in_specs=[whole] * 2,
        out_specs=whole,
        out_shape=jax.ShapeDtypeStruct((depth, 2 * rank), BF16),
        compiler_params=PARAMS,
        name="turn",
    )(*factors)


def some_ranks_kernel(x_ref, s_ref, out_ref):
    out_ref[...] = jnp.dot(x_ref[...], s_ref[...], preferred_element_type=F32)


def some_ranks(x, factors):
    whole = pl.BlockSpec(memory_space=pltpu.VMEM)
    return pl.pallas_call(
        some_ranks_kernel,
        in_specs=[whole] * 2,
        out_specs=whole,
        out_shape=jax.ShapeDtypeStruct((x.shape[0], factors.shape[1]), F32),
        compiler_params=PARAMS,
        name="some_ranks",
    )(x, factors)


def rank_kernel(count, owners_ref, slot_ref, *refs):
    xs, refs = refs[:count], refs[count:]
    s_ref, h_refs, out_ref, placed = refs[0], refs[1:-2], refs[-2], refs[-1]
    rows, rank = xs[0].shape[0], s_ref.shape[1] // 2
    x = jnp.concatenate([ref[...] for ref in xs], 0)
    last = jnp.dot(x, s_ref[...], preferred_element_type=F32)
    segments = slot_ref.shape[0] - 2
    block = 0
    for source in h_refs + (last,):
        for low in range(0, source.shape[0], rows):
            owner = owners_ref[2 * block]
            segment = owner * rows // SEG
            after = jnp.minimum(segment + 1, segments - 1)
            row = owner * rows + lax.broadcasted_iota(jnp.int32, (rows, rank), 0)
            slot = jnp.where(row < (segment + 1) * SEG, slot_ref[segment], slot_ref[after])
            terms = jnp.where(slot == slot_ref[segments + 1], source[low : low + rows, rank:], 0.0)
            terms = jnp.where(slot == slot_ref[segments], source[low : low + rows, :rank], terms)
            placed[pl.ds(pl.multiple_of(owner // 2 * rows, 16), rows), :] = terms
            block += 1
    half = placed.shape[0] // 2
    out_ref[...] = jnp.concatenate([placed[:half, :], placed[half:, :]], 1).astype(out_ref.dtype)


def rank_terms(owners, slots, xs, factors, hs):
    rank = factors.shape[1] // 2
    core_rows = owners.shape[0] // 2 * xs[0].shape[0]
    scalars, whole = pl.BlockSpec(memory_space=pltpu.SMEM), pl.BlockSpec(memory_space=pltpu.VMEM)
    return pl.pallas_call(
        functools.partial(rank_kernel, len(xs)),
        in_specs=[scalars] * 2 + [whole] * (len(xs) + 1 + len(hs)),
        out_specs=whole,
        scratch_shapes=[pltpu.VMEM((core_rows, rank), F32)],
        out_shape=jax.ShapeDtypeStruct((core_rows // 2, 2 * rank), BF16),
        compiler_params=PARAMS,
        name="ranks",
    )(owners, slots, *xs, factors, *hs)


def block_finish_kernel(places_ref, slot_ref, core_ref, total_ref, expand_ref, scale_ref, mine_ref, other_ref, *refs):
    cos_ref, sin_ref, out_ref, h, update, done, sems = refs
    blocks, rows, cols = total_ref.shape
    rank = mine_ref.shape[1] // 2
    even = core_ref[0] == 0
    mine, other = mine_ref[...], other_ref[...]
    for core, terms in enumerate((jnp.where(even, mine, other), jnp.where(even, other, mine))):
        for chip in range(blocks // 2):
            side, at = divmod(chip * rows, terms.shape[0])
            to = (2 * chip + core) * rows
            h[to : to + rows, :] = terms[at : at + rows, side * rank : (side + 1) * rank]
    for segment in range(h.shape[0] // SEG):
        cut = slice(segment * SEG, (segment + 1) * SEG)
        expand = expand_ref[slot_ref[segment]]
        update[cut, :] = jnp.dot(h[cut, :], expand, preferred_element_type=F32)
    copies = []
    for block in range(blocks):
        at = slice(block * rows, (block + 1) * rows)
        cosine, sine = cos_ref[at, :], sin_ref[at, :]
        place = places_ref[block]
        for left in range(0, cols, HD):
            cut = slice(left, left + HD)
            value = total_ref[place, :, cut] * scale_ref[:, cut] + update[at, cut]
            done[at, cut] = rotate(value, cosine, sine).astype(done.dtype)
        if block % 2:
            strip = pl.ds((block - 1) * rows, 2 * rows)
            copies.append(pltpu.make_async_copy(done.at[strip], out_ref.at[strip], sems.at[block // 2]))
            copies[-1].start()
    for copy in copies:
        copy.wait()


def block_finish(places, slots, core, total, expands, scale, mine, other, cosine, sine):
    blocks, rows, cols = total.shape
    rank = expands.shape[1]
    scalars, whole = pl.BlockSpec(memory_space=pltpu.SMEM), pl.BlockSpec(memory_space=pltpu.VMEM)
    return pl.pallas_call(
        block_finish_kernel,
        in_specs=[scalars] * 3 + [whole] * 7,
        out_specs=pl.BlockSpec(memory_space=pl.ANY),
        scratch_shapes=[
            pltpu.VMEM((blocks * rows, rank), BF16),
            pltpu.VMEM((blocks * rows, cols), F32),
            pltpu.VMEM((blocks * rows, cols), BF16),
            pltpu.SemaphoreType.DMA((blocks // 2,)),
        ],
        out_shape=jax.ShapeDtypeStruct((blocks * rows, cols), BF16),
        compiler_params=PARAMS,
        name="finish",
    )(places, slots, core, total, expands, scale, mine, other, cosine, sine)


def ring_plan(parts, tokens, weights, scale, shrinks, expands, indices):
    rows, depth = tokens.shape
    tile = depth // 16
    me = lax.axis_index("tensor")
    owners_table = block_owners()
    send = lambda value, pairs: lax.ppermute(value, "tensor", pairs)
    swap = lambda value: send(value, [(i, i ^ 1) for i in range(parts)])
    out, home = ring_pairs((1, -1)), ring_pairs((-1, 1))

    half = depth // 2
    hs, counts = [], []

    def multiply(xs, total, ranked):
        total, h = block_product(xs, weights, factors, 0, depth, tile, total, sum(counts), ranked)
        hs.extend(h)
        counts.append(len(xs))
        return total

    streams = [send(tokens, out), None]
    own, raw = [tokens, swap(tokens)], [shrinks[0], swap(shrinks[0])]
    part = 2 * tile
    total, _ = block_product(own, weights, None, 0, part, tile, None, 0, False)
    second, total = lax.optimization_barrier((tokens, total))
    streams[1] = send(second, home)
    total, _ = block_product(own, weights, None, part, depth, tile, total, 0, False)
    factors = turn(raw)
    hs, total = lax.optimization_barrier(([some_ranks(tokens, factors)], total))
    counts.append(len(own))

    def make_tables(me, indices):
        segment_slot, cosine, sine = small_tables(*indices, parts * rows)
        owners = jnp.asarray(owners_table)[me]
        places = jnp.asarray(np.argsort(owners_table, axis=1).astype(np.int32))[me]
        slots = jnp.concatenate([segment_slot, jnp.stack([me, me ^ 1]).astype(jnp.int32)])
        core = (me % 2)[None].astype(jnp.int32)
        return owners, places, slots, core, segment_slot, cosine, sine

    blocks, hops = [], 2 * ROUNDS - 1
    totals = [total] * 2
    for hop in range(hops):
        arrived, _ = lax.optimization_barrier((streams[hop % 2], totals[hop if hop % 2 else hop + 1]))
        if hop + 2 < hops:
            streams[hop % 2] = send(arrived, home if hop % 2 else out)
        if hop % 2:
            late = [arrived, swap(arrived)]
            total = multiply(blocks, total, hop < hops - 2)
            blocks = late
        else:
            blocks += [arrived, swap(arrived)]
        if hop == hops - 3:
            early = [some_ranks(part, factors) for part in blocks[::2]]
            early, total = lax.optimization_barrier((early, total))
        if hop == hops - 2:
            hs += early
            last, _ = lax.optimization_barrier((arrived, total))
            hs.append(some_ranks(last, factors))
            hs, total = lax.optimization_barrier((hs, total))
        if hop == 1:
            known, total = lax.optimization_barrier(((me, indices), total))
            tables, total = lax.optimization_barrier((make_tables(*known), total))
        totals.append(total)
    held = sum(counts)
    owners, places, slots, core, segment_slot, cosine, sine = tables
    h = rank_terms(owners, slots, blocks[2:3], factors, hs)
    beside = lambda step: send(h, [(i, i ^ step) for i in range(parts)])

    def last_product(low, high, total):
        xs, _ = lax.optimization_barrier((blocks, h))
        return block_product(xs, weights, factors, low, high, tile, total, held, False)[0]

    near = [beside(step) for step in (2, 4, 6)]
    near, total = lax.optimization_barrier((near, last_product(0, half, total)))
    h = h + near[0] + near[1] + near[2]
    far = [beside(step) for step in (8, 1, 9)]
    far, total = lax.optimization_barrier((far, last_product(half, depth, total)))
    mine, other = h + far[0], far[1] + far[2]
    return block_finish(places, segment_slot, core, total, expands, scale, mine, other, cosine, sine)


def body(parts, tokens, weight_codes, column_scale, shrink_store, expand_store, row_adapter, placement, document_lengths):
    rows = tokens.shape[0]
    total_rows = rows * parts
    shrinks = jnp.swapaxes(shrink_store, 1, 2)
    expands = jnp.swapaxes(expand_store, 1, 2)
    ring = parts == 2 * len(SNAKE) and rows % 16 == 0 and shrinks.shape[0] == 1 and total_rows % (2 * SEG) == 0
    ring = ring and shrinks.shape[1] == 64 and tokens.shape[1] % 2048 == 0
    plan = ring_plan if ring else gather_plan
    indices = (row_adapter, placement, document_lengths)
    return plan(parts, tokens, weight_codes, column_scale[None, :], shrinks, expands, indices)


def solution(mesh):
    placed = (
        P(("groups", "tensor"), None),
        P(None, "tensor"),
        P("tensor"),
        P(("groups", "tensor"), None, None),
        P("groups", "tensor", None),
        P("groups"),
        P("groups"),
        P("groups"),
    )
    return jax.shard_map(
        functools.partial(body, mesh.shape["tensor"]),
        mesh=mesh,
        in_specs=placed,
        out_specs=P("groups", "tensor"),
        check_vma=False,
    )
```

```python
import functools

import jax
import jax.numpy as jnp
import numpy as np
from jax import lax
from jax.experimental import pallas as pl
from jax.experimental.pallas import tpu as pltpu
from jax.sharding import PartitionSpec as P

HD = 128
SEG = 128
VMEM = 20 * 1024 * 1024
F32 = jnp.float32
BF16 = jnp.bfloat16
NT = (((1,), (1,)), ((), ()))
SLOTS = 4
CHUNK = 256
BIG_VMEM = 24 * 1024 * 1024
PARAMS = pltpu.CompilerParams(vmem_limit_bytes=VMEM)
SNAKE = (0, 2, 4, 6, 7, 5, 3, 1)
ROUNDS = len(SNAKE) // 2


def row_positions(document_lengths, total_rows):
    ends = jnp.cumsum(document_lengths)
    row_index = jnp.arange(total_rows, dtype=jnp.int32)
    passed = (row_index[:, None] >= ends[None, :]).astype(jnp.int32)
    return row_index - jnp.sum(passed * document_lengths[None, :], axis=1)


def rotary_tables(positions):
    half_size = HD // 2
    freq_index = jnp.arange(half_size, dtype=F32)
    inverse = jnp.exp(freq_index * (-2.0 / HD) * jnp.log(F32(500000.0)))
    angles = positions.astype(F32)[:, None] * inverse[None, :]
    cosine, sine = jnp.cos(angles), jnp.sin(angles)
    return jnp.concatenate([cosine, cosine], 1), jnp.concatenate([-sine, sine], 1)


def small_tables(row_adapter, placement, document_lengths, total_rows):
    segment_slot = placement[row_adapter[::SEG]]
    return segment_slot, *rotary_tables(row_positions(document_lengths, total_rows))


def rotate(value, cosine, sine):
    return value * cosine + pltpu.roll(value, HD // 2, 1) * sine


def shrink_kernel(x_ref, s_ref, h_out):
    @pl.when(pl.program_id(0) == 0)
    def _():
        h_out[...] = jnp.zeros_like(h_out)

    h_out[...] += lax.dot_general(x_ref[...], s_ref[...], NT, preferred_element_type=F32)


def shrink_all(x, shrink, tile):
    rows, depth = x.shape
    rank = shrink.shape[0]
    return pl.pallas_call(
        shrink_kernel,
        grid=(depth // tile,),
        in_specs=[
            pl.BlockSpec((rows, tile), lambda k: (0, k)),
            pl.BlockSpec((rank, tile), lambda k: (0, k)),
        ],
        out_specs=pl.BlockSpec((rows, rank), lambda k: (0, 0)),
        out_shape=jax.ShapeDtypeStruct((rows, rank), F32),
        compiler_params=PARAMS,
        name="shrink",
    )(x, shrink)


def project_kernel(x_ref, w_ref, acc_out):
    @pl.when(pl.program_id(0) == 0)
    def _():
        acc_out[...] = jnp.zeros_like(acc_out)

    acc_out[...] += jnp.dot(x_ref[...], w_ref[...], preferred_element_type=F32)


def project_all(x, weights, tile):
    rows, depth = x.shape
    cols = weights.shape[1]
    return pl.pallas_call(
        project_kernel,
        grid=(depth // tile,),
        in_specs=[
            pl.BlockSpec((rows, tile), lambda k: (0, k)),
            pl.BlockSpec((tile, cols), lambda k: (k, 0)),
        ],
        out_specs=pl.BlockSpec((rows, cols), lambda k: (0, 0)),
        out_shape=jax.ShapeDtypeStruct((rows, cols), F32),
        compiler_params=PARAMS,
        name="project",
    )(x, weights)


def segment_finish_kernel(acc_ref, scale_ref, h_ref, expand_ref, cos_ref, sin_ref, out_ref):
    update = jnp.dot(h_ref[...], expand_ref[0], preferred_element_type=F32)
    for head in range(out_ref.shape[1] // HD):
        cut = slice(head * HD, (head + 1) * HD)
        value = acc_ref[:, cut] * scale_ref[:, cut] + update[:, cut]
        out_ref[:, cut] = rotate(value, cos_ref[...], sin_ref[...]).astype(out_ref.dtype)


def segment_finish(acc, scale, h, expand, cosine, sine):
    rows, cols = acc.shape
    rank = h.shape[1]
    return pl.pallas_call(
        segment_finish_kernel,
        grid=(rows // SEG,),
        in_specs=[
            pl.BlockSpec((SEG, cols), lambda r: (r, 0)),
            pl.BlockSpec((1, cols), lambda r: (0, 0)),
            pl.BlockSpec((SEG, rank), lambda r: (r, 0)),
            pl.BlockSpec((1, rank, cols), lambda r: (r, 0, 0)),
            pl.BlockSpec((SEG, HD), lambda r: (r, 0)),
            pl.BlockSpec((SEG, HD), lambda r: (r, 0)),
        ],
        out_specs=pl.BlockSpec((SEG, cols), lambda r: (r, 0)),
        out_shape=jax.ShapeDtypeStruct((rows, cols), BF16),
        compiler_params=PARAMS,
        name="finish",
    )(acc, scale, h, expand, cosine, sine)


def spread(h, parts):
    step = 1
    while step < parts:
        h = h + lax.ppermute(h, "tensor", [(i, i ^ step) for i in range(parts)])
        step *= 2
    return h


def gather_plan(parts, tokens, weights, scale, shrinks, expands, indices):
    segment_slot, cosine, sine = small_tables(*indices, tokens.shape[0] * parts)
    held, rank, depth = shrinks.shape
    tile = depth // 16
    x = lax.all_gather(tokens, "tensor", axis=0, tiled=True)
    row_slot = jnp.repeat(segment_slot, SEG, total_repeat_length=x.shape[0])
    h = jnp.zeros((x.shape[0], rank), BF16)
    for i in range(held):
        mine = (row_slot == lax.axis_index("tensor") * held + i)[:, None]
        h = jnp.where(mine, shrink_all(x, shrinks[i], tile).astype(BF16), h)
    h = spread(h, parts)
    acc = project_all(x, weights, tile)
    return segment_finish(acc, scale, h, expands[segment_slot], cosine, sine)


def block_owners():
    chips = len(SNAKE)
    owners = np.zeros((2 * chips, 2 * chips), np.int32)
    for place, chip in enumerate(SNAKE):
        for core in (0, 1):
            row = [2 * chip + core, 2 * chip + 1 - core]
            for r in range(1, ROUNDS + 1):
                far, near = place - r * (1 - 2 * core), place + r * (1 - 2 * core)
                far, near = 2 * SNAKE[far % chips], 2 * SNAKE[near % chips]
                row += [far + core, near + 1 - core]
                if r < ROUNDS:
                    row += [near + core, far + 1 - core]
            owners[2 * chip + core] = row
    return owners


def ring_pairs(ways):
    chips = len(SNAKE)
    pairs = []
    for place, chip in enumerate(SNAKE):
        for core in (0, 1):
            pairs.append((2 * chip + core, 2 * SNAKE[(place + ways[core]) % chips] + core))
    return pairs


def block_kernel(count, low, tile, steps, first, base, fresh, ranked, *refs):
    xs, w_ref, refs = refs[:count], refs[count], refs[count + 1 :]
    if ranked:
        s_ref, refs = refs[0], refs[1:]
    if not first:
        refs = refs[1:]
    total, refs = refs[0], refs[1:]
    if ranked:
        h_out, refs = refs[0], refs[1:]
    x_slots, w_slots, s_slots, sems = refs
    here = slice(base, base + count)
    rows = xs[0].shape[0]

    def copies(step):
        slot = lax.rem(step, SLOTS)
        at = pl.multiple_of(step * tile, tile)
        sem = lambda i: sems.at[slot, i]
        out = [pltpu.make_async_copy(w_ref.at[pl.ds(low + at, tile)], w_slots.at[slot], sem(count))]
        for i in range(count):
            cut = xs[i].at[:, pl.ds(low + at, tile)]
            out.append(pltpu.make_async_copy(cut, x_slots.at[slot, pl.ds(i * rows, rows)], sem(i)))
        if ranked:
            cut = s_ref.at[pl.ds(low + at, tile)]
            out.append(pltpu.make_async_copy(cut, s_slots.at[slot], sem(count + 1)))
        return out

    def start(step):
        for copy in copies(step):
            copy.start()

    for step in range(min(SLOTS, steps)):
        start(jnp.int32(step))
    if fresh:
        total[here] = jnp.zeros((count,) + total.shape[1:], F32)
    if ranked:
        h_out[...] = jnp.zeros_like(h_out)

    @pl.loop(0, steps)
    def _(step):
        for copy in copies(step):
            copy.wait()
        slot = lax.rem(step, SLOTS)
        x = x_slots[slot]
        for left in range(0, total.shape[2], CHUNK):
            cut = slice(left, left + CHUNK)
            product = jnp.dot(x, w_slots[slot, :, cut], preferred_element_type=F32)
            total[here, :, cut] += product.reshape(count, rows, CHUNK)
        if ranked:
            mine = jnp.concatenate([x[i * rows : (i + 1) * rows] for i in range(0, count, 2)], 0)
            h_out[...] += jnp.dot(mine, s_slots[slot], preferred_element_type=F32)

        @pl.when(step + SLOTS < steps)
        def _():
            start(step + SLOTS)


def block_product(xs, weights, factors, low, high, tile, total, base, ranked):
    count = len(xs)
    rows = xs[0].shape[0]
    cols = weights.shape[1]
    rank = factors.shape[1] if ranked else 128
    fresh, first = low == 0, total is None
    anywhere, whole = pl.BlockSpec(memory_space=pl.ANY), pl.BlockSpec(memory_space=pltpu.VMEM)
    operands = list(xs) + [weights]
    specs = [anywhere] * (count + 1)
    if ranked:
        operands.append(factors)
        specs.append(anywhere)
    aliases = {}
    if not first:
        aliases = {len(operands): 0}
        operands.append(total)
        specs.append(whole)
    outs, out_specs = [jax.ShapeDtypeStruct(total_shape(rows, cols), F32)], [whole]
    if ranked:
        outs.append(jax.ShapeDtypeStruct((count // 2 * rows, rank), F32))
        out_specs.append(whole)
    steps = (high - low) // tile
    result = pl.pallas_call(
        functools.partial(block_kernel, count, low, tile, steps, first, base, fresh, ranked),
        in_specs=specs,
        out_specs=out_specs,
        out_shape=outs,
        scratch_shapes=[
            pltpu.VMEM((SLOTS, count * rows, tile), BF16),
            pltpu.VMEM((SLOTS, tile, cols), BF16),
            pltpu.VMEM((SLOTS, tile, rank), BF16),
            pltpu.SemaphoreType.DMA((SLOTS, count + 2)),
        ],
        input_output_aliases=aliases,
        compiler_params=pltpu.CompilerParams(vmem_limit_bytes=BIG_VMEM),
        cost_estimate=pl.CostEstimate(
            flops=2 * count * rows * (high - low) * cols,
            bytes_accessed=2 * (high - low) * cols,
            transcendentals=0,
        ),
        name="blocks",
    )(*operands)
    return result[0], result[1:]


def total_shape(rows, cols):
    return (2 * len(SNAKE), rows, cols)


def turn_kernel(a_ref, b_ref, out_ref):
    width = 2 * a_ref.shape[0]
    together = 16

    @pl.loop(0, a_ref.shape[1] // (width * together))
    def _(step):
        for i in range(together):
            cut = pl.ds(pl.multiple_of((step * together + i) * width, width), width)
            both = jnp.concatenate([a_ref[:, cut], b_ref[:, cut]], 0)
            out_ref[cut, :] = both.T


def turn(factors):
    rank, depth = factors[0].shape
    whole = pl.BlockSpec(memory_space=pltpu.VMEM)
    return pl.pallas_call(
        turn_kernel,
        in_specs=[whole] * 2,
        out_specs=whole,
        out_shape=jax.ShapeDtypeStruct((depth, 2 * rank), BF16),
        compiler_params=PARAMS,
        name="turn",
    )(*factors)


def some_ranks_kernel(x_ref, s_ref, out_ref):
    out_ref[...] = jnp.dot(x_ref[...], s_ref[...], preferred_element_type=F32)


def some_ranks(x, factors):
    whole = pl.BlockSpec(memory_space=pltpu.VMEM)
    return pl.pallas_call(
        some_ranks_kernel,
        in_specs=[whole] * 2,
        out_specs=whole,
        out_shape=jax.ShapeDtypeStruct((x.shape[0], factors.shape[1]), F32),
        compiler_params=PARAMS,
        name="some_ranks",
    )(x, factors)


def rank_kernel(count, owners_ref, slot_ref, *refs):
    xs, refs = refs[:count], refs[count:]
    s_ref, h_refs, out_ref, placed = refs[0], refs[1:-2], refs[-2], refs[-1]
    rows, rank = xs[0].shape[0], s_ref.shape[1] // 2
    x = jnp.concatenate([ref[...] for ref in xs], 0)
    last = jnp.dot(x, s_ref[...], preferred_element_type=F32)
    segments = slot_ref.shape[0] - 2
    block = 0
    for source in h_refs + (last,):
        for low in range(0, source.shape[0], rows):
            owner = owners_ref[2 * block]
            segment = owner * rows // SEG
            after = jnp.minimum(segment + 1, segments - 1)
            row = owner * rows + lax.broadcasted_iota(jnp.int32, (rows, rank), 0)
            slot = jnp.where(row < (segment + 1) * SEG, slot_ref[segment], slot_ref[after])
            terms = jnp.where(slot == slot_ref[segments + 1], source[low : low + rows, rank:], 0.0)
            terms = jnp.where(slot == slot_ref[segments], source[low : low + rows, :rank], terms)
            placed[pl.ds(pl.multiple_of(owner // 2 * rows, 16), rows), :] = terms
            block += 1
    half = placed.shape[0] // 2
    out_ref[...] = jnp.concatenate([placed[:half, :], placed[half:, :]], 1).astype(out_ref.dtype)


def rank_terms(owners, slots, xs, factors, hs):
    rank = factors.shape[1] // 2
    core_rows = owners.shape[0] // 2 * xs[0].shape[0]
    scalars, whole = pl.BlockSpec(memory_space=pltpu.SMEM), pl.BlockSpec(memory_space=pltpu.VMEM)
    return pl.pallas_call(
        functools.partial(rank_kernel, len(xs)),
        in_specs=[scalars] * 2 + [whole] * (len(xs) + 1 + len(hs)),
        out_specs=whole,
        scratch_shapes=[pltpu.VMEM((core_rows, rank), F32)],
        out_shape=jax.ShapeDtypeStruct((core_rows // 2, 2 * rank), BF16),
        compiler_params=PARAMS,
        name="ranks",
    )(owners, slots, *xs, factors, *hs)


def block_finish_kernel(places_ref, slot_ref, core_ref, total_ref, expand_ref, scale_ref, mine_ref, other_ref, *refs):
    cos_ref, sin_ref, out_ref, h, update, done, sems = refs
    blocks, rows, cols = total_ref.shape
    rank = mine_ref.shape[1] // 2
    even = core_ref[0] == 0
    mine, other = mine_ref[...], other_ref[...]
    for core, terms in enumerate((jnp.where(even, mine, other), jnp.where(even, other, mine))):
        for chip in range(blocks // 2):
            side, at = divmod(chip * rows, terms.shape[0])
            to = (2 * chip + core) * rows
            h[to : to + rows, :] = terms[at : at + rows, side * rank : (side + 1) * rank]
    for segment in range(h.shape[0] // SEG):
        cut = slice(segment * SEG, (segment + 1) * SEG)
        expand = expand_ref[slot_ref[segment]]
        update[cut, :] = jnp.dot(h[cut, :], expand, preferred_element_type=F32)
    copies = []
    for block in range(blocks):
        at = slice(block * rows, (block + 1) * rows)
        cosine, sine = cos_ref[at, :], sin_ref[at, :]
        place = places_ref[block]
        for left in range(0, cols, HD):
            cut = slice(left, left + HD)
            value = total_ref[place, :, cut] * scale_ref[:, cut] + update[at, cut]
            done[at, cut] = rotate(value, cosine, sine).astype(done.dtype)
        if block % 2:
            strip = pl.ds((block - 1) * rows, 2 * rows)
            copies.append(pltpu.make_async_copy(done.at[strip], out_ref.at[strip], sems.at[block // 2]))
            copies[-1].start()
    for copy in copies:
        copy.wait()


def block_finish(places, slots, core, total, expands, scale, mine, other, cosine, sine):
    blocks, rows, cols = total.shape
    rank = expands.shape[1]
    scalars, whole = pl.BlockSpec(memory_space=pltpu.SMEM), pl.BlockSpec(memory_space=pltpu.VMEM)
    return pl.pallas_call(
        block_finish_kernel,
        in_specs=[scalars] * 3 + [whole] * 7,
        out_specs=pl.BlockSpec(memory_space=pl.ANY),
        scratch_shapes=[
            pltpu.VMEM((blocks * rows, rank), BF16),
            pltpu.VMEM((blocks * rows, cols), F32),
            pltpu.VMEM((blocks * rows, cols), BF16),
            pltpu.SemaphoreType.DMA((blocks // 2,)),
        ],
        out_shape=jax.ShapeDtypeStruct((blocks * rows, cols), BF16),
        compiler_params=PARAMS,
        name="finish",
    )(places, slots, core, total, expands, scale, mine, other, cosine, sine)


def ring_plan(parts, tokens, weights, scale, shrinks, expands, indices):
    rows, depth = tokens.shape
    tile = depth // 16
    me = lax.axis_index("tensor")
    owners_table = block_owners()
    send = lambda value, pairs: lax.ppermute(value, "tensor", pairs)
    swap = lambda value: send(value, [(i, i ^ 1) for i in range(parts)])
    out, home = ring_pairs((1, -1)), ring_pairs((-1, 1))

    half = depth // 2
    hs, counts = [], []

    def multiply(xs, total, ranked):
        total, h = block_product(xs, weights, factors, 0, depth, tile, total, sum(counts), ranked)
        hs.extend(h)
        counts.append(len(xs))
        return total

    streams = [send(tokens, out), None]
    own, raw = [tokens, swap(tokens)], [shrinks[0], swap(shrinks[0])]
    part = 2 * tile
    total, _ = block_product(own, weights, None, 0, part, tile, None, 0, False)
    second, total = lax.optimization_barrier((tokens, total))
    streams[1] = send(second, home)
    total, _ = block_product(own, weights, None, part, depth, tile, total, 0, False)
    factors = turn(raw)
    hs, total = lax.optimization_barrier(([some_ranks(tokens, factors)], total))
    counts.append(len(own))

    def make_tables(me, indices):
        segment_slot, cosine, sine = small_tables(*indices, parts * rows)
        owners = jnp.asarray(owners_table)[me]
        places = jnp.asarray(np.argsort(owners_table, axis=1).astype(np.int32))[me]
        slots = jnp.concatenate([segment_slot, jnp.stack([me, me ^ 1]).astype(jnp.int32)])
        core = (me % 2)[None].astype(jnp.int32)
        return owners, places, slots, core, segment_slot, cosine, sine

    blocks, hops = [], 2 * ROUNDS - 1
    totals = [total] * 2
    for hop in range(hops):
        arrived, _ = lax.optimization_barrier((streams[hop % 2], totals[hop if hop % 2 else hop + 1]))
        if hop + 2 < hops:
            streams[hop % 2] = send(arrived, home if hop % 2 else out)
        if hop % 2:
            late = [arrived, swap(arrived)]
            total = multiply(blocks, total, hop < hops - 2)
            blocks = late
        else:
            blocks += [arrived, swap(arrived)]
        if hop == hops - 3:
            early = [some_ranks(part, factors) for part in blocks[::2]]
            early, total = lax.optimization_barrier((early, total))
        if hop == hops - 2:
            hs += early
            last, _ = lax.optimization_barrier((arrived, total))
            hs.append(some_ranks(last, factors))
            hs, total = lax.optimization_barrier((hs, total))
        if hop == 1:
            known, total = lax.optimization_barrier(((me, indices), total))
            tables, total = lax.optimization_barrier((make_tables(*known), total))
        totals.append(total)
    held = sum(counts)
    owners, places, slots, core, segment_slot, cosine, sine = tables
    h = rank_terms(owners, slots, blocks[2:3], factors, hs)
    beside = lambda step: send(h, [(i, i ^ step) for i in range(parts)])

    def last_product(low, high, total):
        xs, _ = lax.optimization_barrier((blocks, h))
        return block_product(xs, weights, factors, low, high, tile, total, held, False)[0]

    near = [beside(step) for step in (2, 4, 6)]
    near, total = lax.optimization_barrier((near, last_product(0, half, total)))
    h = h + near[0] + near[1] + near[2]
    far = [beside(step) for step in (8, 1, 9)]
    far, total = lax.optimization_barrier((far, last_product(half, depth, total)))
    mine, other = h + far[0], far[1] + far[2]
    return block_finish(places, segment_slot, core, total, expands, scale, mine, other, cosine, sine)


def body(parts, tokens, weight_codes, column_scale, shrink_store, expand_store, row_adapter, placement, document_lengths):
    rows = tokens.shape[0]
    total_rows = rows * parts
    shrinks = jnp.swapaxes(shrink_store, 1, 2)
    expands = jnp.swapaxes(expand_store, 1, 2)
    ring = parts == 2 * len(SNAKE) and rows % 16 == 0 and shrinks.shape[0] == 1 and total_rows % (2 * SEG) == 0
    ring = ring and shrinks.shape[1] == 64 and tokens.shape[1] % 2048 == 0
    plan = ring_plan if ring else gather_plan
    indices = (row_adapter, placement, document_lengths)
    return plan(parts, tokens, weight_codes, column_scale[None, :], shrinks, expands, indices)


def solution(mesh):
    placed = (
        P(("groups", "tensor"), None),
        P(None, "tensor"),
        P("tensor"),
        P(("groups", "tensor"), None, None),
        P("groups", "tensor", None),
        P("groups"),
        P("groups"),
        P("groups"),
    )
    return jax.shard_map(
        functools.partial(body, mesh.shape["tensor"]),
        mesh=mesh,
        in_specs=placed,
        out_specs=P("groups", "tensor"),
        check_vma=False,
    )
```

```python
import functools

import jax
import jax.numpy as jnp
import numpy as np
from jax import lax
from jax.experimental import pallas as pl
from jax.experimental.pallas import tpu as pltpu
from jax.sharding import PartitionSpec as P

HD = 128
SEG = 128
VMEM = 16 * 1024 * 1024
F32 = jnp.float32
BF16 = jnp.bfloat16
NT = (((1,), (1,)), ((), ()))
SLOTS = 4
CHUNK = 256
KEEP = 6
BIG_VMEM = 16 * 1024 * 1024
PARAMS = pltpu.CompilerParams(vmem_limit_bytes=VMEM)
SNAKE = (0, 2, 4, 6, 7, 5, 3, 1)
ROUNDS = len(SNAKE) // 2


def row_positions(document_lengths, total_rows):
    ends = jnp.cumsum(document_lengths)
    row_index = jnp.arange(total_rows, dtype=jnp.int32)
    passed = (row_index[:, None] >= ends[None, :]).astype(jnp.int32)
    return row_index - jnp.sum(passed * document_lengths[None, :], axis=1)


def rotary_tables(positions):
    half_size = HD // 2
    freq_index = jnp.arange(half_size, dtype=F32)
    inverse = jnp.exp(freq_index * (-2.0 / HD) * jnp.log(F32(500000.0)))
    angles = positions.astype(F32)[:, None] * inverse[None, :]
    cosine, sine = jnp.cos(angles), jnp.sin(angles)
    return jnp.concatenate([cosine, cosine], 1), jnp.concatenate([-sine, sine], 1)


def small_tables(row_adapter, placement, document_lengths, total_rows):
    segment_slot = placement[row_adapter[::SEG]]
    return segment_slot, *rotary_tables(row_positions(document_lengths, total_rows))


def rotate(value, cosine, sine):
    return value * cosine + pltpu.roll(value, HD // 2, 1) * sine


def shrink_kernel(x_ref, s_ref, h_out):
    @pl.when(pl.program_id(0) == 0)
    def _():
        h_out[...] = jnp.zeros_like(h_out)

    h_out[...] += lax.dot_general(x_ref[...], s_ref[...], NT, preferred_element_type=F32)


def shrink_all(x, shrink, tile):
    rows, depth = x.shape
    rank = shrink.shape[0]
    return pl.pallas_call(
        shrink_kernel,
        grid=(depth // tile,),
        in_specs=[
            pl.BlockSpec((rows, tile), lambda k: (0, k)),
            pl.BlockSpec((rank, tile), lambda k: (0, k)),
        ],
        out_specs=pl.BlockSpec((rows, rank), lambda k: (0, 0)),
        out_shape=jax.ShapeDtypeStruct((rows, rank), F32),
        compiler_params=PARAMS,
        name="shrink",
    )(x, shrink)


def project_kernel(x_ref, w_ref, acc_out):
    @pl.when(pl.program_id(0) == 0)
    def _():
        acc_out[...] = jnp.zeros_like(acc_out)

    acc_out[...] += jnp.dot(x_ref[...], w_ref[...], preferred_element_type=F32)


def project_all(x, weights, tile):
    rows, depth = x.shape
    cols = weights.shape[1]
    return pl.pallas_call(
        project_kernel,
        grid=(depth // tile,),
        in_specs=[
            pl.BlockSpec((rows, tile), lambda k: (0, k)),
            pl.BlockSpec((tile, cols), lambda k: (k, 0)),
        ],
        out_specs=pl.BlockSpec((rows, cols), lambda k: (0, 0)),
        out_shape=jax.ShapeDtypeStruct((rows, cols), F32),
        compiler_params=PARAMS,
        name="project",
    )(x, weights)


def segment_finish_kernel(acc_ref, scale_ref, h_ref, expand_ref, cos_ref, sin_ref, out_ref):
    update = jnp.dot(h_ref[...], expand_ref[0], preferred_element_type=F32)
    for head in range(out_ref.shape[1] // HD):
        cut = slice(head * HD, (head + 1) * HD)
        value = acc_ref[:, cut] * scale_ref[:, cut] + update[:, cut]
        out_ref[:, cut] = rotate(value, cos_ref[...], sin_ref[...]).astype(out_ref.dtype)


def segment_finish(acc, scale, h, expand, cosine, sine):
    rows, cols = acc.shape
    rank = h.shape[1]
    return pl.pallas_call(
        segment_finish_kernel,
        grid=(rows // SEG,),
        in_specs=[
            pl.BlockSpec((SEG, cols), lambda r: (r, 0)),
            pl.BlockSpec((1, cols), lambda r: (0, 0)),
            pl.BlockSpec((SEG, rank), lambda r: (r, 0)),
            pl.BlockSpec((1, rank, cols), lambda r: (r, 0, 0)),
            pl.BlockSpec((SEG, HD), lambda r: (r, 0)),
            pl.BlockSpec((SEG, HD), lambda r: (r, 0)),
        ],
        out_specs=pl.BlockSpec((SEG, cols), lambda r: (r, 0)),
        out_shape=jax.ShapeDtypeStruct((rows, cols), BF16),
        compiler_params=PARAMS,
        name="finish",
    )(acc, scale, h, expand, cosine, sine)


def spread(h, parts):
    step = 1
    while step < parts:
        h = h + lax.ppermute(h, "tensor", [(i, i ^ step) for i in range(parts)])
        step *= 2
    return h


def gather_plan(parts, tokens, weights, scale, shrinks, expands, indices):
    segment_slot, cosine, sine = small_tables(*indices, tokens.shape[0] * parts)
    held, rank, depth = shrinks.shape
    tile = depth // 16
    x = lax.all_gather(tokens, "tensor", axis=0, tiled=True)
    row_slot = jnp.repeat(segment_slot, SEG, total_repeat_length=x.shape[0])
    h = jnp.zeros((x.shape[0], rank), BF16)
    for i in range(held):
        mine = (row_slot == lax.axis_index("tensor") * held + i)[:, None]
        h = jnp.where(mine, shrink_all(x, shrinks[i], tile).astype(BF16), h)
    h = spread(h, parts)
    acc = project_all(x, weights, tile)
    return segment_finish(acc, scale, h, expands[segment_slot], cosine, sine)


def block_owners():
    chips = len(SNAKE)
    owners = np.zeros((2 * chips, 2 * chips), np.int32)
    for place, chip in enumerate(SNAKE):
        for core in (0, 1):
            row = [2 * chip + core, 2 * chip + 1 - core]
            for r in range(1, ROUNDS + 1):
                far, near = place - r * (1 - 2 * core), place + r * (1 - 2 * core)
                far, near = 2 * SNAKE[far % chips], 2 * SNAKE[near % chips]
                row += [far + core, near + 1 - core]
                if r < ROUNDS:
                    row += [near + core, far + 1 - core]
            owners[2 * chip + core] = row
    return owners


def ring_pairs(ways):
    chips = len(SNAKE)
    pairs = []
    for place, chip in enumerate(SNAKE):
        for core in (0, 1):
            pairs.append((2 * chip + core, 2 * SNAKE[(place + ways[core]) % chips] + core))
    return pairs


def block_kernel(count, low, tile, steps, kept, first, base, fresh, ranked, *refs):
    xs, w_ref, refs = refs[:count], refs[count], refs[count + 1 :]
    if ranked:
        s_ref, refs = refs[0], refs[1:]
    if kept:
        w_kept, refs = refs[0], refs[1:]
    if not first:
        refs = refs[1:]
    total, refs = refs[0], refs[1:]
    if ranked:
        h_out, refs = refs[0], refs[1:]
    x_slots, w_slots, s_slots, sems = refs
    here = slice(base, base + count)
    rows = xs[0].shape[0]

    def copies(step):
        slot = lax.rem(step, SLOTS)
        at = low + step * tile
        if kept:
            at = jnp.where(step < kept, w_ref.shape[0], low) + (step - kept) * tile
        at = pl.multiple_of(at, tile)
        out = []
        for i in range(count):
            cut = xs[i].at[:, pl.ds(at, tile)]
            out.append(pltpu.make_async_copy(cut, x_slots.at[slot, pl.ds(i * rows, rows)], sems.at[slot, i]))
        if ranked:
            cut = s_ref.at[pl.ds(at, tile)]
            out.append(pltpu.make_async_copy(cut, s_slots.at[slot], sems.at[slot, count + 1]))
        return out

    def weights(index):
        slot = lax.rem(index, SLOTS)
        cut = w_ref.at[pl.ds(pl.multiple_of(low + index * tile, tile), tile)]
        return pltpu.make_async_copy(cut, w_slots.at[slot], sems.at[slot, count])

    def start(step):
        for copy in copies(step):
            copy.start()

    for index in range(min(SLOTS, steps - kept)):
        weights(jnp.int32(index)).start()
    for step in range(min(SLOTS, steps)):
        start(jnp.int32(step))
    if fresh:
        total[here] = jnp.zeros((count,) + total.shape[1:], F32)
    if ranked:
        h_out[...] = jnp.zeros_like(h_out)

    def take(step, weight):
        slot = lax.rem(step, SLOTS)
        x = x_slots[slot]
        for left in range(0, total.shape[2], CHUNK):
            cut = slice(left, left + CHUNK)
            product = jnp.dot(x, weight(cut), preferred_element_type=F32)
            total[here, :, cut] += product.reshape(count, rows, CHUNK)
        if ranked:
            mine = jnp.concatenate([x[i * rows : (i + 1) * rows] for i in range(0, count, 2)], 0)
            h_out[...] += jnp.dot(mine, s_slots[slot], preferred_element_type=F32)

    if kept:
        @pl.loop(0, kept)
        def _(step):
            for copy in copies(step):
                copy.wait()
            take(step, lambda cut: w_kept[pl.ds(pl.multiple_of(step * tile, tile), tile), cut])

            @pl.when(step + SLOTS < steps)
            def _():
                start(step + SLOTS)

    @pl.loop(kept, steps)
    def _(step):
        index = step - kept
        for copy in copies(step) + [weights(index)]:
            copy.wait()
        take(step, lambda cut: w_slots[lax.rem(index, SLOTS), :, cut])

        @pl.when(step + SLOTS < steps)
        def _():
            start(step + SLOTS)
            weights(index + SLOTS).start()


def block_product(xs, weights, factors, low, high, tile, total, base, ranked, fresh=None, kept=None):
    count = len(xs)
    rows = xs[0].shape[0]
    cols = weights.shape[1]
    rank = factors.shape[1] if ranked else 128
    fresh, first = low == 0 if fresh is None else fresh, total is None
    anywhere, whole = pl.BlockSpec(memory_space=pl.ANY), pl.BlockSpec(memory_space=pltpu.VMEM)
    operands = list(xs) + [weights]
    specs = [anywhere] * (count + 1)
    if ranked:
        operands.append(factors)
        specs.append(anywhere)
    kept_steps = 0
    if kept is not None:
        operands.append(kept)
        specs.append(whole)
        kept_steps = kept.shape[0] // tile
    aliases = {}
    if not first:
        aliases = {len(operands): 0}
        operands.append(total)
        specs.append(whole)
    outs, out_specs = [jax.ShapeDtypeStruct(total_shape(rows, cols), F32)], [whole]
    if ranked:
        outs.append(jax.ShapeDtypeStruct((count // 2 * rows, rank), F32))
        out_specs.append(whole)
    steps = (high - low) // tile + kept_steps
    result = pl.pallas_call(
        functools.partial(block_kernel, count, low, tile, steps, kept_steps, first, base, fresh, ranked),
        in_specs=specs,
        out_specs=out_specs,
        out_shape=outs,
        scratch_shapes=[
            pltpu.VMEM((SLOTS, count * rows, tile), BF16),
            pltpu.VMEM((SLOTS, tile, cols), BF16),
            pltpu.VMEM((SLOTS, tile, rank), BF16),
            pltpu.SemaphoreType.DMA((SLOTS, count + 2)),
        ],
        input_output_aliases=aliases,
        compiler_params=pltpu.CompilerParams(vmem_limit_bytes=BIG_VMEM),
        cost_estimate=pl.CostEstimate(
            flops=2 * count * rows * (high - low) * cols,
            bytes_accessed=2 * (high - low) * cols,
            transcendentals=0,
        ),
        name="blocks",
    )(*operands)
    return result[0], result[1:]


def keep_kernel(low, w_ref, out_ref, sem):
    copy = pltpu.make_async_copy(w_ref.at[pl.ds(low, out_ref.shape[0])], out_ref, sem)
    copy.start()
    copy.wait()


def keep_weights(weights, low):
    depth, cols = weights.shape
    return pl.pallas_call(
        functools.partial(keep_kernel, low),
        in_specs=[pl.BlockSpec(memory_space=pl.ANY)],
        out_specs=pl.BlockSpec(memory_space=pltpu.VMEM),
        out_shape=jax.ShapeDtypeStruct((depth - low, cols), weights.dtype),
        scratch_shapes=[pltpu.SemaphoreType.DMA],
        compiler_params=PARAMS,
        name="keep",
    )(weights)


def total_shape(rows, cols):
    return (2 * len(SNAKE), rows, cols)


def turn_kernel(a_ref, b_ref, out_ref):
    width = 2 * a_ref.shape[0]
    together = 16

    @pl.loop(0, a_ref.shape[1] // (width * together))
    def _(step):
        for i in range(together):
            cut = pl.ds(pl.multiple_of((step * together + i) * width, width), width)
            both = jnp.concatenate([a_ref[:, cut], b_ref[:, cut]], 0)
            out_ref[cut, :] = both.T


def turn(factors):
    rank, depth = factors[0].shape
    whole = pl.BlockSpec(memory_space=pltpu.VMEM)
    return pl.pallas_call(
        turn_kernel,
        in_specs=[whole] * 2,
        out_specs=whole,
        out_shape=jax.ShapeDtypeStruct((depth, 2 * rank), BF16),
        compiler_params=PARAMS,
        name="turn",
    )(*factors)


def some_ranks_kernel(x_ref, s_ref, out_ref):
    out_ref[...] = jnp.dot(x_ref[...], s_ref[...], preferred_element_type=F32)


def some_ranks(x, factors):
    whole = pl.BlockSpec(memory_space=pltpu.VMEM)
    return pl.pallas_call(
        some_ranks_kernel,
        in_specs=[whole] * 2,
        out_specs=whole,
        out_shape=jax.ShapeDtypeStruct((x.shape[0], factors.shape[1]), F32),
        compiler_params=PARAMS,
        name="some_ranks",
    )(x, factors)


def rank_kernel(count, owners_ref, slot_ref, *refs):
    xs, refs = refs[:count], refs[count:]
    s_ref, h_refs, out_ref, placed = refs[0], refs[1:-2], refs[-2], refs[-1]
    rows, rank = xs[0].shape[0], s_ref.shape[1] // 2
    x = jnp.concatenate([ref[...] for ref in xs], 0)
    last = jnp.dot(x, s_ref[...], preferred_element_type=F32)
    segments = slot_ref.shape[0] - 2
    block = 0
    for source in h_refs + (last,):
        for low in range(0, source.shape[0], rows):
            owner = owners_ref[2 * block]
            segment = owner * rows // SEG
            after = jnp.minimum(segment + 1, segments - 1)
            row = owner * rows + lax.broadcasted_iota(jnp.int32, (rows, rank), 0)
            slot = jnp.where(row < (segment + 1) * SEG, slot_ref[segment], slot_ref[after])
            terms = jnp.where(slot == slot_ref[segments + 1], source[low : low + rows, rank:], 0.0)
            terms = jnp.where(slot == slot_ref[segments], source[low : low + rows, :rank], terms)
            placed[pl.ds(pl.multiple_of(owner // 2 * rows, 16), rows), :] = terms
            block += 1
    half = placed.shape[0] // 2
    out_ref[...] = jnp.concatenate([placed[:half, :], placed[half:, :]], 1).astype(out_ref.dtype)


def rank_terms(owners, slots, xs, factors, hs):
    rank = factors.shape[1] // 2
    core_rows = owners.shape[0] // 2 * xs[0].shape[0]
    scalars, whole = pl.BlockSpec(memory_space=pltpu.SMEM), pl.BlockSpec(memory_space=pltpu.VMEM)
    return pl.pallas_call(
        functools.partial(rank_kernel, len(xs)),
        in_specs=[scalars] * 2 + [whole] * (len(xs) + 1 + len(hs)),
        out_specs=whole,
        scratch_shapes=[pltpu.VMEM((core_rows, rank), F32)],
        out_shape=jax.ShapeDtypeStruct((core_rows // 2, 2 * rank), BF16),
        compiler_params=PARAMS,
        name="ranks",
    )(owners, slots, *xs, factors, *hs)


def block_finish_kernel(places_ref, slot_ref, core_ref, total_ref, expand_ref, scale_ref, mine_ref, other_ref, *refs):
    cos_ref, sin_ref, out_ref, h, update, done, sems = refs
    blocks, rows, cols = total_ref.shape
    rank = mine_ref.shape[1] // 2
    even = core_ref[0] == 0
    mine, other = mine_ref[...], other_ref[...]
    for core, terms in enumerate((jnp.where(even, mine, other), jnp.where(even, other, mine))):
        for chip in range(blocks // 2):
            side, at = divmod(chip * rows, terms.shape[0])
            to = (2 * chip + core) * rows
            h[to : to + rows, :] = terms[at : at + rows, side * rank : (side + 1) * rank]
    for segment in range(h.shape[0] // SEG):
        cut = slice(segment * SEG, (segment + 1) * SEG)
        expand = expand_ref[slot_ref[segment]]
        update[cut, :] = jnp.dot(h[cut, :], expand, preferred_element_type=F32)
    copies = []
    for block in range(blocks):
        at = slice(block * rows, (block + 1) * rows)
        cosine, sine = cos_ref[at, :], sin_ref[at, :]
        place = places_ref[block]
        for left in range(0, cols, HD):
            cut = slice(left, left + HD)
            value = total_ref[place, :, cut] * scale_ref[:, cut] + update[at, cut]
            done[at, cut] = rotate(value, cosine, sine).astype(done.dtype)
        if block % 2:
            strip = pl.ds((block - 1) * rows, 2 * rows)
            copies.append(pltpu.make_async_copy(done.at[strip], out_ref.at[strip], sems.at[block // 2]))
            copies[-1].start()
    for copy in copies:
        copy.wait()


def block_finish(places, slots, core, total, expands, scale, mine, other, cosine, sine):
    blocks, rows, cols = total.shape
    rank = expands.shape[1]
    scalars, whole = pl.BlockSpec(memory_space=pltpu.SMEM), pl.BlockSpec(memory_space=pltpu.VMEM)
    return pl.pallas_call(
        block_finish_kernel,
        in_specs=[scalars] * 3 + [whole] * 7,
        out_specs=pl.BlockSpec(memory_space=pl.ANY),
        scratch_shapes=[
            pltpu.VMEM((blocks * rows, rank), BF16),
            pltpu.VMEM((blocks * rows, cols), F32),
            pltpu.VMEM((blocks * rows, cols), BF16),
            pltpu.SemaphoreType.DMA((blocks // 2,)),
        ],
        out_shape=jax.ShapeDtypeStruct((blocks * rows, cols), BF16),
        compiler_params=PARAMS,
        name="finish",
    )(places, slots, core, total, expands, scale, mine, other, cosine, sine)


def ring_plan(parts, tokens, weights, scale, shrinks, expands, indices):
    rows, depth = tokens.shape
    tile = depth // 16
    me = lax.axis_index("tensor")
    owners_table = block_owners()
    send = lambda value, pairs: lax.ppermute(value, "tensor", pairs)
    swap = lambda value: send(value, [(i, i ^ 1) for i in range(parts)])
    out, home = ring_pairs((1, -1)), ring_pairs((-1, 1))

    half = depth // 2
    hs, counts = [], []
    streamed = depth - KEEP * tile

    def multiply(xs, total, ranked):
        total, h = block_product(xs, weights, factors, 0, depth, tile, total, sum(counts), ranked)
        hs.extend(h)
        counts.append(len(xs))
        return total

    streams = [send(tokens, out), None]
    own, raw = [tokens, swap(tokens)], [shrinks[0], swap(shrinks[0])]
    part = 2 * tile
    total, _ = block_product(own, weights, None, 0, part, tile, None, 0, False)
    second, total = lax.optimization_barrier((tokens, total))
    streams[1] = send(second, home)
    total, _ = block_product(own, weights, None, part, depth, tile, total, 0, False)
    factors = turn(raw)
    hs, total = lax.optimization_barrier(([some_ranks(tokens, factors)], total))
    counts.append(len(own))

    def make_tables(me, indices):
        segment_slot, cosine, sine = small_tables(*indices, parts * rows)
        owners = jnp.asarray(owners_table)[me]
        places = jnp.asarray(np.argsort(owners_table, axis=1).astype(np.int32))[me]
        slots = jnp.concatenate([segment_slot, jnp.stack([me, me ^ 1]).astype(jnp.int32)])
        core = (me % 2)[None].astype(jnp.int32)
        return owners, places, slots, core, segment_slot, cosine, sine

    blocks, hops = [], 2 * ROUNDS - 1
    totals = [total] * 2
    for hop in range(hops):
        arrived, _ = lax.optimization_barrier((streams[hop % 2], totals[hop if hop % 2 else hop + 1]))
        if hop + 2 < hops:
            streams[hop % 2] = send(arrived, home if hop % 2 else out)
        if hop % 2:
            late = [arrived, swap(arrived)]
            total = multiply(blocks, total, hop < hops - 2)
            blocks = late
        else:
            blocks += [arrived, swap(arrived)]
        if hop == hops - 3:
            early = [some_ranks(part, factors) for part in blocks[::2]]
            early, total = lax.optimization_barrier((early, total))
        if hop == hops - 2:
            hs += early
            last, _ = lax.optimization_barrier((arrived, total))
            hs.append(some_ranks(last, factors))
            hs, total = lax.optimization_barrier((hs, total))
        if hop == 3:
            known, total = lax.optimization_barrier((weights, total))
            kept, total = lax.optimization_barrier((keep_weights(known, streamed), total))
        if hop == 1:
            known, total = lax.optimization_barrier(((me, indices), total))
            tables, total = lax.optimization_barrier((make_tables(*known), total))
        totals.append(total)
    held = sum(counts)
    owners, places, slots, core, segment_slot, cosine, sine = tables
    h = rank_terms(owners, slots, blocks[2:3], factors, hs)
    beside = lambda step: send(h, [(i, i ^ step) for i in range(parts)])

    def last_product(low, high, total, **more):
        xs, _ = lax.optimization_barrier((blocks, h))
        return block_product(xs, weights, factors, low, high, tile, total, held, False, **more)[0]

    middle = streamed // (2 * tile) * tile
    near = [beside(step) for step in (2, 4, 6)]
    near, total = lax.optimization_barrier((near, last_product(0, middle, total, kept=kept)))
    h = h + near[0] + near[1] + near[2]
    far = [beside(step) for step in (8, 1, 9)]
    far, total = lax.optimization_barrier((far, last_product(middle, streamed, total, fresh=False)))
    mine, other = h + far[0], far[1] + far[2]
    return block_finish(places, segment_slot, core, total, expands, scale, mine, other, cosine, sine)


def body(parts, tokens, weight_codes, column_scale, shrink_store, expand_store, row_adapter, placement, document_lengths):
    rows = tokens.shape[0]
    total_rows = rows * parts
    shrinks = jnp.swapaxes(shrink_store, 1, 2)
    expands = jnp.swapaxes(expand_store, 1, 2)
    ring = parts == 2 * len(SNAKE) and rows % 16 == 0 and shrinks.shape[0] == 1 and total_rows % (2 * SEG) == 0
    ring = ring and shrinks.shape[1] == 64 and tokens.shape[1] % 2048 == 0
    plan = ring_plan if ring else gather_plan
    indices = (row_adapter, placement, document_lengths)
    return plan(parts, tokens, weight_codes, column_scale[None, :], shrinks, expands, indices)


def solution(mesh):
    placed = (
        P(("groups", "tensor"), None),
        P(None, "tensor"),
        P("tensor"),
        P(("groups", "tensor"), None, None),
        P("groups", "tensor", None),
        P("groups"),
        P("groups"),
        P("groups"),
    )
    return jax.shard_map(
        functools.partial(body, mesh.shape["tensor"]),
        mesh=mesh,
        in_specs=placed,
        out_specs=P("groups", "tensor"),
        check_vma=False,
    )
```

```python
import functools

import jax
import jax.numpy as jnp
import numpy as np
from jax import lax
from jax.experimental import pallas as pl
from jax.experimental.pallas import tpu as pltpu
from jax.sharding import PartitionSpec as P

HD = 128
SEG = 128
VMEM = 16 * 1024 * 1024
F32 = jnp.float32
BF16 = jnp.bfloat16
NT = (((1,), (1,)), ((), ()))
SLOTS = 4
CHUNK = 256
KEEP = 6
BIG_VMEM = 16 * 1024 * 1024
PARAMS = pltpu.CompilerParams(vmem_limit_bytes=VMEM)
SNAKE = (0, 2, 4, 6, 7, 5, 3, 1)
ROUNDS = len(SNAKE) // 2


def row_positions(document_lengths, total_rows):
    ends = jnp.cumsum(document_lengths)
    row_index = jnp.arange(total_rows, dtype=jnp.int32)
    passed = (row_index[:, None] >= ends[None, :]).astype(jnp.int32)
    return row_index - jnp.sum(passed * document_lengths[None, :], axis=1)


def rotary_tables(positions):
    half_size = HD // 2
    freq_index = jnp.arange(half_size, dtype=F32)
    inverse = jnp.exp(freq_index * (-2.0 / HD) * jnp.log(F32(500000.0)))
    angles = positions.astype(F32)[:, None] * inverse[None, :]
    cosine, sine = jnp.cos(angles), jnp.sin(angles)
    return jnp.concatenate([cosine, cosine], 1), jnp.concatenate([-sine, sine], 1)


def small_tables(row_adapter, placement, document_lengths, total_rows):
    segment_slot = placement[row_adapter[::SEG]]
    return segment_slot, *rotary_tables(row_positions(document_lengths, total_rows))


def rotate(value, cosine, sine):
    return value * cosine + pltpu.roll(value, HD // 2, 1) * sine


def shrink_kernel(x_ref, s_ref, h_out):
    @pl.when(pl.program_id(0) == 0)
    def _():
        h_out[...] = jnp.zeros_like(h_out)

    h_out[...] += lax.dot_general(x_ref[...], s_ref[...], NT, preferred_element_type=F32)


def shrink_all(x, shrink, tile):
    rows, depth = x.shape
    rank = shrink.shape[0]
    return pl.pallas_call(
        shrink_kernel,
        grid=(depth // tile,),
        in_specs=[
            pl.BlockSpec((rows, tile), lambda k: (0, k)),
            pl.BlockSpec((rank, tile), lambda k: (0, k)),
        ],
        out_specs=pl.BlockSpec((rows, rank), lambda k: (0, 0)),
        out_shape=jax.ShapeDtypeStruct((rows, rank), F32),
        compiler_params=PARAMS,
        name="shrink",
    )(x, shrink)


def project_kernel(x_ref, w_ref, acc_out):
    @pl.when(pl.program_id(0) == 0)
    def _():
        acc_out[...] = jnp.zeros_like(acc_out)

    acc_out[...] += jnp.dot(x_ref[...], w_ref[...], preferred_element_type=F32)


def project_all(x, weights, tile):
    rows, depth = x.shape
    cols = weights.shape[1]
    return pl.pallas_call(
        project_kernel,
        grid=(depth // tile,),
        in_specs=[
            pl.BlockSpec((rows, tile), lambda k: (0, k)),
            pl.BlockSpec((tile, cols), lambda k: (k, 0)),
        ],
        out_specs=pl.BlockSpec((rows, cols), lambda k: (0, 0)),
        out_shape=jax.ShapeDtypeStruct((rows, cols), F32),
        compiler_params=PARAMS,
        name="project",
    )(x, weights)


def segment_finish_kernel(acc_ref, scale_ref, h_ref, expand_ref, cos_ref, sin_ref, out_ref):
    update = jnp.dot(h_ref[...], expand_ref[0], preferred_element_type=F32)
    for head in range(out_ref.shape[1] // HD):
        cut = slice(head * HD, (head + 1) * HD)
        value = acc_ref[:, cut] * scale_ref[:, cut] + update[:, cut]
        out_ref[:, cut] = rotate(value, cos_ref[...], sin_ref[...]).astype(out_ref.dtype)


def segment_finish(acc, scale, h, expand, cosine, sine):
    rows, cols = acc.shape
    rank = h.shape[1]
    return pl.pallas_call(
        segment_finish_kernel,
        grid=(rows // SEG,),
        in_specs=[
            pl.BlockSpec((SEG, cols), lambda r: (r, 0)),
            pl.BlockSpec((1, cols), lambda r: (0, 0)),
            pl.BlockSpec((SEG, rank), lambda r: (r, 0)),
            pl.BlockSpec((1, rank, cols), lambda r: (r, 0, 0)),
            pl.BlockSpec((SEG, HD), lambda r: (r, 0)),
            pl.BlockSpec((SEG, HD), lambda r: (r, 0)),
        ],
        out_specs=pl.BlockSpec((SEG, cols), lambda r: (r, 0)),
        out_shape=jax.ShapeDtypeStruct((rows, cols), BF16),
        compiler_params=PARAMS,
        name="finish",
    )(acc, scale, h, expand, cosine, sine)


def spread(h, parts):
    step = 1
    while step < parts:
        h = h + lax.ppermute(h, "tensor", [(i, i ^ step) for i in range(parts)])
        step *= 2
    return h


def gather_plan(parts, tokens, weights, scale, shrinks, expands, indices):
    segment_slot, cosine, sine = small_tables(*indices, tokens.shape[0] * parts)
    held, rank, depth = shrinks.shape
    tile = depth // 16
    x = lax.all_gather(tokens, "tensor", axis=0, tiled=True)
    row_slot = jnp.repeat(segment_slot, SEG, total_repeat_length=x.shape[0])
    h = jnp.zeros((x.shape[0], rank), BF16)
    for i in range(held):
        mine = (row_slot == lax.axis_index("tensor") * held + i)[:, None]
        h = jnp.where(mine, shrink_all(x, shrinks[i], tile).astype(BF16), h)
    h = spread(h, parts)
    acc = project_all(x, weights, tile)
    return segment_finish(acc, scale, h, expands[segment_slot], cosine, sine)


def block_owners():
    chips = len(SNAKE)
    owners = np.zeros((2 * chips, 2 * chips), np.int32)
    for place, chip in enumerate(SNAKE):
        for core in (0, 1):
            row = [2 * chip + core, 2 * chip + 1 - core]
            for r in range(1, ROUNDS + 1):
                far, near = place - r * (1 - 2 * core), place + r * (1 - 2 * core)
                far, near = 2 * SNAKE[far % chips], 2 * SNAKE[near % chips]
                row += [far + core, near + 1 - core]
                if r < ROUNDS:
                    row += [near + core, far + 1 - core]
            owners[2 * chip + core] = row
    return owners


def ring_pairs(ways):
    chips = len(SNAKE)
    pairs = []
    for place, chip in enumerate(SNAKE):
        for core in (0, 1):
            pairs.append((2 * chip + core, 2 * SNAKE[(place + ways[core]) % chips] + core))
    return pairs


def block_kernel(count, low, tile, steps, kept, first, base, fresh, ranked, *refs):
    xs, w_ref, refs = refs[:count], refs[count], refs[count + 1 :]
    if ranked:
        s_ref, refs = refs[0], refs[1:]
    if kept:
        w_kept, refs = refs[0], refs[1:]
    if not first:
        refs = refs[1:]
    total, refs = refs[0], refs[1:]
    if ranked:
        h_out, refs = refs[0], refs[1:]
    x_slots, w_slots, s_slots, sems = refs
    here = slice(base, base + count)
    rows = xs[0].shape[0]

    def copies(step):
        slot = lax.rem(step, SLOTS)
        at = low + step * tile
        if kept:
            at = jnp.where(step < kept, w_ref.shape[0], low) + (step - kept) * tile
        at = pl.multiple_of(at, tile)
        out = []
        for i in range(count):
            cut = xs[i].at[:, pl.ds(at, tile)]
            out.append(pltpu.make_async_copy(cut, x_slots.at[slot, pl.ds(i * rows, rows)], sems.at[slot, i]))
        if ranked:
            cut = s_ref.at[pl.ds(at, tile)]
            out.append(pltpu.make_async_copy(cut, s_slots.at[slot], sems.at[slot, count + 1]))
        return out

    def weights(index):
        slot = lax.rem(index, SLOTS)
        cut = w_ref.at[pl.ds(pl.multiple_of(low + index * tile, tile), tile)]
        return pltpu.make_async_copy(cut, w_slots.at[slot], sems.at[slot, count])

    def start(step):
        for copy in copies(step):
            copy.start()

    for step in range(min(SLOTS, steps)):
        if step < steps - kept:
            weights(jnp.int32(step)).start()
        start(jnp.int32(step))
    if fresh:
        total[here] = jnp.zeros((count,) + total.shape[1:], F32)
    if ranked:
        h_out[...] = jnp.zeros_like(h_out)

    def take(step, weight):
        slot = lax.rem(step, SLOTS)
        x = x_slots[slot]
        for left in range(0, total.shape[2], CHUNK):
            cut = slice(left, left + CHUNK)
            product = jnp.dot(x, weight(cut), preferred_element_type=F32)
            total[here, :, cut] += product.reshape(count, rows, CHUNK)
        if ranked:
            mine = jnp.concatenate([x[i * rows : (i + 1) * rows] for i in range(0, count, 2)], 0)
            h_out[...] += jnp.dot(mine, s_slots[slot], preferred_element_type=F32)

    if kept:
        @pl.loop(0, kept)
        def _(step):
            for copy in copies(step):
                copy.wait()
            take(step, lambda cut: w_kept[pl.ds(pl.multiple_of(step * tile, tile), tile), cut])

            @pl.when(step + SLOTS < steps)
            def _():
                start(step + SLOTS)

    @pl.loop(kept, steps)
    def _(step):
        index = step - kept
        for copy in [weights(index)] + copies(step):
            copy.wait()
        take(step, lambda cut: w_slots[lax.rem(index, SLOTS), :, cut])

        @pl.when(step + SLOTS < steps)
        def _():
            weights(index + SLOTS).start()
            start(step + SLOTS)


def block_product(xs, weights, factors, low, high, tile, total, base, ranked, fresh=None, kept=None):
    count = len(xs)
    rows = xs[0].shape[0]
    cols = weights.shape[1]
    rank = factors.shape[1] if ranked else 128
    fresh, first = low == 0 if fresh is None else fresh, total is None
    anywhere, whole = pl.BlockSpec(memory_space=pl.ANY), pl.BlockSpec(memory_space=pltpu.VMEM)
    operands = list(xs) + [weights]
    specs = [anywhere] * (count + 1)
    if ranked:
        operands.append(factors)
        specs.append(anywhere)
    kept_steps = 0
    if kept is not None:
        operands.append(kept)
        specs.append(whole)
        kept_steps = kept.shape[0] // tile
    aliases = {}
    if not first:
        aliases = {len(operands): 0}
        operands.append(total)
        specs.append(whole)
    outs, out_specs = [jax.ShapeDtypeStruct(total_shape(rows, cols), F32)], [whole]
    if ranked:
        outs.append(jax.ShapeDtypeStruct((count // 2 * rows, rank), F32))
        out_specs.append(whole)
    steps = (high - low) // tile + kept_steps
    result = pl.pallas_call(
        functools.partial(block_kernel, count, low, tile, steps, kept_steps, first, base, fresh, ranked),
        in_specs=specs,
        out_specs=out_specs,
        out_shape=outs,
        scratch_shapes=[
            pltpu.VMEM((SLOTS, count * rows, tile), BF16),
            pltpu.VMEM((SLOTS, tile, cols), BF16),
            pltpu.VMEM((SLOTS, tile, rank), BF16),
            pltpu.SemaphoreType.DMA((SLOTS, count + 2)),
        ],
        input_output_aliases=aliases,
        compiler_params=pltpu.CompilerParams(vmem_limit_bytes=BIG_VMEM),
        cost_estimate=pl.CostEstimate(
            flops=2 * count * rows * (high - low) * cols,
            bytes_accessed=2 * (high - low) * cols,
            transcendentals=0,
        ),
        name="blocks",
    )(*operands)
    return result[0], result[1:]


def keep_kernel(low, w_ref, out_ref, sem):
    copy = pltpu.make_async_copy(w_ref.at[pl.ds(low, out_ref.shape[0])], out_ref, sem)
    copy.start()
    copy.wait()


def keep_weights(weights, low):
    depth, cols = weights.shape
    return pl.pallas_call(
        functools.partial(keep_kernel, low),
        in_specs=[pl.BlockSpec(memory_space=pl.ANY)],
        out_specs=pl.BlockSpec(memory_space=pltpu.VMEM),
        out_shape=jax.ShapeDtypeStruct((depth - low, cols), weights.dtype),
        scratch_shapes=[pltpu.SemaphoreType.DMA],
        compiler_params=PARAMS,
        name="keep",
    )(weights)


def total_shape(rows, cols):
    return (2 * len(SNAKE), rows, cols)


def turn_kernel(a_ref, b_ref, out_ref):
    width = 2 * a_ref.shape[0]
    together = 16

    @pl.loop(0, a_ref.shape[1] // (width * together))
    def _(step):
        for i in range(together):
            cut = pl.ds(pl.multiple_of((step * together + i) * width, width), width)
            both = jnp.concatenate([a_ref[:, cut], b_ref[:, cut]], 0)
            out_ref[cut, :] = both.T


def turn(factors):
    rank, depth = factors[0].shape
    whole = pl.BlockSpec(memory_space=pltpu.VMEM)
    return pl.pallas_call(
        turn_kernel,
        in_specs=[whole] * 2,
        out_specs=whole,
        out_shape=jax.ShapeDtypeStruct((depth, 2 * rank), BF16),
        compiler_params=PARAMS,
        name="turn",
    )(*factors)


def some_ranks_kernel(x_ref, s_ref, out_ref):
    out_ref[...] = jnp.dot(x_ref[...], s_ref[...], preferred_element_type=F32)


def some_ranks(x, factors):
    whole = pl.BlockSpec(memory_space=pltpu.VMEM)
    return pl.pallas_call(
        some_ranks_kernel,
        in_specs=[whole] * 2,
        out_specs=whole,
        out_shape=jax.ShapeDtypeStruct((x.shape[0], factors.shape[1]), F32),
        compiler_params=PARAMS,
        name="some_ranks",
    )(x, factors)


def rank_kernel(count, owners_ref, slot_ref, *refs):
    xs, refs = refs[:count], refs[count:]
    s_ref, h_refs, out_ref, placed = refs[0], refs[1:-2], refs[-2], refs[-1]
    rows, rank = xs[0].shape[0], s_ref.shape[1] // 2
    x = jnp.concatenate([ref[...] for ref in xs], 0)
    last = jnp.dot(x, s_ref[...], preferred_element_type=F32)
    segments = slot_ref.shape[0] - 2
    block = 0
    for source in h_refs + (last,):
        for low in range(0, source.shape[0], rows):
            owner = owners_ref[2 * block]
            segment = owner * rows // SEG
            after = jnp.minimum(segment + 1, segments - 1)
            row = owner * rows + lax.broadcasted_iota(jnp.int32, (rows, rank), 0)
            slot = jnp.where(row < (segment + 1) * SEG, slot_ref[segment], slot_ref[after])
            terms = jnp.where(slot == slot_ref[segments + 1], source[low : low + rows, rank:], 0.0)
            terms = jnp.where(slot == slot_ref[segments], source[low : low + rows, :rank], terms)
            placed[pl.ds(pl.multiple_of(owner // 2 * rows, 16), rows), :] = terms
            block += 1
    half = placed.shape[0] // 2
    out_ref[...] = jnp.concatenate([placed[:half, :], placed[half:, :]], 1).astype(out_ref.dtype)


def rank_terms(owners, slots, xs, factors, hs):
    rank = factors.shape[1] // 2
    core_rows = owners.shape[0] // 2 * xs[0].shape[0]
    scalars, whole = pl.BlockSpec(memory_space=pltpu.SMEM), pl.BlockSpec(memory_space=pltpu.VMEM)
    return pl.pallas_call(
        functools.partial(rank_kernel, len(xs)),
        in_specs=[scalars] * 2 + [whole] * (len(xs) + 1 + len(hs)),
        out_specs=whole,
        scratch_shapes=[pltpu.VMEM((core_rows, rank), F32)],
        out_shape=jax.ShapeDtypeStruct((core_rows // 2, 2 * rank), BF16),
        compiler_params=PARAMS,
        name="ranks",
    )(owners, slots, *xs, factors, *hs)


def block_finish_kernel(places_ref, slot_ref, core_ref, total_ref, expand_ref, scale_ref, mine_ref, other_ref, *refs):
    cos_ref, sin_ref, out_ref, h, update, done, sems = refs
    blocks, rows, cols = total_ref.shape
    rank = mine_ref.shape[1] // 2
    even = core_ref[0] == 0
    mine, other = mine_ref[...], other_ref[...]
    for core, terms in enumerate((jnp.where(even, mine, other), jnp.where(even, other, mine))):
        for chip in range(blocks // 2):
            side, at = divmod(chip * rows, terms.shape[0])
            to = (2 * chip + core) * rows
            h[to : to + rows, :] = terms[at : at + rows, side * rank : (side + 1) * rank]
    for segment in range(h.shape[0] // SEG):
        cut = slice(segment * SEG, (segment + 1) * SEG)
        expand = expand_ref[slot_ref[segment]]
        update[cut, :] = jnp.dot(h[cut, :], expand, preferred_element_type=F32)
    copies = []
    for block in range(blocks):
        at = slice(block * rows, (block + 1) * rows)
        cosine, sine = cos_ref[at, :], sin_ref[at, :]
        place = places_ref[block]
        for left in range(0, cols, HD):
            cut = slice(left, left + HD)
            value = total_ref[place, :, cut] * scale_ref[:, cut] + update[at, cut]
            done[at, cut] = rotate(value, cosine, sine).astype(done.dtype)
        if block % 2:
            strip = pl.ds((block - 1) * rows, 2 * rows)
            copies.append(pltpu.make_async_copy(done.at[strip], out_ref.at[strip], sems.at[block // 2]))
            copies[-1].start()
    for copy in copies:
        copy.wait()


def block_finish(places, slots, core, total, expands, scale, mine, other, cosine, sine):
    blocks, rows, cols = total.shape
    rank = expands.shape[1]
    scalars, whole = pl.BlockSpec(memory_space=pltpu.SMEM), pl.BlockSpec(memory_space=pltpu.VMEM)
    return pl.pallas_call(
        block_finish_kernel,
        in_specs=[scalars] * 3 + [whole] * 7,
        out_specs=pl.BlockSpec(memory_space=pl.ANY),
        scratch_shapes=[
            pltpu.VMEM((blocks * rows, rank), BF16),
            pltpu.VMEM((blocks * rows, cols), F32),
            pltpu.VMEM((blocks * rows, cols), BF16),
            pltpu.SemaphoreType.DMA((blocks // 2,)),
        ],
        out_shape=jax.ShapeDtypeStruct((blocks * rows, cols), BF16),
        compiler_params=PARAMS,
        name="finish",
    )(places, slots, core, total, expands, scale, mine, other, cosine, sine)


def ring_plan(parts, tokens, weights, scale, shrinks, expands, indices):
    rows, depth = tokens.shape
    tile = depth // 16
    me = lax.axis_index("tensor")
    owners_table = block_owners()
    send = lambda value, pairs: lax.ppermute(value, "tensor", pairs)
    swap = lambda value: send(value, [(i, i ^ 1) for i in range(parts)])
    out, home = ring_pairs((1, -1)), ring_pairs((-1, 1))

    half = depth // 2
    hs, counts = [], []
    streamed = depth - KEEP * tile

    def multiply(xs, total, ranked):
        total, h = block_product(xs, weights, factors, 0, depth, tile, total, sum(counts), ranked)
        hs.extend(h)
        counts.append(len(xs))
        return total

    streams = [send(tokens, out), None]
    own, raw = [tokens, swap(tokens)], [shrinks[0], swap(shrinks[0])]
    part = 2 * tile
    total, _ = block_product(own, weights, None, 0, part, tile, None, 0, False)
    second, total = lax.optimization_barrier((tokens, total))
    streams[1] = send(second, home)
    total, _ = block_product(own, weights, None, part, depth, tile, total, 0, False)
    factors = turn(raw)
    hs, total = lax.optimization_barrier(([some_ranks(tokens, factors)], total))
    counts.append(len(own))

    def make_tables(me, indices):
        segment_slot, cosine, sine = small_tables(*indices, parts * rows)
        owners = jnp.asarray(owners_table)[me]
        places = jnp.asarray(np.argsort(owners_table, axis=1).astype(np.int32))[me]
        slots = jnp.concatenate([segment_slot, jnp.stack([me, me ^ 1]).astype(jnp.int32)])
        core = (me % 2)[None].astype(jnp.int32)
        return owners, places, slots, core, segment_slot, cosine, sine

    blocks, hops = [], 2 * ROUNDS - 1
    totals = [total] * 2
    for hop in range(hops):
        arrived, _ = lax.optimization_barrier((streams[hop % 2], totals[hop if hop % 2 else hop + 1]))
        if hop + 2 < hops:
            streams[hop % 2] = send(arrived, home if hop % 2 else out)
        if hop % 2:
            late = [arrived, swap(arrived)]
            total = multiply(blocks, total, hop < hops - 2)
            blocks = late
        else:
            blocks += [arrived, swap(arrived)]
        if hop == hops - 3:
            early = [some_ranks(part, factors) for part in blocks[::2]]
            early, total = lax.optimization_barrier((early, total))
        if hop == hops - 2:
            hs += early
            last, _ = lax.optimization_barrier((arrived, total))
            hs.append(some_ranks(last, factors))
            hs, total = lax.optimization_barrier((hs, total))
        if hop == 3:
            known, total = lax.optimization_barrier((weights, total))
            kept, total = lax.optimization_barrier((keep_weights(known, streamed), total))
        if hop == 1:
            known, total = lax.optimization_barrier(((me, indices), total))
            tables, total = lax.optimization_barrier((make_tables(*known), total))
        totals.append(total)
    held = sum(counts)
    owners, places, slots, core, segment_slot, cosine, sine = tables
    h = rank_terms(owners, slots, blocks[2:3], factors, hs)
    beside = lambda step: send(h, [(i, i ^ step) for i in range(parts)])

    def last_product(low, high, total, **more):
        xs, _ = lax.optimization_barrier((blocks, h))
        return block_product(xs, weights, factors, low, high, tile, total, held, False, **more)[0]

    middle = streamed // (2 * tile) * tile
    near = [beside(step) for step in (2, 4, 6)]
    near, total = lax.optimization_barrier((near, last_product(0, middle, total, kept=kept)))
    h = h + near[0] + near[1] + near[2]
    far = [beside(step) for step in (8, 1, 9)]
    far, total = lax.optimization_barrier((far, last_product(middle, streamed, total, fresh=False)))
    mine, other = h + far[0], far[1] + far[2]
    return block_finish(places, segment_slot, core, total, expands, scale, mine, other, cosine, sine)


def body(parts, tokens, weight_codes, column_scale, shrink_store, expand_store, row_adapter, placement, document_lengths):
    rows = tokens.shape[0]
    total_rows = rows * parts
    shrinks = jnp.swapaxes(shrink_store, 1, 2)
    expands = jnp.swapaxes(expand_store, 1, 2)
    ring = parts == 2 * len(SNAKE) and rows % 16 == 0 and shrinks.shape[0] == 1 and total_rows % (2 * SEG) == 0
    ring = ring and shrinks.shape[1] == 64 and tokens.shape[1] % 2048 == 0
    plan = ring_plan if ring else gather_plan
    indices = (row_adapter, placement, document_lengths)
    return plan(parts, tokens, weight_codes, column_scale[None, :], shrinks, expands, indices)


def solution(mesh):
    placed = (
        P(("groups", "tensor"), None),
        P(None, "tensor"),
        P("tensor"),
        P(("groups", "tensor"), None, None),
        P("groups", "tensor", None),
        P("groups"),
        P("groups"),
        P("groups"),
    )
    return jax.shard_map(
        functools.partial(body, mesh.shape["tensor"]),
        mesh=mesh,
        in_specs=placed,
        out_specs=P("groups", "tensor"),
        check_vma=False,
    )
```

```python
import functools

import jax
import jax.numpy as jnp
import numpy as np
from jax import lax
from jax.experimental import pallas as pl
from jax.experimental.pallas import tpu as pltpu
from jax.sharding import PartitionSpec as P

HD = 128
SEG = 128
VMEM = 16 * 1024 * 1024
F32 = jnp.float32
BF16 = jnp.bfloat16
NT = (((1,), (1,)), ((), ()))
SLOTS = 4
CHUNK = 256
KEEP = 8
BIG_VMEM = 16 * 1024 * 1024
PARAMS = pltpu.CompilerParams(vmem_limit_bytes=VMEM)
SNAKE = (0, 2, 4, 6, 7, 5, 3, 1)
ROUNDS = len(SNAKE) // 2


def row_positions(document_lengths, total_rows):
    ends = jnp.cumsum(document_lengths)
    row_index = jnp.arange(total_rows, dtype=jnp.int32)
    passed = (row_index[:, None] >= ends[None, :]).astype(jnp.int32)
    return row_index - jnp.sum(passed * document_lengths[None, :], axis=1)


def rotary_tables(positions):
    half_size = HD // 2
    freq_index = jnp.arange(half_size, dtype=F32)
    inverse = jnp.exp(freq_index * (-2.0 / HD) * jnp.log(F32(500000.0)))
    angles = positions.astype(F32)[:, None] * inverse[None, :]
    cosine, sine = jnp.cos(angles), jnp.sin(angles)
    return jnp.concatenate([cosine, cosine], 1), jnp.concatenate([-sine, sine], 1)


def small_tables(row_adapter, placement, document_lengths, total_rows):
    segment_slot = placement[row_adapter[::SEG]]
    return segment_slot, *rotary_tables(row_positions(document_lengths, total_rows))


def rotate(value, cosine, sine):
    return value * cosine + pltpu.roll(value, HD // 2, 1) * sine


def shrink_kernel(x_ref, s_ref, h_out):
    @pl.when(pl.program_id(0) == 0)
    def _():
        h_out[...] = jnp.zeros_like(h_out)

    h_out[...] += lax.dot_general(x_ref[...], s_ref[...], NT, preferred_element_type=F32)


def shrink_all(x, shrink, tile):
    rows, depth = x.shape
    rank = shrink.shape[0]
    return pl.pallas_call(
        shrink_kernel,
        grid=(depth // tile,),
        in_specs=[
            pl.BlockSpec((rows, tile), lambda k: (0, k)),
            pl.BlockSpec((rank, tile), lambda k: (0, k)),
        ],
        out_specs=pl.BlockSpec((rows, rank), lambda k: (0, 0)),
        out_shape=jax.ShapeDtypeStruct((rows, rank), F32),
        compiler_params=PARAMS,
        name="shrink",
    )(x, shrink)


def project_kernel(x_ref, w_ref, acc_out):
    @pl.when(pl.program_id(0) == 0)
    def _():
        acc_out[...] = jnp.zeros_like(acc_out)

    acc_out[...] += jnp.dot(x_ref[...], w_ref[...], preferred_element_type=F32)


def project_all(x, weights, tile):
    rows, depth = x.shape
    cols = weights.shape[1]
    return pl.pallas_call(
        project_kernel,
        grid=(depth // tile,),
        in_specs=[
            pl.BlockSpec((rows, tile), lambda k: (0, k)),
            pl.BlockSpec((tile, cols), lambda k: (k, 0)),
        ],
        out_specs=pl.BlockSpec((rows, cols), lambda k: (0, 0)),
        out_shape=jax.ShapeDtypeStruct((rows, cols), F32),
        compiler_params=PARAMS,
        name="project",
    )(x, weights)


def segment_finish_kernel(acc_ref, scale_ref, h_ref, expand_ref, cos_ref, sin_ref, out_ref):
    update = jnp.dot(h_ref[...], expand_ref[0], preferred_element_type=F32)
    for head in range(out_ref.shape[1] // HD):
        cut = slice(head * HD, (head + 1) * HD)
        value = acc_ref[:, cut] * scale_ref[:, cut] + update[:, cut]
        out_ref[:, cut] = rotate(value, cos_ref[...], sin_ref[...]).astype(out_ref.dtype)


def segment_finish(acc, scale, h, expand, cosine, sine):
    rows, cols = acc.shape
    rank = h.shape[1]
    return pl.pallas_call(
        segment_finish_kernel,
        grid=(rows // SEG,),
        in_specs=[
            pl.BlockSpec((SEG, cols), lambda r: (r, 0)),
            pl.BlockSpec((1, cols), lambda r: (0, 0)),
            pl.BlockSpec((SEG, rank), lambda r: (r, 0)),
            pl.BlockSpec((1, rank, cols), lambda r: (r, 0, 0)),
            pl.BlockSpec((SEG, HD), lambda r: (r, 0)),
            pl.BlockSpec((SEG, HD), lambda r: (r, 0)),
        ],
        out_specs=pl.BlockSpec((SEG, cols), lambda r: (r, 0)),
        out_shape=jax.ShapeDtypeStruct((rows, cols), BF16),
        compiler_params=PARAMS,
        name="finish",
    )(acc, scale, h, expand, cosine, sine)


def spread(h, parts):
    step = 1
    while step < parts:
        h = h + lax.ppermute(h, "tensor", [(i, i ^ step) for i in range(parts)])
        step *= 2
    return h


def gather_plan(parts, tokens, weights, scale, shrinks, expands, indices):
    segment_slot, cosine, sine = small_tables(*indices, tokens.shape[0] * parts)
    held, rank, depth = shrinks.shape
    tile = depth // 16
    x = lax.all_gather(tokens, "tensor", axis=0, tiled=True)
    row_slot = jnp.repeat(segment_slot, SEG, total_repeat_length=x.shape[0])
    h = jnp.zeros((x.shape[0], rank), BF16)
    for i in range(held):
        mine = (row_slot == lax.axis_index("tensor") * held + i)[:, None]
        h = jnp.where(mine, shrink_all(x, shrinks[i], tile).astype(BF16), h)
    h = spread(h, parts)
    acc = project_all(x, weights, tile)
    return segment_finish(acc, scale, h, expands[segment_slot], cosine, sine)


def block_owners():
    chips = len(SNAKE)
    owners = np.zeros((2 * chips, 2 * chips), np.int32)
    for place, chip in enumerate(SNAKE):
        for core in (0, 1):
            row = [2 * chip + core, 2 * chip + 1 - core]
            for r in range(1, ROUNDS + 1):
                far, near = place - r * (1 - 2 * core), place + r * (1 - 2 * core)
                far, near = 2 * SNAKE[far % chips], 2 * SNAKE[near % chips]
                row += [far + core, near + 1 - core]
                if r < ROUNDS:
                    row += [near + core, far + 1 - core]
            owners[2 * chip + core] = row
    return owners


def ring_pairs(ways):
    chips = len(SNAKE)
    pairs = []
    for place, chip in enumerate(SNAKE):
        for core in (0, 1):
            pairs.append((2 * chip + core, 2 * SNAKE[(place + ways[core]) % chips] + core))
    return pairs


def block_kernel(count, low, tile, steps, kept, first, base, fresh, ranked, *refs):
    xs, w_ref, refs = refs[:count], refs[count], refs[count + 1 :]
    if ranked:
        s_ref, refs = refs[0], refs[1:]
    if kept:
        w_kept, refs = refs[0], refs[1:]
    if not first:
        refs = refs[1:]
    total, refs = refs[0], refs[1:]
    if ranked:
        h_out, refs = refs[0], refs[1:]
    x_slots, w_slots, s_slots, sems = refs
    here = slice(base, base + count)
    rows = xs[0].shape[0]

    def copies(step):
        slot = lax.rem(step, SLOTS)
        at = low + step * tile
        if kept:
            at = jnp.where(step < kept, w_ref.shape[0], low) + (step - kept) * tile
        at = pl.multiple_of(at, tile)
        out = []
        for i in range(count):
            cut = xs[i].at[:, pl.ds(at, tile)]
            out.append(pltpu.make_async_copy(cut, x_slots.at[slot, pl.ds(i * rows, rows)], sems.at[slot, i]))
        if ranked:
            cut = s_ref.at[pl.ds(at, tile)]
            out.append(pltpu.make_async_copy(cut, s_slots.at[slot], sems.at[slot, count + 1]))
        return out

    def weights(index):
        slot = lax.rem(index, SLOTS)
        cut = w_ref.at[pl.ds(pl.multiple_of(low + index * tile, tile), tile)]
        return pltpu.make_async_copy(cut, w_slots.at[slot], sems.at[slot, count])

    def start(step):
        for copy in copies(step):
            copy.start()

    for step in range(min(SLOTS, steps)):
        if step < steps - kept:
            weights(jnp.int32(step)).start()
        start(jnp.int32(step))
    if fresh:
        total[here] = jnp.zeros((count,) + total.shape[1:], F32)
    if ranked:
        h_out[...] = jnp.zeros_like(h_out)

    def take(step, weight):
        slot = lax.rem(step, SLOTS)
        x = x_slots[slot]
        for left in range(0, total.shape[2], CHUNK):
            cut = slice(left, left + CHUNK)
            product = jnp.dot(x, weight(cut), preferred_element_type=F32)
            total[here, :, cut] += product.reshape(count, rows, CHUNK)
        if ranked:
            mine = jnp.concatenate([x[i * rows : (i + 1) * rows] for i in range(0, count, 2)], 0)
            h_out[...] += jnp.dot(mine, s_slots[slot], preferred_element_type=F32)

    if kept:
        @pl.loop(0, kept)
        def _(step):
            for copy in copies(step):
                copy.wait()
            take(step, lambda cut: w_kept[pl.ds(pl.multiple_of(step * tile, tile), tile), cut])

            @pl.when(step + SLOTS < steps)
            def _():
                start(step + SLOTS)

    @pl.loop(kept, steps)
    def _(step):
        index = step - kept
        for copy in [weights(index)] + copies(step):
            copy.wait()
        take(step, lambda cut: w_slots[lax.rem(index, SLOTS), :, cut])

        @pl.when(step + SLOTS < steps)
        def _():
            weights(index + SLOTS).start()
            start(step + SLOTS)


def block_product(xs, weights, factors, low, high, tile, total, base, ranked, fresh=None, kept=None):
    count = len(xs)
    rows = xs[0].shape[0]
    cols = weights.shape[1]
    rank = factors.shape[1] if ranked else 128
    fresh, first = low == 0 if fresh is None else fresh, total is None
    anywhere, whole = pl.BlockSpec(memory_space=pl.ANY), pl.BlockSpec(memory_space=pltpu.VMEM)
    operands = list(xs) + [weights]
    specs = [anywhere] * (count + 1)
    if ranked:
        operands.append(factors)
        specs.append(anywhere)
    kept_steps = 0
    if kept is not None:
        operands.append(kept)
        specs.append(whole)
        kept_steps = kept.shape[0] // tile
    aliases = {}
    if not first:
        aliases = {len(operands): 0}
        operands.append(total)
        specs.append(whole)
    outs, out_specs = [jax.ShapeDtypeStruct(total_shape(rows, cols), F32)], [whole]
    if ranked:
        outs.append(jax.ShapeDtypeStruct((count // 2 * rows, rank), F32))
        out_specs.append(whole)
    steps = (high - low) // tile + kept_steps
    result = pl.pallas_call(
        functools.partial(block_kernel, count, low, tile, steps, kept_steps, first, base, fresh, ranked),
        in_specs=specs,
        out_specs=out_specs,
        out_shape=outs,
        scratch_shapes=[
            pltpu.VMEM((SLOTS, count * rows, tile), BF16),
            pltpu.VMEM((SLOTS, tile, cols), BF16),
            pltpu.VMEM((SLOTS, tile, rank), BF16),
            pltpu.SemaphoreType.DMA((SLOTS, count + 2)),
        ],
        input_output_aliases=aliases,
        compiler_params=pltpu.CompilerParams(vmem_limit_bytes=BIG_VMEM),
        cost_estimate=pl.CostEstimate(
            flops=2 * count * rows * (high - low) * cols,
            bytes_accessed=2 * (high - low) * cols,
            transcendentals=0,
        ),
        name="blocks",
    )(*operands)
    return result[0], result[1:]


def keep_kernel(low, w_ref, out_ref, sem):
    copy = pltpu.make_async_copy(w_ref.at[pl.ds(low, out_ref.shape[0])], out_ref, sem)
    copy.start()
    copy.wait()


def keep_weights(weights, low):
    depth, cols = weights.shape
    return pl.pallas_call(
        functools.partial(keep_kernel, low),
        in_specs=[pl.BlockSpec(memory_space=pl.ANY)],
        out_specs=pl.BlockSpec(memory_space=pltpu.VMEM),
        out_shape=jax.ShapeDtypeStruct((depth - low, cols), weights.dtype),
        scratch_shapes=[pltpu.SemaphoreType.DMA],
        compiler_params=PARAMS,
        name="keep",
    )(weights)


def total_shape(rows, cols):
    return (2 * len(SNAKE), rows, cols)


def turn_kernel(a_ref, b_ref, out_ref):
    width = 2 * a_ref.shape[0]
    together = 16

    @pl.loop(0, a_ref.shape[1] // (width * together))
    def _(step):
        for i in range(together):
            cut = pl.ds(pl.multiple_of((step * together + i) * width, width), width)
            both = jnp.concatenate([a_ref[:, cut], b_ref[:, cut]], 0)
            out_ref[cut, :] = both.T


def turn(factors):
    rank, depth = factors[0].shape
    whole = pl.BlockSpec(memory_space=pltpu.VMEM)
    return pl.pallas_call(
        turn_kernel,
        in_specs=[whole] * 2,
        out_specs=whole,
        out_shape=jax.ShapeDtypeStruct((depth, 2 * rank), BF16),
        compiler_params=PARAMS,
        name="turn",
    )(*factors)


def some_ranks_kernel(x_ref, s_ref, out_ref):
    out_ref[...] = jnp.dot(x_ref[...], s_ref[...], preferred_element_type=F32)


def some_ranks(x, factors):
    whole = pl.BlockSpec(memory_space=pltpu.VMEM)
    return pl.pallas_call(
        some_ranks_kernel,
        in_specs=[whole] * 2,
        out_specs=whole,
        out_shape=jax.ShapeDtypeStruct((x.shape[0], factors.shape[1]), F32),
        compiler_params=PARAMS,
        name="some_ranks",
    )(x, factors)


def rank_kernel(count, owners_ref, slot_ref, *refs):
    xs, refs = refs[:count], refs[count:]
    s_ref, h_refs, out_ref, placed = refs[0], refs[1:-2], refs[-2], refs[-1]
    rows, rank = xs[0].shape[0], s_ref.shape[1] // 2
    x = jnp.concatenate([ref[...] for ref in xs], 0)
    last = jnp.dot(x, s_ref[...], preferred_element_type=F32)
    segments = slot_ref.shape[0] - 2
    block = 0
    for source in h_refs + (last,):
        for low in range(0, source.shape[0], rows):
            owner = owners_ref[2 * block]
            segment = owner * rows // SEG
            after = jnp.minimum(segment + 1, segments - 1)
            row = owner * rows + lax.broadcasted_iota(jnp.int32, (rows, rank), 0)
            slot = jnp.where(row < (segment + 1) * SEG, slot_ref[segment], slot_ref[after])
            terms = jnp.where(slot == slot_ref[segments + 1], source[low : low + rows, rank:], 0.0)
            terms = jnp.where(slot == slot_ref[segments], source[low : low + rows, :rank], terms)
            placed[pl.ds(pl.multiple_of(owner // 2 * rows, 16), rows), :] = terms
            block += 1
    half = placed.shape[0] // 2
    out_ref[...] = jnp.concatenate([placed[:half, :], placed[half:, :]], 1).astype(out_ref.dtype)


def rank_terms(owners, slots, xs, factors, hs):
    rank = factors.shape[1] // 2
    core_rows = owners.shape[0] // 2 * xs[0].shape[0]
    scalars, whole = pl.BlockSpec(memory_space=pltpu.SMEM), pl.BlockSpec(memory_space=pltpu.VMEM)
    return pl.pallas_call(
        functools.partial(rank_kernel, len(xs)),
        in_specs=[scalars] * 2 + [whole] * (len(xs) + 1 + len(hs)),
        out_specs=whole,
        scratch_shapes=[pltpu.VMEM((core_rows, rank), F32)],
        out_shape=jax.ShapeDtypeStruct((core_rows // 2, 2 * rank), BF16),
        compiler_params=PARAMS,
        name="ranks",
    )(owners, slots, *xs, factors, *hs)


def block_finish_kernel(places_ref, slot_ref, core_ref, total_ref, expand_ref, scale_ref, mine_ref, other_ref, *refs):
    cos_ref, sin_ref, out_ref, h, update, done, sems = refs
    blocks, rows, cols = total_ref.shape
    rank = mine_ref.shape[1] // 2
    even = core_ref[0] == 0
    mine, other = mine_ref[...], other_ref[...]
    for core, terms in enumerate((jnp.where(even, mine, other), jnp.where(even, other, mine))):
        for chip in range(blocks // 2):
            side, at = divmod(chip * rows, terms.shape[0])
            to = (2 * chip + core) * rows
            h[to : to + rows, :] = terms[at : at + rows, side * rank : (side + 1) * rank]
    for segment in range(h.shape[0] // SEG):
        cut = slice(segment * SEG, (segment + 1) * SEG)
        expand = expand_ref[slot_ref[segment]]
        update[cut, :] = jnp.dot(h[cut, :], expand, preferred_element_type=F32)
    copies = []
    for block in range(blocks):
        at = slice(block * rows, (block + 1) * rows)
        cosine, sine = cos_ref[at, :], sin_ref[at, :]
        place = places_ref[block]
        for left in range(0, cols, HD):
            cut = slice(left, left + HD)
            value = total_ref[place, :, cut] * scale_ref[:, cut] + update[at, cut]
            done[at, cut] = rotate(value, cosine, sine).astype(done.dtype)
        if block % 2:
            strip = pl.ds((block - 1) * rows, 2 * rows)
            copies.append(pltpu.make_async_copy(done.at[strip], out_ref.at[strip], sems.at[block // 2]))
            copies[-1].start()
    for copy in copies:
        copy.wait()


def block_finish(places, slots, core, total, expands, scale, mine, other, cosine, sine):
    blocks, rows, cols = total.shape
    rank = expands.shape[1]
    scalars, whole = pl.BlockSpec(memory_space=pltpu.SMEM), pl.BlockSpec(memory_space=pltpu.VMEM)
    return pl.pallas_call(
        block_finish_kernel,
        in_specs=[scalars] * 3 + [whole] * 7,
        out_specs=pl.BlockSpec(memory_space=pl.ANY),
        scratch_shapes=[
            pltpu.VMEM((blocks * rows, rank), BF16),
            pltpu.VMEM((blocks * rows, cols), F32),
            pltpu.VMEM((blocks * rows, cols), BF16),
            pltpu.SemaphoreType.DMA((blocks // 2,)),
        ],
        out_shape=jax.ShapeDtypeStruct((blocks * rows, cols), BF16),
        compiler_params=PARAMS,
        name="finish",
    )(places, slots, core, total, expands, scale, mine, other, cosine, sine)


def ring_plan(parts, tokens, weights, scale, shrinks, expands, indices):
    rows, depth = tokens.shape
    tile = depth // 16
    me = lax.axis_index("tensor")
    owners_table = block_owners()
    send = lambda value, pairs: lax.ppermute(value, "tensor", pairs)
    swap = lambda value: send(value, [(i, i ^ 1) for i in range(parts)])
    out, home = ring_pairs((1, -1)), ring_pairs((-1, 1))

    half = depth // 2
    hs, counts = [], []
    streamed = depth - KEEP * tile

    def multiply(xs, total, ranked):
        total, h = block_product(xs, weights, factors, 0, depth, tile, total, sum(counts), ranked)
        hs.extend(h)
        counts.append(len(xs))
        return total

    streams = [send(tokens, out), None]
    own, raw = [tokens, swap(tokens)], [shrinks[0], swap(shrinks[0])]
    part = 2 * tile
    total, _ = block_product(own, weights, None, 0, part, tile, None, 0, False)
    second, total = lax.optimization_barrier((tokens, total))
    streams[1] = send(second, home)
    total, _ = block_product(own, weights, None, part, depth, tile, total, 0, False)
    factors = turn(raw)
    hs, total = lax.optimization_barrier(([some_ranks(tokens, factors)], total))
    counts.append(len(own))

    def make_tables(me, indices):
        segment_slot, cosine, sine = small_tables(*indices, parts * rows)
        owners = jnp.asarray(owners_table)[me]
        places = jnp.asarray(np.argsort(owners_table, axis=1).astype(np.int32))[me]
        slots = jnp.concatenate([segment_slot, jnp.stack([me, me ^ 1]).astype(jnp.int32)])
        core = (me % 2)[None].astype(jnp.int32)
        return owners, places, slots, core, segment_slot, cosine, sine

    blocks, hops = [], 2 * ROUNDS - 1
    totals = [total] * 2
    for hop in range(hops):
        arrived, _ = lax.optimization_barrier((streams[hop % 2], totals[hop if hop % 2 else hop + 1]))
        if hop + 2 < hops:
            streams[hop % 2] = send(arrived, home if hop % 2 else out)
        if hop % 2:
            late = [arrived, swap(arrived)]
            total = multiply(blocks, total, hop < hops - 2)
            blocks = late
        else:
            blocks += [arrived, swap(arrived)]
        if hop == hops - 3:
            early = [some_ranks(part, factors) for part in blocks[::2]]
            early, total = lax.optimization_barrier((early, total))
        if hop == hops - 2:
            hs += early
            last, _ = lax.optimization_barrier((arrived, total))
            hs.append(some_ranks(last, factors))
            hs, total = lax.optimization_barrier((hs, total))
        if hop == 3:
            known, total = lax.optimization_barrier((weights, total))
            kept, total = lax.optimization_barrier((keep_weights(known, streamed), total))
        if hop == 1:
            known, total = lax.optimization_barrier(((me, indices), total))
            tables, total = lax.optimization_barrier((make_tables(*known), total))
        totals.append(total)
    held = sum(counts)
    owners, places, slots, core, segment_slot, cosine, sine = tables
    h = rank_terms(owners, slots, blocks[2:3], factors, hs)
    beside = lambda step: send(h, [(i, i ^ step) for i in range(parts)])

    def last_product(low, high, total, **more):
        xs, _ = lax.optimization_barrier((blocks, h))
        return block_product(xs, weights, factors, low, high, tile, total, held, False, **more)[0]

    middle = streamed // (2 * tile) * tile
    near = [beside(step) for step in (2, 4, 6)]
    near, total = lax.optimization_barrier((near, last_product(0, middle, total, kept=kept)))
    h = h + near[0] + near[1] + near[2]
    far = [beside(step) for step in (8, 1, 9)]
    far, total = lax.optimization_barrier((far, last_product(middle, streamed, total, fresh=False)))
    mine, other = h + far[0], far[1] + far[2]
    return block_finish(places, segment_slot, core, total, expands, scale, mine, other, cosine, sine)


def body(parts, tokens, weight_codes, column_scale, shrink_store, expand_store, row_adapter, placement, document_lengths):
    rows = tokens.shape[0]
    total_rows = rows * parts
    shrinks = jnp.swapaxes(shrink_store, 1, 2)
    expands = jnp.swapaxes(expand_store, 1, 2)
    ring = parts == 2 * len(SNAKE) and rows % 16 == 0 and shrinks.shape[0] == 1 and total_rows % (2 * SEG) == 0
    ring = ring and shrinks.shape[1] == 64 and tokens.shape[1] % 2048 == 0
    plan = ring_plan if ring else gather_plan
    indices = (row_adapter, placement, document_lengths)
    return plan(parts, tokens, weight_codes, column_scale[None, :], shrinks, expands, indices)


def solution(mesh):
    placed = (
        P(("groups", "tensor"), None),
        P(None, "tensor"),
        P("tensor"),
        P(("groups", "tensor"), None, None),
        P("groups", "tensor", None),
        P("groups"),
        P("groups"),
        P("groups"),
    )
    return jax.shard_map(
        functools.partial(body, mesh.shape["tensor"]),
        mesh=mesh,
        in_specs=placed,
        out_specs=P("groups", "tensor"),
        check_vma=False,
    )
```
